32 devices in a mesh: segment: 4 (over y, x), dp: 8 (over z, core).
Axes of the slice: x: 2, y: 2, z: 4, core: 2. Of those that a mesh axis runs over, the one named last changes fastest.
Arguments:
- inputs: bfloat16 [8, 8, 576, 128], P('segment', 'dp'), may hold values from -6 to 6
- grid_size: int32 [8, 8, 2], P(None, 'dp'), may hold values from 12 to 24, as said below
- keep_mask: int32 [8, 8, 4], P(None, 'dp'), may hold values 0 or 1
- cotangent: bfloat16 [8, 8, 576, 128], P('segment', 'dp'), may hold values from -6 to 6
- norm_gain: float32 [2, 4, 128], replicated, may hold values from 0.5 to 1.5
- norm_shift: float32 [2, 4, 128], replicated, may hold values from -1.5 to 1.5
- query_weight: bfloat16 [2, 128, 128], replicated, may hold values from -0.5 to 0.5
- query_bias: float32 [2, 128], replicated, may hold values from -1.5 to 1.5
- pool_four: bfloat16 [2, 2048, 128], replicated, may hold values from -0.125 to 0.125
- pool_two: bfloat16 [2, 512, 128], replicated, may hold values from -0.25 to 0.25
- keyval_weight: bfloat16 [2, 2, 128, 128], replicated, may hold values from -0.5 to 0.5
- value_bias: float32 [2, 2, 64], replicated, may hold values from -1.5 to 1.5
- local_kernel: float32 [2, 2, 9, 64], replicated, may hold values from -1 to 1
- proj_weight: bfloat16 [2, 128, 128], replicated, may hold values from -1.5 to 1.5
- proj_bias: float32 [2, 128], replicated, may hold values from -1.5 to 1.5
- hidden_weight: bfloat16 [2, 128, 1024], replicated, may hold values from -0.5 to 0.5
- hidden_bias: float32 [2, 1024], replicated, may hold values from -1.5 to 1.5
- mixer_kernel: float32 [2, 9, 1024], replicated, may hold values from -1 to 1
- mixer_bias: float32 [2, 1024], replicated, may hold values from -1.5 to 1.5
- output_weight: bfloat16 [2, 1024, 128], replicated, may hold values from -0.1875 to 0.1875
- output_bias: float32 [2, 128], replicated, may hold values from -1.5 to 1.5
Outputs:
- outputs: bfloat16 [8, 8, 576, 128], P('segment', 'dp')
- input_grad: bfloat16 [8, 8, 576, 128], P('segment', 'dp')
- grad_norm_gain: float32 [2, 4, 128], replicated
- grad_norm_shift: float32 [2, 4, 128], replicated
- grad_query_weight: float32 [2, 128, 128], replicated
- grad_query_bias: float32 [2, 128], replicated
- grad_pool_four: float32 [2, 2048, 128], replicated
- grad_pool_two: float32 [2, 512, 128], replicated
- grad_keyval_weight: float32 [2, 2, 128, 128], replicated
- grad_value_bias: float32 [2, 2, 64], replicated
- grad_local_kernel: float32 [2, 2, 9, 64], replicated
- grad_proj_weight: float32 [2, 128, 128], replicated
- grad_proj_bias: float32 [2, 128], replicated
- grad_hidden_weight: float32 [2, 128, 1024], replicated
- grad_hidden_bias: float32 [2, 1024], replicated
- grad_mixer_kernel: float32 [2, 9, 1024], replicated
- grad_mixer_bias: float32 [2, 1024], replicated
- grad_output_weight: float32 [2, 1024, 128], replicated
- grad_output_bias: float32 [2, 128], replicated
The draws below stay inside these ranges and needn't reach their ends.
Inputs may be any that keep to these rules, and one draw needn't show every extreme that they name: `grid_size`: rows then columns of valid patches, top-left aligned; for every image one of the two equals 24.
All inputs are finite; a program needn't handle non-finite values. No bound on the sum of `keep_mask` on one device may be relied on, other than what follows from the above.
Results may differ from the reference program's by a relative error of at most 0.019.
Values may be sent and summed in bfloat16 or wider, within the bound.
A program may use at most 256 MiB of HBM per device.

```python
import jax
import jax.numpy as jnp
from jax import lax

C = 128
HEADS = 4
FF = 1024
GRID = 24
BLOCKS = 2
MICRO = 8
IMG_DEV = 1
IMAGES = 8
N_DP = 8


def draw_grid_size(key, part):
    key = jax.random.fold_in(key, 11)
    key_one, key_two = jax.random.split(key)
    shorter = jax.random.randint(key_one, (MICRO, IMAGES), GRID // 2, GRID + 1)
    landscape = jax.random.randint(key_two, (MICRO, IMAGES), 0, 2)
    height = jnp.where(landscape == 0, GRID, shorter)
    across = jnp.where(landscape == 0, shorter, GRID)
    return jnp.stack([height, across], axis=-1).astype(jnp.int32)


def with_ends(array, key, low, top_value):
    longest = array.shape.index(max(array.shape))
    spots = []
    for shift in (0, 1):
        where = [jax.random.randint(jax.random.fold_in(key, axis), (), 0, length) for axis, length in enumerate(array.shape)]
        where[longest] = (where[longest] + shift) % array.shape[longest]
        spots.append(tuple(where))
    return array.at[spots[0]].set(low).at[spots[1]].set(top_value)


def level_of(rng, dims, cuts, low, top_value):
    level, own = 1.0, jax.random.fold_in(rng, 6)
    for position, blocks in cuts:
        draws = jnp.exp(jax.random.uniform(jax.random.fold_in(own, position), (blocks,), jnp.float32, low / len(cuts), top_value / len(cuts)))
        level = level * jnp.repeat(draws, dims[position] // blocks).reshape([-1 if axis == position else 1 for axis in range(len(dims))])
    return level


def normal_values(own_key, shape, scale, limit, cuts=(), kind=jnp.bfloat16):
    gain = level_of(own_key, shape, cuts, -0.22, 0.18) if cuts else 1.0
    entries = jax.random.normal(own_key, shape, jnp.float32) * scale * gain
    return jnp.minimum(jnp.maximum(entries, -limit), limit).astype(kind)


def setup_inputs(seed: int = 0) -> dict:
    streams_of = jax.random.split(jax.random.key(seed), 22)
    inputs = normal_values(streams_of[0], (MICRO, IMAGES, GRID * GRID, C), 1.0, 6.0, ((0, 4), (1, 8)))
    grid_size = draw_grid_size(jax.random.fold_in(streams_of[21], 71), 0)
    keep_mask = with_ends((jax.random.randint(streams_of[2], (MICRO, IMAGES, 2 * BLOCKS), 0, 4) < 3).astype(jnp.int32), jax.random.fold_in(streams_of[2], 1), 0, 1)
    cotangent = normal_values(streams_of[3], (MICRO, IMAGES, GRID * GRID, C), 1.0, 6.0, ((0, 4), (1, 8)))
    norm_gain = jnp.clip(1.0 + 0.1 * jax.random.normal(streams_of[4], (BLOCKS, 4, C), jnp.float32), 0.5, 1.5)
    norm_shift = normal_values(streams_of[5], (BLOCKS, 4, C), 0.3, 1.5, (), jnp.float32)
    query_weight = normal_values(streams_of[6], (BLOCKS, C, C), C ** -0.5, 0.5)
    query_bias = normal_values(streams_of[7], (BLOCKS, C), 0.3, 1.5, (), jnp.float32)
    pool_four = normal_values(streams_of[8], (BLOCKS, 16 * C, C), (16 * C) ** -0.5, 0.125)
    pool_two = normal_values(streams_of[9], (BLOCKS, 4 * C, C), (4 * C) ** -0.5, 0.25)
    keyval_weight = normal_values(streams_of[10], (BLOCKS, 2, C, C), C ** -0.5, 0.5)
    value_bias = normal_values(streams_of[11], (BLOCKS, 2, C // 2), 0.3, 1.5, (), jnp.float32)
    local_kernel = normal_values(streams_of[12], (BLOCKS, 2, 9, C // 2), 0.2, 1.0, (), jnp.float32)
    proj_weight = normal_values(streams_of[13], (BLOCKS, C, C), (C // 8) ** -0.5, 1.5)
    proj_bias = normal_values(streams_of[14], (BLOCKS, C), 0.3, 1.5, (), jnp.float32)
    hidden_weight = normal_values(streams_of[15], (BLOCKS, C, FF), C ** -0.5, 0.5)
    hidden_bias = normal_values(streams_of[16], (BLOCKS, FF), 0.3, 1.5, (), jnp.float32)
    mixer_kernel = normal_values(streams_of[17], (BLOCKS, 9, FF), 0.2, 1.0, (), jnp.float32)
    mixer_bias = normal_values(streams_of[18], (BLOCKS, FF), 0.3, 1.5, (), jnp.float32)
    output_weight = normal_values(streams_of[19], (BLOCKS, FF, C), FF ** -0.5, 0.1875)
    output_bias = normal_values(streams_of[20], (BLOCKS, C), 0.3, 1.5, (), jnp.float32)
    return {"inputs": inputs, "grid_size": grid_size, "keep_mask": keep_mask, "cotangent": cotangent, "norm_gain": norm_gain, "norm_shift": norm_shift, "query_weight": query_weight, "query_bias": query_bias, "pool_four": pool_four, "pool_two": pool_two, "keyval_weight": keyval_weight, "value_bias": value_bias, "local_kernel": local_kernel, "proj_weight": proj_weight, "proj_bias": proj_bias, "hidden_weight": hidden_weight, "hidden_bias": hidden_bias, "mixer_kernel": mixer_kernel, "mixer_bias": mixer_bias, "output_weight": output_weight, "output_bias": output_bias}


epsilon = 1e-06
keep_rate = 0.8

@jax.custom_vjp
def low(v):
    return lax.optimization_barrier(v.astype(jnp.bfloat16)).astype(jnp.float32)

@jax.custom_vjp
def low_back(v):
    return v

def low_keep(v):
    return (low(v), None)

def low_pass(kept, grad):
    return (grad,)

def back_keep(v):
    return (v, None)

def back_low(kept, grad):
    return (low(grad),)
low.defvjp(low_keep, low_pass)
low_back.defvjp(back_keep, back_low)

def matmul_low(left_in, right_in):
    return jnp.matmul(left_in, right_in, precision=lax.Precision.HIGHEST)

def score_product(queries, key_rows):
    return jnp.einsum('nhqd,nhkd->nhqk', queries, key_rows, precision=lax.Precision.HIGHEST)

def value_product(weights, values):
    return jnp.einsum('nhqk,nhkd->nhqd', weights, values, precision=lax.Precision.HIGHEST)

def layer_norm(value_in, gain_row, shift_row):
    average = lax.optimization_barrier(jnp.mean(value_in, axis=-1, keepdims=True))
    centred = value_in - average
    variance = lax.optimization_barrier(jnp.mean(centred * centred, axis=-1, keepdims=True))
    return centred * lax.rsqrt(variance + epsilon) * gain_row + shift_row

def depthwise(field_in, kernel, side_len):
    number = field_in.shape[0]
    channels = field_in.shape[-1]
    square = field_in.reshape(number, side_len, side_len, channels)
    padded = jnp.pad(square, ((0, 0), (1, 1), (1, 1), (0, 0)))
    summed = jnp.zeros_like(square)
    for offset_row in range(3):
        for offset_col in range(3):
            summed = summed + padded[:, offset_row:offset_row + side_len, offset_col:offset_col + side_len, :] * kernel[offset_row * 3 + offset_col]
    return summed.reshape(number, side_len * side_len, channels)

def to_patches(field_in, stride):
    number = field_in.shape[0]
    channels = field_in.shape[-1]
    pooled_side = GRID // stride
    grid_view = field_in.reshape(number, pooled_side, stride, pooled_side, stride, channels)
    grid_view = jnp.transpose(grid_view, (0, 1, 3, 2, 4, 5))
    return grid_view.reshape(number, pooled_side * pooled_side, stride * stride * channels)

def masks_of(sizes_here):
    number = sizes_here.shape[0]
    places = jnp.arange(GRID, dtype=jnp.int32)
    height = sizes_here[:, 0]
    across = sizes_here[:, 1]
    validity = (places[None, :, None] < height[:, None, None]) & (places[None, None, :] < across[:, None, None])
    validity = validity.reshape(number, GRID * GRID).astype(jnp.float32)
    key_masks = []
    for stride in (4, 2):
        pooled_side = GRID // stride
        pooled_at = jnp.arange(pooled_side, dtype=jnp.int32)
        tall_cells = (height + stride - 1) // stride
        wide_cells = (across + stride - 1) // stride
        inside = (pooled_at[None, :, None] < tall_cells[:, None, None]) & (pooled_at[None, None, :] < wide_cells[:, None, None])
        key_masks.append(inside.reshape(number, pooled_side * pooled_side).astype(jnp.float32))
    return (validity, key_masks)

def attention_branch(residual, validity, key_masks, scales, params):
    number, patch_count, model_width = residual.shape
    half_width = model_width // 2
    head_size = model_width // HEADS
    group_heads = HEADS // 2
    normed = low(layer_norm(residual, params[0][0], params[1][0]))
    queries = low(low_back(matmul_low(normed, params[2]) + params[3]))
    masked = normed * validity[:, :, None]
    mixed_groups = []
    for group_id in range(2):
        stride = (4, 2)[group_id]
        pooled = low_back(matmul_low(to_patches(masked, stride), params[4 + group_id]))
        key_input = low(jax.nn.gelu(layer_norm(pooled, params[0][1 + group_id], params[1][1 + group_id]), approximate=False))
        keyval = low_back(matmul_low(key_input, params[6][group_id]))
        key_rows = low(keyval[:, :, :half_width])
        inside = key_masks[group_id]
        values = (keyval[:, :, half_width:] + params[7][group_id]) * inside[:, :, None]
        values = low(values + depthwise(values, params[8][group_id], GRID // stride))
        pooled_count = values.shape[1]
        query_heads = queries[:, :, group_id * half_width:(group_id + 1) * half_width].reshape(number, patch_count, group_heads, head_size).transpose(0, 2, 1, 3)
        key_heads = key_rows.reshape(number, pooled_count, group_heads, head_size).transpose(0, 2, 1, 3)
        value_heads = values.reshape(number, pooled_count, group_heads, head_size).transpose(0, 2, 1, 3)
        scores = low_back(score_product(query_heads, key_heads)) * head_size ** (-0.5)
        scores = jnp.where(inside[:, None, None, :] > 0, scores, -1e+30)
        largest = lax.optimization_barrier(jnp.max(scores, axis=-1, keepdims=True))
        exponent = jnp.exp(scores - largest)
        weights = low(exponent / lax.optimization_barrier(jnp.sum(exponent, axis=-1, keepdims=True)))
        mixed_heads = low(low_back(value_product(weights, value_heads)))
        mixed_groups.append(mixed_heads.transpose(0, 2, 1, 3).reshape(number, patch_count, half_width))
    joined = jnp.concatenate(mixed_groups, axis=-1)
    branch = low_back(matmul_low(joined, params[9]) + params[10])
    return residual + (scales[:, None] * validity)[:, :, None] * branch

def mlp_branch(residual, validity, scales, params):
    normed = low(layer_norm(residual, params[0][3], params[1][3]))
    hidden = low_back(matmul_low(normed, params[11]) + params[12])
    mixed_field = hidden + depthwise(hidden * validity[:, :, None], params[13], GRID) + params[14]
    activated = low(jax.nn.gelu(mixed_field, approximate=False))
    branch = low_back(matmul_low(activated, params[15]) + params[16])
    return residual + (scales[:, None] * validity)[:, :, None] * branch

def pair_blocks(source, validity, key_masks, scales, params):
    current = low_back(source)
    for block_id in range(BLOCKS):
        picked = tuple((tensor[block_id] for tensor in params))
        current = attention_branch(current, validity, key_masks, scales[:, 2 * block_id], picked)
        current = low(low_back(current))
        current = mlp_branch(current, validity, scales[:, 2 * block_id + 1], picked)
        if block_id + 1 < BLOCKS:
            current = low(low_back(current))
    return low(current)

def reference(inputs, grid_size, keep_mask, cotangent, norm_gain, norm_shift, query_weight, query_bias, pool_four, pool_two, keyval_weight, value_bias, local_kernel, proj_weight, proj_bias, hidden_weight, hidden_bias, mixer_kernel, mixer_bias, output_weight, output_bias):
    params = tuple((tensor.astype(jnp.float32) for tensor in (norm_gain, norm_shift, query_weight, query_bias, pool_four, pool_two, keyval_weight, value_bias, local_kernel, proj_weight, proj_bias, hidden_weight, hidden_bias, mixer_kernel, mixer_bias, output_weight, output_bias)))
    groups = MICRO * N_DP
    shape_in = (groups, IMG_DEV, GRID * GRID, C)
    flat_inputs = inputs.reshape(shape_in)
    flat_cots = cotangent.reshape(shape_in)
    flat_sizes = grid_size.reshape(groups, IMG_DEV, 2)
    flat_keeps = keep_mask.reshape(groups, IMG_DEV, 2 * BLOCKS)

    def one_group(totals, pieces):
        block_in, sizes_here, keep_rows, block_cot = pieces
        validity, key_masks = masks_of(sizes_here)
        scales = keep_rows.astype(jnp.float32) / keep_rate

        def forward(weights, source):
            return pair_blocks(source, validity, key_masks, scales, weights)
        result, pullback = jax.vjp(forward, params, block_in.astype(jnp.float32))
        grad_params, grad_input = pullback(block_cot.astype(jnp.float32))
        totals = jax.tree.map(jnp.add, totals, grad_params)
        return (totals, (result.astype(jnp.bfloat16), grad_input.astype(jnp.bfloat16)))
    zero_grads = tuple((jnp.zeros_like(tensor) for tensor in params))
    totals, (results, grad_inputs) = lax.scan(one_group, zero_grads, (flat_inputs, flat_sizes, flat_keeps, flat_cots))
    return (results.reshape(inputs.shape), grad_inputs.reshape(inputs.shape), totals[0], totals[1], totals[2], totals[3], totals[4], totals[5], totals[6], totals[7], totals[8], totals[9], totals[10], totals[11], totals[12], totals[13], totals[14], totals[15], totals[16])
```

```python
import jax
import jax.numpy as jnp
from jax import lax
from jax.sharding import PartitionSpec as P

HEADS = 4
GRID = 24
BLOCKS = 2


epsilon = 1e-06
keep_rate = 0.8


def round_value(v):
    return lax.optimization_barrier(v.astype(jnp.bfloat16)).astype(jnp.float32)


def round_keep(v):
    return (round_value(v), None)


def round_pass(kept, grad):
    return (grad,)


def low_rule():
    rounded = jax.custom_vjp(round_value)
    rounded.defvjp(round_keep, round_pass)
    return rounded


def low(v):
    return low_rule()(v)


def same_value(v):
    return v


def same_keep(v):
    return (v, None)


def same_back(kept, grad):
    return (round_value(grad),)


def back_rule():
    passed = jax.custom_vjp(same_value)
    passed.defvjp(same_keep, same_back)
    return passed


def low_back(v):
    return back_rule()(v)


def matmul_plain(left_in, right_in):
    return jnp.dot(
        left_in.astype(jnp.bfloat16),
        right_in.astype(jnp.bfloat16),
        preferred_element_type=jnp.float32,
    )


def matmul_keep(left_in, right_in):
    return (matmul_plain(left_in, right_in), (left_in, right_in))


def matmul_back(saved, grad_in):
    left_in, right_in = saved
    inner_dim = left_in.shape[-1]
    outer_dim = right_in.shape[-1]
    grad_low = grad_in.astype(jnp.bfloat16).reshape(-1, outer_dim)
    left_low = left_in.astype(jnp.bfloat16).reshape(-1, inner_dim)
    grad_left = lax.dot_general(
        grad_low,
        right_in.astype(jnp.bfloat16),
        (((1,), (1,)), ((), ())),
        preferred_element_type=jnp.float32,
    )
    grad_right = lax.dot_general(
        left_low, grad_low, (((0,), (0,)), ((), ())), preferred_element_type=jnp.float32
    )
    return (grad_left.reshape(left_in.shape), grad_right)


def matmul_rule():
    wrapped = jax.custom_vjp(matmul_plain)
    wrapped.defvjp(matmul_keep, matmul_back)
    return wrapped


def matmul_low(left_in, right_in):
    return matmul_rule()(left_in, right_in)


def score_plain(queries, key_rows):
    return jnp.einsum(
        "nhqd,nhkd->nhqk",
        queries.astype(jnp.bfloat16),
        key_rows.astype(jnp.bfloat16),
        preferred_element_type=jnp.float32,
    )


def score_keep(queries, key_rows):
    return (score_plain(queries, key_rows), (queries, key_rows))


def score_back(saved, grad_in):
    queries, key_rows = saved
    grad_low = grad_in.astype(jnp.bfloat16)
    grad_queries = jnp.einsum(
        "nhqk,nhkd->nhqd",
        grad_low,
        key_rows.astype(jnp.bfloat16),
        preferred_element_type=jnp.float32,
    )
    grad_keys = jnp.einsum(
        "nhqk,nhqd->nhkd",
        grad_low,
        queries.astype(jnp.bfloat16),
        preferred_element_type=jnp.float32,
    )
    return (grad_queries, grad_keys)


def score_rule():
    wrapped = jax.custom_vjp(score_plain)
    wrapped.defvjp(score_keep, score_back)
    return wrapped


def score_product(queries, key_rows):
    return score_rule()(queries, key_rows)


def value_plain(weights, values):
    return jnp.einsum(
        "nhqk,nhkd->nhqd",
        weights.astype(jnp.bfloat16),
        values.astype(jnp.bfloat16),
        preferred_element_type=jnp.float32,
    )


def value_keep(weights, values):
    return (value_plain(weights, values), (weights, values))


def value_back(saved, grad_in):
    weights, values = saved
    grad_low = grad_in.astype(jnp.bfloat16)
    grad_weights = jnp.einsum(
        "nhqd,nhkd->nhqk", grad_low, values.astype(jnp.bfloat16), preferred_element_type=jnp.float32
    )
    grad_values = jnp.einsum(
        "nhqk,nhqd->nhkd",
        weights.astype(jnp.bfloat16),
        grad_low,
        preferred_element_type=jnp.float32,
    )
    return (grad_weights, grad_values)


def value_rule():
    wrapped = jax.custom_vjp(value_plain)
    wrapped.defvjp(value_keep, value_back)
    return wrapped


def value_product(weights, values):
    return value_rule()(weights, values)


def layer_norm(value_in, gain_row, shift_row):
    average = jnp.mean(value_in, axis=-1, keepdims=True)
    centred = value_in - average
    variance = jnp.mean(centred * centred, axis=-1, keepdims=True)
    return centred * lax.rsqrt(variance + epsilon) * gain_row + shift_row


def depthwise(field_in, kernel, side_len):
    number = field_in.shape[0]
    channels = field_in.shape[-1]
    square = field_in.reshape(number, side_len, side_len, channels)
    padded = jnp.pad(square, ((0, 0), (1, 1), (1, 1), (0, 0)))
    summed = jnp.zeros_like(square)
    for offset_row in range(3):
        for offset_col in range(3):
            summed = (
                summed
                + padded[
                    :, offset_row : offset_row + side_len, offset_col : offset_col + side_len, :
                ]
                * kernel[offset_row * 3 + offset_col]
            )
    return summed.reshape(number, side_len * side_len, channels)


def to_patches(field_in, stride):
    number = field_in.shape[0]
    channels = field_in.shape[-1]
    pooled_side = GRID // stride
    grid_view = field_in.reshape(number, pooled_side, stride, pooled_side, stride, channels)
    grid_view = jnp.transpose(grid_view, (0, 1, 3, 2, 4, 5))
    return grid_view.reshape(number, pooled_side * pooled_side, stride * stride * channels)


def masks_of(sizes_here):
    number = sizes_here.shape[0]
    places = jnp.arange(GRID, dtype=jnp.int32)
    height = sizes_here[:, 0]
    across = sizes_here[:, 1]
    validity = (places[None, :, None] < height[:, None, None]) & (
        places[None, None, :] < across[:, None, None]
    )
    validity = validity.reshape(number, GRID * GRID).astype(jnp.float32)
    key_masks = []
    for stride in (4, 2):
        pooled_side = GRID // stride
        pooled_at = jnp.arange(pooled_side, dtype=jnp.int32)
        tall_cells = (height + stride - 1) // stride
        wide_cells = (across + stride - 1) // stride
        inside = (pooled_at[None, :, None] < tall_cells[:, None, None]) & (
            pooled_at[None, None, :] < wide_cells[:, None, None]
        )
        key_masks.append(inside.reshape(number, pooled_side * pooled_side).astype(jnp.float32))
    return (validity, key_masks)


def attention_branch(residual, validity, key_masks, scales, params):
    number, patch_count, model_width = residual.shape
    half_width = model_width // 2
    head_size = model_width // HEADS
    group_heads = HEADS // 2
    normed = low(layer_norm(residual, params[0][0], params[1][0]))
    queries = low(low_back(matmul_low(normed, params[2]) + params[3]))
    masked = normed * validity[:, :, None]
    mixed_groups = []
    for group_id in range(2):
        stride = (4, 2)[group_id]
        pooled = low_back(matmul_low(to_patches(masked, stride), params[4 + group_id]))
        key_input = low(
            jax.nn.gelu(
                layer_norm(pooled, params[0][1 + group_id], params[1][1 + group_id]),
                approximate=False,
            )
        )
        keyval = low_back(matmul_low(key_input, params[6][group_id]))
        key_rows = low(keyval[:, :, :half_width])
        inside = key_masks[group_id]
        values = (keyval[:, :, half_width:] + params[7][group_id]) * inside[:, :, None]
        values = low(values + depthwise(values, params[8][group_id], GRID // stride))
        pooled_count = values.shape[1]
        query_heads = (
            queries[:, :, group_id * half_width : (group_id + 1) * half_width]
            .reshape(number, patch_count, group_heads, head_size)
            .transpose(0, 2, 1, 3)
        )
        key_heads = key_rows.reshape(number, pooled_count, group_heads, head_size).transpose(
            0, 2, 1, 3
        )
        value_heads = values.reshape(number, pooled_count, group_heads, head_size).transpose(
            0, 2, 1, 3
        )
        scores = low_back(score_product(query_heads, key_heads)) * head_size ** (-0.5)
        scores = jnp.where(inside[:, None, None, :] > 0, scores, -1e30)
        largest = jnp.max(scores, axis=-1, keepdims=True)
        exponent = jnp.exp(scores - largest)
        weights = low(exponent / jnp.sum(exponent, axis=-1, keepdims=True))
        mixed_heads = low(low_back(value_product(weights, value_heads)))
        mixed_groups.append(
            mixed_heads.transpose(0, 2, 1, 3).reshape(number, patch_count, half_width)
        )
    joined = jnp.concatenate(mixed_groups, axis=-1)
    branch = low_back(matmul_low(joined, params[9]) + params[10])
    return residual + (scales[:, None] * validity)[:, :, None] * branch


def mlp_branch(residual, validity, scales, params):
    normed = low(layer_norm(residual, params[0][3], params[1][3]))
    hidden = low_back(matmul_low(normed, params[11]) + params[12])
    mixed_field = hidden + depthwise(hidden * validity[:, :, None], params[13], GRID) + params[14]
    activated = low(jax.nn.gelu(mixed_field, approximate=False))
    branch = low_back(matmul_low(activated, params[15]) + params[16])
    return residual + (scales[:, None] * validity)[:, :, None] * branch


def on_device(
    inputs,
    grid_size,
    keep_mask,
    cotangent,
    norm_gain,
    norm_shift,
    query_weight,
    query_bias,
    pool_four,
    pool_two,
    keyval_weight,
    value_bias,
    local_kernel,
    proj_weight,
    proj_bias,
    hidden_weight,
    hidden_bias,
    mixer_kernel,
    mixer_bias,
    output_weight,
    output_bias,
):
    segment_id = lax.axis_index("segment")
    arrays = (
        norm_gain,
        norm_shift,
        query_weight,
        query_bias,
        pool_four,
        pool_two,
        keyval_weight,
        value_bias,
        local_kernel,
        proj_weight,
        proj_bias,
        hidden_weight,
        hidden_bias,
        mixer_kernel,
        mixer_bias,
        output_weight,
        output_bias,
    )
    params = [
        tuple(tensor[block_id].astype(jnp.float32) for tensor in arrays)
        for block_id in range(BLOCKS)
    ]
    own_count = inputs.shape[0]
    images = own_count * inputs.shape[1]
    tokens, width = inputs.shape[2:]
    source = inputs.reshape(images, tokens, width)
    cots = cotangent.reshape(images, tokens, width)
    sizes_here = lax.dynamic_slice_in_dim(grid_size, segment_id * own_count, own_count, 0)
    validity, key_masks = masks_of(sizes_here.reshape(images, 2))
    keep_rows = lax.dynamic_slice_in_dim(keep_mask, segment_id * own_count, own_count, 0)
    scales = keep_rows.reshape(images, -1).astype(jnp.float32) / keep_rate

    def block_of(block_id):
        def run(weights, stream):
            current = attention_branch(
                stream, validity, key_masks, scales[:, 2 * block_id], weights
            )
            current = low(low_back(current))
            return mlp_branch(current, validity, scales[:, 2 * block_id + 1], weights)

        return run

    stream = source.astype(jnp.float32)
    pulls = []
    for block_id in range(BLOCKS):
        stream, pull = jax.vjp(block_of(block_id), params[block_id], stream)
        stream = round_value(stream)
        pulls.append(pull)
    outputs = stream.astype(jnp.bfloat16)
    grad = cots.astype(jnp.float32)
    block_flats = [None] * BLOCKS
    for block_id in reversed(range(BLOCKS)):
        grad_params, grad = pulls[block_id](grad)
        grad = round_value(grad)
        flat = jnp.concatenate([tensor.reshape(-1) for tensor in grad_params])
        if block_id == 0:
            flat = flat.astype(jnp.bfloat16)
        block_flats[block_id] = lax.psum(flat, ("segment", "dp")).astype(jnp.float32)
    weight_grads = []
    offset = 0
    for tensor in arrays:
        length = tensor.size // BLOCKS
        pieces = [flat[offset : offset + length].reshape(tensor.shape[1:]) for flat in block_flats]
        weight_grads.append(jnp.stack(pieces))
        offset = offset + length
    return (outputs.reshape(inputs.shape), grad.astype(jnp.bfloat16).reshape(inputs.shape)) + tuple(
        weight_grads
    )


def solution(mesh):
    return jax.shard_map(
        on_device,
        mesh=mesh,
        in_specs=(
            P("segment", "dp", None, None),
            P(None, "dp", None),
            P(None, "dp", None),
            P("segment", "dp", None, None),
            P(),
            P(),
            P(),
            P(),
            P(),
            P(),
            P(),
            P(),
            P(),
            P(),
            P(),
            P(),
            P(),
            P(),
            P(),
            P(),
            P(),
        ),
        out_specs=(
            P("segment", "dp", None, None),
            P("segment", "dp", None, None),
            P(),
            P(),
            P(),
            P(),
            P(),
            P(),
            P(),
            P(),
            P(),
            P(),
            P(),
            P(),
            P(),
            P(),
            P(),
            P(),
            P(),
        ),
        check_vma=False,
    )
```

```python
import functools

import jax
import jax.numpy as jnp
import numpy as np
from jax import lax
from jax.experimental import pallas as pl
from jax.experimental.pallas import tpu as pltpu
from jax.sharding import PartitionSpec as P

GRID = 24
TOK = GRID * GRID
C = 128
FF = 1024
HEAD = 32
BLOCKS = 2
SIDES = (6, 12)
STRIDES = (4, 2)
CELLS = (48, 144)
SEGS = ((0, 48), (48, 96), (96, 240), (240, 384))
KEYS = 384
PERM = 16 * 48 + 4 * 144
TAPS = 9
UW = TAPS * C + C
CHUNK = 256
TILE = 96

R_P4, R_P2, R_KV, R_Q, R_PROJ, R_HID, R_OUT, R_BLOCK = 0, 2048, 2560, 2816, 2944, 3072, 4096, 5120
S_GAIN, S_SHIFT, S_QB, S_VB, S_PB, S_OB, S_LK, S_HB, S_MB, S_MK, S_BLOCK = (
    0,
    4,
    8,
    9,
    10,
    11,
    16,
    32,
    40,
    48,
    192,
)
R_SMALL = BLOCKS * R_BLOCK
ROWS = R_SMALL + 512

epsilon = 1e-06
keep_rate = 0.8
ROOT = HEAD**-0.5
LOG2E = 1.4426950408889634
f32, bf16 = jnp.float32, jnp.bfloat16


def block_row(block_id):
    return (BLOCKS - 1 - block_id) * R_BLOCK


def permutation():
    matrix = np.zeros((PERM, TOK), np.float32)
    base = 0
    for stride, side, cells in zip(STRIDES, SIDES, CELLS):
        for row_off in range(stride):
            for col_off in range(stride):
                for a in range(side):
                    for b in range(side):
                        token = (a * stride + row_off) * GRID + b * stride + col_off
                        matrix[base + a * side + b, token] = 1.0
                base += cells
    return matrix


def cell_places():
    places = np.full((2, sum(CELLS), 128), 99.0, np.float32)
    base = 0
    for side, cells in zip(SIDES, CELLS):
        for a in range(side):
            for b in range(side):
                places[0, base + a * side + b] = a
                places[1, base + a * side + b] = b
        base += cells
    return places


def nn(left, right):
    return jnp.dot(left, right, preferred_element_type=f32)


def nt(left, right):
    return lax.dot_general(left, right, (((1,), (1,)), ((), ())), preferred_element_type=f32)


def tn(left, right):
    return lax.dot_general(left, right, (((0,), (0,)), ((), ())), preferred_element_type=f32)


def gelu_parts(m):
    t = pl.reciprocal(1.0 + (0.3275911 * 0.5**0.5) * jnp.abs(m))
    e = jnp.exp2(m * m * (-0.5 * LOG2E))
    poly = 0.5 * 1.061405429
    for coef in (-1.453152027, 1.421413741, -0.284496736, 0.254829592):
        poly = poly * t + 0.5 * coef
    tail = poly * t * e
    phi = jnp.where(m >= 0, 1.0 - tail, tail)
    return m * phi, phi + m * e * 0.3989422804014327


def norm_parts(x):
    centred = x - jnp.mean(x, axis=-1, keepdims=True)
    scale = lax.rsqrt(jnp.mean(centred * centred, axis=-1, keepdims=True) + epsilon)
    return centred * scale, scale


def norm_back(du, xhat, scale, gain):
    dxhat = du * gain
    first = jnp.mean(dxhat, axis=-1, keepdims=True)
    second = jnp.mean(dxhat * xhat, axis=-1, keepdims=True)
    return scale * (dxhat - first - xhat * second)


def col_sum(x):
    return jnp.sum(x, axis=0, keepdims=True)


def compute_kernel(
    own,
    images,
    grid_ref,
    keep_ref,
    x_ref,
    cot_ref,
    ng,
    ns,
    qw,
    qb,
    p4w,
    p2w,
    kvw,
    vb,
    lk,
    pw,
    pb,
    hw,
    hb,
    mk,
    mb,
    ow,
    ob,
    perm,
    perm_t,
    places,
    out_ref,
    dx_ref,
    gp,
    xs,
    valid,
    sval,
    um,
    u_all,
    ut,
    wc,
    ex,
    xh_a,
    sc_a,
    xh_m,
    sc_m,
    u_a,
    q_a,
    p4,
    p2,
    xh_p,
    sc_p,
    ge_p,
    kin,
    wv,
    kb,
    vbd,
    pt,
    o_t,
    o_n,
    a_all,
    g_all,
    dm,
    db,
    db_t,
    acc,
    kmask,
    near,
    small,
    pc,
    st,
    scale_ref,
):
    n = images
    rows = n * TOK
    seg = lax.axis_index("segment")
    lane = lax.broadcasted_iota(jnp.int32, (8, 128), 1)[0:1]

    def head_lanes(h):
        return (lane >= h * HEAD) & (lane < (h + 1) * HEAD)

    def tiles(fn, total=rows, step=TILE):
        def body(t, carry):
            fn(pl.ds(pl.multiple_of(t * step, step), step))
            return carry

        lax.fori_loop(0, total // step, body, 0)

    def row(ref, j, k=None):
        return ref[j, pl.ds(k, 1), :] if k is not None else ref[pl.ds(j, 1), :]

    def shifted_rows(v, by):
        if by == 0:
            return v
        pad = jnp.zeros((abs(by), v.shape[1]), v.dtype)
        if by > 0:
            return jnp.concatenate([v[by:], pad], axis=0)
        return jnp.concatenate([pad, v[:by]], axis=0)

    col = lax.broadcasted_iota(jnp.int32, (GRID, GRID, 128), 1).reshape(TOK, 128)

    def taps_of(v):
        left = jnp.where(col > 0, pltpu.roll(v, 1, 0), 0.0)
        right = jnp.where(col < GRID - 1, pltpu.roll(v, TOK - 1, 0), 0.0)
        for row_off in range(3):
            for col_off, piece in enumerate((left, v, right)):
                yield row_off * 3 + col_off, shifted_rows(piece, (row_off - 1) * GRID)

    small[...] = jnp.zeros_like(small)
    sizes = []
    lane_row = lax.broadcasted_iota(jnp.int32, (TOK, 128), 1)
    for i in range(n):
        m_id, d_id = seg * own + i // (n // own), i % (n // own)
        high, wide = grid_ref[m_id, d_id, 0], grid_ref[m_id, d_id, 1]
        sizes.append((high, wide))
        line = lax.broadcasted_iota(jnp.int32, (GRID, GRID, 128), 0).reshape(TOK, 128)
        good = jnp.where((line < high) & (col < wide), 1.0, 0.0)
        valid[i * TOK : (i + 1) * TOK, :] = good
        for k in range(2 * BLOCKS):
            kept = keep_ref[m_id, d_id, k].astype(f32) / keep_rate
            scale_ref[i, k] = kept
        flags = jnp.where((lane_row == 16) | (lane_row == 48), 1.0, 0.0)
        for off, piece in taps_of(good):
            flags = jnp.where((lane_row == off) | (lane_row == 32 + off), piece, flags)
        for j in range(BLOCKS):
            u_all[j, i * TOK : (i + 1) * TOK, TAPS * C :] = flags.astype(bf16)
        base = 0
        for t in range(2):
            span = slice(base, base + CELLS[t])
            tall = (high + STRIDES[t] - 1) // STRIDES[t]
            across = (wide + STRIDES[t] - 1) // STRIDES[t]
            inside = (places[0, span, :] < tall.astype(f32)) & (
                places[1, span, :] < across.astype(f32)
            )
            kmask[i, span, :] = jnp.where(inside, 1.0, 0.0)
            base += CELLS[t]
    base = 0
    for t in range(2):
        span = slice(base, base + CELLS[t])
        a, b = places[0, span, :], places[1, span, :]
        for off in range(9):
            dr, dc = float(off // 3 - 1), float(off % 3 - 1)
            top = float(SIDES[t])
            ok = (a + dr >= 0) & (a + dr < top) & (b + dc >= 0) & (b + dc < top)
            near[off, span, :] = jnp.where(ok, 1.0, 0.0)
        base += CELLS[t]

    xs[...] = x_ref[...].astype(f32)

    def set_sval(k):
        for i in range(n):
            span = slice(i * TOK, (i + 1) * TOK)
            sval[span, :] = valid[span, :] * scale_ref[i, k]

    def cell_spans(t):
        start = 0 if t == 0 else n * CELLS[0]
        return [slice(start + i * CELLS[t], start + (i + 1) * CELLS[t]) for i in range(n)]

    def cells_all(t):
        return slice(0, n * CELLS[0]) if t == 0 else slice(n * CELLS[0], n * sum(CELLS))

    place_span = (slice(0, CELLS[0]), slice(CELLS[0], sum(CELLS)))
    half = lane < 64
    own_half = (half, jnp.logical_not(half))

    def near_shift(t, off):
        return ((off // 3 - 1) * SIDES[t] + off % 3 - 1) % CELLS[t]

    def attention_forward(j):
        def first(ts):
            xhat, scale = norm_parts(xs[ts, :])
            xh_a[j, ts, :] = xhat
            sc_a[j, ts, :] = jnp.broadcast_to(scale, xhat.shape)
            u_a[j, ts, :] = (xhat * row(ng, j, 0) + row(ns, j, 0)).astype(bf16)

        tiles(first)
        for i in range(n):
            span = slice(i * TOK, (i + 1) * TOK)
            u = u_a[j, span, :]
            q_a[j, span, :] = (nn(u, qw[j]) + row(qb, j)).astype(bf16)
            um[:, i * C : (i + 1) * C] = (u.astype(f32) * valid[span, :]).astype(bf16)
        pc[...] = nn(perm[...], um[...]).astype(bf16)
        base = 0
        for t, ref in enumerate((p4, p2)):
            for k in range(STRIDES[t] ** 2):
                for i in range(n):
                    ref[j, i * CELLS[t] : (i + 1) * CELLS[t], k * C : (k + 1) * C] = pc[
                        base : base + CELLS[t], i * C : (i + 1) * C
                    ]
                base += CELLS[t]
        for t, (ref, weight) in enumerate(((p4, p4w), (p2, p2w))):
            xhat, scale = norm_parts(nn(ref[j], weight[j]))
            act, slope = gelu_parts(xhat * row(ng, j, 1 + t) + row(ns, j, 1 + t))
            act = act.astype(bf16)
            span = cells_all(t)
            xh_p[j, span, :] = xhat
            sc_p[j, span, :] = jnp.broadcast_to(scale, xhat.shape)
            ge_p[j, span, :] = slope
            kin[j, span, :] = act
            keyval = nn(act, kvw[j, t])
            turned = pltpu.roll(keyval, 64, 1)
            keys, vals = (keyval, turned) if t == 0 else (turned, keyval)
            bias = jnp.concatenate([row(vb, j, 0), row(vb, j, 1)], axis=1)
            kernel = jnp.concatenate([lk[j, 0], lk[j, 1]], axis=1)
            for i in range(n):
                part = slice(i * CELLS[t], (i + 1) * CELLS[t])
                w = (vals[part] + bias) * kmask[i, place_span[t], :]
                wv[j, cell_spans(t)[i], :] = w
                v = w
                for off in range(9):
                    by = near_shift(t, off)
                    moved = pltpu.roll(w, (CELLS[t] - by) % CELLS[t], 0) if by else w
                    v = v + moved * (near[off, place_span[t], :] * kernel[off : off + 1])
                for h in (2 * t, 2 * t + 1):
                    seg_rows = slice(*SEGS[h])
                    kb[j, i, seg_rows, :] = jnp.where(head_lanes(h), keys[part], 0.0).astype(bf16)
                    vbd[j, i, seg_rows, :] = jnp.where(head_lanes(h), v, 0.0).astype(bf16)
        for i in range(n):
            span = slice(i * TOK, (i + 1) * TOK)
            st[...] = nt(kb[j, i], q_a[j, span, :])
            for h, (low, top) in enumerate(SEGS):
                mask = kmask[i, place_span[h // 2], 0:1] > 0
                for c0 in range(0, TOK, 128):
                    c1 = min(c0 + 128, TOK)
                    s = jnp.where(mask, st[low:top, c0:c1], -1e30)
                    e = jnp.exp2((s - jnp.max(s, axis=0, keepdims=True)) * (ROOT * LOG2E))
                    weight = e * pl.reciprocal(jnp.sum(e, axis=0, keepdims=True))
                    pt[j, i, low:top, c0:c1] = weight.astype(bf16)
            mixed = tn(vbd[j, i], pt[j, i])
            o_t[j, i] = mixed.astype(bf16)
            o_n[span, :] = mixed.T.astype(bf16)
        set_sval(2 * j)
        for i in range(n):
            span = slice(i * TOK, (i + 1) * TOK)
            branch = nn(o_n[span, :], pw[j]) + row(pb, j)
            xs[span, :] = (xs[span, :] + sval[span, :] * branch).astype(bf16).astype(f32)

    def build_wc(j):
        bias = row(hb, j)

        def tap(off, carry):
            factor = mk[j, pl.ds(off, 1), :] + jnp.where(off == 4, 1.0, 0.0)
            for r0 in range(0, C, 32):
                wc[j, pl.ds(pl.multiple_of(off * C + r0, 32), 32), :] = (
                    hw[j, r0 : r0 + 32, :].astype(f32) * factor
                ).astype(bf16)
            return carry

        lax.fori_loop(0, TAPS, tap, 0)
        ex[...] = jnp.zeros_like(ex)
        each = mk[j] * bias
        both = bias + row(mb, j)
        each_high = each.astype(bf16).astype(f32)
        both_high = both.astype(bf16).astype(f32)
        ex[0:9, :] = each_high
        ex[16:17, :] = both_high
        ex[32:41, :] = each - each_high
        ex[48:49, :] = both - both_high
        wc[j, TAPS * C :, :] = ex[...].astype(bf16)

    def mlp_forward(j):
        build_wc(j)

        def first(ts):
            xhat, scale = norm_parts(xs[ts, :])
            xh_m[j, ts, :] = xhat
            sc_m[j, ts, :] = jnp.broadcast_to(scale, xhat.shape)
            u = (xhat * row(ng, j, 3) + row(ns, j, 3)).astype(bf16).astype(f32)
            acc[0, ts, :] = u * valid[ts, :]

        tiles(first)
        for i in range(n):
            span = slice(i * TOK, (i + 1) * TOK)
            for off, piece in taps_of(acc[0, span, :]):
                u_all[j, span, off * C : (off + 1) * C] = piece.astype(bf16)

        def chunk(step, carry):
            cols = pl.ds(pl.multiple_of(step * CHUNK, CHUNK), CHUNK)
            for i in range(n):
                field = nn(u_all[j, i * TOK : (i + 1) * TOK, :], wc[j, :, cols])
                for r0 in range(0, TOK, 32):
                    act, slope = gelu_parts(field[r0 : r0 + 32])
                    part = slice(i * TOK + r0, i * TOK + r0 + 32)
                    a_all[j, part, cols] = act.astype(bf16)
                    g_all[j, part, cols] = slope.astype(bf16)
            return carry

        lax.fori_loop(0, FF // CHUNK, chunk, 0)
        set_sval(2 * j + 1)
        for i in range(n):
            span = slice(i * TOK, (i + 1) * TOK)
            branch = nn(a_all[j, span, :], ow[j]) + row(ob, j)
            xs[span, :] = (xs[span, :] + sval[span, :] * branch).astype(bf16).astype(f32)

    def mlp_backward(j):
        base, sb = block_row(j), j * S_BLOCK
        set_sval(2 * j + 1)

        def first(ts):
            grad = (xs[ts, :] * sval[ts, :]).astype(bf16)
            db[ts, :] = grad
            small[sb + S_OB : sb + S_OB + 1, :] += col_sum(grad.astype(f32))

        tiles(first)
        db_t[...] = db[...].T
        for off in range(TAPS + 1):
            ut[off * C : (off + 1) * C, :] = u_all[j, :, off * C : (off + 1) * C].T
        bias = row(hb, j)

        def chunk(step, carry):
            cols = pl.ds(pl.multiple_of(step * CHUNK, CHUNK), CHUNK)
            for i in range(n):
                span = slice(i * TOK, (i + 1) * TOK)
                da = nt(db[span, :], ow[j, cols, :])
                dm[span, cols] = (da * g_all[j, span, cols].astype(f32)).astype(bf16)
            dfield = dm[:, cols]
            dow = nn(db_t[...], a_all[j, :, cols])
            gp[pl.ds(pl.multiple_of(base + R_OUT + step * CHUNK, CHUNK), CHUNK), :] = dow.T.astype(
                bf16
            )
            cross = nn(ut[...], dfield)
            flag_rows = cross[TAPS * C : TAPS * C + 24]
            total = flag_rows[16:17]
            dhb = total
            weight = hw[j, :, cols].astype(f32)
            dweight = jnp.zeros((C, CHUNK), f32)
            b = hb[pl.ds(j, 1), cols]
            for off in range(TAPS):
                piece = cross[off * C : (off + 1) * C]
                factor = mk[j, off : off + 1, cols]
                flag = flag_rows[off : off + 1]
                dweight = dweight + piece * (factor + (1.0 if off == 4 else 0.0))
                dk = col_sum(piece * weight) + b * flag
                dhb = dhb + factor * flag
                for s in range(CHUNK // C):
                    at = sb + S_MK + 16 * (step * (CHUNK // C) + s) + off
                    small[pl.ds(at, 1), :] = dk[:, s * C : (s + 1) * C]
            for s in range(CHUNK // C):
                at = step * (CHUNK // C) + s
                part = slice(s * C, (s + 1) * C)
                small[pl.ds(sb + S_HB + at, 1), :] = dhb[:, part]
                small[pl.ds(sb + S_MB + at, 1), :] = total[:, part]
                gp[pl.ds(pl.multiple_of(base + R_HID + at * C, C), C), :] = dweight[
                    :, part
                ].astype(bf16)
            return carry

        lax.fori_loop(0, FF // CHUNK, chunk, 0)
        acc[...] = jnp.zeros_like(acc)
        for first_off in range(0, TAPS, 2):
            width = min(2, TAPS - first_off)
            for i in range(n):
                at = i * TOK
                moved = nt(
                    dm[at : at + TOK, :], wc[j, first_off * C : (first_off + width) * C, :]
                )
                for s in range(width):
                    off = first_off + s
                    by = (off // 3 - 1) * GRID
                    piece = moved[:, s * C : (s + 1) * C]
                    if by >= 0:
                        acc[off % 3, at + by : at + TOK, :] += piece[: TOK - by]
                    else:
                        acc[off % 3, at : at + TOK + by, :] += piece[-by:]
        for i in range(n):
            span = slice(i * TOK, (i + 1) * TOK)
            left = pltpu.roll(jnp.where(col > 0, acc[0, span, :], 0.0), TOK - 1, 0)
            right = pltpu.roll(jnp.where(col < GRID - 1, acc[2, span, :], 0.0), 1, 0)
            acc[1, span, :] = (acc[1, span, :] + left + right) * valid[span, :]

        def last(ts):
            du = acc[1, ts, :]
            xhat = xh_m[j, ts, :]
            small[sb + S_GAIN + 3 : sb + S_GAIN + 4, :] += col_sum(du * xhat)
            small[sb + S_SHIFT + 3 : sb + S_SHIFT + 4, :] += col_sum(du)
            back = norm_back(du, xhat, sc_m[j, ts, :], row(ng, j, 3))
            xs[ts, :] = (xs[ts, :] + back).astype(bf16).astype(f32)

        tiles(last)

    def attention_backward(j):
        base, sb = block_row(j), j * S_BLOCK
        set_sval(2 * j)

        def first(ts):
            grad = (xs[ts, :] * sval[ts, :]).astype(bf16)
            db[ts, :] = grad
            small[sb + S_PB : sb + S_PB + 1, :] += col_sum(grad.astype(f32))

        tiles(first)
        dproj = jnp.zeros((C, C), f32)
        kernel = jnp.concatenate([lk[j, 0], lk[j, 1]], axis=1)
        dkernel = [jnp.zeros((1, C), f32) for _ in range(9)]
        dbias = jnp.zeros((1, C), f32)
        for i in range(n):
            span = slice(i * TOK, (i + 1) * TOK)
            dproj = dproj + nn(o_t[j, i], db[span, :])
            do = nt(db[span, :], pw[j]).astype(bf16)
            st[...] = nt(vbd[j, i], do)
            dvals = nn(pt[j, i], do)
            for low, top in SEGS:
                for c0 in range(0, TOK, 128):
                    c1 = min(c0 + 128, TOK)
                    weight = pt[j, i, low:top, c0:c1].astype(f32)
                    dweight = st[low:top, c0:c1]
                    dot = jnp.sum(weight * dweight, axis=0, keepdims=True)
                    pt[j, i, low:top, c0:c1] = (weight * (dweight - dot)).astype(bf16)
            dkeys = nn(pt[j, i], q_a[j, span, :]) * ROOT
            dq = tn(kb[j, i], pt[j, i]) * ROOT
            o_n[span, :] = dq.T.astype(bf16)
            for t in range(2):
                dk = jnp.zeros((CELLS[t], C), f32)
                dv = jnp.zeros((CELLS[t], C), f32)
                for h in (2 * t, 2 * t + 1):
                    dk = dk + jnp.where(head_lanes(h), dkeys[slice(*SEGS[h])], 0.0)
                    dv = dv + jnp.where(head_lanes(h), dvals[slice(*SEGS[h])], 0.0)
                w = wv[j, cell_spans(t)[i], :]
                dw = dv
                for off in range(9):
                    by = near_shift(t, off)
                    part = dv * near[off, place_span[t], :]
                    moved = pltpu.roll(w, (CELLS[t] - by) % CELLS[t], 0) if by else w
                    dkernel[off] = dkernel[off] + col_sum(part * moved)
                    part = part * kernel[off : off + 1]
                    dw = dw + (pltpu.roll(part, by, 0) if by else part)
                dw = dw * kmask[i, place_span[t], :]
                dbias = dbias + col_sum(dw)
                if t == 0:
                    dkeyval = dk + pltpu.roll(dw, 64, 1)
                else:
                    dkeyval = pltpu.roll(dk, 64, 1) + dw
                wv[j, cell_spans(t)[i], :] = dkeyval
        gp[base + R_PROJ : base + R_PROJ + C, :] = dproj.astype(bf16)
        small[sb + S_VB : sb + S_VB + 1, :] = dbias
        for off in range(9):
            small[sb + S_LK + off : sb + S_LK + off + 1, :] = dkernel[off]
        base_perm = 0
        for t, (ref, weight) in enumerate(((p4, p4w), (p2, p2w))):
            span = cells_all(t)
            dkeyval = wv[j, span, :].astype(bf16)
            at = base + R_KV + t * C
            gp[at : at + C, :] = tn(kin[j, span, :], dkeyval).astype(bf16)
            dy = nt(dkeyval, kvw[j, t]) * ge_p[j, span, :]
            xhat = xh_p[j, span, :]
            small[sb + S_GAIN + 1 + t : sb + S_GAIN + 2 + t, :] = col_sum(dy * xhat)
            small[sb + S_SHIFT + 1 + t : sb + S_SHIFT + 2 + t, :] = col_sum(dy)
            dpool = norm_back(dy, xhat, sc_p[j, span, :], row(ng, j, 1 + t)).astype(bf16)
            at = base + (R_P4, R_P2)[t]
            for k in range(STRIDES[t] ** 2):
                gp[at + k * C : at + (k + 1) * C, :] = tn(
                    ref[j, :, k * C : (k + 1) * C], dpool
                ).astype(bf16)
                back = nt(dpool, weight[j, k * C : (k + 1) * C, :]).astype(bf16)
                for i in range(n):
                    pc[base_perm : base_perm + CELLS[t], i * C : (i + 1) * C] = back[
                        i * CELLS[t] : (i + 1) * CELLS[t]
                    ]
                base_perm += CELLS[t]
        spread = nn(perm_t[...], pc[...])
        for i in range(n):
            span = slice(i * TOK, (i + 1) * TOK)
            back = nt(o_n[span, :], qw[j])
            acc[0, span, :] = back + spread[:, i * C : (i + 1) * C] * valid[span, :]
        at = base + R_Q
        gp[at : at + C, :] = tn(u_a[j], o_n[...]).astype(bf16)

        def last(ts):
            du = acc[0, ts, :]
            xhat = xh_a[j, ts, :]
            small[sb + S_QB : sb + S_QB + 1, :] += col_sum(o_n[ts, :].astype(f32))
            small[sb + S_GAIN : sb + S_GAIN + 1, :] += col_sum(du * xhat)
            small[sb + S_SHIFT : sb + S_SHIFT + 1, :] += col_sum(du)
            back = norm_back(du, xhat, sc_a[j, ts, :], row(ng, j, 0))
            xs[ts, :] = (xs[ts, :] + back).astype(bf16).astype(f32)

        tiles(last)

    for j in range(BLOCKS):
        attention_forward(j)
        mlp_forward(j)
    out_ref[...] = xs[...].astype(bf16)
    xs[...] = cot_ref[...].astype(f32)
    for j in reversed(range(BLOCKS)):
        mlp_backward(j)
        attention_backward(j)
    dx_ref[...] = xs[...].astype(bf16)
    gp[R_SMALL:, :] = small[...].astype(bf16)


def compute(own, images, grid_size, keep_mask, x, cot, weights):
    n = images
    rows = n * TOK
    cells = n * sum(CELLS)
    vmem = pl.BlockSpec(memory_space=pltpu.VMEM)
    smem = pl.BlockSpec(memory_space=pltpu.SMEM)
    matrix = permutation()
    consts = (
        jnp.asarray(matrix, bf16),
        jnp.asarray(matrix.T, bf16),
        jnp.asarray(cell_places()),
    )
    B = BLOCKS
    scratch = [
        pltpu.VMEM((rows, C), f32),
        pltpu.VMEM((rows, C), f32),
        pltpu.VMEM((rows, C), f32),
        pltpu.VMEM((TOK, n * C), bf16),
        pltpu.VMEM((B, rows, UW), bf16),
        pltpu.VMEM((UW, rows), bf16),
        pltpu.VMEM((B, UW, FF), bf16),
        pltpu.VMEM((C, FF), f32),
        pltpu.VMEM((B, rows, C), f32),
        pltpu.VMEM((B, rows, C), f32),
        pltpu.VMEM((B, rows, C), f32),
        pltpu.VMEM((B, rows, C), f32),
        pltpu.VMEM((B, rows, C), bf16),
        pltpu.VMEM((B, rows, C), bf16),
        pltpu.VMEM((B, n * CELLS[0], 16 * C), bf16),
        pltpu.VMEM((B, n * CELLS[1], 4 * C), bf16),
        pltpu.VMEM((B, cells, C), f32),
        pltpu.VMEM((B, cells, C), f32),
        pltpu.VMEM((B, cells, C), f32),
        pltpu.VMEM((B, cells, C), bf16),
        pltpu.VMEM((B, cells, C), f32),
        pltpu.VMEM((B, n, KEYS, C), bf16),
        pltpu.VMEM((B, n, KEYS, C), bf16),
        pltpu.VMEM((B, n, KEYS, TOK), bf16),
        pltpu.VMEM((B, n, C, TOK), bf16),
        pltpu.VMEM((rows, C), bf16),
        pltpu.VMEM((B, rows, FF), bf16),
        pltpu.VMEM((B, rows, FF), bf16),
        pltpu.VMEM((rows, FF), bf16),
        pltpu.VMEM((rows, C), bf16),
        pltpu.VMEM((C, rows), bf16),
        pltpu.VMEM((3, rows, C), f32),
        pltpu.VMEM((n, sum(CELLS), C), f32),
        pltpu.VMEM((9, sum(CELLS), C), f32),
        pltpu.VMEM((ROWS - R_SMALL, C), f32),
        pltpu.VMEM((PERM, n * C), bf16),
        pltpu.VMEM((KEYS, TOK), f32),
        pltpu.SMEM((n, 2 * BLOCKS), f32),
    ]
    return pl.pallas_call(
        functools.partial(compute_kernel, own, images),
        out_shape=(
            jax.ShapeDtypeStruct((rows, C), bf16),
            jax.ShapeDtypeStruct((rows, C), bf16),
            jax.ShapeDtypeStruct((ROWS, C), bf16),
        ),
        in_specs=[smem, smem] + [vmem] * (2 + len(weights) + len(consts)),
        out_specs=(vmem, vmem, vmem),
        scratch_shapes=scratch,
        compiler_params=pltpu.CompilerParams(vmem_limit_bytes=60 * 2**20),
        name="compute",
    )(grid_size, keep_mask, x, cot, *weights, *consts)


def unpack_kernel(
    gp, gain, shift, qw, qb, p4, p2, kvw, vb, lk, pw, pb, hw, hb, mk, mb, ow, ob
):
    for j in range(BLOCKS):
        base, sb = block_row(j), R_SMALL + j * S_BLOCK
        p4[j] = gp[base + R_P4 : base + R_P2, :].astype(f32)
        p2[j] = gp[base + R_P2 : base + R_KV, :].astype(f32)
        for t in range(2):
            kvw[j, t] = gp[base + R_KV + t * C : base + R_KV + (t + 1) * C, :].astype(f32)
        qw[j] = gp[base + R_Q : base + R_PROJ, :].astype(f32)
        pw[j] = gp[base + R_PROJ : base + R_HID, :].astype(f32)
        for s in range(FF // C):
            at = base + R_HID + s * C
            hw[j, :, s * C : (s + 1) * C] = gp[at : at + C, :].astype(f32)
        ow[j] = gp[base + R_OUT : base + R_BLOCK, :].astype(f32)
        head = gp[sb : sb + 48, :].astype(f32)
        gain[j] = head[S_GAIN : S_GAIN + 4]
        shift[j] = head[S_SHIFT : S_SHIFT + 4]
        qb[j : j + 1, :] = head[S_QB : S_QB + 1]
        vb[j, 0:1, :] = head[S_VB : S_VB + 1, 0:64]
        vb[j, 1:2, :] = head[S_VB : S_VB + 1, 64:128]
        pb[j : j + 1, :] = head[S_PB : S_PB + 1]
        ob[j : j + 1, :] = head[S_OB : S_OB + 1]
        lk[j, 0] = head[S_LK : S_LK + 9, 0:64]
        lk[j, 1] = head[S_LK : S_LK + 9, 64:128]
        for s in range(FF // C):
            part = slice(s * C, (s + 1) * C)
            hb[j : j + 1, part] = head[S_HB + s : S_HB + s + 1]
            mb[j : j + 1, part] = head[S_MB + s : S_MB + s + 1]
            at = sb + S_MK + 16 * s
            mk[j, :, part] = gp[at : at + 16, :].astype(f32)[0:9]


def unpack(packed, weights):
    vmem = pl.BlockSpec(memory_space=pltpu.VMEM)
    return pl.pallas_call(
        unpack_kernel,
        out_shape=tuple(jax.ShapeDtypeStruct(w.shape, f32) for w in weights),
        in_specs=[vmem],
        out_specs=(vmem,) * len(weights),
        compiler_params=pltpu.CompilerParams(vmem_limit_bytes=40 * 2**20),
        name="unpack",
    )(packed)


def on_device(inputs, grid_size, keep_mask, cotangent, *weights):
    own, per = inputs.shape[:2]
    images = own * per
    flat = (images * TOK, C)
    outputs, input_grad, packed = compute(
        own, images, grid_size, keep_mask, inputs.reshape(flat), cotangent.reshape(flat), weights
    )
    packed = lax.psum(packed, ("segment", "dp"))
    grads = unpack(packed, weights)
    return (outputs.reshape(inputs.shape), input_grad.reshape(inputs.shape)) + tuple(grads)


def solution(mesh):
    stream = P("segment", "dp", None, None)
    picked = P(None, "dp", None)
    return jax.shard_map(
        on_device,
        mesh=mesh,
        in_specs=(stream, picked, picked, stream) + (P(),) * 17,
        out_specs=(stream, stream) + (P(),) * 17,
        check_vma=False,
    )
```

```python
import functools

import jax
import jax.numpy as jnp
import numpy as np
from jax import lax
from jax.experimental import pallas as pl
from jax.experimental.pallas import tpu as pltpu
from jax.sharding import PartitionSpec as P

GRID = 24
TOK = GRID * GRID
C = 128
FF = 1024
HEAD = 32
BLOCKS = 2
SIDES = (6, 12)
STRIDES = (4, 2)
CELLS = (48, 144)
SEGS = ((0, 48), (48, 96), (96, 240), (240, 384))
KEYS = 384
PERM = 16 * 48 + 4 * 144
TAPS = 9
UW = TAPS * C + C
CHUNK = 256
TILE = 96

R_P4, R_P2, R_KV, R_Q, R_PROJ, R_ATT = 0, 2048, 2560, 2816, 2944, 3072
R_HID, R_OUT, R_MLP = 0, 1024, 2048
ATT_AT = (R_ATT + 2 * R_MLP, 0)
MLP_AT = (R_ATT + R_MLP, R_ATT)
S_GAIN, S_SHIFT, S_QB, S_VB, S_PB, S_OB, S_LK, S_HB, S_MB, S_MK, S_BLOCK = (
    0,
    4,
    8,
    9,
    10,
    11,
    16,
    32,
    40,
    48,
    192,
)
R_SMALL = BLOCKS * (R_ATT + R_MLP)
ROWS = R_SMALL + 512
PIECES = (
    (MLP_AT[1], R_MLP),
    (ATT_AT[1], R_ATT),
    (MLP_AT[0], R_MLP),
    (ATT_AT[0], R_ATT + 512),
)

epsilon = 1e-06
keep_rate = 0.8
ROOT = HEAD**-0.5
LOG2E = 1.4426950408889634
f32, bf16 = jnp.float32, jnp.bfloat16


def permutation():
    matrix = np.zeros((PERM, TOK), np.float32)
    base = 0
    for stride, side, cells in zip(STRIDES, SIDES, CELLS):
        for row_off in range(stride):
            for col_off in range(stride):
                for a in range(side):
                    for b in range(side):
                        token = (a * stride + row_off) * GRID + b * stride + col_off
                        matrix[base + a * side + b, token] = 1.0
                base += cells
    return matrix


def cell_places():
    places = np.full((2, sum(CELLS), 128), 99.0, np.float32)
    base = 0
    for side, cells in zip(SIDES, CELLS):
        for a in range(side):
            for b in range(side):
                places[0, base + a * side + b] = a
                places[1, base + a * side + b] = b
        base += cells
    return places


def nn(left, right):
    return jnp.dot(left, right, preferred_element_type=f32)


def nt(left, right):
    return lax.dot_general(left, right, (((1,), (1,)), ((), ())), preferred_element_type=f32)


def tn(left, right):
    return lax.dot_general(left, right, (((0,), (0,)), ((), ())), preferred_element_type=f32)


def gelu_parts(m):
    t = pl.reciprocal(1.0 + (0.3275911 * 0.5**0.5) * jnp.abs(m))
    e = jnp.exp2(m * m * (-0.5 * LOG2E))
    poly = 0.5 * 1.061405429
    for coef in (-1.453152027, 1.421413741, -0.284496736, 0.254829592):
        poly = poly * t + 0.5 * coef
    tail = poly * t * e
    phi = jnp.where(m >= 0, 1.0 - tail, tail)
    return m * phi, phi + m * e * 0.3989422804014327


def norm_parts(x):
    centred = x - jnp.mean(x, axis=-1, keepdims=True)
    scale = lax.rsqrt(jnp.mean(centred * centred, axis=-1, keepdims=True) + epsilon)
    return centred * scale, scale


def norm_back(du, xhat, scale, gain):
    dxhat = du * gain
    first = jnp.mean(dxhat, axis=-1, keepdims=True)
    second = jnp.mean(dxhat * xhat, axis=-1, keepdims=True)
    return scale * (dxhat - first - xhat * second)


def col_sum(x):
    return jnp.sum(x, axis=0, keepdims=True)


def compute_kernel(
    own,
    images,
    grid_ref,
    keep_ref,
    x_ref,
    cot_ref,
    ng,
    ns,
    qw,
    qb,
    p4w,
    p2w,
    kvw,
    vb,
    lk,
    pw,
    pb,
    hw,
    hb,
    mk,
    mb,
    ow,
    ob,
    perm,
    perm_t,
    places,
    out_ref,
    dx_ref,
    gp,
    xs,
    valid,
    sval,
    um,
    u_all,
    ut,
    wc,
    ex,
    xh_a,
    sc_a,
    xh_m,
    sc_m,
    u_a,
    q_a,
    p4,
    p2,
    xh_p,
    sc_p,
    ge_p,
    kin,
    wv,
    kb,
    vbd,
    pt,
    o_t,
    o_n,
    a_all,
    g_all,
    dm,
    db,
    db_t,
    acc,
    kmask,
    near,
    small,
    pc,
    st,
    scale_ref,
):
    n = images
    rows = n * TOK
    seg = lax.axis_index("segment")
    lane = lax.broadcasted_iota(jnp.int32, (8, 128), 1)[0:1]

    def head_lanes(h):
        return (lane >= h * HEAD) & (lane < (h + 1) * HEAD)

    def tiles(fn, total=rows, step=TILE):
        def body(t, carry):
            fn(pl.ds(pl.multiple_of(t * step, step), step))
            return carry

        lax.fori_loop(0, total // step, body, 0)

    def row(ref, j, k=None):
        return ref[j, pl.ds(k, 1), :] if k is not None else ref[pl.ds(j, 1), :]

    def shifted_rows(v, by):
        if by == 0:
            return v
        pad = jnp.zeros((abs(by), v.shape[1]), v.dtype)
        if by > 0:
            return jnp.concatenate([v[by:], pad], axis=0)
        return jnp.concatenate([pad, v[:by]], axis=0)

    col = lax.broadcasted_iota(jnp.int32, (GRID, GRID, 128), 1).reshape(TOK, 128)

    def taps_of(v):
        left = jnp.where(col > 0, pltpu.roll(v, 1, 0), 0.0)
        right = jnp.where(col < GRID - 1, pltpu.roll(v, TOK - 1, 0), 0.0)
        for row_off in range(3):
            for col_off, piece in enumerate((left, v, right)):
                yield row_off * 3 + col_off, shifted_rows(piece, (row_off - 1) * GRID)

    small[...] = jnp.zeros_like(small)
    sizes = []
    lane_row = lax.broadcasted_iota(jnp.int32, (TOK, 128), 1)
    for i in range(n):
        m_id, d_id = seg * own + i // (n // own), i % (n // own)
        high, wide = grid_ref[m_id, d_id, 0], grid_ref[m_id, d_id, 1]
        sizes.append((high, wide))
        line = lax.broadcasted_iota(jnp.int32, (GRID, GRID, 128), 0).reshape(TOK, 128)
        good = jnp.where((line < high) & (col < wide), 1.0, 0.0)
        valid[i * TOK : (i + 1) * TOK, :] = good
        for k in range(2 * BLOCKS):
            kept = keep_ref[m_id, d_id, k].astype(f32) / keep_rate
            scale_ref[i, k] = kept
        flags = jnp.where((lane_row == 16) | (lane_row == 48), 1.0, 0.0)
        for off, piece in taps_of(good):
            flags = jnp.where((lane_row == off) | (lane_row == 32 + off), piece, flags)
        for j in range(BLOCKS):
            u_all[j, i * TOK : (i + 1) * TOK, TAPS * C :] = flags.astype(bf16)
        base = 0
        for t in range(2):
            span = slice(base, base + CELLS[t])
            tall = (high + STRIDES[t] - 1) // STRIDES[t]
            across = (wide + STRIDES[t] - 1) // STRIDES[t]
            inside = (places[0, span, :] < tall.astype(f32)) & (
                places[1, span, :] < across.astype(f32)
            )
            kmask[i, span, :] = jnp.where(inside, 1.0, 0.0)
            base += CELLS[t]
    base = 0
    for t in range(2):
        span = slice(base, base + CELLS[t])
        a, b = places[0, span, :], places[1, span, :]
        for off in range(9):
            dr, dc = float(off // 3 - 1), float(off % 3 - 1)
            top = float(SIDES[t])
            ok = (a + dr >= 0) & (a + dr < top) & (b + dc >= 0) & (b + dc < top)
            near[off, span, :] = jnp.where(ok, 1.0, 0.0)
        base += CELLS[t]

    xs[...] = x_ref[...].astype(f32)

    def set_sval(k):
        for i in range(n):
            span = slice(i * TOK, (i + 1) * TOK)
            sval[span, :] = valid[span, :] * scale_ref[i, k]

    def cell_spans(t):
        start = 0 if t == 0 else n * CELLS[0]
        return [slice(start + i * CELLS[t], start + (i + 1) * CELLS[t]) for i in range(n)]

    def cells_all(t):
        return slice(0, n * CELLS[0]) if t == 0 else slice(n * CELLS[0], n * sum(CELLS))

    place_span = (slice(0, CELLS[0]), slice(CELLS[0], sum(CELLS)))
    half = lane < 64
    own_half = (half, jnp.logical_not(half))

    def near_shift(t, off):
        return ((off // 3 - 1) * SIDES[t] + off % 3 - 1) % CELLS[t]

    def attention_forward(j):
        def first(ts):
            xhat, scale = norm_parts(xs[ts, :])
            xh_a[j, ts, :] = xhat
            sc_a[j, ts, :] = jnp.broadcast_to(scale, xhat.shape)
            u_a[j, ts, :] = (xhat * row(ng, j, 0) + row(ns, j, 0)).astype(bf16)

        tiles(first)
        for i in range(n):
            span = slice(i * TOK, (i + 1) * TOK)
            u = u_a[j, span, :]
            q_a[j, span, :] = (nn(u, qw[j]) + row(qb, j)).astype(bf16)
            um[:, i * C : (i + 1) * C] = (u.astype(f32) * valid[span, :]).astype(bf16)
        pc[...] = nn(perm[...], um[...]).astype(bf16)
        base = 0
        for t, ref in enumerate((p4, p2)):
            for k in range(STRIDES[t] ** 2):
                for i in range(n):
                    ref[j, i * CELLS[t] : (i + 1) * CELLS[t], k * C : (k + 1) * C] = pc[
                        base : base + CELLS[t], i * C : (i + 1) * C
                    ]
                base += CELLS[t]
        for t, (ref, weight) in enumerate(((p4, p4w), (p2, p2w))):
            xhat, scale = norm_parts(nn(ref[j], weight[j]))
            act, slope = gelu_parts(xhat * row(ng, j, 1 + t) + row(ns, j, 1 + t))
            act = act.astype(bf16)
            span = cells_all(t)
            xh_p[j, span, :] = xhat
            sc_p[j, span, :] = jnp.broadcast_to(scale, xhat.shape)
            ge_p[j, span, :] = slope
            kin[j, span, :] = act
            keyval = nn(act, kvw[j, t])
            turned = pltpu.roll(keyval, 64, 1)
            keys, vals = (keyval, turned) if t == 0 else (turned, keyval)
            bias = jnp.concatenate([row(vb, j, 0), row(vb, j, 1)], axis=1)
            kernel = jnp.concatenate([lk[j, 0], lk[j, 1]], axis=1)
            for i in range(n):
                part = slice(i * CELLS[t], (i + 1) * CELLS[t])
                w = (vals[part] + bias) * kmask[i, place_span[t], :]
                wv[j, cell_spans(t)[i], :] = w
                v = w
                for off in range(9):
                    by = near_shift(t, off)
                    moved = pltpu.roll(w, (CELLS[t] - by) % CELLS[t], 0) if by else w
                    v = v + moved * (near[off, place_span[t], :] * kernel[off : off + 1])
                for h in (2 * t, 2 * t + 1):
                    seg_rows = slice(*SEGS[h])
                    kb[j, i, seg_rows, :] = jnp.where(head_lanes(h), keys[part], 0.0).astype(bf16)
                    vbd[j, i, seg_rows, :] = jnp.where(head_lanes(h), v, 0.0).astype(bf16)
        for i in range(n):
            span = slice(i * TOK, (i + 1) * TOK)
            st[...] = nt(kb[j, i], q_a[j, span, :])
            for h, (low, top) in enumerate(SEGS):
                mask = kmask[i, place_span[h // 2], 0:1] > 0
                for c0 in range(0, TOK, 128):
                    c1 = min(c0 + 128, TOK)
                    s = jnp.where(mask, st[low:top, c0:c1], -1e30)
                    e = jnp.exp2((s - jnp.max(s, axis=0, keepdims=True)) * (ROOT * LOG2E))
                    weight = e * pl.reciprocal(jnp.sum(e, axis=0, keepdims=True))
                    pt[j, i, low:top, c0:c1] = weight.astype(bf16)
            mixed = tn(vbd[j, i], pt[j, i])
            o_t[j, i] = mixed.astype(bf16)
            o_n[span, :] = mixed.T.astype(bf16)
        set_sval(2 * j)
        for i in range(n):
            span = slice(i * TOK, (i + 1) * TOK)
            branch = nn(o_n[span, :], pw[j]) + row(pb, j)
            xs[span, :] = (xs[span, :] + sval[span, :] * branch).astype(bf16).astype(f32)

    def build_wc(j):
        bias = row(hb, j)

        def tap(off, carry):
            factor = mk[j, pl.ds(off, 1), :] + jnp.where(off == 4, 1.0, 0.0)
            for r0 in range(0, C, 32):
                wc[j, pl.ds(pl.multiple_of(off * C + r0, 32), 32), :] = (
                    hw[j, r0 : r0 + 32, :].astype(f32) * factor
                ).astype(bf16)
            return carry

        lax.fori_loop(0, TAPS, tap, 0)
        ex[...] = jnp.zeros_like(ex)
        each = mk[j] * bias
        both = bias + row(mb, j)
        each_high = each.astype(bf16).astype(f32)
        both_high = both.astype(bf16).astype(f32)
        ex[0:9, :] = each_high
        ex[16:17, :] = both_high
        ex[32:41, :] = each - each_high
        ex[48:49, :] = both - both_high
        wc[j, TAPS * C :, :] = ex[...].astype(bf16)

    def mlp_forward(j):
        build_wc(j)

        def first(ts):
            xhat, scale = norm_parts(xs[ts, :])
            xh_m[j, ts, :] = xhat
            sc_m[j, ts, :] = jnp.broadcast_to(scale, xhat.shape)
            u = (xhat * row(ng, j, 3) + row(ns, j, 3)).astype(bf16).astype(f32)
            acc[0, ts, :] = u * valid[ts, :]

        tiles(first)
        for i in range(n):
            span = slice(i * TOK, (i + 1) * TOK)
            for off, piece in taps_of(acc[0, span, :]):
                u_all[j, span, off * C : (off + 1) * C] = piece.astype(bf16)

        def chunk(step, carry):
            cols = pl.ds(pl.multiple_of(step * CHUNK, CHUNK), CHUNK)
            for i in range(n):
                field = nn(u_all[j, i * TOK : (i + 1) * TOK, :], wc[j, :, cols])
                for r0 in range(0, TOK, 32):
                    act, slope = gelu_parts(field[r0 : r0 + 32])
                    part = slice(i * TOK + r0, i * TOK + r0 + 32)
                    a_all[j, part, cols] = act.astype(bf16)
                    g_all[j, part, cols] = slope.astype(bf16)
            return carry

        lax.fori_loop(0, FF // CHUNK, chunk, 0)
        set_sval(2 * j + 1)
        for i in range(n):
            span = slice(i * TOK, (i + 1) * TOK)
            branch = nn(a_all[j, span, :], ow[j]) + row(ob, j)
            xs[span, :] = (xs[span, :] + sval[span, :] * branch).astype(bf16).astype(f32)

    def mlp_backward(j):
        base, sb = MLP_AT[j], j * S_BLOCK
        set_sval(2 * j + 1)

        def first(ts):
            grad = (xs[ts, :] * sval[ts, :]).astype(bf16)
            db[ts, :] = grad
            small[sb + S_OB : sb + S_OB + 1, :] += col_sum(grad.astype(f32))

        tiles(first)
        db_t[...] = db[...].T
        for off in range(TAPS + 1):
            ut[off * C : (off + 1) * C, :] = u_all[j, :, off * C : (off + 1) * C].T
        bias = row(hb, j)

        def chunk(step, carry):
            cols = pl.ds(pl.multiple_of(step * CHUNK, CHUNK), CHUNK)
            for i in range(n):
                span = slice(i * TOK, (i + 1) * TOK)
                da = nt(db[span, :], ow[j, cols, :])
                dm[span, cols] = (da * g_all[j, span, cols].astype(f32)).astype(bf16)
            dfield = dm[:, cols]
            dow = nn(db_t[...], a_all[j, :, cols])
            gp[pl.ds(pl.multiple_of(base + R_OUT + step * CHUNK, CHUNK), CHUNK), :] = dow.T.astype(
                bf16
            )
            cross = nn(ut[...], dfield)
            flag_rows = cross[TAPS * C : TAPS * C + 24]
            total = flag_rows[16:17]
            dhb = total
            weight = hw[j, :, cols].astype(f32)
            dweight = jnp.zeros((C, CHUNK), f32)
            b = hb[pl.ds(j, 1), cols]
            for off in range(TAPS):
                piece = cross[off * C : (off + 1) * C]
                factor = mk[j, off : off + 1, cols]
                flag = flag_rows[off : off + 1]
                dweight = dweight + piece * (factor + (1.0 if off == 4 else 0.0))
                dk = col_sum(piece * weight) + b * flag
                dhb = dhb + factor * flag
                for s in range(CHUNK // C):
                    at = sb + S_MK + 16 * (step * (CHUNK // C) + s) + off
                    small[pl.ds(at, 1), :] = dk[:, s * C : (s + 1) * C]
            for s in range(CHUNK // C):
                at = step * (CHUNK // C) + s
                part = slice(s * C, (s + 1) * C)
                small[pl.ds(sb + S_HB + at, 1), :] = dhb[:, part]
                small[pl.ds(sb + S_MB + at, 1), :] = total[:, part]
                gp[pl.ds(pl.multiple_of(base + R_HID + at * C, C), C), :] = dweight[
                    :, part
                ].astype(bf16)
            return carry

        lax.fori_loop(0, FF // CHUNK, chunk, 0)
        acc[...] = jnp.zeros_like(acc)
        for first_off in range(0, TAPS, 2):
            width = min(2, TAPS - first_off)
            for i in range(n):
                at = i * TOK
                moved = nt(
                    dm[at : at + TOK, :], wc[j, first_off * C : (first_off + width) * C, :]
                )
                for s in range(width):
                    off = first_off + s
                    by = (off // 3 - 1) * GRID
                    piece = moved[:, s * C : (s + 1) * C]
                    if by >= 0:
                        acc[off % 3, at + by : at + TOK, :] += piece[: TOK - by]
                    else:
                        acc[off % 3, at : at + TOK + by, :] += piece[-by:]
        for i in range(n):
            span = slice(i * TOK, (i + 1) * TOK)
            left = pltpu.roll(jnp.where(col > 0, acc[0, span, :], 0.0), TOK - 1, 0)
            right = pltpu.roll(jnp.where(col < GRID - 1, acc[2, span, :], 0.0), 1, 0)
            acc[1, span, :] = (acc[1, span, :] + left + right) * valid[span, :]

        def last(ts):
            du = acc[1, ts, :]
            xhat = xh_m[j, ts, :]
            small[sb + S_GAIN + 3 : sb + S_GAIN + 4, :] += col_sum(du * xhat)
            small[sb + S_SHIFT + 3 : sb + S_SHIFT + 4, :] += col_sum(du)
            back = norm_back(du, xhat, sc_m[j, ts, :], row(ng, j, 3))
            xs[ts, :] = (xs[ts, :] + back).astype(bf16).astype(f32)

        tiles(last)

    def attention_backward(j):
        base, sb = ATT_AT[j], j * S_BLOCK
        set_sval(2 * j)

        def first(ts):
            grad = (xs[ts, :] * sval[ts, :]).astype(bf16)
            db[ts, :] = grad
            small[sb + S_PB : sb + S_PB + 1, :] += col_sum(grad.astype(f32))

        tiles(first)
        dproj = jnp.zeros((C, C), f32)
        kernel = jnp.concatenate([lk[j, 0], lk[j, 1]], axis=1)
        dkernel = [jnp.zeros((1, C), f32) for _ in range(9)]
        dbias = jnp.zeros((1, C), f32)
        for i in range(n):
            span = slice(i * TOK, (i + 1) * TOK)
            dproj = dproj + nn(o_t[j, i], db[span, :])
            do = nt(db[span, :], pw[j]).astype(bf16)
            st[...] = nt(vbd[j, i], do)
            dvals = nn(pt[j, i], do)
            for low, top in SEGS:
                for c0 in range(0, TOK, 128):
                    c1 = min(c0 + 128, TOK)
                    weight = pt[j, i, low:top, c0:c1].astype(f32)
                    dweight = st[low:top, c0:c1]
                    dot = jnp.sum(weight * dweight, axis=0, keepdims=True)
                    pt[j, i, low:top, c0:c1] = (weight * (dweight - dot)).astype(bf16)
            dkeys = nn(pt[j, i], q_a[j, span, :]) * ROOT
            dq = tn(kb[j, i], pt[j, i]) * ROOT
            o_n[span, :] = dq.T.astype(bf16)
            for t in range(2):
                dk = jnp.zeros((CELLS[t], C), f32)
                dv = jnp.zeros((CELLS[t], C), f32)
                for h in (2 * t, 2 * t + 1):
                    dk = dk + jnp.where(head_lanes(h), dkeys[slice(*SEGS[h])], 0.0)
                    dv = dv + jnp.where(head_lanes(h), dvals[slice(*SEGS[h])], 0.0)
                w = wv[j, cell_spans(t)[i], :]
                dw = dv
                for off in range(9):
                    by = near_shift(t, off)
                    part = dv * near[off, place_span[t], :]
                    moved = pltpu.roll(w, (CELLS[t] - by) % CELLS[t], 0) if by else w
                    dkernel[off] = dkernel[off] + col_sum(part * moved)
                    part = part * kernel[off : off + 1]
                    dw = dw + (pltpu.roll(part, by, 0) if by else part)
                dw = dw * kmask[i, place_span[t], :]
                dbias = dbias + col_sum(dw)
                if t == 0:
                    dkeyval = dk + pltpu.roll(dw, 64, 1)
                else:
                    dkeyval = pltpu.roll(dk, 64, 1) + dw
                wv[j, cell_spans(t)[i], :] = dkeyval
        gp[base + R_PROJ : base + R_PROJ + C, :] = dproj.astype(bf16)
        small[sb + S_VB : sb + S_VB + 1, :] = dbias
        for off in range(9):
            small[sb + S_LK + off : sb + S_LK + off + 1, :] = dkernel[off]
        base_perm = 0
        for t, (ref, weight) in enumerate(((p4, p4w), (p2, p2w))):
            span = cells_all(t)
            dkeyval = wv[j, span, :].astype(bf16)
            at = base + R_KV + t * C
            gp[at : at + C, :] = tn(kin[j, span, :], dkeyval).astype(bf16)
            dy = nt(dkeyval, kvw[j, t]) * ge_p[j, span, :]
            xhat = xh_p[j, span, :]
            small[sb + S_GAIN + 1 + t : sb + S_GAIN + 2 + t, :] = col_sum(dy * xhat)
            small[sb + S_SHIFT + 1 + t : sb + S_SHIFT + 2 + t, :] = col_sum(dy)
            dpool = norm_back(dy, xhat, sc_p[j, span, :], row(ng, j, 1 + t)).astype(bf16)
            at = base + (R_P4, R_P2)[t]
            for k in range(STRIDES[t] ** 2):
                gp[at + k * C : at + (k + 1) * C, :] = tn(
                    ref[j, :, k * C : (k + 1) * C], dpool
                ).astype(bf16)
                back = nt(dpool, weight[j, k * C : (k + 1) * C, :]).astype(bf16)
                for i in range(n):
                    pc[base_perm : base_perm + CELLS[t], i * C : (i + 1) * C] = back[
                        i * CELLS[t] : (i + 1) * CELLS[t]
                    ]
                base_perm += CELLS[t]
        spread = nn(perm_t[...], pc[...])
        for i in range(n):
            span = slice(i * TOK, (i + 1) * TOK)
            back = nt(o_n[span, :], qw[j])
            acc[0, span, :] = back + spread[:, i * C : (i + 1) * C] * valid[span, :]
        at = base + R_Q
        gp[at : at + C, :] = tn(u_a[j], o_n[...]).astype(bf16)

        def last(ts):
            du = acc[0, ts, :]
            xhat = xh_a[j, ts, :]
            small[sb + S_QB : sb + S_QB + 1, :] += col_sum(o_n[ts, :].astype(f32))
            small[sb + S_GAIN : sb + S_GAIN + 1, :] += col_sum(du * xhat)
            small[sb + S_SHIFT : sb + S_SHIFT + 1, :] += col_sum(du)
            back = norm_back(du, xhat, sc_a[j, ts, :], row(ng, j, 0))
            xs[ts, :] = (xs[ts, :] + back).astype(bf16).astype(f32)

        tiles(last)

    for j in range(BLOCKS):
        attention_forward(j)
        mlp_forward(j)
    out_ref[...] = xs[...].astype(bf16)
    xs[...] = cot_ref[...].astype(f32)
    for j in reversed(range(BLOCKS)):
        mlp_backward(j)
        attention_backward(j)
    dx_ref[...] = xs[...].astype(bf16)
    gp[R_SMALL:, :] = small[...].astype(bf16)


def compute(own, images, grid_size, keep_mask, x, cot, weights):
    n = images
    rows = n * TOK
    cells = n * sum(CELLS)
    vmem = pl.BlockSpec(memory_space=pltpu.VMEM)
    smem = pl.BlockSpec(memory_space=pltpu.SMEM)
    matrix = permutation()
    consts = (
        jnp.asarray(matrix, bf16),
        jnp.asarray(matrix.T, bf16),
        jnp.asarray(cell_places()),
    )
    B = BLOCKS
    scratch = [
        pltpu.VMEM((rows, C), f32),
        pltpu.VMEM((rows, C), f32),
        pltpu.VMEM((rows, C), f32),
        pltpu.VMEM((TOK, n * C), bf16),
        pltpu.VMEM((B, rows, UW), bf16),
        pltpu.VMEM((UW, rows), bf16),
        pltpu.VMEM((B, UW, FF), bf16),
        pltpu.VMEM((C, FF), f32),
        pltpu.VMEM((B, rows, C), f32),
        pltpu.VMEM((B, rows, C), f32),
        pltpu.VMEM((B, rows, C), f32),
        pltpu.VMEM((B, rows, C), f32),
        pltpu.VMEM((B, rows, C), bf16),
        pltpu.VMEM((B, rows, C), bf16),
        pltpu.VMEM((B, n * CELLS[0], 16 * C), bf16),
        pltpu.VMEM((B, n * CELLS[1], 4 * C), bf16),
        pltpu.VMEM((B, cells, C), f32),
        pltpu.VMEM((B, cells, C), f32),
        pltpu.VMEM((B, cells, C), f32),
        pltpu.VMEM((B, cells, C), bf16),
        pltpu.VMEM((B, cells, C), f32),
        pltpu.VMEM((B, n, KEYS, C), bf16),
        pltpu.VMEM((B, n, KEYS, C), bf16),
        pltpu.VMEM((B, n, KEYS, TOK), bf16),
        pltpu.VMEM((B, n, C, TOK), bf16),
        pltpu.VMEM((rows, C), bf16),
        pltpu.VMEM((B, rows, FF), bf16),
        pltpu.VMEM((B, rows, FF), bf16),
        pltpu.VMEM((rows, FF), bf16),
        pltpu.VMEM((rows, C), bf16),
        pltpu.VMEM((C, rows), bf16),
        pltpu.VMEM((3, rows, C), f32),
        pltpu.VMEM((n, sum(CELLS), C), f32),
        pltpu.VMEM((9, sum(CELLS), C), f32),
        pltpu.VMEM((ROWS - R_SMALL, C), f32),
        pltpu.VMEM((PERM, n * C), bf16),
        pltpu.VMEM((KEYS, TOK), f32),
        pltpu.SMEM((n, 2 * BLOCKS), f32),
    ]
    return pl.pallas_call(
        functools.partial(compute_kernel, own, images),
        out_shape=(
            jax.ShapeDtypeStruct((rows, C), bf16),
            jax.ShapeDtypeStruct((rows, C), bf16),
            jax.ShapeDtypeStruct((ROWS, C), bf16),
        ),
        in_specs=[smem, smem] + [vmem] * (2 + len(weights) + len(consts)),
        out_specs=(vmem, vmem, vmem),
        scratch_shapes=scratch,
        compiler_params=pltpu.CompilerParams(vmem_limit_bytes=60 * 2**20),
        name="compute",
    )(grid_size, keep_mask, x, cot, *weights, *consts)


class Summed:
    STEPS = 7

    def __init__(self, place, piece, base, count, refs):
        self.seg, self.dp, self.segments, self.inner, self.outer = place
        self.piece, self.base, self.count = piece, base, count
        (
            self.src,
            self.half_in,
            self.quarter_in,
            self.part_in,
            self.whole_in,
            self.own,
            self.total,
            self.send,
            self.recv,
        ) = refs
        self.core, rest = self.dp % 2, self.dp // 2
        self.part, self.group = rest % self.inner, rest // self.inner
        self.half = count // 2
        self.quarter = self.half // self.segments
        self.share = self.quarter // self.inner
        self.started = []

    def span(self, start, size):
        return pl.ds(pl.multiple_of(start, 16), size)

    def device(self, seg=None, core=None, part=None, group=None):
        seg = self.seg if seg is None else seg
        core = self.core if core is None else core
        part = self.part if part is None else part
        group = self.group if group is None else group
        return (seg, (group * self.inner + part) * 2 + core)

    def copy(self, slot, src, dst, device):
        made = pltpu.make_async_remote_copy(
            src_ref=src,
            dst_ref=dst,
            send_sem=self.send.at[self.piece, slot],
            recv_sem=self.recv.at[self.piece, slot],
            device_id=device,
            device_id_type=pl.DeviceIdType.MESH,
        )
        made.start()
        self.started.append(made)
        return made

    def half_at(self, core):
        return self.span(self.base + core * self.half, self.half)

    def own_at(self, seg, part=None):
        start = self.base // 2 + seg * self.quarter
        if part is None:
            return self.span(start, self.quarter)
        return self.span(start + part * self.share, self.share)

    def total_at(self, seg=None, part=None):
        start = self.base + self.core * self.half
        if seg is None:
            return self.span(start, self.half)
        start = start + seg * self.quarter
        if part is None:
            return self.span(start, self.quarter)
        return self.span(start + part * self.share, self.share)

    def step(self, k):
        (
            self.pair_out,
            self.segment_out,
            self.part_out,
            self.part_back,
            self.segment_back,
            self.pair_back,
            self.finish,
        )[k]()

    def pair_out(self):
        self.waits = [
            self.copy(
                0,
                self.src.at[self.half_at(1 - self.core), :],
                self.half_in.at[self.span(self.base // 2, self.half), :],
                self.device(core=1 - self.core),
            )
        ]

    def arrived(self):
        for made in self.waits:
            made.wait_recv()
        self.waits = []

    def add(self, dst, first, others, count):
        step = 64 if count % 64 == 0 else 16

        def body(t, carry):
            at = t * step
            total = first[0][self.span(first[1] + at, step), :].astype(f32)
            for ref, start in others:
                total = total + ref[self.span(start + at, step), :].astype(f32)
            dst[0][self.span(dst[1] + at, step), :] = total.astype(bf16)
            return carry

        lax.fori_loop(0, count // step, body, 0)

    def segment_out(self):
        self.arrived()
        own = self.base // 2
        self.add(
            (self.own, own),
            (self.src, self.base + self.core * self.half),
            [(self.half_in, own)],
            self.half,
        )
        at = self.span(self.base // 2 // self.segments, self.quarter)
        for d in range(1, self.segments):
            to = self.seg ^ d
            self.waits.append(
                self.copy(
                    d,
                    self.own.at[self.own_at(to), :],
                    self.quarter_in.at[d - 1, at, :],
                    self.device(seg=to),
                )
            )

    def part_out(self):
        self.arrived()
        start = self.base // 2 + self.seg * self.quarter
        at = self.base // 2 // self.segments
        others = [(self.quarter_in.at[d], at) for d in range(self.segments - 1)]
        self.add((self.own, start), (self.own, start), others, self.quarter)
        at = self.span(self.base // 2 // self.segments // self.inner, self.share)
        for d in range(1, self.inner):
            to = self.part ^ d
            self.waits.append(
                self.copy(
                    self.segments + d - 1,
                    self.own.at[self.own_at(self.seg, to), :],
                    self.part_in.at[d - 1, at, :],
                    self.device(part=to),
                )
            )

    def part_back(self):
        self.arrived()
        start = self.base // 2 + self.seg * self.quarter + self.part * self.share
        at = self.base // 2 // self.segments // self.inner
        others = [(self.part_in.at[d], at) for d in range(self.inner - 1)]
        into = self.base + self.core * self.half + self.seg * self.quarter + self.part * self.share
        slot = self.segments + self.inner - 1
        if self.outer > 1:
            self.add((self.own, start), (self.own, start), others, self.share)
            span = self.span(at, self.share)
            for d in range(1, self.outer):
                self.waits.append(
                    self.copy(
                        slot + d - 1,
                        self.own.at[self.own_at(self.seg, self.part), :],
                        self.whole_in.at[d - 1, span, :],
                        self.device(group=self.group ^ d),
                    )
                )
            self.arrived()
            others = [(self.whole_in.at[d], at) for d in range(self.outer - 1)]
            slot += self.outer - 1
        self.add((self.total, into), (self.own, start), others, self.share)
        at = self.total_at(self.seg, self.part)
        for d in range(1, self.inner):
            made = self.copy(
                slot + d - 1, self.total.at[at, :], self.total.at[at, :], self.device(part=self.part ^ d)
            )
            self.waits.append(made)
        self.slot = slot + self.inner - 1

    def segment_back(self):
        self.arrived()
        at = self.total_at(self.seg)
        for d in range(1, self.segments):
            made = self.copy(
                self.slot + d - 1,
                self.total.at[at, :],
                self.total.at[at, :],
                self.device(seg=self.seg ^ d),
            )
            self.waits.append(made)
        self.slot += self.segments - 1

    def pair_back(self):
        self.arrived()
        at = self.total_at()
        self.waits.append(
            self.copy(
                self.slot, self.total.at[at, :], self.total.at[at, :], self.device(core=1 - self.core)
            )
        )

    def finish(self):
        self.arrived()

    def drain(self):
        for made in self.started:
            made.wait_send()


def slots_of(segments, inner, outer):
    return 2 + 2 * (segments - 1) + 2 * (inner - 1) + (outer - 1)


def greet(seg, dp, segments, inner, outer):
    barrier = pltpu.get_barrier_semaphore()
    core, part, group = dp % 2, dp // 2 % inner, dp // 2 // inner
    peers = [(seg, dp + 1 - 2 * core)]
    peers += [(seg ^ d, dp) for d in range(1, segments)]
    peers += [(seg, (group * inner + (part ^ d)) * 2 + core) for d in range(1, inner)]
    peers += [(seg, ((group ^ d) * inner + part) * 2 + core) for d in range(1, outer)]
    for peer in peers:
        pl.semaphore_signal(
            barrier, inc=1, device_id=peer, device_id_type=pl.DeviceIdType.MESH
        )
    pl.semaphore_wait(barrier, len(peers))


def sum_kernel(sizes, src, total, half_in, quarter_in, part_in, whole_in, own, send, recv):
    seg, dp = lax.axis_index("segment"), lax.axis_index("dp")
    greet(seg, dp, *sizes)
    refs = (src, half_in, quarter_in, part_in, whole_in, own, total, send, recv)
    pieces = [
        Summed((seg, dp) + sizes, p, base, count, refs) for p, (base, count) in enumerate(PIECES)
    ]
    for t in range(Summed.STEPS + len(pieces) - 1):
        for p, piece in enumerate(pieces):
            if 0 <= t - p < Summed.STEPS:
                piece.step(t - p)
    for piece in pieces:
        piece.drain()


def sum_scratch(sizes):
    segments, inner, outer = sizes
    quarter = ROWS // 2 // segments
    share = quarter // inner
    slots = slots_of(*sizes)
    return [
        pltpu.VMEM((ROWS // 2, C), bf16),
        pltpu.VMEM((segments - 1, quarter, C), bf16),
        pltpu.VMEM((inner - 1, share, C), bf16),
        pltpu.VMEM((max(outer - 1, 1), share, C), bf16),
        pltpu.VMEM((ROWS // 2, C), bf16),
        pltpu.SemaphoreType.DMA((len(PIECES), slots)),
        pltpu.SemaphoreType.DMA((len(PIECES), slots)),
    ]


def summed(packed):
    segments, pairs = lax.axis_size("segment"), lax.axis_size("dp") // 2
    inner = min(pairs, 4)
    sizes = (segments, inner, pairs // inner)
    vmem = pl.BlockSpec(memory_space=pltpu.VMEM)
    return pl.pallas_call(
        functools.partial(sum_kernel, sizes),
        out_shape=jax.ShapeDtypeStruct((ROWS, C), bf16),
        in_specs=[vmem],
        out_specs=vmem,
        scratch_shapes=sum_scratch(sizes),
        compiler_params=pltpu.CompilerParams(
            collective_id=0, has_side_effects=True, vmem_limit_bytes=40 * 2**20
        ),
        name="summed",
    )(packed)


def unpack_kernel(
    gp, gain, shift, qw, qb, p4, p2, kvw, vb, lk, pw, pb, hw, hb, mk, mb, ow, ob
):
    for j in range(BLOCKS):
        att, mlp, sb = ATT_AT[j], MLP_AT[j], R_SMALL + j * S_BLOCK
        p4[j] = gp[att + R_P4 : att + R_P2, :].astype(f32)
        p2[j] = gp[att + R_P2 : att + R_KV, :].astype(f32)
        for t in range(2):
            kvw[j, t] = gp[att + R_KV + t * C : att + R_KV + (t + 1) * C, :].astype(f32)
        qw[j] = gp[att + R_Q : att + R_PROJ, :].astype(f32)
        pw[j] = gp[att + R_PROJ : att + R_ATT, :].astype(f32)
        for s in range(FF // C):
            at = mlp + R_HID + s * C
            hw[j, :, s * C : (s + 1) * C] = gp[at : at + C, :].astype(f32)
        ow[j] = gp[mlp + R_OUT : mlp + R_MLP, :].astype(f32)
        head = gp[sb : sb + 48, :].astype(f32)
        gain[j] = head[S_GAIN : S_GAIN + 4]
        shift[j] = head[S_SHIFT : S_SHIFT + 4]
        qb[j : j + 1, :] = head[S_QB : S_QB + 1]
        vb[j, 0:1, :] = head[S_VB : S_VB + 1, 0:64]
        vb[j, 1:2, :] = head[S_VB : S_VB + 1, 64:128]
        pb[j : j + 1, :] = head[S_PB : S_PB + 1]
        ob[j : j + 1, :] = head[S_OB : S_OB + 1]
        lk[j, 0] = head[S_LK : S_LK + 9, 0:64]
        lk[j, 1] = head[S_LK : S_LK + 9, 64:128]
        for s in range(FF // C):
            part = slice(s * C, (s + 1) * C)
            hb[j : j + 1, part] = head[S_HB + s : S_HB + s + 1]
            mb[j : j + 1, part] = head[S_MB + s : S_MB + s + 1]
            at = sb + S_MK + 16 * s
            mk[j, :, part] = gp[at : at + 16, :].astype(f32)[0:9]


def unpack(packed, weights):
    vmem = pl.BlockSpec(memory_space=pltpu.VMEM)
    return pl.pallas_call(
        unpack_kernel,
        out_shape=tuple(jax.ShapeDtypeStruct(w.shape, f32) for w in weights),
        in_specs=[vmem],
        out_specs=(vmem,) * len(weights),
        compiler_params=pltpu.CompilerParams(vmem_limit_bytes=40 * 2**20),
        name="unpack",
    )(packed)


def on_device(inputs, grid_size, keep_mask, cotangent, *weights):
    own, per = inputs.shape[:2]
    images = own * per
    flat = (images * TOK, C)
    outputs, input_grad, packed = compute(
        own, images, grid_size, keep_mask, inputs.reshape(flat), cotangent.reshape(flat), weights
    )
    grads = unpack(summed(packed), weights)
    return (outputs.reshape(inputs.shape), input_grad.reshape(inputs.shape)) + tuple(grads)


def solution(mesh):
    stream = P("segment", "dp", None, None)
    picked = P(None, "dp", None)
    return jax.shard_map(
        on_device,
        mesh=mesh,
        in_specs=(stream, picked, picked, stream) + (P(),) * 17,
        out_specs=(stream, stream) + (P(),) * 17,
        check_vma=False,
    )
```

```python
import functools

import jax
import jax.numpy as jnp
import numpy as np
from jax import lax
from jax.experimental import pallas as pl
from jax.experimental.pallas import tpu as pltpu
from jax.sharding import PartitionSpec as P

GRID = 24
TOK = GRID * GRID
C = 128
FF = 1024
HEAD = 32
BLOCKS = 2
SIDES = (6, 12)
STRIDES = (4, 2)
CELLS = (48, 144)
SEGS = ((0, 48), (48, 96), (96, 240), (240, 384))
KEYS = 384
PERM = 16 * 48 + 4 * 144
TAPS = 9
UW = TAPS * C + C
CHUNK = 256
TILE = 96

R_P4, R_P2, R_KV, R_Q, R_PROJ, R_ATT = 0, 2048, 2560, 2816, 2944, 3072
R_HID, R_OUT, R_MLP = 0, 1024, 2048
ATT_AT = (R_ATT + 2 * R_MLP, 0)
MLP_AT = (R_ATT + R_MLP, R_ATT)
S_GAIN, S_SHIFT, S_QB, S_VB, S_PB, S_OB, S_LK, S_HB, S_MB, S_MK, S_BLOCK = (
    0,
    4,
    8,
    9,
    10,
    11,
    16,
    32,
    40,
    48,
    192,
)
R_SMALL = BLOCKS * (R_ATT + R_MLP)
ROWS = R_SMALL + 512
PIECES = (
    (MLP_AT[1], R_MLP),
    (ATT_AT[1], R_ATT),
    (MLP_AT[0], R_MLP),
    (ATT_AT[0], R_ATT // 2),
    (ATT_AT[0] + R_ATT // 2, R_ATT // 2),
    (R_SMALL, ROWS - R_SMALL),
)

LK, MK = 8, 13

epsilon = 1e-06
keep_rate = 0.8
ROOT = HEAD**-0.5
LOG2E = 1.4426950408889634
f32, bf16 = jnp.float32, jnp.bfloat16


def permutation():
    matrix = np.zeros((PERM, TOK), np.float32)
    base = 0
    for stride, side, cells in zip(STRIDES, SIDES, CELLS):
        for row_off in range(stride):
            for col_off in range(stride):
                for a in range(side):
                    for b in range(side):
                        token = (a * stride + row_off) * GRID + b * stride + col_off
                        matrix[base + a * side + b, token] = 1.0
                base += cells
    return matrix


def cell_places():
    places = np.full((2, sum(CELLS), 128), 99.0, np.float32)
    base = 0
    for side, cells in zip(SIDES, CELLS):
        for a in range(side):
            for b in range(side):
                places[0, base + a * side + b] = a
                places[1, base + a * side + b] = b
        base += cells
    return places


def nn(left, right):
    return jnp.dot(left, right, preferred_element_type=f32)


def nt(left, right):
    return lax.dot_general(left, right, (((1,), (1,)), ((), ())), preferred_element_type=f32)


def tn(left, right):
    return lax.dot_general(left, right, (((0,), (0,)), ((), ())), preferred_element_type=f32)


def gelu_parts(m):
    t = pl.reciprocal(1.0 + (0.3275911 * 0.5**0.5) * jnp.abs(m))
    e = jnp.exp2(m * m * (-0.5 * LOG2E))
    poly = 0.5 * 1.061405429
    for coef in (-1.453152027, 1.421413741, -0.284496736, 0.254829592):
        poly = poly * t + 0.5 * coef
    tail = poly * t * e
    phi = jnp.where(m >= 0, 1.0 - tail, tail)
    return m * phi, phi + m * e * 0.3989422804014327


def norm_parts(x):
    centred = x - jnp.mean(x, axis=-1, keepdims=True)
    scale = lax.rsqrt(jnp.mean(centred * centred, axis=-1, keepdims=True) + epsilon)
    return centred * scale, scale


def norm_back(du, xhat, scale, gain):
    dxhat = du * gain
    first = jnp.mean(dxhat, axis=-1, keepdims=True)
    second = jnp.mean(dxhat * xhat, axis=-1, keepdims=True)
    return scale * (dxhat - first - xhat * second)


def col_sum(x):
    return jnp.sum(x, axis=0, keepdims=True)


class Summed:
    STEPS = 7

    def __init__(self, place, piece, base, count, refs):
        self.seg, self.dp, self.segments, self.inner, self.outer = place
        self.piece, self.base, self.count = piece, base, count
        (
            self.src,
            self.half_in,
            self.quarter_in,
            self.part_in,
            self.whole_in,
            self.own,
            self.total,
            self.send,
            self.recv,
        ) = refs
        self.core, rest = self.dp % 2, self.dp // 2
        self.part, self.group = rest % self.inner, rest // self.inner
        self.half = count // 2
        self.quarter = self.half // self.segments
        self.share = self.quarter // self.inner
        self.started = []

    def span(self, start, size):
        return pl.ds(pl.multiple_of(start, 16), size)

    def device(self, seg=None, core=None, part=None, group=None):
        seg = self.seg if seg is None else seg
        core = self.core if core is None else core
        part = self.part if part is None else part
        group = self.group if group is None else group
        return (seg, (group * self.inner + part) * 2 + core)

    def copy(self, slot, src, dst, device):
        made = pltpu.make_async_remote_copy(
            src_ref=src,
            dst_ref=dst,
            send_sem=self.send.at[self.piece, slot],
            recv_sem=self.recv.at[self.piece, slot],
            device_id=device,
            device_id_type=pl.DeviceIdType.MESH,
        )
        made.start()
        self.started.append(made)
        return made

    def half_at(self, core):
        return self.span(self.base + core * self.half, self.half)

    def own_at(self, seg, part=None):
        start = self.base // 2 + seg * self.quarter
        if part is None:
            return self.span(start, self.quarter)
        return self.span(start + part * self.share, self.share)

    def total_at(self, seg=None, part=None):
        start = self.base + self.core * self.half
        if seg is None:
            return self.span(start, self.half)
        start = start + seg * self.quarter
        if part is None:
            return self.span(start, self.quarter)
        return self.span(start + part * self.share, self.share)

    def step(self, k):
        (
            self.pair_out,
            self.segment_out,
            self.part_out,
            self.part_back,
            self.segment_back,
            self.pair_back,
            self.finish,
        )[k]()

    def pair_out(self):
        self.waits = [
            self.copy(
                0,
                self.src.at[self.half_at(1 - self.core), :],
                self.half_in.at[self.span(self.base // 2, self.half), :],
                self.device(core=1 - self.core),
            )
        ]

    def arrived(self):
        for made in self.waits:
            made.wait_recv()
        self.waits = []

    def add(self, dst, first, others, count):
        step = 64 if count % 64 == 0 else 16

        def body(t, carry):
            at = t * step
            total = first[0][self.span(first[1] + at, step), :].astype(f32)
            for ref, start in others:
                total = total + ref[self.span(start + at, step), :].astype(f32)
            dst[0][self.span(dst[1] + at, step), :] = total.astype(bf16)
            return carry

        lax.fori_loop(0, count // step, body, 0)

    def segment_out(self):
        self.arrived()
        own = self.base // 2
        self.add(
            (self.own, own),
            (self.src, self.base + self.core * self.half),
            [(self.half_in, own)],
            self.half,
        )
        at = self.span(self.base // 2 // self.segments, self.quarter)
        for d in range(1, self.segments):
            to = self.seg ^ d
            self.waits.append(
                self.copy(
                    d,
                    self.own.at[self.own_at(to), :],
                    self.quarter_in.at[d - 1, at, :],
                    self.device(seg=to),
                )
            )

    def part_out(self):
        self.arrived()
        start = self.base // 2 + self.seg * self.quarter
        at = self.base // 2 // self.segments
        others = [(self.quarter_in.at[d], at) for d in range(self.segments - 1)]
        self.add((self.own, start), (self.own, start), others, self.quarter)
        at = self.span(self.base // 2 // self.segments // self.inner, self.share)
        for d in range(1, self.inner):
            to = self.part ^ d
            self.waits.append(
                self.copy(
                    self.segments + d - 1,
                    self.own.at[self.own_at(self.seg, to), :],
                    self.part_in.at[d - 1, at, :],
                    self.device(part=to),
                )
            )

    def part_back(self):
        self.arrived()
        start = self.base // 2 + self.seg * self.quarter + self.part * self.share
        at = self.base // 2 // self.segments // self.inner
        others = [(self.part_in.at[d], at) for d in range(self.inner - 1)]
        into = self.base + self.core * self.half + self.seg * self.quarter + self.part * self.share
        slot = self.segments + self.inner - 1
        if self.outer > 1:
            self.add((self.own, start), (self.own, start), others, self.share)
            span = self.span(at, self.share)
            for d in range(1, self.outer):
                self.waits.append(
                    self.copy(
                        slot + d - 1,
                        self.own.at[self.own_at(self.seg, self.part), :],
                        self.whole_in.at[d - 1, span, :],
                        self.device(group=self.group ^ d),
                    )
                )
            self.arrived()
            others = [(self.whole_in.at[d], at) for d in range(self.outer - 1)]
            slot += self.outer - 1
        self.add((self.total, into), (self.own, start), others, self.share)
        at = self.total_at(self.seg, self.part)
        for d in range(1, self.inner):
            made = self.copy(
                slot + d - 1, self.total.at[at, :], self.total.at[at, :], self.device(part=self.part ^ d)
            )
            self.waits.append(made)
        self.slot = slot + self.inner - 1

    def segment_back(self):
        self.arrived()
        at = self.total_at(self.seg)
        for d in range(1, self.segments):
            made = self.copy(
                self.slot + d - 1,
                self.total.at[at, :],
                self.total.at[at, :],
                self.device(seg=self.seg ^ d),
            )
            self.waits.append(made)
        self.slot += self.segments - 1

    def pair_back(self):
        self.arrived()
        at = self.total_at()
        self.waits.append(
            self.copy(
                self.slot, self.total.at[at, :], self.total.at[at, :], self.device(core=1 - self.core)
            )
        )

    def finish(self):
        self.arrived()

    def drain(self):
        for made in self.started:
            made.wait_send()


def slots_of(segments, inner, outer):
    return 2 + 2 * (segments - 1) + 2 * (inner - 1) + (outer - 1)


def greet(seg, dp, segments, inner, outer):
    barrier = pltpu.get_barrier_semaphore()
    core, part, group = dp % 2, dp // 2 % inner, dp // 2 // inner
    peers = [(seg, dp + 1 - 2 * core)]
    peers += [(seg ^ d, dp) for d in range(1, segments)]
    peers += [(seg, (group * inner + (part ^ d)) * 2 + core) for d in range(1, inner)]
    peers += [(seg, ((group ^ d) * inner + part) * 2 + core) for d in range(1, outer)]
    for peer in peers:
        pl.semaphore_signal(
            barrier, inc=1, device_id=peer, device_id_type=pl.DeviceIdType.MESH
        )
    return lambda: pl.semaphore_wait(barrier, len(peers))


def sum_scratch(sizes):
    segments, inner, outer = sizes
    quarter = ROWS // 2 // segments
    share = quarter // inner
    slots = slots_of(*sizes)
    return [
        pltpu.VMEM((ROWS // 2, C), bf16),
        pltpu.VMEM((segments - 1, quarter, C), bf16),
        pltpu.VMEM((inner - 1, share, C), bf16),
        pltpu.VMEM((max(outer - 1, 1), share, C), bf16),
        pltpu.VMEM((ROWS // 2, C), bf16),
        pltpu.SemaphoreType.DMA((len(PIECES), slots)),
        pltpu.SemaphoreType.DMA((len(PIECES), slots)),
    ]


def compute_kernel(
    own,
    images,
    sizes,
    grid_ref,
    keep_ref,
    x_ref,
    cot_ref,
    ng,
    ns,
    qw,
    qb,
    p4w,
    p2w,
    kvw,
    vb,
    lk,
    pw,
    pb,
    hw,
    hb,
    mk,
    mb,
    ow,
    ob,
    perm,
    perm_t,
    places,
    out_ref,
    dx_ref,
    summed_ref,
    xs,
    valid,
    sval,
    um,
    u_all,
    ut,
    wc,
    ex,
    xh_a,
    sc_a,
    xh_m,
    sc_m,
    u_a,
    q_a,
    p4,
    p2,
    xh_p,
    sc_p,
    ge_p,
    kin,
    wv,
    kb,
    vbd,
    pt,
    o_t,
    o_n,
    a_all,
    g_all,
    db,
    db_t,
    acc,
    kmask,
    near,
    small,
    pc,
    st,
    scale_ref,
    gp,
    half_in,
    quarter_in,
    part_in,
    whole_in,
    own_part,
    send,
    recv,
):
    n = images
    rows = n * TOK
    seg, dp = lax.axis_index("segment"), lax.axis_index("dp")
    all_here = greet(seg, dp, *sizes)
    refs = (gp, half_in, quarter_in, part_in, whole_in, own_part, summed_ref, send, recv)
    pieces = [
        Summed((seg, dp) + sizes, p, base, count, refs) for p, (base, count) in enumerate(PIECES)
    ]

    def move(*steps):
        for p, k in steps:
            pieces[p].step(k)

    lane = lax.broadcasted_iota(jnp.int32, (8, 128), 1)[0:1]

    def head_lanes(h):
        return (lane >= h * HEAD) & (lane < (h + 1) * HEAD)

    def tiles(fn, total=rows, step=TILE):
        def body(t, carry):
            fn(pl.ds(pl.multiple_of(t * step, step), step))
            return carry

        lax.fori_loop(0, total // step, body, 0)

    def row(ref, j, k=None):
        return ref[j, pl.ds(k, 1), :] if k is not None else ref[pl.ds(j, 1), :]

    def shifted_rows(v, by):
        if by == 0:
            return v
        pad = jnp.zeros((abs(by), v.shape[1]), v.dtype)
        if by > 0:
            return jnp.concatenate([v[by:], pad], axis=0)
        return jnp.concatenate([pad, v[:by]], axis=0)

    col = lax.broadcasted_iota(jnp.int32, (GRID, GRID, 128), 1).reshape(TOK, 128)

    def taps_of(v):
        left = jnp.where(col > 0, pltpu.roll(v, 1, 0), 0.0)
        right = jnp.where(col < GRID - 1, pltpu.roll(v, TOK - 1, 0), 0.0)
        for row_off in range(3):
            for col_off, piece in enumerate((left, v, right)):
                yield row_off * 3 + col_off, shifted_rows(piece, (row_off - 1) * GRID)

    small[...] = jnp.zeros_like(small)
    sizes = []
    lane_row = lax.broadcasted_iota(jnp.int32, (TOK, 128), 1)
    for i in range(n):
        m_id, d_id = seg * own + i // (n // own), i % (n // own)
        high, wide = grid_ref[d_id, 0, m_id], grid_ref[d_id, 1, m_id]
        sizes.append((high, wide))
        line = lax.broadcasted_iota(jnp.int32, (GRID, GRID, 128), 0).reshape(TOK, 128)
        good = jnp.where((line < high) & (col < wide), 1.0, 0.0)
        valid[i * TOK : (i + 1) * TOK, :] = good
        for k in range(2 * BLOCKS):
            kept = keep_ref[d_id, k, m_id].astype(f32) / keep_rate
            scale_ref[i, k] = kept
        flags = jnp.where((lane_row == 16) | (lane_row == 48), 1.0, 0.0)
        for off, piece in taps_of(good):
            flags = jnp.where((lane_row == off) | (lane_row == 32 + off), piece, flags)
        for j in range(BLOCKS):
            u_all[j, i * TOK : (i + 1) * TOK, TAPS * C :] = flags.astype(bf16)
        base = 0
        for t in range(2):
            span = slice(base, base + CELLS[t])
            tall = (high + STRIDES[t] - 1) // STRIDES[t]
            across = (wide + STRIDES[t] - 1) // STRIDES[t]
            inside = (places[0, span, :] < tall.astype(f32)) & (
                places[1, span, :] < across.astype(f32)
            )
            kmask[i, span, :] = jnp.where(inside, 1.0, 0.0)
            base += CELLS[t]
    base = 0
    for t in range(2):
        span = slice(base, base + CELLS[t])
        a, b = places[0, span, :], places[1, span, :]
        for off in range(9):
            dr, dc = float(off // 3 - 1), float(off % 3 - 1)
            top = float(SIDES[t])
            ok = (a + dr >= 0) & (a + dr < top) & (b + dc >= 0) & (b + dc < top)
            near[off, span, :] = jnp.where(ok, 1.0, 0.0)
        base += CELLS[t]

    xs[...] = x_ref[...].astype(f32)

    def set_sval(k):
        for i in range(n):
            span = slice(i * TOK, (i + 1) * TOK)
            sval[span, :] = valid[span, :] * scale_ref[i, k]

    def cell_spans(t):
        start = 0 if t == 0 else n * CELLS[0]
        return [slice(start + i * CELLS[t], start + (i + 1) * CELLS[t]) for i in range(n)]

    def cells_all(t):
        return slice(0, n * CELLS[0]) if t == 0 else slice(n * CELLS[0], n * sum(CELLS))

    place_span = (slice(0, CELLS[0]), slice(CELLS[0], sum(CELLS)))
    half = lane < 64
    own_half = (half, jnp.logical_not(half))

    def near_shift(t, off):
        return ((off // 3 - 1) * SIDES[t] + off % 3 - 1) % CELLS[t]

    def attention_forward(j):
        def first(ts):
            xhat, scale = norm_parts(xs[ts, :])
            xh_a[j, ts, :] = xhat
            sc_a[j, ts, :] = jnp.broadcast_to(scale, xhat.shape)
            u_a[j, ts, :] = (xhat * row(ng, j, 0) + row(ns, j, 0)).astype(bf16)

        tiles(first)
        for i in range(n):
            span = slice(i * TOK, (i + 1) * TOK)
            u = u_a[j, span, :]
            q_a[j, span, :] = (nn(u, qw[j]) + row(qb, j)).astype(bf16)
            um[:, i * C : (i + 1) * C] = (u.astype(f32) * valid[span, :]).astype(bf16)
        pc[...] = nn(perm[...], um[...]).astype(bf16)
        base = 0
        for t, ref in enumerate((p4, p2)):
            for k in range(STRIDES[t] ** 2):
                for i in range(n):
                    ref[j, i * CELLS[t] : (i + 1) * CELLS[t], k * C : (k + 1) * C] = pc[
                        base : base + CELLS[t], i * C : (i + 1) * C
                    ]
                base += CELLS[t]
        for t, (ref, weight) in enumerate(((p4, p4w), (p2, p2w))):
            xhat, scale = norm_parts(nn(ref[j], weight[j]))
            act, slope = gelu_parts(xhat * row(ng, j, 1 + t) + row(ns, j, 1 + t))
            act = act.astype(bf16)
            span = cells_all(t)
            xh_p[j, span, :] = xhat
            sc_p[j, span, :] = jnp.broadcast_to(scale, xhat.shape)
            ge_p[j, span, :] = slope
            kin[j, span, :] = act
            keyval = nn(act, kvw[j, t])
            turned = pltpu.roll(keyval, 64, 1)
            keys, vals = (keyval, turned) if t == 0 else (turned, keyval)
            bias = jnp.concatenate([row(vb, j, 0), row(vb, j, 1)], axis=1)
            kernel = jnp.concatenate([lk[j, :, 0, :], lk[j, :, 1, :]], axis=1)
            for i in range(n):
                part = slice(i * CELLS[t], (i + 1) * CELLS[t])
                w = (vals[part] + bias) * kmask[i, place_span[t], :]
                wv[j, cell_spans(t)[i], :] = w
                v = w
                for off in range(9):
                    by = near_shift(t, off)
                    moved = pltpu.roll(w, (CELLS[t] - by) % CELLS[t], 0) if by else w
                    v = v + moved * (near[off, place_span[t], :] * kernel[off : off + 1])
                for h in (2 * t, 2 * t + 1):
                    seg_rows = slice(*SEGS[h])
                    kb[j, i, seg_rows, :] = jnp.where(head_lanes(h), keys[part], 0.0).astype(bf16)
                    vbd[j, i, seg_rows, :] = jnp.where(head_lanes(h), v, 0.0).astype(bf16)
        for i in range(n):
            span = slice(i * TOK, (i + 1) * TOK)
            st[...] = nt(kb[j, i], q_a[j, span, :])
            for h, (low, top) in enumerate(SEGS):
                mask = kmask[i, place_span[h // 2], 0:1] > 0
                for c0 in range(0, TOK, 128):
                    c1 = min(c0 + 128, TOK)
                    s = jnp.where(mask, st[low:top, c0:c1], -1e30)
                    e = jnp.exp2((s - jnp.max(s, axis=0, keepdims=True)) * (ROOT * LOG2E))
                    weight = e * pl.reciprocal(jnp.sum(e, axis=0, keepdims=True))
                    pt[j, i, low:top, c0:c1] = weight.astype(bf16)
            mixed = tn(vbd[j, i], pt[j, i])
            o_t[j, i] = mixed.astype(bf16)
            o_n[span, :] = mixed.T.astype(bf16)
        set_sval(2 * j)
        for i in range(n):
            span = slice(i * TOK, (i + 1) * TOK)
            branch = nn(o_n[span, :], pw[j]) + row(pb, j)
            xs[span, :] = (xs[span, :] + sval[span, :] * branch).astype(bf16).astype(f32)

    def build_wc(j):
        bias = row(hb, j)

        def tap(off, carry):
            factor = mk[off, j : j + 1, :] + jnp.where(off == 4, 1.0, 0.0)
            for r0 in range(0, C, 32):
                wc[j, pl.ds(pl.multiple_of(off * C + r0, 32), 32), :] = (
                    hw[j, r0 : r0 + 32, :].astype(f32) * factor
                ).astype(bf16)
            return carry

        lax.fori_loop(0, TAPS, tap, 0)
        ex[...] = jnp.zeros_like(ex)
        each = mk[:, j, :] * bias
        both = bias + row(mb, j)
        each_high = each.astype(bf16).astype(f32)
        both_high = both.astype(bf16).astype(f32)
        ex[0:9, :] = each_high
        ex[16:17, :] = both_high
        ex[32:41, :] = each - each_high
        ex[48:49, :] = both - both_high
        wc[j, TAPS * C :, :] = ex[...].astype(bf16)

    def mlp_forward(j):
        build_wc(j)

        def first(ts):
            xhat, scale = norm_parts(xs[ts, :])
            xh_m[j, ts, :] = xhat
            sc_m[j, ts, :] = jnp.broadcast_to(scale, xhat.shape)
            u = (xhat * row(ng, j, 3) + row(ns, j, 3)).astype(bf16).astype(f32)
            acc[0, ts, :] = u * valid[ts, :]

        tiles(first)
        for i in range(n):
            span = slice(i * TOK, (i + 1) * TOK)
            for off, piece in taps_of(acc[0, span, :]):
                u_all[j, span, off * C : (off + 1) * C] = piece.astype(bf16)

        def chunk(step, carry):
            cols = pl.ds(pl.multiple_of(step * CHUNK, CHUNK), CHUNK)
            for i in range(n):
                field = nn(u_all[j, i * TOK : (i + 1) * TOK, :], wc[j, :, cols])
                for r0 in range(0, TOK, 32):
                    act, slope = gelu_parts(field[r0 : r0 + 32])
                    part = slice(i * TOK + r0, i * TOK + r0 + 32)
                    a_all[j, part, cols] = act.astype(bf16)
                    g_all[j, part, cols] = slope.astype(bf16)
            return carry

        lax.fori_loop(0, FF // CHUNK, chunk, 0)
        set_sval(2 * j + 1)
        for i in range(n):
            span = slice(i * TOK, (i + 1) * TOK)
            branch = nn(a_all[j, span, :], ow[j]) + row(ob, j)
            xs[span, :] = (xs[span, :] + sval[span, :] * branch).astype(bf16).astype(f32)

    def mlp_backward(j):
        base, sb = MLP_AT[j], j * S_BLOCK
        set_sval(2 * j + 1)

        def first(ts):
            grad = (xs[ts, :] * sval[ts, :]).astype(bf16)
            db[ts, :] = grad
            small[sb + S_OB : sb + S_OB + 1, :] += col_sum(grad.astype(f32))

        tiles(first)
        db_t[...] = db[...].T
        for off in range(TAPS + 1):
            ut[off * C : (off + 1) * C, :] = u_all[j, :, off * C : (off + 1) * C].T
        bias = row(hb, j)

        def chunk(step, carry):
            cols = pl.ds(pl.multiple_of(step * CHUNK, CHUNK), CHUNK)
            for i in range(n):
                span = slice(i * TOK, (i + 1) * TOK)
                da = nt(db[span, :], ow[j, cols, :])
                g_all[j, span, cols] = (da * g_all[j, span, cols].astype(f32)).astype(bf16)
            dfield = g_all[j, :, cols]
            dow = nn(db_t[...], a_all[j, :, cols])
            gp[pl.ds(pl.multiple_of(base + R_OUT + step * CHUNK, CHUNK), CHUNK), :] = dow.T.astype(
                bf16
            )
            cross = nn(ut[...], dfield)
            flag_rows = cross[TAPS * C : TAPS * C + 24]
            total = flag_rows[16:17]
            dhb = total
            weight = hw[j, :, cols].astype(f32)
            dweight = jnp.zeros((C, CHUNK), f32)
            b = hb[pl.ds(j, 1), cols]
            for off in range(TAPS):
                piece = cross[off * C : (off + 1) * C]
                factor = mk[off, j : j + 1, cols]
                flag = flag_rows[off : off + 1]
                dweight = dweight + piece * (factor + (1.0 if off == 4 else 0.0))
                dk = col_sum(piece * weight) + b * flag
                dhb = dhb + factor * flag
                for s in range(CHUNK // C):
                    at = sb + S_MK + 16 * (step * (CHUNK // C) + s) + off
                    small[pl.ds(at, 1), :] = dk[:, s * C : (s + 1) * C]
            for s in range(CHUNK // C):
                at = step * (CHUNK // C) + s
                part = slice(s * C, (s + 1) * C)
                small[pl.ds(sb + S_HB + at, 1), :] = dhb[:, part]
                small[pl.ds(sb + S_MB + at, 1), :] = total[:, part]
                gp[pl.ds(pl.multiple_of(base + R_HID + at * C, C), C), :] = dweight[
                    :, part
                ].astype(bf16)
            return carry

        half = FF // CHUNK // 2
        lax.fori_loop(0, half, chunk, 0)
        if j == 0:
            move((0, 6), (1, 1))
        lax.fori_loop(half, FF // CHUNK, chunk, 0)
        if j == 1:
            all_here()
            move((0, 0))
        else:
            move((1, 2), (2, 0))
        acc[...] = jnp.zeros_like(acc)
        for first_off in range(0, TAPS, 2):
            width = min(2, TAPS - first_off)
            for i in range(n):
                at = i * TOK
                moved = nt(
                    g_all[j, at : at + TOK, :], wc[j, first_off * C : (first_off + width) * C, :]
                )
                for s in range(width):
                    off = first_off + s
                    by = (off // 3 - 1) * GRID
                    piece = moved[:, s * C : (s + 1) * C]
                    if by >= 0:
                        acc[off % 3, at + by : at + TOK, :] += piece[: TOK - by]
                    else:
                        acc[off % 3, at : at + TOK + by, :] += piece[-by:]
        move(*(((0, 1),) if j == 1 else ((1, 3), (2, 1))))
        for i in range(n):
            span = slice(i * TOK, (i + 1) * TOK)
            left = pltpu.roll(jnp.where(col > 0, acc[0, span, :], 0.0), TOK - 1, 0)
            right = pltpu.roll(jnp.where(col < GRID - 1, acc[2, span, :], 0.0), 1, 0)
            acc[1, span, :] = (acc[1, span, :] + left + right) * valid[span, :]

        def last(ts):
            du = acc[1, ts, :]
            xhat = xh_m[j, ts, :]
            small[sb + S_GAIN + 3 : sb + S_GAIN + 4, :] += col_sum(du * xhat)
            small[sb + S_SHIFT + 3 : sb + S_SHIFT + 4, :] += col_sum(du)
            back = norm_back(du, xhat, sc_m[j, ts, :], row(ng, j, 3))
            xs[ts, :] = (xs[ts, :] + back).astype(bf16).astype(f32)

        tiles(last)
        if j == 0:
            move((1, 4), (2, 2))

    def attention_backward(j):
        base, sb = ATT_AT[j], j * S_BLOCK
        set_sval(2 * j)

        def first(ts):
            grad = (xs[ts, :] * sval[ts, :]).astype(bf16)
            db[ts, :] = grad
            small[sb + S_PB : sb + S_PB + 1, :] += col_sum(grad.astype(f32))

        tiles(first)
        dproj = jnp.zeros((C, C), f32)
        kernel = jnp.concatenate([lk[j, :, 0, :], lk[j, :, 1, :]], axis=1)
        dkernel = [jnp.zeros((1, C), f32) for _ in range(9)]
        dbias = jnp.zeros((1, C), f32)
        for i in range(n):
            span = slice(i * TOK, (i + 1) * TOK)
            dproj = dproj + nn(o_t[j, i], db[span, :])
            do = nt(db[span, :], pw[j]).astype(bf16)
            st[...] = nt(vbd[j, i], do)
            dvals = nn(pt[j, i], do)
            for low, top in SEGS:
                for c0 in range(0, TOK, 128):
                    c1 = min(c0 + 128, TOK)
                    weight = pt[j, i, low:top, c0:c1].astype(f32)
                    dweight = st[low:top, c0:c1]
                    dot = jnp.sum(weight * dweight, axis=0, keepdims=True)
                    pt[j, i, low:top, c0:c1] = (weight * (dweight - dot)).astype(bf16)
            dkeys = nn(pt[j, i], q_a[j, span, :]) * ROOT
            dq = tn(kb[j, i], pt[j, i]) * ROOT
            o_n[span, :] = dq.T.astype(bf16)
            for t in range(2):
                dk = jnp.zeros((CELLS[t], C), f32)
                dv = jnp.zeros((CELLS[t], C), f32)
                for h in (2 * t, 2 * t + 1):
                    dk = dk + jnp.where(head_lanes(h), dkeys[slice(*SEGS[h])], 0.0)
                    dv = dv + jnp.where(head_lanes(h), dvals[slice(*SEGS[h])], 0.0)
                w = wv[j, cell_spans(t)[i], :]
                dw = dv
                for off in range(9):
                    by = near_shift(t, off)
                    part = dv * near[off, place_span[t], :]
                    moved = pltpu.roll(w, (CELLS[t] - by) % CELLS[t], 0) if by else w
                    dkernel[off] = dkernel[off] + col_sum(part * moved)
                    part = part * kernel[off : off + 1]
                    dw = dw + (pltpu.roll(part, by, 0) if by else part)
                dw = dw * kmask[i, place_span[t], :]
                dbias = dbias + col_sum(dw)
                if t == 0:
                    dkeyval = dk + pltpu.roll(dw, 64, 1)
                else:
                    dkeyval = pltpu.roll(dk, 64, 1) + dw
                wv[j, cell_spans(t)[i], :] = dkeyval
            if j == 1:
                move((0, 2 + min(i, 1)) if i < 2 else ())
            else:
                move(*((((1, 5), (2, 3)), ((1, 6), (2, 4)))[i] if i < 2 else ()))
        gp[base + R_PROJ : base + R_PROJ + C, :] = dproj.astype(bf16)
        small[sb + S_VB : sb + S_VB + 1, :] = dbias
        for off in range(9):
            small[sb + S_LK + off : sb + S_LK + off + 1, :] = dkernel[off]
        base_perm = 0
        for t, (ref, weight) in enumerate(((p4, p4w), (p2, p2w))):
            span = cells_all(t)
            dkeyval = wv[j, span, :].astype(bf16)
            at = base + R_KV + t * C
            gp[at : at + C, :] = tn(kin[j, span, :], dkeyval).astype(bf16)
            dy = nt(dkeyval, kvw[j, t]) * ge_p[j, span, :]
            xhat = xh_p[j, span, :]
            small[sb + S_GAIN + 1 + t : sb + S_GAIN + 2 + t, :] = col_sum(dy * xhat)
            small[sb + S_SHIFT + 1 + t : sb + S_SHIFT + 2 + t, :] = col_sum(dy)
            dpool = norm_back(dy, xhat, sc_p[j, span, :], row(ng, j, 1 + t)).astype(bf16)
            at = base + (R_P4, R_P2)[t]
            for k in range(STRIDES[t] ** 2):
                gp[at + k * C : at + (k + 1) * C, :] = tn(
                    ref[j, :, k * C : (k + 1) * C], dpool
                ).astype(bf16)
                back = nt(dpool, weight[j, k * C : (k + 1) * C, :]).astype(bf16)
                for i in range(n):
                    pc[base_perm : base_perm + CELLS[t], i * C : (i + 1) * C] = back[
                        i * CELLS[t] : (i + 1) * CELLS[t]
                    ]
                base_perm += CELLS[t]
            if j == 0 and t == 0:
                move((3, 0))
        at = base + R_Q
        gp[at : at + C, :] = tn(u_a[j], o_n[...]).astype(bf16)
        if j == 1:
            move((0, 4), (1, 0))
        else:
            move((2, 5), (4, 0))
        spread = nn(perm_t[...], pc[...])
        for i in range(n):
            span = slice(i * TOK, (i + 1) * TOK)
            back = nt(o_n[span, :], qw[j])
            acc[0, span, :] = back + spread[:, i * C : (i + 1) * C] * valid[span, :]
        if j == 0:
            move((3, 1))

        def last(ts):
            du = acc[0, ts, :]
            xhat = xh_a[j, ts, :]
            small[sb + S_QB : sb + S_QB + 1, :] += col_sum(o_n[ts, :].astype(f32))
            small[sb + S_GAIN : sb + S_GAIN + 1, :] += col_sum(du * xhat)
            small[sb + S_SHIFT : sb + S_SHIFT + 1, :] += col_sum(du)
            back = norm_back(du, xhat, sc_a[j, ts, :], row(ng, j, 0))
            xs[ts, :] = (xs[ts, :] + back).astype(bf16).astype(f32)

        tiles(last)
        if j == 1:
            move((0, 5))

    for j in range(BLOCKS):
        attention_forward(j)
        mlp_forward(j)
    out_ref[...] = xs[...].astype(bf16)
    xs[...] = cot_ref[...].astype(f32)
    for j in reversed(range(BLOCKS)):
        mlp_backward(j)
        attention_backward(j)
    gp[R_SMALL:, :] = small[...].astype(bf16)
    move((2, 6), (5, 0), (4, 1), (3, 2))
    dx_ref[...] = xs[...].astype(bf16)
    for k in range(3, Summed.STEPS + 2):
        for p, late in ((3, 0), (4, 1), (5, 2)):
            if k - late < Summed.STEPS:
                move((p, k - late))
    for piece in pieces:
        piece.drain()


def compute(own, images, grid_size, keep_mask, x, cot, weights):
    segments, pairs = lax.axis_size("segment"), lax.axis_size("dp") // 2
    inner = min(pairs, 4)
    sizes = (segments, inner, pairs // inner)
    n = images
    rows = n * TOK
    cells = n * sum(CELLS)
    vmem = pl.BlockSpec(memory_space=pltpu.VMEM)
    smem = pl.BlockSpec(memory_space=pltpu.SMEM)
    matrix = permutation()
    consts = (
        jnp.asarray(matrix, bf16),
        jnp.asarray(matrix.T, bf16),
        jnp.asarray(cell_places()),
    )
    B = BLOCKS
    scratch = [
        pltpu.VMEM((rows, C), f32),
        pltpu.VMEM((rows, C), f32),
        pltpu.VMEM((rows, C), f32),
        pltpu.VMEM((TOK, n * C), bf16),
        pltpu.VMEM((B, rows, UW), bf16),
        pltpu.VMEM((UW, rows), bf16),
        pltpu.VMEM((B, UW, FF), bf16),
        pltpu.VMEM((C, FF), f32),
        pltpu.VMEM((B, rows, C), f32),
        pltpu.VMEM((B, rows, C), f32),
        pltpu.VMEM((B, rows, C), f32),
        pltpu.VMEM((B, rows, C), f32),
        pltpu.VMEM((B, rows, C), bf16),
        pltpu.VMEM((B, rows, C), bf16),
        pltpu.VMEM((B, n * CELLS[0], 16 * C), bf16),
        pltpu.VMEM((B, n * CELLS[1], 4 * C), bf16),
        pltpu.VMEM((B, cells, C), f32),
        pltpu.VMEM((B, cells, C), f32),
        pltpu.VMEM((B, cells, C), f32),
        pltpu.VMEM((B, cells, C), bf16),
        pltpu.VMEM((B, cells, C), f32),
        pltpu.VMEM((B, n, KEYS, C), bf16),
        pltpu.VMEM((B, n, KEYS, C), bf16),
        pltpu.VMEM((B, n, KEYS, TOK), bf16),
        pltpu.VMEM((B, n, C, TOK), bf16),
        pltpu.VMEM((rows, C), bf16),
        pltpu.VMEM((B, rows, FF), bf16),
        pltpu.VMEM((B, rows, FF), bf16),
        pltpu.VMEM((rows, C), bf16),
        pltpu.VMEM((C, rows), bf16),
        pltpu.VMEM((3, rows, C), f32),
        pltpu.VMEM((n, sum(CELLS), C), f32),
        pltpu.VMEM((9, sum(CELLS), C), f32),
        pltpu.VMEM((ROWS - R_SMALL, C), f32),
        pltpu.VMEM((PERM, n * C), bf16),
        pltpu.VMEM((KEYS, TOK), f32),
        pltpu.SMEM((n, 2 * BLOCKS), f32),
        pltpu.VMEM((ROWS, C), bf16),
    ] + sum_scratch(sizes)
    return pl.pallas_call(
        functools.partial(compute_kernel, own, images, sizes),
        out_shape=(
            jax.ShapeDtypeStruct((rows, C), bf16),
            jax.ShapeDtypeStruct((rows, C), bf16),
            jax.ShapeDtypeStruct((ROWS, C), bf16),
        ),
        in_specs=[smem, smem] + [vmem] * (2 + len(weights) + len(consts)),
        out_specs=(vmem, vmem, vmem),
        scratch_shapes=scratch,
        compiler_params=pltpu.CompilerParams(
            collective_id=0, has_side_effects=True, vmem_limit_bytes=62 * 2**20
        ),
        name="compute",
    )(grid_size, keep_mask, x, cot, *weights, *consts)


def unpack_kernel(gp, out_in, dx_in, *refs):
    out_ref, dx_ref = refs[:2]
    gain, shift, qw, qb, p4, p2, kvw, vb, lk, pw, pb, hw, hb, mk, mb, ow, ob = refs[2:]
    out_ref[...] = out_in[...]
    dx_ref[...] = dx_in[...]
    for j in range(BLOCKS):
        att, mlp, sb = ATT_AT[j], MLP_AT[j], R_SMALL + j * S_BLOCK
        p4[j] = gp[att + R_P4 : att + R_P2, :].astype(f32)
        p2[j] = gp[att + R_P2 : att + R_KV, :].astype(f32)
        for t in range(2):
            kvw[j, t] = gp[att + R_KV + t * C : att + R_KV + (t + 1) * C, :].astype(f32)
        qw[j] = gp[att + R_Q : att + R_PROJ, :].astype(f32)
        pw[j] = gp[att + R_PROJ : att + R_ATT, :].astype(f32)
        for s in range(FF // C):
            at = mlp + R_HID + s * C
            hw[j, :, s * C : (s + 1) * C] = gp[at : at + C, :].astype(f32)
        ow[j] = gp[mlp + R_OUT : mlp + R_MLP, :].astype(f32)
        head = gp[sb : sb + 48, :].astype(f32)
        gain[j] = head[S_GAIN : S_GAIN + 4]
        shift[j] = head[S_SHIFT : S_SHIFT + 4]
        qb[j : j + 1, :] = head[S_QB : S_QB + 1]
        vb[j, 0:1, :] = head[S_VB : S_VB + 1, 0:64]
        vb[j, 1:2, :] = head[S_VB : S_VB + 1, 64:128]
        pb[j : j + 1, :] = head[S_PB : S_PB + 1]
        ob[j : j + 1, :] = head[S_OB : S_OB + 1]
        lk[j, :, 0, :] = head[S_LK : S_LK + 9, 0:64]
        lk[j, :, 1, :] = head[S_LK : S_LK + 9, 64:128]
        for s in range(FF // C):
            part = slice(s * C, (s + 1) * C)
            hb[j : j + 1, part] = head[S_HB + s : S_HB + s + 1]
            mb[j : j + 1, part] = head[S_MB + s : S_MB + s + 1]
            at = sb + S_MK + 16 * s
            mk[:, j, part] = gp[at : at + 16, :].astype(f32)[0:9]


def unpack(packed, outputs, input_grad, weights):
    vmem = pl.BlockSpec(memory_space=pltpu.VMEM)
    streams = (jax.ShapeDtypeStruct(outputs.shape, bf16),) * 2
    return pl.pallas_call(
        unpack_kernel,
        out_shape=streams + tuple(jax.ShapeDtypeStruct(w.shape, f32) for w in weights),
        in_specs=[vmem] * 3,
        out_specs=(vmem,) * (2 + len(weights)),
        compiler_params=pltpu.CompilerParams(vmem_limit_bytes=40 * 2**20),
        name="unpack",
    )(packed, outputs, input_grad)


def on_device(inputs, grid_size, keep_mask, cotangent, *weights):
    own, per = inputs.shape[:2]
    images = own * per
    flat = (images * TOK, C)
    turned = list(weights)
    turned[LK] = jnp.transpose(turned[LK], (0, 2, 1, 3))
    turned[MK] = jnp.transpose(turned[MK], (1, 0, 2))
    outputs, input_grad, packed = compute(
        own,
        images,
        jnp.transpose(grid_size, (1, 2, 0)),
        jnp.transpose(keep_mask, (1, 2, 0)),
        inputs.reshape(flat),
        cotangent.reshape(flat),
        turned,
    )
    outputs, input_grad, *grads = unpack(packed, outputs, input_grad, turned)
    grads[LK] = jnp.transpose(grads[LK], (0, 2, 1, 3))
    grads[MK] = jnp.transpose(grads[MK], (1, 0, 2))
    return (outputs.reshape(inputs.shape), input_grad.reshape(inputs.shape)) + tuple(grads)


def solution(mesh):
    stream = P("segment", "dp", None, None)
    picked = P(None, "dp", None)
    return jax.shard_map(
        on_device,
        mesh=mesh,
        in_specs=(stream, picked, picked, stream) + (P(),) * 17,
        out_specs=(stream, stream) + (P(),) * 17,
        check_vma=False,
    )
```

```python
import functools

import jax
import jax.numpy as jnp
import numpy as np
from jax import lax
from jax.experimental import pallas as pl
from jax.experimental.pallas import tpu as pltpu
from jax.sharding import PartitionSpec as P

GRID = 24
TOK = GRID * GRID
C = 128
FF = 1024
HEAD = 32
BLOCKS = 2
SIDES = (6, 12)
STRIDES = (4, 2)
CELLS = (48, 144)
SEGS = ((0, 48), (48, 96), (96, 240), (240, 384))
KEYS = 384
PERM = 16 * 48 + 4 * 144
TAPS = 9
UW = TAPS * C + C
CHUNK = 512
TILE = 96

R_P4, R_P2, R_KV, R_Q, R_PROJ, R_ATT = 0, 2048, 2560, 2816, 2944, 3072
R_HID, R_OUT, R_MLP = 0, 1024, 2048
ATT_AT = (R_ATT + 2 * R_MLP, 0)
MLP_AT = (R_ATT + R_MLP, R_ATT)
S_GAIN, S_SHIFT, S_QB, S_VB, S_PB, S_OB, S_LK, S_HB, S_MB, S_MK, S_BLOCK = (
    0,
    4,
    8,
    9,
    10,
    11,
    16,
    32,
    40,
    48,
    192,
)
R_SMALL = BLOCKS * (R_ATT + R_MLP)
ROWS = R_SMALL + 512
PIECES = (
    (MLP_AT[1], R_MLP),
    (ATT_AT[1], R_ATT),
    (MLP_AT[0], R_MLP),
    (ATT_AT[0], R_ATT // 2),
    (ATT_AT[0] + R_ATT // 2, R_ATT // 2),
    (R_SMALL, ROWS - R_SMALL),
)

LK, MK = 8, 13

epsilon = 1e-06
keep_rate = 0.8
ROOT = HEAD**-0.5
LOG2E = 1.4426950408889634
f32, bf16 = jnp.float32, jnp.bfloat16


def permutation():
    matrix = np.zeros((PERM, TOK), np.float32)
    base = 0
    for stride, side, cells in zip(STRIDES, SIDES, CELLS):
        for row_off in range(stride):
            for col_off in range(stride):
                for a in range(side):
                    for b in range(side):
                        token = (a * stride + row_off) * GRID + b * stride + col_off
                        matrix[base + a * side + b, token] = 1.0
                base += cells
    return matrix


def cell_places():
    places = np.full((2, sum(CELLS), 128), 99.0, np.float32)
    base = 0
    for side, cells in zip(SIDES, CELLS):
        for a in range(side):
            for b in range(side):
                places[0, base + a * side + b] = a
                places[1, base + a * side + b] = b
        base += cells
    return places


def nn(left, right):
    return jnp.dot(left, right, preferred_element_type=f32)


def nt(left, right):
    return lax.dot_general(left, right, (((1,), (1,)), ((), ())), preferred_element_type=f32)


def tn(left, right):
    return lax.dot_general(left, right, (((0,), (0,)), ((), ())), preferred_element_type=f32)


def gelu_parts(m):
    size = jnp.abs(m)
    t = pl.reciprocal(1.0 + (0.3275911 * 0.5**0.5) * size, approx=True)
    e = jnp.exp2(m * (m * (-0.5 * LOG2E)))
    poly = 0.5 * 1.061405429
    for coef in (-1.453152027, 1.421413741, -0.284496736, 0.254829592):
        poly = poly * t + 0.5 * coef
    poly = poly * t
    tail = poly * e
    slope = (poly - size * 0.3989422804014327) * e
    return jnp.maximum(m, 0.0) - size * tail, jnp.where(m >= 0, 1.0 - slope, slope)


def norm_parts(x):
    centred = x - jnp.mean(x, axis=-1, keepdims=True)
    scale = lax.rsqrt(jnp.mean(centred * centred, axis=-1, keepdims=True) + epsilon)
    return centred * scale, scale


def norm_back(du, xhat, scale, gain):
    dxhat = du * gain
    first = jnp.mean(dxhat, axis=-1, keepdims=True)
    second = jnp.mean(dxhat * xhat, axis=-1, keepdims=True)
    return scale * (dxhat - first - xhat * second)


def col_sum(x):
    return jnp.sum(x, axis=0, keepdims=True)


def folded(x):
    return jnp.sum(x.reshape(-1, 8, x.shape[-1]), axis=0)


class Summed:
    STEPS = 7

    def __init__(self, place, piece, base, count, refs):
        self.seg, self.dp, self.segments, self.inner, self.outer = place
        self.piece, self.base, self.count = piece, base, count
        (
            self.src,
            self.half_in,
            self.quarter_in,
            self.part_in,
            self.whole_in,
            self.own,
            self.total,
            self.send,
            self.recv,
        ) = refs
        self.core, rest = self.dp % 2, self.dp // 2
        self.part, self.group = rest % self.inner, rest // self.inner
        self.half = count // 2
        self.quarter = self.half // self.segments
        self.share = self.quarter // self.inner
        self.started = []

    def span(self, start, size):
        return pl.ds(pl.multiple_of(start, 16), size)

    def device(self, seg=None, core=None, part=None, group=None):
        seg = self.seg if seg is None else seg
        core = self.core if core is None else core
        part = self.part if part is None else part
        group = self.group if group is None else group
        return (seg, (group * self.inner + part) * 2 + core)

    def copy(self, slot, src, dst, device):
        made = pltpu.make_async_remote_copy(
            src_ref=src,
            dst_ref=dst,
            send_sem=self.send.at[self.piece, slot],
            recv_sem=self.recv.at[self.piece, slot],
            device_id=device,
            device_id_type=pl.DeviceIdType.MESH,
        )
        made.start()
        self.started.append(made)
        return made

    def half_at(self, core):
        return self.span(self.base + core * self.half, self.half)

    def own_at(self, seg, part=None):
        start = self.base // 2 + seg * self.quarter
        if part is None:
            return self.span(start, self.quarter)
        return self.span(start + part * self.share, self.share)

    def total_at(self, seg=None, part=None):
        start = self.base + self.core * self.half
        if seg is None:
            return self.span(start, self.half)
        start = start + seg * self.quarter
        if part is None:
            return self.span(start, self.quarter)
        return self.span(start + part * self.share, self.share)

    def step(self, k):
        (
            self.pair_out,
            self.segment_out,
            self.part_out,
            self.part_back,
            self.segment_back,
            self.pair_back,
            self.finish,
        )[k]()

    def pair_out(self):
        self.waits = [
            self.copy(
                0,
                self.src.at[self.half_at(1 - self.core), :],
                self.half_in.at[self.span(self.base // 2, self.half), :],
                self.device(core=1 - self.core),
            )
        ]

    def arrived(self):
        for made in self.waits:
            made.wait_recv()
        self.waits = []

    def add(self, dst, first, others, count):
        step = 64 if count % 64 == 0 else 16

        def body(t, carry):
            at = t * step
            total = first[0][self.span(first[1] + at, step), :].astype(f32)
            for ref, start in others:
                total = total + ref[self.span(start + at, step), :].astype(f32)
            dst[0][self.span(dst[1] + at, step), :] = total.astype(bf16)
            return carry

        lax.fori_loop(0, count // step, body, 0)

    def segment_out(self):
        self.arrived()
        own = self.base // 2
        self.add(
            (self.own, own),
            (self.src, self.base + self.core * self.half),
            [(self.half_in, own)],
            self.half,
        )
        at = self.span(self.base // 2 // self.segments, self.quarter)
        for d in range(1, self.segments):
            to = self.seg ^ d
            self.waits.append(
                self.copy(
                    d,
                    self.own.at[self.own_at(to), :],
                    self.quarter_in.at[d - 1, at, :],
                    self.device(seg=to),
                )
            )

    def part_out(self):
        self.arrived()
        start = self.base // 2 + self.seg * self.quarter
        at = self.base // 2 // self.segments
        others = [(self.quarter_in.at[d], at) for d in range(self.segments - 1)]
        self.add((self.own, start), (self.own, start), others, self.quarter)
        at = self.span(self.base // 2 // self.segments // self.inner, self.share)
        for d in range(1, self.inner):
            to = self.part ^ d
            self.waits.append(
                self.copy(
                    self.segments + d - 1,
                    self.own.at[self.own_at(self.seg, to), :],
                    self.part_in.at[d - 1, at, :],
                    self.device(part=to),
                )
            )

    def part_back(self):
        self.arrived()
        start = self.base // 2 + self.seg * self.quarter + self.part * self.share
        at = self.base // 2 // self.segments // self.inner
        others = [(self.part_in.at[d], at) for d in range(self.inner - 1)]
        into = self.base + self.core * self.half + self.seg * self.quarter + self.part * self.share
        slot = self.segments + self.inner - 1
        if self.outer > 1:
            self.add((self.own, start), (self.own, start), others, self.share)
            span = self.span(at, self.share)
            for d in range(1, self.outer):
                self.waits.append(
                    self.copy(
                        slot + d - 1,
                        self.own.at[self.own_at(self.seg, self.part), :],
                        self.whole_in.at[d - 1, span, :],
                        self.device(group=self.group ^ d),
                    )
                )
            self.arrived()
            others = [(self.whole_in.at[d], at) for d in range(self.outer - 1)]
            slot += self.outer - 1
        self.add((self.total, into), (self.own, start), others, self.share)
        at = self.total_at(self.seg, self.part)
        for d in range(1, self.inner):
            made = self.copy(
                slot + d - 1, self.total.at[at, :], self.total.at[at, :], self.device(part=self.part ^ d)
            )
            self.waits.append(made)
        self.slot = slot + self.inner - 1

    def segment_back(self):
        self.arrived()
        at = self.total_at(self.seg)
        for d in range(1, self.segments):
            made = self.copy(
                self.slot + d - 1,
                self.total.at[at, :],
                self.total.at[at, :],
                self.device(seg=self.seg ^ d),
            )
            self.waits.append(made)
        self.slot += self.segments - 1

    def pair_back(self):
        self.arrived()
        at = self.total_at()
        self.waits.append(
            self.copy(
                self.slot, self.total.at[at, :], self.total.at[at, :], self.device(core=1 - self.core)
            )
        )

    def finish(self):
        self.arrived()

    def drain(self):
        for made in self.started:
            made.wait_send()


def slots_of(segments, inner, outer):
    return 2 + 2 * (segments - 1) + 2 * (inner - 1) + (outer - 1)


def greet(seg, dp, segments, inner, outer):
    barrier = pltpu.get_barrier_semaphore()
    core, part, group = dp % 2, dp // 2 % inner, dp // 2 // inner
    peers = [(seg, dp + 1 - 2 * core)]
    peers += [(seg ^ d, dp) for d in range(1, segments)]
    peers += [(seg, (group * inner + (part ^ d)) * 2 + core) for d in range(1, inner)]
    peers += [(seg, ((group ^ d) * inner + part) * 2 + core) for d in range(1, outer)]
    for peer in peers:
        pl.semaphore_signal(
            barrier, inc=1, device_id=peer, device_id_type=pl.DeviceIdType.MESH
        )
    return lambda: pl.semaphore_wait(barrier, len(peers))


def sum_scratch(sizes):
    segments, inner, outer = sizes
    quarter = ROWS // 2 // segments
    share = quarter // inner
    slots = slots_of(*sizes)
    return [
        pltpu.VMEM((ROWS // 2, C), bf16),
        pltpu.VMEM((segments - 1, quarter, C), bf16),
        pltpu.VMEM((inner - 1, share, C), bf16),
        pltpu.VMEM((max(outer - 1, 1), share, C), bf16),
        pltpu.VMEM((ROWS // 2, C), bf16),
        pltpu.SemaphoreType.DMA((len(PIECES), slots)),
        pltpu.SemaphoreType.DMA((len(PIECES), slots)),
    ]


def compute_kernel(
    own,
    images,
    grid_ref,
    keep_ref,
    x_ref,
    cot_ref,
    ng,
    ns,
    qw,
    qb,
    p4w,
    p2w,
    kvw,
    vb,
    lk,
    pw,
    pb,
    hw,
    hb,
    mk,
    mb,
    ow,
    ob,
    perm,
    perm_t,
    places,
    out_ref,
    dx_ref,
    gp,
    xs,
    valid,
    sval,
    um,
    u_all,
    ut,
    wc,
    ex,
    xh_a,
    sc_a,
    xh_m,
    sc_m,
    u_a,
    q_a,
    p4,
    p2,
    xh_p,
    sc_p,
    ge_p,
    kin,
    wv,
    kb,
    vbd,
    pt,
    o_t,
    o_n,
    a_all,
    g_all,
    db,
    db_t,
    acc,
    kmask,
    near,
    small,
    pc,
    scale_ref,
):
    n = images
    rows = n * TOK
    seg = lax.axis_index("segment")
    lane = lax.broadcasted_iota(jnp.int32, (8, 128), 1)[0:1]

    def head_lanes(h):
        return (lane >= h * HEAD) & (lane < (h + 1) * HEAD)

    def tiles(fn, step=TILE):
        sums = None
        for start in range(0, rows, step):
            got = fn(slice(start, start + step))
            if got is not None:
                sums = got if sums is None else [x + y for x, y in zip(sums, got)]
        return None if sums is None else [col_sum(x) for x in sums]

    def row(ref, j, k=None):
        return ref[j, pl.ds(k, 1), :] if k is not None else ref[pl.ds(j, 1), :]

    def shifted_rows(v, by):
        if by == 0:
            return v
        pad = jnp.zeros((abs(by), v.shape[1]), v.dtype)
        if by > 0:
            return jnp.concatenate([v[by:], pad], axis=0)
        return jnp.concatenate([pad, v[:by]], axis=0)

    col = lax.broadcasted_iota(jnp.int32, (GRID, GRID, 128), 1).reshape(TOK, 128)

    def taps_of(v):
        left = jnp.where(col > 0, pltpu.roll(v, 1, 0), 0.0)
        right = jnp.where(col < GRID - 1, pltpu.roll(v, TOK - 1, 0), 0.0)
        for row_off in range(3):
            for col_off, piece in enumerate((left, v, right)):
                yield row_off * 3 + col_off, shifted_rows(piece, (row_off - 1) * GRID)

    small[...] = jnp.zeros_like(small)
    sizes = []
    lane_row = lax.broadcasted_iota(jnp.int32, (TOK, 128), 1)
    for i in range(n):
        m_id, d_id = seg * own + i // (n // own), i % (n // own)
        high, wide = grid_ref[d_id, 0, m_id], grid_ref[d_id, 1, m_id]
        sizes.append((high, wide))
        line = lax.broadcasted_iota(jnp.int32, (GRID, GRID, 128), 0).reshape(TOK, 128)
        good = jnp.where((line < high) & (col < wide), 1.0, 0.0)
        valid[i * TOK : (i + 1) * TOK, :] = good
        for k in range(2 * BLOCKS):
            kept = keep_ref[d_id, k, m_id].astype(f32) / keep_rate
            scale_ref[i, k] = kept
        flags = jnp.where((lane_row == 16) | (lane_row == 48), 1.0, 0.0)
        for off, piece in taps_of(good):
            flags = jnp.where((lane_row == off) | (lane_row == 32 + off), piece, flags)
        for j in range(BLOCKS):
            u_all[j, i * TOK : (i + 1) * TOK, TAPS * C :] = flags.astype(bf16)
        base = 0
        for t in range(2):
            span = slice(base, base + CELLS[t])
            tall = (high + STRIDES[t] - 1) // STRIDES[t]
            across = (wide + STRIDES[t] - 1) // STRIDES[t]
            inside = (places[0, span, :] < tall.astype(f32)) & (
                places[1, span, :] < across.astype(f32)
            )
            kmask[i, span, :] = jnp.where(inside, 1.0, 0.0)
            base += CELLS[t]
    base = 0
    for t in range(2):
        span = slice(base, base + CELLS[t])
        a, b = places[0, span, :], places[1, span, :]
        for off in range(9):
            dr, dc = float(off // 3 - 1), float(off % 3 - 1)
            top = float(SIDES[t])
            ok = (a + dr >= 0) & (a + dr < top) & (b + dc >= 0) & (b + dc < top)
            near[off, span, :] = jnp.where(ok, 1.0, 0.0)
        base += CELLS[t]

    xs[...] = x_ref[...].astype(f32)

    def set_sval(k):
        for i in range(n):
            span = slice(i * TOK, (i + 1) * TOK)
            sval[span, :] = valid[span, :] * scale_ref[i, k]

    def cell_spans(t):
        start = 0 if t == 0 else n * CELLS[0]
        return [slice(start + i * CELLS[t], start + (i + 1) * CELLS[t]) for i in range(n)]

    def cells_all(t):
        return slice(0, n * CELLS[0]) if t == 0 else slice(n * CELLS[0], n * sum(CELLS))

    place_span = (slice(0, CELLS[0]), slice(CELLS[0], sum(CELLS)))
    half = lane < 64
    own_half = (half, jnp.logical_not(half))

    def near_shift(t, off):
        return ((off // 3 - 1) * SIDES[t] + off % 3 - 1) % CELLS[t]

    def attention_forward(j):
        def first(ts):
            xhat, scale = norm_parts(xs[ts, :])
            xh_a[j, ts, :] = xhat
            sc_a[j, ts, :] = jnp.broadcast_to(scale, xhat.shape)
            u_a[j, ts, :] = (xhat * row(ng, j, 0) + row(ns, j, 0)).astype(bf16)

        tiles(first)
        for i in range(n):
            span = slice(i * TOK, (i + 1) * TOK)
            u = u_a[j, span, :]
            q_a[j, span, :] = (nn(u, qw[j]) + row(qb, j)).astype(bf16)
            um[:, i * C : (i + 1) * C] = (u.astype(f32) * valid[span, :]).astype(bf16)
        pc[...] = nn(perm[...], um[...]).astype(bf16)
        base = 0
        for t, ref in enumerate((p4, p2)):
            for k in range(STRIDES[t] ** 2):
                for i in range(n):
                    ref[j, i * CELLS[t] : (i + 1) * CELLS[t], k * C : (k + 1) * C] = pc[
                        base : base + CELLS[t], i * C : (i + 1) * C
                    ]
                base += CELLS[t]
        for t, (ref, weight) in enumerate(((p4, p4w), (p2, p2w))):
            xhat, scale = norm_parts(nn(ref[j], weight[j]))
            act, slope = gelu_parts(xhat * row(ng, j, 1 + t) + row(ns, j, 1 + t))
            act = act.astype(bf16)
            span = cells_all(t)
            xh_p[j, span, :] = xhat
            sc_p[j, span, :] = jnp.broadcast_to(scale, xhat.shape)
            ge_p[j, span, :] = slope
            kin[j, span, :] = act
            keyval = nn(act, kvw[j, t])
            turned = pltpu.roll(keyval, 64, 1)
            keys, vals = (keyval, turned) if t == 0 else (turned, keyval)
            bias = jnp.concatenate([row(vb, j, 0), row(vb, j, 1)], axis=1)
            kernel = jnp.concatenate([lk[j, :, 0, :], lk[j, :, 1, :]], axis=1)
            for i in range(n):
                part = slice(i * CELLS[t], (i + 1) * CELLS[t])
                w = (vals[part] + bias) * kmask[i, place_span[t], :]
                wv[j, cell_spans(t)[i], :] = w
                v = w
                for off in range(9):
                    by = near_shift(t, off)
                    moved = pltpu.roll(w, (CELLS[t] - by) % CELLS[t], 0) if by else w
                    v = v + moved * (near[off, place_span[t], :] * kernel[off : off + 1])
                for h in (2 * t, 2 * t + 1):
                    seg_rows = slice(*SEGS[h])
                    kb[j, i, seg_rows, :] = jnp.where(head_lanes(h), keys[part], 0.0).astype(bf16)
                    vbd[j, i, seg_rows, :] = jnp.where(head_lanes(h), v, 0.0).astype(bf16)
        for i in range(n):
            span = slice(i * TOK, (i + 1) * TOK)
            scores = nt(kb[j, i], q_a[j, span, :])
            for h, (low, top) in enumerate(SEGS):
                mask = kmask[i, place_span[h // 2], 0:1] > 0
                for c0 in range(0, TOK, 128):
                    c1 = min(c0 + 128, TOK)
                    s = jnp.where(mask, scores[low:top, c0:c1], -1e30)
                    e = jnp.exp2((s - jnp.max(s, axis=0, keepdims=True)) * (ROOT * LOG2E))
                    weight = e * pl.reciprocal(jnp.sum(e, axis=0, keepdims=True), approx=True)
                    pt[j, i, low:top, c0:c1] = weight.astype(bf16)
            mixed = tn(vbd[j, i], pt[j, i])
            o_t[j, i] = mixed.astype(bf16)
            o_n[span, :] = mixed.T.astype(bf16)
        set_sval(2 * j)
        for i in range(n):
            span = slice(i * TOK, (i + 1) * TOK)
            branch = nn(o_n[span, :], pw[j]) + row(pb, j)
            xs[span, :] = (xs[span, :] + sval[span, :] * branch).astype(bf16).astype(f32)

    def build_wc(j):
        bias = row(hb, j)

        def tap(off, carry):
            factor = mk[off, j : j + 1, :] + jnp.where(off == 4, 1.0, 0.0)
            for r0 in range(0, C, 32):
                wc[j, pl.ds(pl.multiple_of(off * C + r0, 32), 32), :] = (
                    hw[j, r0 : r0 + 32, :].astype(f32) * factor
                ).astype(bf16)
            return carry

        lax.fori_loop(0, TAPS, tap, 0)
        ex[...] = jnp.zeros_like(ex)
        each = mk[:, j, :] * bias
        both = bias + row(mb, j)
        each_high = each.astype(bf16).astype(f32)
        both_high = both.astype(bf16).astype(f32)
        ex[0:9, :] = each_high
        ex[16:17, :] = both_high
        ex[32:41, :] = each - each_high
        ex[48:49, :] = both - both_high
        wc[j, TAPS * C :, :] = ex[...].astype(bf16)

    def mlp_forward(j):
        build_wc(j)

        def first(ts):
            xhat, scale = norm_parts(xs[ts, :])
            xh_m[j, ts, :] = xhat
            sc_m[j, ts, :] = jnp.broadcast_to(scale, xhat.shape)
            u = (xhat * row(ng, j, 3) + row(ns, j, 3)).astype(bf16).astype(f32)
            acc[0, ts, :] = u * valid[ts, :]

        tiles(first)
        for i in range(n):
            span = slice(i * TOK, (i + 1) * TOK)
            for off, piece in taps_of(acc[0, span, :]):
                u_all[j, span, off * C : (off + 1) * C] = piece.astype(bf16)

        for start in range(0, FF, CHUNK):
            cols = slice(start, start + CHUNK)
            for i in range(n):
                field = nn(u_all[j, i * TOK : (i + 1) * TOK, :], wc[j, :, cols])
                for r0 in range(0, TOK, 16):
                    act, slope = gelu_parts(field[r0 : r0 + 16])
                    part = slice(i * TOK + r0, i * TOK + r0 + 16)
                    a_all[j, part, cols] = act.astype(bf16)
                    g_all[j, part, cols] = slope.astype(bf16)
        set_sval(2 * j + 1)
        for i in range(n):
            span = slice(i * TOK, (i + 1) * TOK)
            branch = nn(a_all[j, span, :], ow[j]) + row(ob, j)
            xs[span, :] = (xs[span, :] + sval[span, :] * branch).astype(bf16).astype(f32)

    def mlp_backward(j):
        base, sb = MLP_AT[j], j * S_BLOCK
        set_sval(2 * j + 1)

        def first(ts):
            grad = (xs[ts, :] * sval[ts, :]).astype(bf16)
            db[ts, :] = grad
            return [folded(grad.astype(f32))]

        (small[sb + S_OB : sb + S_OB + 1, :],) = tiles(first)
        db_t[...] = db[...].T
        for off in range(TAPS + 1):
            ut[off * C : (off + 1) * C, :] = u_all[j, :, off * C : (off + 1) * C].T
        bias = row(hb, j)

        def chunk(step):
            cols = slice(step * CHUNK, (step + 1) * CHUNK)
            for i in range(n):
                span = slice(i * TOK, (i + 1) * TOK)
                da = nt(db[span, :], ow[j, cols, :])
                g_all[j, span, cols] = (da * g_all[j, span, cols].astype(f32)).astype(bf16)
            dfield = g_all[j, :, cols]
            dow = nn(db_t[...], a_all[j, :, cols])
            at = base + R_OUT + step * CHUNK
            gp[at : at + CHUNK, :] = dow.T.astype(bf16)
            cross = nn(ut[...], dfield)
            flag_rows = cross[TAPS * C : TAPS * C + 24]
            total = flag_rows[16:17]
            dhb = total
            weight = hw[j, :, cols].astype(f32)
            dweight = jnp.zeros((C, CHUNK), f32)
            b = hb[pl.ds(j, 1), cols]
            for off in range(TAPS):
                piece = cross[off * C : (off + 1) * C]
                factor = mk[off, j : j + 1, cols]
                flag = flag_rows[off : off + 1]
                dweight = dweight + piece * (factor + (1.0 if off == 4 else 0.0))
                dk = col_sum(piece * weight) + b * flag
                dhb = dhb + factor * flag
                for s in range(CHUNK // C):
                    at = sb + S_MK + 16 * (step * (CHUNK // C) + s) + off
                    small[at : at + 1, :] = dk[:, s * C : (s + 1) * C]
            for s in range(CHUNK // C):
                at = step * (CHUNK // C) + s
                part = slice(s * C, (s + 1) * C)
                small[sb + S_HB + at : sb + S_HB + at + 1, :] = dhb[:, part]
                small[sb + S_MB + at : sb + S_MB + at + 1, :] = total[:, part]
                at = base + R_HID + at * C
                gp[at : at + C, :] = dweight[:, part].astype(bf16)

        for step in range(FF // CHUNK):
            chunk(step)
        acc[...] = jnp.zeros_like(acc)
        for first_off in range(0, TAPS, 2):
            width = min(2, TAPS - first_off)
            for i in range(n):
                at = i * TOK
                moved = nt(
                    g_all[j, at : at + TOK, :], wc[j, first_off * C : (first_off + width) * C, :]
                )
                for s in range(width):
                    off = first_off + s
                    by = (off // 3 - 1) * GRID
                    piece = moved[:, s * C : (s + 1) * C]
                    if by >= 0:
                        acc[off % 3, at + by : at + TOK, :] += piece[: TOK - by]
                    else:
                        acc[off % 3, at : at + TOK + by, :] += piece[-by:]
        for i in range(n):
            span = slice(i * TOK, (i + 1) * TOK)
            left = pltpu.roll(jnp.where(col > 0, acc[0, span, :], 0.0), TOK - 1, 0)
            right = pltpu.roll(jnp.where(col < GRID - 1, acc[2, span, :], 0.0), 1, 0)
            acc[1, span, :] = (acc[1, span, :] + left + right) * valid[span, :]

        def last(ts):
            du = acc[1, ts, :]
            xhat = xh_m[j, ts, :]
            back = norm_back(du, xhat, sc_m[j, ts, :], row(ng, j, 3))
            xs[ts, :] = (xs[ts, :] + back).astype(bf16).astype(f32)
            return [folded(du * xhat), folded(du)]

        gain, shift = tiles(last)
        small[sb + S_GAIN + 3 : sb + S_GAIN + 4, :] = gain
        small[sb + S_SHIFT + 3 : sb + S_SHIFT + 4, :] = shift

    def attention_backward(j):
        base, sb = ATT_AT[j], j * S_BLOCK
        set_sval(2 * j)

        def first(ts):
            grad = (xs[ts, :] * sval[ts, :]).astype(bf16)
            db[ts, :] = grad
            return [folded(grad.astype(f32))]

        (small[sb + S_PB : sb + S_PB + 1, :],) = tiles(first)
        dproj = jnp.zeros((C, C), f32)
        kernel = jnp.concatenate([lk[j, :, 0, :], lk[j, :, 1, :]], axis=1)
        dkernel = [jnp.zeros((1, C), f32) for _ in range(9)]
        dbias = jnp.zeros((1, C), f32)
        for i in range(n):
            span = slice(i * TOK, (i + 1) * TOK)
            dproj = dproj + nn(o_t[j, i], db[span, :])
            do = nt(db[span, :], pw[j]).astype(bf16)
            dprobs = nt(vbd[j, i], do)
            dvals = nn(pt[j, i], do)
            for low, top in SEGS:
                for c0 in range(0, TOK, 128):
                    c1 = min(c0 + 128, TOK)
                    weight = pt[j, i, low:top, c0:c1].astype(f32)
                    dweight = dprobs[low:top, c0:c1]
                    dot = jnp.sum(weight * dweight, axis=0, keepdims=True)
                    pt[j, i, low:top, c0:c1] = (weight * (dweight - dot)).astype(bf16)
            dkeys = nn(pt[j, i], q_a[j, span, :]) * ROOT
            dq = tn(kb[j, i], pt[j, i]) * ROOT
            o_n[span, :] = dq.T.astype(bf16)
            for t in range(2):
                dk = jnp.zeros((CELLS[t], C), f32)
                dv = jnp.zeros((CELLS[t], C), f32)
                for h in (2 * t, 2 * t + 1):
                    dk = dk + jnp.where(head_lanes(h), dkeys[slice(*SEGS[h])], 0.0)
                    dv = dv + jnp.where(head_lanes(h), dvals[slice(*SEGS[h])], 0.0)
                w = wv[j, cell_spans(t)[i], :]
                dw = dv
                for off in range(9):
                    by = near_shift(t, off)
                    part = dv * near[off, place_span[t], :]
                    moved = pltpu.roll(w, (CELLS[t] - by) % CELLS[t], 0) if by else w
                    dkernel[off] = dkernel[off] + col_sum(part * moved)
                    part = part * kernel[off : off + 1]
                    dw = dw + (pltpu.roll(part, by, 0) if by else part)
                dw = dw * kmask[i, place_span[t], :]
                dbias = dbias + col_sum(dw)
                if t == 0:
                    dkeyval = dk + pltpu.roll(dw, 64, 1)
                else:
                    dkeyval = pltpu.roll(dk, 64, 1) + dw
                wv[j, cell_spans(t)[i], :] = dkeyval
        gp[base + R_PROJ : base + R_PROJ + C, :] = dproj.astype(bf16)
        small[sb + S_VB : sb + S_VB + 1, :] = dbias
        for off in range(9):
            small[sb + S_LK + off : sb + S_LK + off + 1, :] = dkernel[off]
        base_perm = 0
        for t, (ref, weight) in enumerate(((p4, p4w), (p2, p2w))):
            span = cells_all(t)
            dkeyval = wv[j, span, :].astype(bf16)
            at = base + R_KV + t * C
            gp[at : at + C, :] = tn(kin[j, span, :], dkeyval).astype(bf16)
            dy = nt(dkeyval, kvw[j, t]) * ge_p[j, span, :]
            xhat = xh_p[j, span, :]
            small[sb + S_GAIN + 1 + t : sb + S_GAIN + 2 + t, :] = col_sum(dy * xhat)
            small[sb + S_SHIFT + 1 + t : sb + S_SHIFT + 2 + t, :] = col_sum(dy)
            dpool = norm_back(dy, xhat, sc_p[j, span, :], row(ng, j, 1 + t)).astype(bf16)
            at = base + (R_P4, R_P2)[t]
            for k in range(STRIDES[t] ** 2):
                gp[at + k * C : at + (k + 1) * C, :] = tn(
                    ref[j, :, k * C : (k + 1) * C], dpool
                ).astype(bf16)
                back = nt(dpool, weight[j, k * C : (k + 1) * C, :]).astype(bf16)
                for i in range(n):
                    pc[base_perm : base_perm + CELLS[t], i * C : (i + 1) * C] = back[
                        i * CELLS[t] : (i + 1) * CELLS[t]
                    ]
                base_perm += CELLS[t]
        at = base + R_Q
        gp[at : at + C, :] = tn(u_a[j], o_n[...]).astype(bf16)
        spread = nn(perm_t[...], pc[...])
        for i in range(n):
            span = slice(i * TOK, (i + 1) * TOK)
            back = nt(o_n[span, :], qw[j])
            acc[0, span, :] = back + spread[:, i * C : (i + 1) * C] * valid[span, :]

        def last(ts):
            du = acc[0, ts, :]
            xhat = xh_a[j, ts, :]
            back = norm_back(du, xhat, sc_a[j, ts, :], row(ng, j, 0))
            xs[ts, :] = (xs[ts, :] + back).astype(bf16).astype(f32)
            return [folded(o_n[ts, :].astype(f32)), folded(du * xhat), folded(du)]

        bias, gain, shift = tiles(last)
        small[sb + S_QB : sb + S_QB + 1, :] = bias
        small[sb + S_GAIN : sb + S_GAIN + 1, :] = gain
        small[sb + S_SHIFT : sb + S_SHIFT + 1, :] = shift

    for j in range(BLOCKS):
        attention_forward(j)
        mlp_forward(j)
    out_ref[...] = xs[...].astype(bf16)
    xs[...] = cot_ref[...].astype(f32)
    for j in reversed(range(BLOCKS)):
        mlp_backward(j)
        attention_backward(j)
    gp[R_SMALL:, :] = small[...].astype(bf16)
    dx_ref[...] = xs[...].astype(bf16)


def compute(own, images, grid_size, keep_mask, x, cot, weights):
    n = images
    rows = n * TOK
    cells = n * sum(CELLS)
    vmem = pl.BlockSpec(memory_space=pltpu.VMEM)
    smem = pl.BlockSpec(memory_space=pltpu.SMEM)
    matrix = permutation()
    consts = (
        jnp.asarray(matrix, bf16),
        jnp.asarray(matrix.T, bf16),
        jnp.asarray(cell_places()),
    )
    B = BLOCKS
    scratch = [
        pltpu.VMEM((rows, C), f32),
        pltpu.VMEM((rows, C), f32),
        pltpu.VMEM((rows, C), f32),
        pltpu.VMEM((TOK, n * C), bf16),
        pltpu.VMEM((B, rows, UW), bf16),
        pltpu.VMEM((UW, rows), bf16),
        pltpu.VMEM((B, UW, FF), bf16),
        pltpu.VMEM((C, FF), f32),
        pltpu.VMEM((B, rows, C), f32),
        pltpu.VMEM((B, rows, C), f32),
        pltpu.VMEM((B, rows, C), f32),
        pltpu.VMEM((B, rows, C), f32),
        pltpu.VMEM((B, rows, C), bf16),
        pltpu.VMEM((B, rows, C), bf16),
        pltpu.VMEM((B, n * CELLS[0], 16 * C), bf16),
        pltpu.VMEM((B, n * CELLS[1], 4 * C), bf16),
        pltpu.VMEM((B, cells, C), f32),
        pltpu.VMEM((B, cells, C), f32),
        pltpu.VMEM((B, cells, C), f32),
        pltpu.VMEM((B, cells, C), bf16),
        pltpu.VMEM((B, cells, C), f32),
        pltpu.VMEM((B, n, KEYS, C), bf16),
        pltpu.VMEM((B, n, KEYS, C), bf16),
        pltpu.VMEM((B, n, KEYS, TOK), bf16),
        pltpu.VMEM((B, n, C, TOK), bf16),
        pltpu.VMEM((rows, C), bf16),
        pltpu.VMEM((B, rows, FF), bf16),
        pltpu.VMEM((B, rows, FF), bf16),
        pltpu.VMEM((rows, C), bf16),
        pltpu.VMEM((C, rows), bf16),
        pltpu.VMEM((3, rows, C), f32),
        pltpu.VMEM((n, sum(CELLS), C), f32),
        pltpu.VMEM((9, sum(CELLS), C), f32),
        pltpu.VMEM((ROWS - R_SMALL, C), f32),
        pltpu.VMEM((PERM, n * C), bf16),
        pltpu.SMEM((n, 2 * BLOCKS), f32),
    ]
    return pl.pallas_call(
        functools.partial(compute_kernel, own, images),
        out_shape=(
            jax.ShapeDtypeStruct((rows, C), bf16),
            jax.ShapeDtypeStruct((rows, C), bf16),
            jax.ShapeDtypeStruct((ROWS, C), bf16),
        ),
        in_specs=[smem, smem] + [vmem] * (2 + len(weights) + len(consts)),
        out_specs=(vmem, vmem, vmem),
        scratch_shapes=scratch,
        compiler_params=pltpu.CompilerParams(vmem_limit_bytes=62 * 2**20),
        name="compute",
    )(grid_size, keep_mask, x, cot, *weights, *consts)


def sum_kernel(sizes, src, total, half_in, quarter_in, part_in, whole_in, own, send, recv):
    seg, dp = lax.axis_index("segment"), lax.axis_index("dp")
    greet(seg, dp, *sizes)()
    refs = (src, half_in, quarter_in, part_in, whole_in, own, total, send, recv)
    pieces = [
        Summed((seg, dp) + sizes, p, base, count, refs) for p, (base, count) in enumerate(PIECES)
    ]
    for t in range(Summed.STEPS + len(pieces) - 1):
        for p, piece in enumerate(pieces):
            if 0 <= t - p < Summed.STEPS:
                piece.step(t - p)
    for piece in pieces:
        piece.drain()


def summed(packed):
    segments, pairs = lax.axis_size("segment"), lax.axis_size("dp") // 2
    inner = min(pairs, 4)
    sizes = (segments, inner, pairs // inner)
    vmem = pl.BlockSpec(memory_space=pltpu.VMEM)
    return pl.pallas_call(
        functools.partial(sum_kernel, sizes),
        out_shape=jax.ShapeDtypeStruct((ROWS, C), bf16),
        in_specs=[vmem],
        out_specs=vmem,
        scratch_shapes=sum_scratch(sizes),
        compiler_params=pltpu.CompilerParams(
            collective_id=0, has_side_effects=True, vmem_limit_bytes=40 * 2**20
        ),
        name="summed",
    )(packed)


def unpack_kernel(gp, out_in, dx_in, *refs):
    out_ref, dx_ref = refs[:2]
    gain, shift, qw, qb, p4, p2, kvw, vb, lk, pw, pb, hw, hb, mk, mb, ow, ob = refs[2:]
    out_ref[...] = out_in[...]
    dx_ref[...] = dx_in[...]
    for j in range(BLOCKS):
        att, mlp, sb = ATT_AT[j], MLP_AT[j], R_SMALL + j * S_BLOCK
        p4[j] = gp[att + R_P4 : att + R_P2, :].astype(f32)
        p2[j] = gp[att + R_P2 : att + R_KV, :].astype(f32)
        for t in range(2):
            kvw[j, t] = gp[att + R_KV + t * C : att + R_KV + (t + 1) * C, :].astype(f32)
        qw[j] = gp[att + R_Q : att + R_PROJ, :].astype(f32)
        pw[j] = gp[att + R_PROJ : att + R_ATT, :].astype(f32)
        for s in range(FF // C):
            at = mlp + R_HID + s * C
            hw[j, :, s * C : (s + 1) * C] = gp[at : at + C, :].astype(f32)
        ow[j] = gp[mlp + R_OUT : mlp + R_MLP, :].astype(f32)
        head = gp[sb : sb + 48, :].astype(f32)
        gain[j] = head[S_GAIN : S_GAIN + 4]
        shift[j] = head[S_SHIFT : S_SHIFT + 4]
        qb[j : j + 1, :] = head[S_QB : S_QB + 1]
        vb[j, 0:1, :] = head[S_VB : S_VB + 1, 0:64]
        vb[j, 1:2, :] = head[S_VB : S_VB + 1, 64:128]
        pb[j : j + 1, :] = head[S_PB : S_PB + 1]
        ob[j : j + 1, :] = head[S_OB : S_OB + 1]
        lk[j, :, 0, :] = head[S_LK : S_LK + 9, 0:64]
        lk[j, :, 1, :] = head[S_LK : S_LK + 9, 64:128]
        for s in range(FF // C):
            part = slice(s * C, (s + 1) * C)
            hb[j : j + 1, part] = head[S_HB + s : S_HB + s + 1]
            mb[j : j + 1, part] = head[S_MB + s : S_MB + s + 1]
            at = sb + S_MK + 16 * s
            mk[:, j, part] = gp[at : at + 16, :].astype(f32)[0:9]


def unpack(packed, outputs, input_grad, weights):
    vmem = pl.BlockSpec(memory_space=pltpu.VMEM)
    streams = (jax.ShapeDtypeStruct(outputs.shape, bf16),) * 2
    return pl.pallas_call(
        unpack_kernel,
        out_shape=streams + tuple(jax.ShapeDtypeStruct(w.shape, f32) for w in weights),
        in_specs=[vmem] * 3,
        out_specs=(vmem,) * (2 + len(weights)),
        compiler_params=pltpu.CompilerParams(vmem_limit_bytes=40 * 2**20),
        name="unpack",
    )(packed, outputs, input_grad)


def on_device(inputs, grid_size, keep_mask, cotangent, *weights):
    own, per = inputs.shape[:2]
    images = own * per
    flat = (images * TOK, C)
    turned = list(weights)
    turned[LK] = jnp.transpose(turned[LK], (0, 2, 1, 3))
    turned[MK] = jnp.transpose(turned[MK], (1, 0, 2))
    outputs, input_grad, packed = compute(
        own,
        images,
        jnp.transpose(grid_size, (1, 2, 0)),
        jnp.transpose(keep_mask, (1, 2, 0)),
        inputs.reshape(flat),
        cotangent.reshape(flat),
        turned,
    )
    outputs, input_grad, *grads = unpack(summed(packed), outputs, input_grad, turned)
    grads[LK] = jnp.transpose(grads[LK], (0, 2, 1, 3))
    grads[MK] = jnp.transpose(grads[MK], (1, 0, 2))
    return (outputs.reshape(inputs.shape), input_grad.reshape(inputs.shape)) + tuple(grads)


def solution(mesh):
    stream = P("segment", "dp", None, None)
    picked = P(None, "dp", None)
    return jax.shard_map(
        on_device,
        mesh=mesh,
        in_specs=(stream, picked, picked, stream) + (P(),) * 17,
        out_specs=(stream, stream) + (P(),) * 17,
        check_vma=False,
    )
```

```python
import functools

import jax
import jax.numpy as jnp
import numpy as np
from jax import lax
from jax.experimental import pallas as pl
from jax.experimental.pallas import tpu as pltpu
from jax.sharding import PartitionSpec as P

GRID = 24
TOK = GRID * GRID
C = 128
FF = 1024
HEAD = 32
BLOCKS = 2
SIDES = (6, 12)
STRIDES = (4, 2)
CELLS = (48, 144)
SEGS = ((0, 48), (48, 96), (96, 240), (240, 384))
KEYS = 384
PERM = 16 * 48 + 4 * 144
TAPS = 9
UW = TAPS * C + C
CHUNK = 512
TILE = 96

R_P4, R_P2, R_KV, R_Q, R_PROJ, R_ATT = 0, 2048, 2560, 2816, 2944, 3072
R_MLP = 2048
ATT_AT = (R_ATT, 0)
MLP_AT = (2 * R_ATT + R_MLP, 2 * R_ATT)
S_GAIN, S_SHIFT, S_QB, S_VB, S_PB, S_OB, S_LK, S_HB, S_MB, S_MK, S_BLOCK = (
    0,
    4,
    8,
    9,
    10,
    11,
    16,
    32,
    40,
    48,
    192,
)
R_SMALL = BLOCKS * (R_ATT + R_MLP)
ROWS = R_SMALL + 512
PIECES = (
    (ATT_AT[1], R_ATT, False),
    (ATT_AT[0], R_ATT, False),
    (MLP_AT[1], R_MLP, False),
    (MLP_AT[0], R_MLP // 2, True),
    (MLP_AT[0] + R_MLP // 2, R_MLP // 2 + ROWS - R_SMALL, True),
)

LK, HW, MK, OW = 8, 11, 13, 15

epsilon = 1e-06
keep_rate = 0.8
ROOT = HEAD**-0.5
LOG2E = 1.4426950408889634
f32, bf16 = jnp.float32, jnp.bfloat16


def hidden_row(tile):
    return tile // (CHUNK // C) * 2 * CHUNK + tile % (CHUNK // C) * C


def output_row(step):
    return step * 2 * CHUNK + CHUNK


def permutation():
    matrix = np.zeros((PERM, TOK), np.float32)
    base = 0
    for stride, side, cells in zip(STRIDES, SIDES, CELLS):
        for row_off in range(stride):
            for col_off in range(stride):
                for a in range(side):
                    for b in range(side):
                        token = (a * stride + row_off) * GRID + b * stride + col_off
                        matrix[base + a * side + b, token] = 1.0
                base += cells
    return matrix


def cell_places():
    places = np.full((2, sum(CELLS), 128), 99.0, np.float32)
    base = 0
    for side, cells in zip(SIDES, CELLS):
        for a in range(side):
            for b in range(side):
                places[0, base + a * side + b] = a
                places[1, base + a * side + b] = b
        base += cells
    return places


def nn(left, right):
    return jnp.dot(left, right, preferred_element_type=f32)


def nt(left, right):
    return lax.dot_general(left, right, (((1,), (1,)), ((), ())), preferred_element_type=f32)


def tn(left, right):
    return lax.dot_general(left, right, (((0,), (0,)), ((), ())), preferred_element_type=f32)


def gelu_parts(m):
    size = jnp.abs(m)
    t = pl.reciprocal(1.0 + (0.3275911 * 0.5**0.5) * size, approx=True)
    e = jnp.exp2(m * (m * (-0.5 * LOG2E)))
    poly = 0.5 * 1.061405429
    for coef in (-1.453152027, 1.421413741, -0.284496736, 0.254829592):
        poly = poly * t + 0.5 * coef
    poly = poly * t
    tail = poly * e
    slope = (poly - size * 0.3989422804014327) * e
    return jnp.maximum(m, 0.0) - size * tail, jnp.where(m >= 0, 1.0 - slope, slope)


def norm_parts(x):
    centred = x - jnp.mean(x, axis=-1, keepdims=True)
    scale = lax.rsqrt(jnp.mean(centred * centred, axis=-1, keepdims=True) + epsilon)
    return centred * scale, scale


def norm_back(du, xhat, scale, gain):
    dxhat = du * gain
    first = jnp.mean(dxhat, axis=-1, keepdims=True)
    second = jnp.mean(dxhat * xhat, axis=-1, keepdims=True)
    return scale * (dxhat - first - xhat * second)


def col_sum(x):
    return jnp.sum(x, axis=0, keepdims=True)


def folded(x):
    return jnp.sum(x.reshape(-1, 8, x.shape[-1]), axis=0)


class Summed:
    def __init__(self, place, piece, base, count, short, refs):
        self.seg, self.dp, self.segments, self.inner, self.outer = place
        self.piece, self.base, self.count = piece, base, count
        self.short = short
        (
            self.src,
            self.half_in,
            self.quarter_in,
            self.part_in,
            self.cross_in,
            self.whole_in,
            self.own,
            self.total,
            self.send,
            self.recv,
        ) = refs
        self.core, rest = self.dp % 2, self.dp // 2
        self.part, self.group = rest % self.inner, rest // self.inner
        self.half = count // 2
        self.quarter = self.half // self.segments
        self.share = self.quarter // self.inner
        self.started = []

    def span(self, start, size):
        return pl.ds(pl.multiple_of(start, 16), size)

    def device(self, seg=None, core=None, part=None, group=None):
        seg = self.seg if seg is None else seg
        core = self.core if core is None else core
        part = self.part if part is None else part
        group = self.group if group is None else group
        return (seg, (group * self.inner + part) * 2 + core)

    def copy(self, slot, src, dst, device):
        made = pltpu.make_async_remote_copy(
            src_ref=src,
            dst_ref=dst,
            send_sem=self.send.at[self.piece, slot],
            recv_sem=self.recv.at[self.piece, slot],
            device_id=device,
            device_id_type=pl.DeviceIdType.MESH,
        )
        made.start()
        self.started.append(made)
        return made

    def half_at(self, core):
        return self.span(self.base + core * self.half, self.half)

    def own_at(self, seg, part=None):
        start = self.base // 2 + seg * self.quarter
        if part is None:
            return self.span(start, self.quarter)
        return self.span(start + part * self.share, self.share)

    def total_at(self, seg=None, part=None):
        start = self.base + self.core * self.half
        if seg is None:
            return self.span(start, self.half)
        start = start + seg * self.quarter
        if part is None:
            return self.span(start, self.quarter)
        return self.span(start + part * self.share, self.share)

    def step(self, k):
        if self.short:
            steps = (self.pair_out, self.cross_out, self.cross_back, self.pair_back, self.finish)
        else:
            steps = (
                self.pair_out,
                self.segment_out,
                self.part_out,
                self.part_back,
                self.segment_back,
                self.pair_back,
                self.finish,
            )
        steps[k]()

    def pair_out(self):
        self.waits = [
            self.copy(
                0,
                self.src.at[self.half_at(1 - self.core), :],
                self.half_in.at[self.span(self.base // 2, self.half), :],
                self.device(core=1 - self.core),
            )
        ]

    def arrived(self):
        for made in self.waits:
            made.wait_recv()
        self.waits = []

    def add(self, dst, first, others, count):
        step = next(size for size in (128, 96, 80, 64, 48, 32, 16) if count % size == 0)

        def body(t, carry):
            at = t * step
            total = first[0][self.span(first[1] + at, step), :].astype(f32)
            for ref, start in others:
                total = total + ref[self.span(start + at, step), :].astype(f32)
            dst[0][self.span(dst[1] + at, step), :] = total.astype(bf16)
            return carry

        lax.fori_loop(0, count // step, body, 0)

    def pair_sum(self):
        self.arrived()
        own = self.base // 2
        self.add(
            (self.own, own),
            (self.src, self.base + self.core * self.half),
            [(self.half_in, own)],
            self.half,
        )

    def segment_out(self):
        self.pair_sum()
        at = self.span(self.base // 2 // self.segments, self.quarter)
        for d in range(1, self.segments):
            to = self.seg ^ d
            self.waits.append(
                self.copy(
                    d,
                    self.own.at[self.own_at(to), :],
                    self.quarter_in.at[d - 1, at, :],
                    self.device(seg=to),
                )
            )

    def part_out(self):
        self.arrived()
        start = self.base // 2 + self.seg * self.quarter
        at = self.base // 2 // self.segments
        others = [(self.quarter_in.at[d], at) for d in range(self.segments - 1)]
        self.add((self.own, start), (self.own, start), others, self.quarter)
        at = self.span(self.base // 2 // self.segments // self.inner, self.share)
        for d in range(1, self.inner):
            to = self.part ^ d
            self.waits.append(
                self.copy(
                    self.segments + d - 1,
                    self.own.at[self.own_at(self.seg, to), :],
                    self.part_in.at[d - 1, at, :],
                    self.device(part=to),
                )
            )

    def crossed(self):
        for d in range(1, self.segments * self.inner):
            yield d - 1, self.seg ^ (d // self.inner), self.part ^ (d % self.inner)

    def share_in(self):
        return self.base // 2 // self.segments // self.inner

    def cross_out(self):
        self.pair_sum()
        at = self.span(self.share_in(), self.share)
        for slot, seg, part in self.crossed():
            self.waits.append(
                self.copy(
                    1 + slot,
                    self.own.at[self.own_at(seg, part), :],
                    self.cross_in.at[slot, at, :],
                    self.device(seg=seg, part=part),
                )
            )

    def share_sum(self, received, slot):
        self.arrived()
        start = self.base // 2 + self.seg * self.quarter + self.part * self.share
        at = self.share_in()
        others = [(received.at[d], at) for d in range(received.shape[0])]
        into = self.base + self.core * self.half + self.seg * self.quarter + self.part * self.share
        if self.outer > 1:
            self.add((self.own, start), (self.own, start), others, self.share)
            for d in range(1, self.outer):
                self.waits.append(
                    self.copy(
                        slot + d - 1,
                        self.own.at[self.own_at(self.seg, self.part), :],
                        self.whole_in.at[d - 1, self.span(at, self.share), :],
                        self.device(group=self.group ^ d),
                    )
                )
            self.arrived()
            others = [(self.whole_in.at[d], at) for d in range(self.outer - 1)]
            slot += self.outer - 1
        self.add((self.total, into), (self.own, start), others, self.share)
        return slot

    def part_back(self):
        slot = self.share_sum(self.part_in, self.segments + self.inner - 1)
        at = self.total_at(self.seg, self.part)
        for d in range(1, self.inner):
            made = self.copy(
                slot + d - 1, self.total.at[at, :], self.total.at[at, :], self.device(part=self.part ^ d)
            )
            self.waits.append(made)
        self.slot = slot + self.inner - 1

    def cross_back(self):
        peers = self.segments * self.inner - 1
        slot = self.share_sum(self.cross_in, 1 + peers)
        at = self.total_at(self.seg, self.part)
        for d, seg, part in self.crossed():
            made = self.copy(
                slot + d, self.total.at[at, :], self.total.at[at, :], self.device(seg=seg, part=part)
            )
            self.waits.append(made)
        self.slot = slot + peers

    def segment_back(self):
        self.arrived()
        at = self.total_at(self.seg)
        for d in range(1, self.segments):
            made = self.copy(
                self.slot + d - 1,
                self.total.at[at, :],
                self.total.at[at, :],
                self.device(seg=self.seg ^ d),
            )
            self.waits.append(made)
        self.slot += self.segments - 1

    def pair_back(self):
        self.arrived()
        at = self.total_at()
        self.waits.append(
            self.copy(
                self.slot, self.total.at[at, :], self.total.at[at, :], self.device(core=1 - self.core)
            )
        )

    def finish(self):
        self.arrived()

    def drain(self):
        for made in self.started:
            made.wait_send()


def slots_of(segments, inner, outer):
    return 2 + 2 * (segments * inner - 1) + (outer - 1)


def greet(seg, dp, segments, inner, outer):
    barrier = pltpu.get_barrier_semaphore()
    core, part, group = dp % 2, dp // 2 % inner, dp // 2 // inner
    peers = [(seg, dp + 1 - 2 * core)]
    peers += [
        (seg ^ (d // inner), (group * inner + (part ^ (d % inner))) * 2 + core)
        for d in range(1, segments * inner)
    ]
    peers += [(seg, ((group ^ d) * inner + part) * 2 + core) for d in range(1, outer)]
    for peer in peers:
        pl.semaphore_signal(
            barrier, inc=1, device_id=peer, device_id_type=pl.DeviceIdType.MESH
        )
    return lambda: pl.semaphore_wait(barrier, len(peers))


def sum_scratch(sizes):
    segments, inner, outer = sizes
    quarter = ROWS // 2 // segments
    share = quarter // inner
    slots = slots_of(*sizes)
    return [
        pltpu.VMEM((ROWS // 2, C), bf16),
        pltpu.VMEM((segments - 1, quarter, C), bf16),
        pltpu.VMEM((inner - 1, share, C), bf16),
        pltpu.VMEM((segments * inner - 1, share, C), bf16),
        pltpu.VMEM((max(outer - 1, 1), share, C), bf16),
        pltpu.VMEM((ROWS // 2, C), bf16),
        pltpu.VMEM((ROWS, C), bf16),
        pltpu.SemaphoreType.DMA((len(PIECES), slots)),
        pltpu.SemaphoreType.DMA((len(PIECES), slots)),
    ]


def compute_kernel(
    own,
    images,
    sizes,
    grid_ref,
    keep_ref,
    x_ref,
    cot_in,
    ng,
    ns,
    qw,
    qb,
    p4w,
    p2w,
    kvw,
    vb,
    lk,
    pw,
    pb,
    hw_in,
    hb,
    mk,
    mb,
    ow_in,
    ob,
    perm,
    perm_t_in,
    places,
    out_ref,
    dx_ref,
    summed_ref,
    xs,
    valid,
    um,
    u_all,
    ut,
    wc,
    ex,
    xh_a,
    xh_m,
    sc,
    u_a,
    q_a,
    p4,
    p2,
    xh_p,
    sc_p,
    ge_p,
    kin,
    wv,
    kb,
    vbd,
    pt,
    o_t,
    o_n,
    a_all,
    g_all,
    db,
    db_t,
    acc,
    kmask,
    near,
    small,
    pc,
    scale_ref,
    cot_ref,
    hw,
    ow,
    perm_t,
    out_st,
    dx_st,
    sems,
    gp,
    half_in,
    quarter_in,
    part_in,
    cross_in,
    whole_in,
    own_part,
    total_ref,
    send,
    recv,
):
    n = images
    rows = n * TOK
    seg, dp = lax.axis_index("segment"), lax.axis_index("dp")
    all_here = greet(seg, dp, *sizes)
    late = [
        pltpu.make_async_copy(src, dst, sems.at[k])
        for k, (src, dst) in enumerate(
            ((hw_in, hw), (ow_in, ow), (cot_in, cot_ref), (perm_t_in, perm_t))
        )
    ]
    for made in late:
        made.start()
    leaving = []

    def leave(src, dst):
        made = pltpu.make_async_copy(src, dst, sems.at[len(late) + len(leaving)])
        made.start()
        leaving.append(made)

    refs = (
        gp,
        half_in,
        quarter_in,
        part_in,
        cross_in,
        whole_in,
        own_part,
        total_ref,
        send,
        recv,
    )
    pieces = [
        Summed((seg, dp) + sizes, p, base, count, short, refs)
        for p, (base, count, short) in enumerate(PIECES)
    ]

    def move(*steps):
        for p, k in steps:
            pieces[p].step(k)
            if k == (4 if PIECES[p][2] else 6):
                rows_of = pl.ds(PIECES[p][0], PIECES[p][1])
                leave(total_ref.at[rows_of, :], summed_ref.at[rows_of, :])

    lane = lax.broadcasted_iota(jnp.int32, (8, 128), 1)[0:1]

    def head_lanes(h):
        return (lane >= h * HEAD) & (lane < (h + 1) * HEAD)

    def tiles(fn, step=TILE):
        sums = None
        for start in range(0, rows, step):
            got = fn(slice(start, start + step))
            if got is not None:
                sums = got if sums is None else [x + y for x, y in zip(sums, got)]
        return None if sums is None else [col_sum(x) for x in sums]

    def row(ref, j, k=None):
        return ref[j, pl.ds(k, 1), :] if k is not None else ref[pl.ds(j, 1), :]

    def shifted_rows(v, by):
        if by == 0:
            return v
        pad = jnp.zeros((abs(by), v.shape[1]), v.dtype)
        if by > 0:
            return jnp.concatenate([v[by:], pad], axis=0)
        return jnp.concatenate([pad, v[:by]], axis=0)

    col = lax.broadcasted_iota(jnp.int32, (GRID, GRID, 128), 1).reshape(TOK, 128)

    def taps_of(v):
        left = jnp.where(col > 0, pltpu.roll(v, 1, 0), 0.0)
        right = jnp.where(col < GRID - 1, pltpu.roll(v, TOK - 1, 0), 0.0)
        for row_off in range(3):
            for col_off, piece in enumerate((left, v, right)):
                yield row_off * 3 + col_off, shifted_rows(piece, (row_off - 1) * GRID)

    small[...] = jnp.zeros_like(small)
    sizes = []
    lane_row = lax.broadcasted_iota(jnp.int32, (TOK, 128), 1)
    for i in range(n):
        m_id, d_id = seg * own + i // (n // own), i % (n // own)
        high, wide = grid_ref[d_id, 0, m_id], grid_ref[d_id, 1, m_id]
        sizes.append((high, wide))
        line = lax.broadcasted_iota(jnp.int32, (GRID, GRID, 128), 0).reshape(TOK, 128)
        good = jnp.where((line < high) & (col < wide), 1.0, 0.0)
        valid[i * TOK : (i + 1) * TOK, :] = good
        for k in range(2 * BLOCKS):
            kept = keep_ref[d_id, k, m_id].astype(f32) / keep_rate
            scale_ref[i, k] = kept
        flags = jnp.where((lane_row == 16) | (lane_row == 48), 1.0, 0.0)
        for off, piece in taps_of(good):
            flags = jnp.where((lane_row == off) | (lane_row == 32 + off), piece, flags)
        for j in range(BLOCKS):
            u_all[j, i * TOK : (i + 1) * TOK, TAPS * C :] = flags.astype(bf16)
        base = 0
        for t in range(2):
            span = slice(base, base + CELLS[t])
            tall = (high + STRIDES[t] - 1) // STRIDES[t]
            across = (wide + STRIDES[t] - 1) // STRIDES[t]
            inside = (places[0, span, :] < tall.astype(f32)) & (
                places[1, span, :] < across.astype(f32)
            )
            kmask[i, span, :] = jnp.where(inside, 1.0, 0.0)
            base += CELLS[t]
    base = 0
    for t in range(2):
        span = slice(base, base + CELLS[t])
        a, b = places[0, span, :], places[1, span, :]
        for off in range(9):
            dr, dc = float(off // 3 - 1), float(off % 3 - 1)
            top = float(SIDES[t])
            ok = (a + dr >= 0) & (a + dr < top) & (b + dc >= 0) & (b + dc < top)
            near[off, span, :] = jnp.where(ok, 1.0, 0.0)
        base += CELLS[t]

    xs[...] = x_ref[...].astype(f32)

    def scaled(span, k):
        return valid[span, :] * scale_ref[span.start // TOK, k]

    def cell_spans(t):
        start = 0 if t == 0 else n * CELLS[0]
        return [slice(start + i * CELLS[t], start + (i + 1) * CELLS[t]) for i in range(n)]

    def cells_all(t):
        return slice(0, n * CELLS[0]) if t == 0 else slice(n * CELLS[0], n * sum(CELLS))

    place_span = (slice(0, CELLS[0]), slice(CELLS[0], sum(CELLS)))
    half = lane < 64
    own_half = (half, jnp.logical_not(half))

    def near_shift(t, off):
        return ((off // 3 - 1) * SIDES[t] + off % 3 - 1) % CELLS[t]

    def attention_forward(j):
        def first(ts):
            xhat, scale = norm_parts(xs[ts, :])
            xh_a[j, ts, :] = xhat
            sc[j, ts, 0:1] = scale
            u_a[j, ts, :] = (xhat * row(ng, j, 0) + row(ns, j, 0)).astype(bf16)

        tiles(first)
        for i in range(n):
            span = slice(i * TOK, (i + 1) * TOK)
            u = u_a[j, span, :]
            q_a[j, span, :] = (nn(u, qw[j]) + row(qb, j)).astype(bf16)
            um[:, i * C : (i + 1) * C] = (u.astype(f32) * valid[span, :]).astype(bf16)
        pc[...] = nn(perm[...], um[...]).astype(bf16)
        base = 0
        for t, ref in enumerate((p4, p2)):
            for k in range(STRIDES[t] ** 2):
                for i in range(n):
                    ref[j, i * CELLS[t] : (i + 1) * CELLS[t], k * C : (k + 1) * C] = pc[
                        base : base + CELLS[t], i * C : (i + 1) * C
                    ]
                base += CELLS[t]
        for t, (ref, weight) in enumerate(((p4, p4w), (p2, p2w))):
            xhat, scale = norm_parts(nn(ref[j], weight[j]))
            act, slope = gelu_parts(xhat * row(ng, j, 1 + t) + row(ns, j, 1 + t))
            act = act.astype(bf16)
            span = cells_all(t)
            xh_p[j, span, :] = xhat
            sc_p[j, span, :] = jnp.broadcast_to(scale, xhat.shape)
            ge_p[j, span, :] = slope
            kin[j, span, :] = act
            keyval = nn(act, kvw[j, t])
            turned = pltpu.roll(keyval, 64, 1)
            keys, vals = (keyval, turned) if t == 0 else (turned, keyval)
            bias = jnp.concatenate([row(vb, j, 0), row(vb, j, 1)], axis=1)
            kernel = jnp.concatenate([lk[j, :, 0, :], lk[j, :, 1, :]], axis=1)
            for i in range(n):
                part = slice(i * CELLS[t], (i + 1) * CELLS[t])
                w = (vals[part] + bias) * kmask[i, place_span[t], :]
                wv[j, cell_spans(t)[i], :] = w
                v = w
                for off in range(9):
                    by = near_shift(t, off)
                    moved = pltpu.roll(w, (CELLS[t] - by) % CELLS[t], 0) if by else w
                    v = v + moved * (near[off, place_span[t], :] * kernel[off : off + 1])
                for h in (2 * t, 2 * t + 1):
                    seg_rows = slice(*SEGS[h])
                    kb[j, i, seg_rows, :] = jnp.where(head_lanes(h), keys[part], 0.0).astype(bf16)
                    vbd[j, i, seg_rows, :] = jnp.where(head_lanes(h), v, 0.0).astype(bf16)
        for i in range(n):
            span = slice(i * TOK, (i + 1) * TOK)
            scores = nt(kb[j, i], q_a[j, span, :])
            for h, (low, top) in enumerate(SEGS):
                mask = kmask[i, place_span[h // 2], 0:1] > 0
                for c0 in range(0, TOK, 128):
                    c1 = min(c0 + 128, TOK)
                    s = jnp.where(mask, scores[low:top, c0:c1], -1e30)
                    e = jnp.exp2((s - jnp.max(s, axis=0, keepdims=True)) * (ROOT * LOG2E))
                    weight = e * pl.reciprocal(jnp.sum(e, axis=0, keepdims=True), approx=True)
                    pt[j, i, low:top, c0:c1] = weight.astype(bf16)
            mixed = tn(vbd[j, i], pt[j, i])
            o_t[j, i] = mixed.astype(bf16)
            o_n[span, :] = mixed.T.astype(bf16)
        for i in range(n):
            span = slice(i * TOK, (i + 1) * TOK)
            branch = nn(o_n[span, :], pw[j]) + row(pb, j)
            xs[span, :] = (xs[span, :] + scaled(span, 2 * j) * branch).astype(bf16).astype(f32)

    def build_wc(j):
        bias = row(hb, j)

        def tap(off, carry):
            factor = mk[off, j : j + 1, :] + jnp.where(off == 4, 1.0, 0.0)
            for r0 in range(0, C, 32):
                wc[j, pl.ds(pl.multiple_of(off * C + r0, 32), 32), :] = (
                    hw[j, r0 : r0 + 32, :].astype(f32) * factor
                ).astype(bf16)
            return carry

        lax.fori_loop(0, TAPS, tap, 0)
        ex[...] = jnp.zeros_like(ex)
        each = mk[:, j, :] * bias
        both = bias + row(mb, j)
        each_high = each.astype(bf16).astype(f32)
        both_high = both.astype(bf16).astype(f32)
        ex[0:9, :] = each_high
        ex[16:17, :] = both_high
        ex[32:41, :] = each - each_high
        ex[48:49, :] = both - both_high
        wc[j, TAPS * C :, :] = ex[...].astype(bf16)

    def mlp_forward(j):
        build_wc(j)

        def first(ts):
            xhat, scale = norm_parts(xs[ts, :])
            xh_m[j, ts, :] = xhat
            sc[j, ts, 1:2] = scale
            u = (xhat * row(ng, j, 3) + row(ns, j, 3)).astype(bf16).astype(f32)
            acc[0, ts, :] = u * valid[ts, :]

        tiles(first)
        for i in range(n):
            span = slice(i * TOK, (i + 1) * TOK)
            for off, piece in taps_of(acc[0, span, :]):
                u_all[j, span, off * C : (off + 1) * C] = piece.astype(bf16)

        for start in range(0, FF, CHUNK):
            cols = slice(start, start + CHUNK)
            for i in range(n):
                field = nn(u_all[j, i * TOK : (i + 1) * TOK, :], wc[j, :, cols])
                for r0 in range(0, TOK, 16):
                    act, slope = gelu_parts(field[r0 : r0 + 16])
                    part = slice(i * TOK + r0, i * TOK + r0 + 16)
                    a_all[j, part, cols] = act.astype(bf16)
                    g_all[j, part, cols] = slope.astype(bf16)
        for i in range(n):
            span = slice(i * TOK, (i + 1) * TOK)
            branch = nn(a_all[j, span, :], ow[j]) + row(ob, j)
            xs[span, :] = (xs[span, :] + scaled(span, 2 * j + 1) * branch).astype(bf16).astype(f32)

    def mlp_backward(j):
        sb = j * S_BLOCK

        def first(ts):
            grad = (xs[ts, :] * scaled(ts, 2 * j + 1)).astype(bf16)
            db[ts, :] = grad
            return [folded(grad.astype(f32))]

        (small[sb + S_OB : sb + S_OB + 1, :],) = tiles(first)
        db_t[j] = db[...].T
        for start in range(0, FF, CHUNK):
            cols = slice(start, start + CHUNK)
            for i in range(n):
                span = slice(i * TOK, (i + 1) * TOK)
                da = nt(db[span, :], ow[j, cols, :])
                g_all[j, span, cols] = (da * g_all[j, span, cols].astype(f32)).astype(bf16)
        if j == 0:
            move((0, 1))
        acc[...] = jnp.zeros_like(acc)
        for first_off in range(0, TAPS, 2):
            width = min(2, TAPS - first_off)
            for i in range(n):
                at = i * TOK
                moved = nt(
                    g_all[j, at : at + TOK, :], wc[j, first_off * C : (first_off + width) * C, :]
                )
                for s in range(width):
                    off = first_off + s
                    by = (off // 3 - 1) * GRID
                    piece = moved[:, s * C : (s + 1) * C]
                    if by >= 0:
                        acc[off % 3, at + by : at + TOK, :] += piece[: TOK - by]
                    else:
                        acc[off % 3, at : at + TOK + by, :] += piece[-by:]
        if j == 0:
            move((0, 2))
        for i in range(n):
            span = slice(i * TOK, (i + 1) * TOK)
            left = pltpu.roll(jnp.where(col > 0, acc[0, span, :], 0.0), TOK - 1, 0)
            right = pltpu.roll(jnp.where(col < GRID - 1, acc[2, span, :], 0.0), 1, 0)
            acc[1, span, :] = (acc[1, span, :] + left + right) * valid[span, :]

        def last(ts):
            du = acc[1, ts, :]
            xhat = xh_m[j, ts, :]
            back = norm_back(du, xhat, sc[j, ts, 1:2], row(ng, j, 3))
            xs[ts, :] = (xs[ts, :] + back).astype(bf16).astype(f32)
            return [folded(du * xhat), folded(du)]

        gain, shift = tiles(last)
        small[sb + S_GAIN + 3 : sb + S_GAIN + 4, :] = gain
        small[sb + S_SHIFT + 3 : sb + S_SHIFT + 4, :] = shift

    def mlp_turn(j):
        for off in range(TAPS + 1):
            ut[off * C : (off + 1) * C, :] = u_all[j, :, off * C : (off + 1) * C].T

    def mlp_weights(j, step):
        base, sb = MLP_AT[j], j * S_BLOCK
        cols = slice(step * CHUNK, (step + 1) * CHUNK)
        dow = nn(db_t[j], a_all[j, :, cols])
        at = base + output_row(step)
        gp[at : at + CHUNK, :] = dow.T.astype(bf16)
        cross = nn(ut[...], g_all[j, :, cols])
        flag_rows = cross[TAPS * C : TAPS * C + 24]
        total = flag_rows[16:17]
        dhb = total
        weight = hw[j, :, cols].astype(f32)
        dweight = jnp.zeros((C, CHUNK), f32)
        b = hb[j : j + 1, cols]
        for off in range(TAPS):
            piece = cross[off * C : (off + 1) * C]
            factor = mk[off, j : j + 1, cols]
            flag = flag_rows[off : off + 1]
            dweight = dweight + piece * (factor + (1.0 if off == 4 else 0.0))
            dk = col_sum(piece * weight) + b * flag
            dhb = dhb + factor * flag
            for s in range(CHUNK // C):
                at = sb + S_MK + 16 * (step * (CHUNK // C) + s) + off
                small[at : at + 1, :] = dk[:, s * C : (s + 1) * C]
        for s in range(CHUNK // C):
            tile = step * (CHUNK // C) + s
            part = slice(s * C, (s + 1) * C)
            small[sb + S_HB + tile : sb + S_HB + tile + 1, :] = dhb[:, part]
            small[sb + S_MB + tile : sb + S_MB + tile + 1, :] = total[:, part]
            at = base + hidden_row(tile)
            gp[at : at + C, :] = dweight[:, part].astype(bf16)

    def attention_backward(j):
        base, sb = ATT_AT[j], j * S_BLOCK

        def first(ts):
            grad = (xs[ts, :] * scaled(ts, 2 * j)).astype(bf16)
            db[ts, :] = grad
            return [folded(grad.astype(f32))]

        (small[sb + S_PB : sb + S_PB + 1, :],) = tiles(first)
        dproj = jnp.zeros((C, C), f32)
        kernel = jnp.concatenate([lk[j, :, 0, :], lk[j, :, 1, :]], axis=1)
        dkernel = [jnp.zeros((1, C), f32) for _ in range(9)]
        dbias = jnp.zeros((1, C), f32)
        for i in range(n):
            span = slice(i * TOK, (i + 1) * TOK)
            dproj = dproj + nn(o_t[j, i], db[span, :])
            do = nt(db[span, :], pw[j]).astype(bf16)
            dprobs = nt(vbd[j, i], do)
            dvals = nn(pt[j, i], do)
            for low, top in SEGS:
                for c0 in range(0, TOK, 128):
                    c1 = min(c0 + 128, TOK)
                    weight = pt[j, i, low:top, c0:c1].astype(f32)
                    dweight = dprobs[low:top, c0:c1]
                    dot = jnp.sum(weight * dweight, axis=0, keepdims=True)
                    pt[j, i, low:top, c0:c1] = (weight * (dweight - dot)).astype(bf16)
            dkeys = nn(pt[j, i], q_a[j, span, :]) * ROOT
            dq = tn(kb[j, i], pt[j, i]) * ROOT
            o_n[span, :] = dq.T.astype(bf16)
            for t in range(2):
                dk = jnp.zeros((CELLS[t], C), f32)
                dv = jnp.zeros((CELLS[t], C), f32)
                for h in (2 * t, 2 * t + 1):
                    dk = dk + jnp.where(head_lanes(h), dkeys[slice(*SEGS[h])], 0.0)
                    dv = dv + jnp.where(head_lanes(h), dvals[slice(*SEGS[h])], 0.0)
                w = wv[j, cell_spans(t)[i], :]
                dw = dv
                for off in range(9):
                    by = near_shift(t, off)
                    part = dv * near[off, place_span[t], :]
                    moved = pltpu.roll(w, (CELLS[t] - by) % CELLS[t], 0) if by else w
                    dkernel[off] = dkernel[off] + col_sum(part * moved)
                    part = part * kernel[off : off + 1]
                    dw = dw + (pltpu.roll(part, by, 0) if by else part)
                dw = dw * kmask[i, place_span[t], :]
                dbias = dbias + col_sum(dw)
                if t == 0:
                    dkeyval = dk + pltpu.roll(dw, 64, 1)
                else:
                    dkeyval = pltpu.roll(dk, 64, 1) + dw
                wv[j, cell_spans(t)[i], :] = dkeyval
            if j == 0 and i < 2:
                move((0, 3 + i))
        gp[base + R_PROJ : base + R_PROJ + C, :] = dproj.astype(bf16)
        small[sb + S_VB : sb + S_VB + 1, :] = dbias
        for off in range(9):
            small[sb + S_LK + off : sb + S_LK + off + 1, :] = dkernel[off]
        base_perm = 0
        for t, (ref, weight) in enumerate(((p4, p4w), (p2, p2w))):
            span = cells_all(t)
            dkeyval = wv[j, span, :].astype(bf16)
            at = base + R_KV + t * C
            gp[at : at + C, :] = tn(kin[j, span, :], dkeyval).astype(bf16)
            dy = nt(dkeyval, kvw[j, t]) * ge_p[j, span, :]
            xhat = xh_p[j, span, :]
            small[sb + S_GAIN + 1 + t : sb + S_GAIN + 2 + t, :] = col_sum(dy * xhat)
            small[sb + S_SHIFT + 1 + t : sb + S_SHIFT + 2 + t, :] = col_sum(dy)
            dpool = norm_back(dy, xhat, sc_p[j, span, :], row(ng, j, 1 + t)).astype(bf16)
            at = base + (R_P4, R_P2)[t]
            for k in range(STRIDES[t] ** 2):
                gp[at + k * C : at + (k + 1) * C, :] = tn(
                    ref[j, :, k * C : (k + 1) * C], dpool
                ).astype(bf16)
                back = nt(dpool, weight[j, k * C : (k + 1) * C, :]).astype(bf16)
                for i in range(n):
                    pc[base_perm : base_perm + CELLS[t], i * C : (i + 1) * C] = back[
                        i * CELLS[t] : (i + 1) * CELLS[t]
                    ]
                base_perm += CELLS[t]
        at = base + R_Q
        gp[at : at + C, :] = tn(u_a[j], o_n[...]).astype(bf16)
        at = base + R_Q
        gp[at : at + C, :] = tn(u_a[j], o_n[...]).astype(bf16)
        if j == 1:
            all_here()
            move((0, 0))
        else:
            move(*(((0, k) for k in range(3 + min(n, 2), 6))), (1, 0))
        spread = nn(perm_t[...], pc[...])
        for i in range(n):
            span = slice(i * TOK, (i + 1) * TOK)
            back = nt(o_n[span, :], qw[j])
            acc[0, span, :] = back + spread[:, i * C : (i + 1) * C] * valid[span, :]

        def last(ts):
            du = acc[0, ts, :]
            xhat = xh_a[j, ts, :]
            back = norm_back(du, xhat, sc[j, ts, 0:1], row(ng, j, 0))
            xs[ts, :] = (xs[ts, :] + back).astype(bf16).astype(f32)
            return [folded(o_n[ts, :].astype(f32)), folded(du * xhat), folded(du)]

        bias, gain, shift = tiles(last)
        small[sb + S_QB : sb + S_QB + 1, :] = bias
        small[sb + S_GAIN : sb + S_GAIN + 1, :] = gain
        small[sb + S_SHIFT : sb + S_SHIFT + 1, :] = shift

    for j in range(BLOCKS):
        attention_forward(j)
        if j == 0:
            late[0].wait()
            late[1].wait()
        mlp_forward(j)
    out_st[...] = xs[...].astype(bf16)
    leave(out_st, out_ref)
    late[2].wait()
    late[3].wait()
    xs[...] = cot_ref[...].astype(f32)
    for j in reversed(range(BLOCKS)):
        mlp_backward(j)
        attention_backward(j)
    dx_st[...] = xs[...].astype(bf16)
    leave(dx_st, dx_ref)
    mlp_turn(1)
    move((0, 6), (1, 1))
    mlp_weights(1, 0)
    move((1, 2))
    mlp_weights(1, 1)
    move((1, 3), (2, 0))
    mlp_turn(0)
    move((2, 1))
    mlp_weights(0, 0)
    move((1, 4), (2, 2), (3, 0))
    mlp_weights(0, 1)
    gp[R_SMALL:, :] = small[...].astype(bf16)
    move((1, 5), (4, 0), (2, 3), (3, 1))
    move((1, 6), (4, 1), (2, 4), (3, 2), (4, 2), (2, 5), (3, 3), (4, 3), (2, 6), (3, 4), (4, 4))
    for piece in pieces:
        piece.drain()
    for made in leaving:
        made.wait()


def compute(own, images, grid_size, keep_mask, x, cot, weights):
    segments, pairs = lax.axis_size("segment"), lax.axis_size("dp") // 2
    inner = min(pairs, 4)
    sizes = (segments, inner, pairs // inner)
    n = images
    rows = n * TOK
    cells = n * sum(CELLS)
    vmem = pl.BlockSpec(memory_space=pltpu.VMEM)
    smem = pl.BlockSpec(memory_space=pltpu.SMEM)
    matrix = permutation()
    consts = (
        jnp.asarray(matrix, bf16),
        jnp.asarray(matrix.T, bf16),
        jnp.asarray(cell_places()),
    )
    B = BLOCKS
    scratch = [
        pltpu.VMEM((rows, C), f32),
        pltpu.VMEM((rows, C), f32),
        pltpu.VMEM((TOK, n * C), bf16),
        pltpu.VMEM((B, rows, UW), bf16),
        pltpu.VMEM((UW, rows), bf16),
        pltpu.VMEM((B, UW, FF), bf16),
        pltpu.VMEM((C, FF), f32),
        pltpu.VMEM((B, rows, C), f32),
        pltpu.VMEM((B, rows, C), f32),
        pltpu.VMEM((B, rows, C), f32),
        pltpu.VMEM((B, rows, C), bf16),
        pltpu.VMEM((B, rows, C), bf16),
        pltpu.VMEM((B, n * CELLS[0], 16 * C), bf16),
        pltpu.VMEM((B, n * CELLS[1], 4 * C), bf16),
        pltpu.VMEM((B, cells, C), f32),
        pltpu.VMEM((B, cells, C), f32),
        pltpu.VMEM((B, cells, C), f32),
        pltpu.VMEM((B, cells, C), bf16),
        pltpu.VMEM((B, cells, C), f32),
        pltpu.VMEM((B, n, KEYS, C), bf16),
        pltpu.VMEM((B, n, KEYS, C), bf16),
        pltpu.VMEM((B, n, KEYS, TOK), bf16),
        pltpu.VMEM((B, n, C, TOK), bf16),
        pltpu.VMEM((rows, C), bf16),
        pltpu.VMEM((B, rows, FF), bf16),
        pltpu.VMEM((B, rows, FF), bf16),
        pltpu.VMEM((rows, C), bf16),
        pltpu.VMEM((B, C, rows), bf16),
        pltpu.VMEM((3, rows, C), f32),
        pltpu.VMEM((n, sum(CELLS), C), f32),
        pltpu.VMEM((9, sum(CELLS), C), f32),
        pltpu.VMEM((ROWS - R_SMALL, C), f32),
        pltpu.VMEM((PERM, n * C), bf16),
        pltpu.SMEM((n, 2 * BLOCKS), f32),
        pltpu.VMEM(cot.shape, bf16),
        pltpu.VMEM(weights[HW].shape, bf16),
        pltpu.VMEM(weights[OW].shape, bf16),
        pltpu.VMEM((TOK, PERM), bf16),
        pltpu.VMEM((rows, C), bf16),
        pltpu.VMEM((rows, C), bf16),
        pltpu.SemaphoreType.DMA((6 + len(PIECES),)),
        pltpu.VMEM((ROWS, C), bf16),
    ] + sum_scratch(sizes)
    anywhere = pl.BlockSpec(memory_space=pl.ANY)
    operands = [vmem] * (2 + len(weights) + len(consts))
    for place in (1, 2 + HW, 2 + OW, 2 + len(weights) + 1):
        operands[place] = anywhere
    return pl.pallas_call(
        functools.partial(compute_kernel, own, images, sizes),
        out_shape=(
            jax.ShapeDtypeStruct((rows, C), bf16),
            jax.ShapeDtypeStruct((rows, C), bf16),
            jax.ShapeDtypeStruct((ROWS, C), bf16),
        ),
        in_specs=[smem, smem] + operands,
        out_specs=(anywhere,) * 3,
        scratch_shapes=scratch,
        compiler_params=pltpu.CompilerParams(
            collective_id=0, has_side_effects=True, vmem_limit_bytes=63 * 2**20
        ),
        name="compute",
    )(grid_size, keep_mask, x, cot, *weights, *consts)


def unpack_kernel(packed, out_in, dx_in, out_ref, dx_ref, *refs):
    results, stage = refs[:17], refs[17:34]
    gp, in_sems, out_sems = refs[34:]
    gain, shift, qw, qb, p4, p2, kvw, vb, lk, pw, pb, hw, hb, mk, mb, ow, ob = stage
    leaving = []

    def leave(src, dst):
        made = pltpu.make_async_copy(src, dst, out_sems.at[len(leaving)])
        made.start()
        leaving.append(made)

    def leave_block(j, *places):
        for k in places:
            leave(stage[k].at[j], results[k].at[j])

    parts = (
        (ATT_AT[1], R_ATT),
        (ATT_AT[0], R_ATT),
        (MLP_AT[1], R_MLP),
        (MLP_AT[0], R_MLP),
        (R_SMALL, ROWS - R_SMALL),
    )
    coming = []
    for k, (start, count) in enumerate(parts):
        span = pl.ds(start, count)
        made = pltpu.make_async_copy(packed.at[span, :], gp.at[span, :], in_sems.at[k])
        made.start()
        coming.append(made)
    leave(out_in, out_ref)
    leave(dx_in, dx_ref)
    for k, j in enumerate((1, 0)):
        coming[k].wait()
        att = ATT_AT[j]
        p4[j] = gp[att + R_P4 : att + R_P2, :].astype(f32)
        p2[j] = gp[att + R_P2 : att + R_KV, :].astype(f32)
        for t in range(2):
            kvw[j, t] = gp[att + R_KV + t * C : att + R_KV + (t + 1) * C, :].astype(f32)
        qw[j] = gp[att + R_Q : att + R_PROJ, :].astype(f32)
        pw[j] = gp[att + R_PROJ : att + R_ATT, :].astype(f32)
        leave_block(j, 2, 4, 5, 6, 9)
    for k, j in enumerate((1, 0)):
        coming[2 + k].wait()
        mlp = MLP_AT[j]
        for s in range(FF // C):
            at = mlp + hidden_row(s)
            hw[j, :, s * C : (s + 1) * C] = gp[at : at + C, :].astype(f32)
        for step in range(FF // CHUNK):
            at = mlp + output_row(step)
            ow[j, step * CHUNK : (step + 1) * CHUNK, :] = gp[at : at + CHUNK, :].astype(f32)
        leave_block(j, HW, OW)
    coming[4].wait()
    for j in range(BLOCKS):
        sb = R_SMALL + j * S_BLOCK
        head = gp[sb : sb + 48, :].astype(f32)
        gain[j] = head[S_GAIN : S_GAIN + 4]
        shift[j] = head[S_SHIFT : S_SHIFT + 4]
        qb[j : j + 1, :] = head[S_QB : S_QB + 1]
        vb[j, 0:1, :] = head[S_VB : S_VB + 1, 0:64]
        vb[j, 1:2, :] = head[S_VB : S_VB + 1, 64:128]
        pb[j : j + 1, :] = head[S_PB : S_PB + 1]
        ob[j : j + 1, :] = head[S_OB : S_OB + 1]
        lk[j, :, 0, :] = head[S_LK : S_LK + 9, 0:64]
        lk[j, :, 1, :] = head[S_LK : S_LK + 9, 64:128]
        for s in range(FF // C):
            part = slice(s * C, (s + 1) * C)
            hb[j : j + 1, part] = head[S_HB + s : S_HB + s + 1]
            mb[j : j + 1, part] = head[S_MB + s : S_MB + s + 1]
            at = sb + S_MK + 16 * s
            mk[:, j, part] = gp[at : at + 16, :].astype(f32)[0:9]
    for k in (0, 1, 3, 7, 8, 10, 12, 13, 14, 16):
        leave(stage[k], results[k])
    for made in leaving:
        made.wait()


def unpack(packed, outputs, input_grad, weights):
    anywhere = pl.BlockSpec(memory_space=pl.ANY)
    streams = (jax.ShapeDtypeStruct(outputs.shape, bf16),) * 2
    return pl.pallas_call(
        unpack_kernel,
        out_shape=streams + tuple(jax.ShapeDtypeStruct(w.shape, f32) for w in weights),
        in_specs=[anywhere] * 3,
        out_specs=(anywhere,) * (2 + len(weights)),
        scratch_shapes=[pltpu.VMEM(w.shape, f32) for w in weights]
        + [
            pltpu.VMEM((ROWS, C), bf16),
            pltpu.SemaphoreType.DMA((5,)),
            pltpu.SemaphoreType.DMA((2 + 7 * BLOCKS + 10,)),
        ],
        compiler_params=pltpu.CompilerParams(vmem_limit_bytes=63 * 2**20),
        name="unpack",
    )(packed, outputs, input_grad)


def on_device(inputs, grid_size, keep_mask, cotangent, *weights):
    own, per = inputs.shape[:2]
    images = own * per
    flat = (images * TOK, C)
    turned = list(weights)
    turned[LK] = jnp.transpose(turned[LK], (0, 2, 1, 3))
    turned[MK] = jnp.transpose(turned[MK], (1, 0, 2))
    outputs, input_grad, packed = compute(
        own,
        images,
        jnp.transpose(grid_size, (1, 2, 0)),
        jnp.transpose(keep_mask, (1, 2, 0)),
        inputs.reshape(flat),
        cotangent.reshape(flat),
        turned,
    )
    outputs, input_grad, *grads = unpack(packed, outputs, input_grad, turned)
    grads[LK] = jnp.transpose(grads[LK], (0, 2, 1, 3))
    grads[MK] = jnp.transpose(grads[MK], (1, 0, 2))
    return (outputs.reshape(inputs.shape), input_grad.reshape(inputs.shape)) + tuple(grads)


def solution(mesh):
    stream = P("segment", "dp", None, None)
    picked = P(None, "dp", None)
    return jax.shard_map(
        on_device,
        mesh=mesh,
        in_specs=(stream, picked, picked, stream) + (P(),) * 17,
        out_specs=(stream, stream) + (P(),) * 17,
        check_vma=False,
    )
```

```python
import functools

import jax
import jax.numpy as jnp
import numpy as np
from jax import lax
from jax.experimental import pallas as pl
from jax.experimental.pallas import tpu as pltpu
from jax.sharding import PartitionSpec as P

GRID = 24
TOK = GRID * GRID
C = 128
FF = 1024
HEAD = 32
BLOCKS = 2
SIDES = (6, 12)
STRIDES = (4, 2)
CELLS = (48, 144)
SEGS = ((0, 48), (48, 96), (96, 240), (240, 384))
KEYS = 384
PERM = 16 * 48 + 4 * 144
TAPS = 9
UW = TAPS * C + C
CHUNK = 512
TILE = 96

R_P4, R_P2, R_KV, R_Q, R_PROJ, R_ATT = 0, 2048, 2560, 2816, 2944, 3072
R_MLP = 2048
ATT_AT = (R_ATT, 0)
MLP_AT = (2 * R_ATT + R_MLP, 2 * R_ATT)
S_GAIN, S_SHIFT, S_QB, S_VB, S_PB, S_OB, S_LK, S_HB, S_MB, S_MK, S_BLOCK = (
    0,
    4,
    8,
    9,
    10,
    11,
    16,
    32,
    40,
    48,
    192,
)
R_SMALL = BLOCKS * (R_ATT + R_MLP)
ROWS = R_SMALL + 512
PIECES = (
    (ATT_AT[1], R_ATT, False),
    (ATT_AT[0], R_ATT, False),
    (MLP_AT[1], R_MLP, False),
    (MLP_AT[0], R_MLP + ROWS - R_SMALL, True),
)

LK, HW, MK, OW = 8, 11, 13, 15

epsilon = 1e-06
keep_rate = 0.8
ROOT = HEAD**-0.5
LOG2E = 1.4426950408889634
f32, bf16 = jnp.float32, jnp.bfloat16


def hidden_row(tile):
    return tile // (CHUNK // C) * 2 * CHUNK + tile % (CHUNK // C) * C


def output_row(step):
    return step * 2 * CHUNK + CHUNK


def permutation():
    matrix = np.zeros((PERM, TOK), np.float32)
    base = 0
    for stride, side, cells in zip(STRIDES, SIDES, CELLS):
        for row_off in range(stride):
            for col_off in range(stride):
                for a in range(side):
                    for b in range(side):
                        token = (a * stride + row_off) * GRID + b * stride + col_off
                        matrix[base + a * side + b, token] = 1.0
                base += cells
    return matrix


def cell_places():
    places = np.full((2, sum(CELLS), 128), 99.0, np.float32)
    base = 0
    for side, cells in zip(SIDES, CELLS):
        for a in range(side):
            for b in range(side):
                places[0, base + a * side + b] = a
                places[1, base + a * side + b] = b
        base += cells
    return places


def nn(left, right):
    return jnp.dot(left, right, preferred_element_type=f32)


def nt(left, right):
    return lax.dot_general(left, right, (((1,), (1,)), ((), ())), preferred_element_type=f32)


def tn(left, right):
    return lax.dot_general(left, right, (((0,), (0,)), ((), ())), preferred_element_type=f32)


def gelu_parts(m):
    size = jnp.abs(m)
    t = pl.reciprocal(1.0 + (0.3275911 * 0.5**0.5) * size, approx=True)
    e = jnp.exp2(m * (m * (-0.5 * LOG2E)))
    poly = 0.5 * 1.061405429
    for coef in (-1.453152027, 1.421413741, -0.284496736, 0.254829592):
        poly = poly * t + 0.5 * coef
    poly = poly * t
    tail = poly * e
    slope = (poly - size * 0.3989422804014327) * e
    return jnp.maximum(m, 0.0) - size * tail, jnp.where(m >= 0, 1.0 - slope, slope)


def norm_parts(x):
    centred = x - jnp.mean(x, axis=-1, keepdims=True)
    scale = lax.rsqrt(jnp.mean(centred * centred, axis=-1, keepdims=True) + epsilon)
    return centred * scale, scale


def norm_back(du, xhat, scale, gain):
    dxhat = du * gain
    first = jnp.mean(dxhat, axis=-1, keepdims=True)
    second = jnp.mean(dxhat * xhat, axis=-1, keepdims=True)
    return scale * (dxhat - first - xhat * second)


def col_sum(x):
    return jnp.sum(x, axis=0, keepdims=True)


def folded(x):
    return jnp.sum(x.reshape(-1, 8, x.shape[-1]), axis=0)


class Summed:
    def __init__(self, place, piece, base, count, short, refs):
        self.seg, self.dp, self.segments, self.inner, self.outer = place
        self.piece, self.base, self.count = piece, base, count
        self.short = short
        (
            self.src,
            self.half_in,
            self.quarter_in,
            self.part_in,
            self.cross_in,
            self.whole_in,
            self.own,
            self.total,
            self.send,
            self.recv,
        ) = refs
        self.core, rest = self.dp % 2, self.dp // 2
        self.part, self.group = rest % self.inner, rest // self.inner
        self.half = count // 2
        self.quarter = self.half // self.segments
        self.share = self.quarter // self.inner

    def span(self, start, size):
        return pl.ds(pl.multiple_of(start, 16), size)

    def device(self, seg=None, core=None, part=None, group=None):
        seg = self.seg if seg is None else seg
        core = self.core if core is None else core
        part = self.part if part is None else part
        group = self.group if group is None else group
        return (seg, (group * self.inner + part) * 2 + core)

    def copy(self, slot, src, dst, device):
        made = pltpu.make_async_remote_copy(
            src_ref=src,
            dst_ref=dst,
            send_sem=self.send.at[self.piece, slot],
            recv_sem=self.recv.at[self.piece, slot],
            device_id=device,
            device_id_type=pl.DeviceIdType.MESH,
        )
        made.start()
        self.started.append(made)
        return made

    def half_at(self, core):
        return self.span(self.base + core * self.half, self.half)

    def own_at(self, seg, part=None):
        start = self.base // 2 + seg * self.quarter
        if part is None:
            return self.span(start, self.quarter)
        return self.span(start + part * self.share, self.share)

    def total_at(self, seg=None, part=None):
        start = self.base + self.core * self.half
        if seg is None:
            return self.span(start, self.half)
        start = start + seg * self.quarter
        if part is None:
            return self.span(start, self.quarter)
        return self.span(start + part * self.share, self.share)

    def steps(self):
        return 5 if self.short else 7

    def step(self, k):
        if k > 0:
            for made in self.copies(k - 1):
                made.wait_recv()
            self.gather(k)
        if k + 1 < self.steps():
            for made in self.copies(k):
                made.start()

    def drain(self):
        for k in range(self.steps() - 1):
            for made in self.copies(k):
                made.wait_send()

    def copy(self, slot, src, dst, device):
        return pltpu.make_async_remote_copy(
            src_ref=src,
            dst_ref=dst,
            send_sem=self.send.at[self.piece, slot],
            recv_sem=self.recv.at[self.piece, slot],
            device_id=device,
            device_id_type=pl.DeviceIdType.MESH,
        )

    def half_at(self, core):
        return self.span(self.base + core * self.half, self.half)

    def own_at(self, seg, part=None):
        start = self.base // 2 + seg * self.quarter
        if part is None:
            return self.span(start, self.quarter)
        return self.span(start + part * self.share, self.share)

    def total_at(self, seg=None, part=None):
        start = self.base + self.core * self.half
        if seg is None:
            return self.span(start, self.half)
        start = start + seg * self.quarter
        if part is None:
            return self.span(start, self.quarter)
        return self.span(start + part * self.share, self.share)

    def crossed(self):
        for d in range(1, self.segments * self.inner):
            yield d - 1, self.seg ^ (d // self.inner), self.part ^ (d % self.inner)

    def copies(self, k):
        return (self.short_copies if self.short else self.long_copies)(k)

    def pair_copies(self, back, slot):
        if back:
            at = self.total_at()
            src, dst = self.total.at[at, :], self.total.at[at, :]
        else:
            src = self.src.at[self.half_at(1 - self.core), :]
            dst = self.half_in.at[self.span(self.base // 2, self.half), :]
        return [self.copy(slot, src, dst, self.device(core=1 - self.core))]

    def long_copies(self, k):
        first, peers = 1, self.segments - 1
        if k in (0, 5):
            return self.pair_copies(k == 5, 0 if k == 0 else 1 + 2 * (peers + self.inner - 1))
        made = []
        if k == 1:
            at = self.span(self.base // 2 // self.segments, self.quarter)
            for d in range(1, self.segments):
                src = self.own.at[self.own_at(self.seg ^ d), :]
                dst = self.quarter_in.at[d - 1, at, :]
                made.append(self.copy(first + d - 1, src, dst, self.device(seg=self.seg ^ d)))
        first += peers
        if k == 2:
            at = self.span(self.share_in(), self.share)
            for d in range(1, self.inner):
                src = self.own.at[self.own_at(self.seg, self.part ^ d), :]
                dst = self.part_in.at[d - 1, at, :]
                made.append(self.copy(first + d - 1, src, dst, self.device(part=self.part ^ d)))
        first += self.inner - 1
        if k == 3:
            ref = self.total.at[self.total_at(self.seg, self.part), :]
            for d in range(1, self.inner):
                made.append(self.copy(first + d - 1, ref, ref, self.device(part=self.part ^ d)))
        first += self.inner - 1
        if k == 4:
            ref = self.total.at[self.total_at(self.seg), :]
            for d in range(1, self.segments):
                made.append(self.copy(first + d - 1, ref, ref, self.device(seg=self.seg ^ d)))
        return made

    def short_copies(self, k):
        peers = self.segments * self.inner - 1
        if k in (0, 3):
            return self.pair_copies(k == 3, 0 if k == 0 else 1 + 2 * peers)
        made = []
        at = self.span(self.share_in(), self.share)
        back = self.total.at[self.total_at(self.seg, self.part), :]
        for slot, seg, part in self.crossed():
            if k == 1:
                src, dst = self.own.at[self.own_at(seg, part), :], self.cross_in.at[slot, at, :]
            else:
                src = dst = back
            first = 1 + (k - 1) * peers
            made.append(self.copy(first + slot, src, dst, self.device(seg=seg, part=part)))
        return made

    def outer_copies(self):
        first = slots_of(self.segments, self.inner, 1)
        at = self.span(self.share_in(), self.share)
        src = self.own.at[self.own_at(self.seg, self.part), :]
        return [
            self.copy(
                first + d - 1, src, self.whole_in.at[d - 1, at, :], self.device(group=self.group ^ d)
            )
            for d in range(1, self.outer)
        ]

    def share_in(self):
        return self.base // 2 // self.segments // self.inner

    def gather(self, k):
        half = self.base // 2
        if k == 1:
            first = (self.src, self.base + self.core * self.half)
            self.add((self.own, half), first, [(self.half_in, half)], self.half)
        elif k == 2 and not self.short:
            mine = (self.own, half + self.seg * self.quarter)
            received = [(self.quarter_in.at[d], half // self.segments) for d in range(self.segments - 1)]
            self.add(mine, mine, received, self.quarter)
        elif k == (2 if self.short else 3):
            ref = self.cross_in if self.short else self.part_in
            received = [(ref.at[d], self.share_in()) for d in range(ref.shape[0])]
            start = self.seg * self.quarter + self.part * self.share
            mine = (self.own, half + start)
            into = (self.total, self.base + self.core * self.half + start)
            if self.outer > 1:
                self.add(mine, mine, received, self.share)
                for made in self.outer_copies():
                    made.start()
                for made in self.outer_copies():
                    made.wait_recv()
                for made in self.outer_copies():
                    made.wait_send()
                received = [(self.whole_in.at[d], self.share_in()) for d in range(self.outer - 1)]
            self.add(into, mine, received, self.share)

    def add(self, dst, first, others, count):
        step = next(size for size in (128, 96, 80, 64, 48, 32, 16) if count % size == 0)

        def body(t, carry):
            at = t * step
            total = first[0][self.span(first[1] + at, step), :].astype(f32)
            for ref, start in others:
                total = total + ref[self.span(start + at, step), :].astype(f32)
            dst[0][self.span(dst[1] + at, step), :] = total.astype(bf16)
            return carry

        lax.fori_loop(0, count // step, body, 0)


def slots_of(segments, inner, outer):
    return 2 + 2 * (segments * inner - 1) + (outer - 1)


def greet(seg, dp, segments, inner, outer):
    barrier = pltpu.get_barrier_semaphore()
    core, part, group = dp % 2, dp // 2 % inner, dp // 2 // inner
    peers = [(seg, dp + 1 - 2 * core)]
    peers += [
        (seg ^ (d // inner), (group * inner + (part ^ (d % inner))) * 2 + core)
        for d in range(1, segments * inner)
    ]
    peers += [(seg, ((group ^ d) * inner + part) * 2 + core) for d in range(1, outer)]
    for peer in peers:
        pl.semaphore_signal(
            barrier, inc=1, device_id=peer, device_id_type=pl.DeviceIdType.MESH
        )
    return lambda: pl.semaphore_wait(barrier, len(peers))


def sum_scratch(sizes):
    segments, inner, outer = sizes
    quarter = ROWS // 2 // segments
    share = quarter // inner
    slots = slots_of(*sizes)
    return [
        pltpu.VMEM((ROWS // 2, C), bf16),
        pltpu.VMEM((segments - 1, quarter, C), bf16),
        pltpu.VMEM((inner - 1, share, C), bf16),
        pltpu.VMEM((segments * inner - 1, share, C), bf16),
        pltpu.VMEM((max(outer - 1, 1), share, C), bf16),
        pltpu.VMEM((ROWS // 2, C), bf16),
        pltpu.SemaphoreType.DMA((len(PIECES), slots)),
        pltpu.SemaphoreType.DMA((len(PIECES), slots)),
    ]


def compute_kernel(
    own,
    images,
    grid_ref,
    keep_ref,
    x_ref,
    cot_ref,
    ng,
    ns,
    qw,
    qb,
    p4w,
    p2w,
    kvw,
    vb,
    lk,
    pw,
    pb,
    hw,
    hb,
    mk,
    mb,
    ow,
    ob,
    perm,
    perm_t,
    places,
    out_ref,
    dx_ref,
    gp,
    xs,
    valid,
    um,
    u_all,
    ut,
    wc,
    ex,
    xh_a,
    xh_m,
    sc,
    u_a,
    q_a,
    p4,
    p2,
    xh_p,
    sc_p,
    ge_p,
    kin,
    wv,
    kb,
    vbd,
    pt,
    o_t,
    o_n,
    a_all,
    g_all,
    db,
    db_t,
    acc,
    kmask,
    near,
    small,
    pc,
    scale_ref,
):
    n = images
    rows = n * TOK
    seg = lax.axis_index("segment")
    lane = lax.broadcasted_iota(jnp.int32, (8, 128), 1)[0:1]

    def head_lanes(h):
        return (lane >= h * HEAD) & (lane < (h + 1) * HEAD)

    def tiles(fn, step=TILE):
        sums = None
        for start in range(0, rows, step):
            got = fn(slice(start, start + step))
            if got is not None:
                sums = got if sums is None else [x + y for x, y in zip(sums, got)]
        return None if sums is None else [col_sum(x) for x in sums]

    def row(ref, j, k=None):
        return ref[j, pl.ds(k, 1), :] if k is not None else ref[pl.ds(j, 1), :]

    def put(at, value):
        small[pl.ds(at, 1), :] = value

    def packed(start, count):
        return pl.ds(pl.multiple_of(start, 128), count)

    def hidden(step):
        return pl.ds(pl.multiple_of(step * CHUNK, CHUNK), CHUNK)

    def image_rows(i):
        return pl.ds(pl.multiple_of(i * TOK, 16), TOK)

    def shifted_rows(v, by):
        if by == 0:
            return v
        pad = jnp.zeros((abs(by), v.shape[1]), v.dtype)
        if by > 0:
            return jnp.concatenate([v[by:], pad], axis=0)
        return jnp.concatenate([pad, v[:by]], axis=0)

    col = lax.broadcasted_iota(jnp.int32, (GRID, GRID, 128), 1).reshape(TOK, 128)

    def taps_of(v):
        left = jnp.where(col > 0, pltpu.roll(v, 1, 0), 0.0)
        right = jnp.where(col < GRID - 1, pltpu.roll(v, TOK - 1, 0), 0.0)
        for row_off in range(3):
            for col_off, piece in enumerate((left, v, right)):
                yield row_off * 3 + col_off, shifted_rows(piece, (row_off - 1) * GRID)

    small[...] = jnp.zeros_like(small)
    sizes = []
    lane_row = lax.broadcasted_iota(jnp.int32, (TOK, 128), 1)
    for i in range(n):
        m_id, d_id = seg * own + i // (n // own), i % (n // own)
        high, wide = grid_ref[d_id, 0, m_id], grid_ref[d_id, 1, m_id]
        sizes.append((high, wide))
        line = lax.broadcasted_iota(jnp.int32, (GRID, GRID, 128), 0).reshape(TOK, 128)
        good = jnp.where((line < high) & (col < wide), 1.0, 0.0)
        valid[i * TOK : (i + 1) * TOK, :] = good
        for k in range(2 * BLOCKS):
            kept = keep_ref[d_id, k, m_id].astype(f32) / keep_rate
            scale_ref[i, k] = kept
        flags = jnp.where((lane_row == 16) | (lane_row == 48), 1.0, 0.0)
        for off, piece in taps_of(good):
            flags = jnp.where((lane_row == off) | (lane_row == 32 + off), piece, flags)
        for j in range(BLOCKS):
            u_all[j, i * TOK : (i + 1) * TOK, TAPS * C :] = flags.astype(bf16)
        base = 0
        for t in range(2):
            span = slice(base, base + CELLS[t])
            tall = (high + STRIDES[t] - 1) // STRIDES[t]
            across = (wide + STRIDES[t] - 1) // STRIDES[t]
            inside = (places[0, span, :] < tall.astype(f32)) & (
                places[1, span, :] < across.astype(f32)
            )
            kmask[i, span, :] = jnp.where(inside, 1.0, 0.0)
            base += CELLS[t]
    base = 0
    for t in range(2):
        span = slice(base, base + CELLS[t])
        a, b = places[0, span, :], places[1, span, :]
        for off in range(9):
            dr, dc = float(off // 3 - 1), float(off % 3 - 1)
            top = float(SIDES[t])
            ok = (a + dr >= 0) & (a + dr < top) & (b + dc >= 0) & (b + dc < top)
            near[off, span, :] = jnp.where(ok, 1.0, 0.0)
        base += CELLS[t]

    xs[...] = x_ref[...].astype(f32)

    def scaled(span, k):
        return valid[span, :] * scale_ref[span.start // TOK, k]

    def cell_spans(t):
        start = 0 if t == 0 else n * CELLS[0]
        return [slice(start + i * CELLS[t], start + (i + 1) * CELLS[t]) for i in range(n)]

    def cells_all(t):
        return slice(0, n * CELLS[0]) if t == 0 else slice(n * CELLS[0], n * sum(CELLS))

    place_span = (slice(0, CELLS[0]), slice(CELLS[0], sum(CELLS)))
    half = lane < 64
    own_half = (half, jnp.logical_not(half))

    def near_shift(t, off):
        return ((off // 3 - 1) * SIDES[t] + off % 3 - 1) % CELLS[t]

    def attention_forward(j):
        def first(ts):
            xhat, scale = norm_parts(xs[ts, :])
            xh_a[j, ts, :] = xhat
            sc[j, ts, 0:1] = scale
            u_a[j, ts, :] = (xhat * row(ng, j, 0) + row(ns, j, 0)).astype(bf16)

        tiles(first)
        for i in range(n):
            span = slice(i * TOK, (i + 1) * TOK)
            u = u_a[j, span, :]
            q_a[j, span, :] = (nn(u, qw[j]) + row(qb, j)).astype(bf16)
            um[:, i * C : (i + 1) * C] = (u.astype(f32) * valid[span, :]).astype(bf16)
        pc[...] = nn(perm[...], um[...]).astype(bf16)
        base = 0
        for t, ref in enumerate((p4, p2)):
            for k in range(STRIDES[t] ** 2):
                for i in range(n):
                    ref[j, i * CELLS[t] : (i + 1) * CELLS[t], k * C : (k + 1) * C] = pc[
                        base : base + CELLS[t], i * C : (i + 1) * C
                    ]
                base += CELLS[t]
        for t, (ref, weight) in enumerate(((p4, p4w), (p2, p2w))):
            xhat, scale = norm_parts(nn(ref[j], weight[j]))
            act, slope = gelu_parts(xhat * row(ng, j, 1 + t) + row(ns, j, 1 + t))
            act = act.astype(bf16)
            span = cells_all(t)
            xh_p[j, span, :] = xhat
            sc_p[j, span, :] = jnp.broadcast_to(scale, xhat.shape)
            ge_p[j, span, :] = slope
            kin[j, span, :] = act
            keyval = nn(act, kvw[j, t])
            turned = pltpu.roll(keyval, 64, 1)
            keys, vals = (keyval, turned) if t == 0 else (turned, keyval)
            bias = jnp.concatenate([row(vb, j, 0), row(vb, j, 1)], axis=1)
            kernel = jnp.concatenate([lk[j, :, 0, :], lk[j, :, 1, :]], axis=1)
            for i in range(n):
                part = slice(i * CELLS[t], (i + 1) * CELLS[t])
                w = (vals[part] + bias) * kmask[i, place_span[t], :]
                wv[j, cell_spans(t)[i], :] = w
                v = w
                for off in range(9):
                    by = near_shift(t, off)
                    moved = pltpu.roll(w, (CELLS[t] - by) % CELLS[t], 0) if by else w
                    v = v + moved * (near[off, place_span[t], :] * kernel[off : off + 1])
                for h in (2 * t, 2 * t + 1):
                    seg_rows = slice(*SEGS[h])
                    kb[j, i, seg_rows, :] = jnp.where(head_lanes(h), keys[part], 0.0).astype(bf16)
                    vbd[j, i, seg_rows, :] = jnp.where(head_lanes(h), v, 0.0).astype(bf16)
        for i in range(n):
            span = slice(i * TOK, (i + 1) * TOK)
            scores = nt(kb[j, i], q_a[j, span, :])
            for h, (low, top) in enumerate(SEGS):
                mask = kmask[i, place_span[h // 2], 0:1] > 0
                for c0 in range(0, TOK, 128):
                    c1 = min(c0 + 128, TOK)
                    s = jnp.where(mask, scores[low:top, c0:c1], -1e30)
                    e = jnp.exp2((s - jnp.max(s, axis=0, keepdims=True)) * (ROOT * LOG2E))
                    weight = e * pl.reciprocal(jnp.sum(e, axis=0, keepdims=True), approx=True)
                    pt[j, i, low:top, c0:c1] = weight.astype(bf16)
            mixed = tn(vbd[j, i], pt[j, i])
            o_t[j, i] = mixed.astype(bf16)
            o_n[span, :] = mixed.T.astype(bf16)
        for i in range(n):
            span = slice(i * TOK, (i + 1) * TOK)
            branch = nn(o_n[span, :], pw[j]) + row(pb, j)
            xs[span, :] = (xs[span, :] + scaled(span, 2 * j) * branch).astype(bf16).astype(f32)

    def build_wc(j):
        bias = row(hb, j)

        def tap(off, carry):
            factor = mk[off, pl.ds(j, 1), :] + jnp.where(off == 4, 1.0, 0.0)
            for r0 in range(0, C, 32):
                wc[j, pl.ds(pl.multiple_of(off * C + r0, 32), 32), :] = (
                    hw[j, r0 : r0 + 32, :].astype(f32) * factor
                ).astype(bf16)
            return carry

        lax.fori_loop(0, TAPS, tap, 0)
        ex[...] = jnp.zeros_like(ex)
        for off in range(TAPS + 1):
            at = off if off < TAPS else 16
            value = bias * mk[off, pl.ds(j, 1), :] if off < TAPS else bias + row(mb, j)
            high = value.astype(bf16).astype(f32)
            ex[at : at + 1, :] = high
            ex[at + 32 : at + 33, :] = value - high
        wc[j, TAPS * C :, :] = ex[...].astype(bf16)

    def mlp_forward(j):
        build_wc(j)

        def first(ts):
            xhat, scale = norm_parts(xs[ts, :])
            xh_m[j, ts, :] = xhat
            sc[j, ts, 1:2] = scale
            u = (xhat * row(ng, j, 3) + row(ns, j, 3)).astype(bf16).astype(f32)
            acc[0, ts, :] = u * valid[ts, :]

        tiles(first)
        for i in range(n):
            span = slice(i * TOK, (i + 1) * TOK)
            for off, piece in taps_of(acc[0, span, :]):
                u_all[j, span, off * C : (off + 1) * C] = piece.astype(bf16)

        def chunk(step, carry):
            cols = hidden(step)
            for i in range(n):
                field = nn(u_all[j, i * TOK : (i + 1) * TOK, :], wc[j, :, cols])
                for r0 in range(0, TOK, 16):
                    act, slope = gelu_parts(field[r0 : r0 + 16])
                    part = slice(i * TOK + r0, i * TOK + r0 + 16)
                    a_all[j, part, cols] = act.astype(bf16)
                    g_all[j, part, cols] = slope.astype(bf16)
            return carry

        lax.fori_loop(0, FF // CHUNK, chunk, 0)
        for i in range(n):
            span = slice(i * TOK, (i + 1) * TOK)
            branch = nn(a_all[j, span, :], ow[j]) + row(ob, j)
            xs[span, :] = (xs[span, :] + scaled(span, 2 * j + 1) * branch).astype(bf16).astype(f32)

    def mlp_backward(j):
        sb = j * S_BLOCK

        def first(ts):
            grad = (xs[ts, :] * scaled(ts, 2 * j + 1)).astype(bf16)
            db[ts, :] = grad
            return [folded(grad.astype(f32))]

        put(sb + S_OB, tiles(first)[0])
        db_t[j] = db[...].T

        def chunk(step, carry):
            cols = hidden(step)
            for i in range(n):
                span = slice(i * TOK, (i + 1) * TOK)
                da = nt(db[span, :], ow[j, cols, :])
                g_all[j, span, cols] = (da * g_all[j, span, cols].astype(f32)).astype(bf16)
            return carry

        lax.fori_loop(0, FF // CHUNK, chunk, 0)
        acc[...] = jnp.zeros_like(acc)

        def image(i, carry):
            for first_off in range(0, TAPS, 2):
                width = min(2, TAPS - first_off)
                taps = slice(first_off * C, (first_off + width) * C)
                moved = nt(g_all[j, image_rows(i), :], wc[j, taps, :])
                for s in range(width):
                    off = first_off + s
                    by = (off // 3 - 1) * GRID
                    piece = moved[:, s * C : (s + 1) * C]
                    start = pl.multiple_of(i * TOK + max(by, 0), 8)
                    span = pl.ds(start, TOK - abs(by))
                    acc[off % 3, span, :] += piece[: TOK - by] if by >= 0 else piece[-by:]
            return carry

        lax.fori_loop(0, n, image, 0)
        for i in range(n):
            span = slice(i * TOK, (i + 1) * TOK)
            left = pltpu.roll(jnp.where(col > 0, acc[0, span, :], 0.0), TOK - 1, 0)
            right = pltpu.roll(jnp.where(col < GRID - 1, acc[2, span, :], 0.0), 1, 0)
            acc[1, span, :] = (acc[1, span, :] + left + right) * valid[span, :]

        def last(ts):
            du = acc[1, ts, :]
            xhat = xh_m[j, ts, :]
            back = norm_back(du, xhat, sc[j, ts, 1:2], row(ng, j, 3))
            xs[ts, :] = (xs[ts, :] + back).astype(bf16).astype(f32)
            return [folded(du * xhat), folded(du)]

        gain, shift = tiles(last)
        put(sb + S_GAIN + 3, gain)
        put(sb + S_SHIFT + 3, shift)

    def mlp_turn(j):
        for off in range(TAPS + 1):
            ut[off * C : (off + 1) * C, :] = u_all[j, :, off * C : (off + 1) * C].T

    def mlp_weights(j, step):
        base, sb = MLP_AT[0] + j * (MLP_AT[1] - MLP_AT[0]), j * S_BLOCK
        cols = hidden(step)
        dow = nn(db_t[j], a_all[j, :, cols])
        gp[packed(base + output_row(step), CHUNK), :] = dow.T.astype(bf16)
        cross = nn(ut[...], g_all[j, :, cols])
        flag_rows = cross[TAPS * C : TAPS * C + 24]
        total = flag_rows[16:17]
        dhb = total
        weight = hw[j, :, cols].astype(f32)
        dweight = jnp.zeros((C, CHUNK), f32)
        b = hb[pl.ds(j, 1), cols]
        for off in range(TAPS):
            piece = cross[off * C : (off + 1) * C]
            factor = mk[off, pl.ds(j, 1), cols]
            flag = flag_rows[off : off + 1]
            dweight = dweight + piece * (factor + (1.0 if off == 4 else 0.0))
            dk = col_sum(piece * weight) + b * flag
            dhb = dhb + factor * flag
            for s in range(CHUNK // C):
                tile = step * (CHUNK // C) + s
                put(sb + S_MK + 16 * tile + off, dk[:, s * C : (s + 1) * C])
        for s in range(CHUNK // C):
            tile = step * (CHUNK // C) + s
            part = slice(s * C, (s + 1) * C)
            put(sb + S_HB + tile, dhb[:, part])
            put(sb + S_MB + tile, total[:, part])
            at = base + step * 2 * CHUNK + s * C
            gp[packed(at, C), :] = dweight[:, part].astype(bf16)

    def attention_backward(j):
        base, sb = ATT_AT[0] + j * (ATT_AT[1] - ATT_AT[0]), j * S_BLOCK

        def first(ts):
            grad = (xs[ts, :] * scaled(ts, 2 * j)).astype(bf16)
            db[ts, :] = grad
            return [folded(grad.astype(f32))]

        put(sb + S_PB, tiles(first)[0])
        dproj = jnp.zeros((C, C), f32)
        kernel = jnp.concatenate([lk[j, :, 0, :], lk[j, :, 1, :]], axis=1)
        dkernel = [jnp.zeros((1, C), f32) for _ in range(9)]
        dbias = jnp.zeros((1, C), f32)
        for i in range(n):
            span = slice(i * TOK, (i + 1) * TOK)
            dproj = dproj + nn(o_t[j, i], db[span, :])
            do = nt(db[span, :], pw[j]).astype(bf16)
            dprobs = nt(vbd[j, i], do)
            dvals = nn(pt[j, i], do)
            for low, top in SEGS:
                for c0 in range(0, TOK, 128):
                    c1 = min(c0 + 128, TOK)
                    weight = pt[j, i, low:top, c0:c1].astype(f32)
                    dweight = dprobs[low:top, c0:c1]
                    dot = jnp.sum(weight * dweight, axis=0, keepdims=True)
                    pt[j, i, low:top, c0:c1] = (weight * (dweight - dot)).astype(bf16)
            dkeys = nn(pt[j, i], q_a[j, span, :]) * ROOT
            dq = tn(kb[j, i], pt[j, i]) * ROOT
            o_n[span, :] = dq.T.astype(bf16)
            for t in range(2):
                dk = jnp.zeros((CELLS[t], C), f32)
                dv = jnp.zeros((CELLS[t], C), f32)
                for h in (2 * t, 2 * t + 1):
                    dk = dk + jnp.where(head_lanes(h), dkeys[slice(*SEGS[h])], 0.0)
                    dv = dv + jnp.where(head_lanes(h), dvals[slice(*SEGS[h])], 0.0)
                w = wv[j, cell_spans(t)[i], :]
                dw = dv
                for off in range(9):
                    by = near_shift(t, off)
                    part = dv * near[off, place_span[t], :]
                    moved = pltpu.roll(w, (CELLS[t] - by) % CELLS[t], 0) if by else w
                    dkernel[off] = dkernel[off] + col_sum(part * moved)
                    part = part * kernel[off : off + 1]
                    dw = dw + (pltpu.roll(part, by, 0) if by else part)
                dw = dw * kmask[i, place_span[t], :]
                dbias = dbias + col_sum(dw)
                if t == 0:
                    dkeyval = dk + pltpu.roll(dw, 64, 1)
                else:
                    dkeyval = pltpu.roll(dk, 64, 1) + dw
                wv[j, cell_spans(t)[i], :] = dkeyval
        gp[packed(base + R_PROJ, C), :] = dproj.astype(bf16)
        put(sb + S_VB, dbias)
        for off in range(9):
            put(sb + S_LK + off, dkernel[off])
        base_perm = 0
        for t, (ref, weight) in enumerate(((p4, p4w), (p2, p2w))):
            span = cells_all(t)
            dkeyval = wv[j, span, :].astype(bf16)
            at = base + R_KV + t * C
            gp[packed(at, C), :] = tn(kin[j, span, :], dkeyval).astype(bf16)
            dy = nt(dkeyval, kvw[j, t]) * ge_p[j, span, :]
            xhat = xh_p[j, span, :]
            put(sb + S_GAIN + 1 + t, col_sum(dy * xhat))
            put(sb + S_SHIFT + 1 + t, col_sum(dy))
            dpool = norm_back(dy, xhat, sc_p[j, span, :], row(ng, j, 1 + t)).astype(bf16)
            at = base + (R_P4, R_P2)[t]
            for k in range(STRIDES[t] ** 2):
                cross = tn(ref[j, :, k * C : (k + 1) * C], dpool)
                gp[packed(at + k * C, C), :] = cross.astype(bf16)
                back = nt(dpool, weight[j, k * C : (k + 1) * C, :]).astype(bf16)
                for i in range(n):
                    pc[base_perm : base_perm + CELLS[t], i * C : (i + 1) * C] = back[
                        i * CELLS[t] : (i + 1) * CELLS[t]
                    ]
                base_perm += CELLS[t]
        at = base + R_Q
        gp[packed(at, C), :] = tn(u_a[j], o_n[...]).astype(bf16)
        spread = nn(perm_t[...], pc[...])
        for i in range(n):
            span = slice(i * TOK, (i + 1) * TOK)
            back = nt(o_n[span, :], qw[j])
            acc[0, span, :] = back + spread[:, i * C : (i + 1) * C] * valid[span, :]

        def last(ts):
            du = acc[0, ts, :]
            xhat = xh_a[j, ts, :]
            back = norm_back(du, xhat, sc[j, ts, 0:1], row(ng, j, 0))
            xs[ts, :] = (xs[ts, :] + back).astype(bf16).astype(f32)
            return [folded(o_n[ts, :].astype(f32)), folded(du * xhat), folded(du)]

        bias, gain, shift = tiles(last)
        put(sb + S_QB, bias)
        put(sb + S_GAIN, gain)
        put(sb + S_SHIFT, shift)

    def forward(j, carry):
        attention_forward(j)
        mlp_forward(j)
        return carry

    def backward(k, carry):
        mlp_backward(BLOCKS - 1 - k)
        attention_backward(BLOCKS - 1 - k)
        return carry

    def weights(k, carry):
        j = BLOCKS - 1 - k
        mlp_turn(j)

        def chunk(step, inner):
            mlp_weights(j, step)
            return inner

        return lax.fori_loop(0, FF // CHUNK, chunk, carry)

    lax.fori_loop(0, BLOCKS, forward, 0)
    out_ref[...] = xs[...].astype(bf16)
    xs[...] = cot_ref[...].astype(f32)
    lax.fori_loop(0, BLOCKS, backward, 0)
    dx_ref[...] = xs[...].astype(bf16)
    lax.fori_loop(0, BLOCKS, weights, 0)
    gp[R_SMALL:, :] = small[...].astype(bf16)


def compute(own, images, grid_size, keep_mask, x, cot, weights):
    n = images
    rows = n * TOK
    cells = n * sum(CELLS)
    vmem = pl.BlockSpec(memory_space=pltpu.VMEM)
    smem = pl.BlockSpec(memory_space=pltpu.SMEM)
    matrix = permutation()
    consts = (
        jnp.asarray(matrix, bf16),
        jnp.asarray(matrix.T, bf16),
        jnp.asarray(cell_places()),
    )
    B = BLOCKS
    scratch = [
        pltpu.VMEM((rows, C), f32),
        pltpu.VMEM((rows, C), f32),
        pltpu.VMEM((TOK, n * C), bf16),
        pltpu.VMEM((B, rows, UW), bf16),
        pltpu.VMEM((UW, rows), bf16),
        pltpu.VMEM((B, UW, FF), bf16),
        pltpu.VMEM((C, FF), f32),
        pltpu.VMEM((B, rows, C), f32),
        pltpu.VMEM((B, rows, C), f32),
        pltpu.VMEM((B, rows, C), f32),
        pltpu.VMEM((B, rows, C), bf16),
        pltpu.VMEM((B, rows, C), bf16),
        pltpu.VMEM((B, n * CELLS[0], 16 * C), bf16),
        pltpu.VMEM((B, n * CELLS[1], 4 * C), bf16),
        pltpu.VMEM((B, cells, C), f32),
        pltpu.VMEM((B, cells, C), f32),
        pltpu.VMEM((B, cells, C), f32),
        pltpu.VMEM((B, cells, C), bf16),
        pltpu.VMEM((B, cells, C), f32),
        pltpu.VMEM((B, n, KEYS, C), bf16),
        pltpu.VMEM((B, n, KEYS, C), bf16),
        pltpu.VMEM((B, n, KEYS, TOK), bf16),
        pltpu.VMEM((B, n, C, TOK), bf16),
        pltpu.VMEM((rows, C), bf16),
        pltpu.VMEM((B, rows, FF), bf16),
        pltpu.VMEM((B, rows, FF), bf16),
        pltpu.VMEM((rows, C), bf16),
        pltpu.VMEM((B, C, rows), bf16),
        pltpu.VMEM((3, rows, C), f32),
        pltpu.VMEM((n, sum(CELLS), C), f32),
        pltpu.VMEM((9, sum(CELLS), C), f32),
        pltpu.VMEM((ROWS - R_SMALL, C), f32),
        pltpu.VMEM((PERM, n * C), bf16),
        pltpu.SMEM((n, 2 * BLOCKS), f32),
    ]
    return pl.pallas_call(
        functools.partial(compute_kernel, own, images),
        out_shape=(
            jax.ShapeDtypeStruct((rows, C), bf16),
            jax.ShapeDtypeStruct((rows, C), bf16),
            jax.ShapeDtypeStruct((ROWS, C), bf16),
        ),
        in_specs=[smem, smem] + [vmem] * (2 + len(weights) + len(consts)),
        out_specs=(vmem,) * 3,
        scratch_shapes=scratch,
        compiler_params=pltpu.CompilerParams(vmem_limit_bytes=62 * 2**20),
        name="compute",
    )(grid_size, keep_mask, x, cot, *weights, *consts)


def sum_kernel(sizes, src, total, *scratch):
    seg, dp = lax.axis_index("segment"), lax.axis_index("dp")
    greet(seg, dp, *sizes)()
    refs = (src,) + scratch[:6] + (total,) + scratch[6:]
    pieces = [
        Summed((seg, dp) + sizes, p, base, count, short, refs)
        for p, (base, count, short) in enumerate(PIECES)
    ]
    for t in range(max(p + piece.steps() for p, piece in enumerate(pieces))):
        for p, piece in enumerate(pieces):
            if 0 <= t - p < piece.steps():
                piece.step(t - p)
    for piece in pieces:
        piece.drain()


def summed(packed):
    segments, pairs = lax.axis_size("segment"), lax.axis_size("dp") // 2
    inner = min(pairs, 4)
    sizes = (segments, inner, pairs // inner)
    vmem = pl.BlockSpec(memory_space=pltpu.VMEM)
    return pl.pallas_call(
        functools.partial(sum_kernel, sizes),
        out_shape=jax.ShapeDtypeStruct((ROWS, C), bf16),
        in_specs=[vmem],
        out_specs=vmem,
        scratch_shapes=sum_scratch(sizes),
        compiler_params=pltpu.CompilerParams(
            collective_id=0, has_side_effects=True, vmem_limit_bytes=40 * 2**20
        ),
        name="summed",
    )(packed)


def unpack_kernel(gp, out_in, dx_in, *refs):
    out_ref, dx_ref = refs[:2]
    gain, shift, qw, qb, p4, p2, kvw, vb, lk, pw, pb, hw, hb, mk, mb, ow, ob = refs[2:]
    out_ref[...] = out_in[...]
    dx_ref[...] = dx_in[...]
    for j in range(BLOCKS):
        att, mlp, sb = ATT_AT[j], MLP_AT[j], R_SMALL + j * S_BLOCK
        p4[j] = gp[att + R_P4 : att + R_P2, :].astype(f32)
        p2[j] = gp[att + R_P2 : att + R_KV, :].astype(f32)
        for t in range(2):
            kvw[j, t] = gp[att + R_KV + t * C : att + R_KV + (t + 1) * C, :].astype(f32)
        qw[j] = gp[att + R_Q : att + R_PROJ, :].astype(f32)
        pw[j] = gp[att + R_PROJ : att + R_ATT, :].astype(f32)
        for s in range(FF // C):
            at = mlp + hidden_row(s)
            hw[j, :, s * C : (s + 1) * C] = gp[at : at + C, :].astype(f32)
        for step in range(FF // CHUNK):
            at = mlp + output_row(step)
            ow[j, step * CHUNK : (step + 1) * CHUNK, :] = gp[at : at + CHUNK, :].astype(f32)
        head = gp[sb : sb + 48, :].astype(f32)
        gain[j] = head[S_GAIN : S_GAIN + 4]
        shift[j] = head[S_SHIFT : S_SHIFT + 4]
        qb[j : j + 1, :] = head[S_QB : S_QB + 1]
        vb[j, 0:1, :] = head[S_VB : S_VB + 1, 0:64]
        vb[j, 1:2, :] = head[S_VB : S_VB + 1, 64:128]
        pb[j : j + 1, :] = head[S_PB : S_PB + 1]
        ob[j : j + 1, :] = head[S_OB : S_OB + 1]
        lk[j, :, 0, :] = head[S_LK : S_LK + 9, 0:64]
        lk[j, :, 1, :] = head[S_LK : S_LK + 9, 64:128]
        for s in range(FF // C):
            part = slice(s * C, (s + 1) * C)
            hb[j : j + 1, part] = head[S_HB + s : S_HB + s + 1]
            mb[j : j + 1, part] = head[S_MB + s : S_MB + s + 1]
            at = sb + S_MK + 16 * s
            mk[:, j, part] = gp[at : at + 16, :].astype(f32)[0:9]


def unpack(packed, outputs, input_grad, weights):
    vmem = pl.BlockSpec(memory_space=pltpu.VMEM)
    streams = (jax.ShapeDtypeStruct(outputs.shape, bf16),) * 2
    return pl.pallas_call(
        unpack_kernel,
        out_shape=streams + tuple(jax.ShapeDtypeStruct(w.shape, f32) for w in weights),
        in_specs=[vmem] * 3,
        out_specs=(vmem,) * (2 + len(weights)),
        compiler_params=pltpu.CompilerParams(vmem_limit_bytes=40 * 2**20),
        name="unpack",
    )(packed, outputs, input_grad)


def on_device(inputs, grid_size, keep_mask, cotangent, *weights):
    own, per = inputs.shape[:2]
    images = own * per
    flat = (images * TOK, C)
    turned = list(weights)
    turned[LK] = jnp.transpose(turned[LK], (0, 2, 1, 3))
    turned[MK] = jnp.transpose(turned[MK], (1, 0, 2))
    outputs, input_grad, packed = compute(
        own,
        images,
        jnp.transpose(grid_size, (1, 2, 0)),
        jnp.transpose(keep_mask, (1, 2, 0)),
        inputs.reshape(flat),
        cotangent.reshape(flat),
        turned,
    )
    outputs, input_grad, *grads = unpack(summed(packed), outputs, input_grad, turned)
    grads[LK] = jnp.transpose(grads[LK], (0, 2, 1, 3))
    grads[MK] = jnp.transpose(grads[MK], (1, 0, 2))
    return (outputs.reshape(inputs.shape), input_grad.reshape(inputs.shape)) + tuple(grads)


def solution(mesh):
    stream = P("segment", "dp", None, None)
    picked = P(None, "dp", None)
    return jax.shard_map(
        on_device,
        mesh=mesh,
        in_specs=(stream, picked, picked, stream) + (P(),) * 17,
        out_specs=(stream, stream) + (P(),) * 17,
        check_vma=False,
    )
```

```python
import functools

import jax
import jax.numpy as jnp
import numpy as np
from jax import lax
from jax.experimental import pallas as pl
from jax.experimental.pallas import tpu as pltpu
from jax.sharding import PartitionSpec as P

GRID = 24
TOK = GRID * GRID
C = 128
FF = 1024
HEAD = 32
BLOCKS = 2
SIDES = (6, 12)
STRIDES = (4, 2)
CELLS = (48, 144)
SEGS = ((0, 48), (48, 96), (96, 240), (240, 384))
KEYS = 384
PERM = 16 * 48 + 4 * 144
TAPS = 9
UW = TAPS * C + C
CHUNK = 512
TILE = 96

R_P4, R_P2, R_KV, R_Q, R_PROJ, R_ATT = 0, 2048, 2560, 2816, 2944, 3072
R_MLP = 2048
ATT_AT = (R_ATT + R_MLP, 0)
MLP_AT = (2 * R_ATT + R_MLP, R_ATT)
S_GAIN, S_SHIFT, S_QB, S_VB, S_PB, S_OB, S_LK, S_HB, S_MB, S_MK, S_BLOCK = (
    0,
    4,
    8,
    9,
    10,
    11,
    16,
    32,
    40,
    48,
    192,
)
R_SMALL = BLOCKS * (R_ATT + R_MLP)
ROWS = R_SMALL + 512
PIECES = (
    (ATT_AT[1], R_ATT, False),
    (MLP_AT[1], R_MLP, False),
    (ATT_AT[0], R_ATT, False),
    (MLP_AT[0], R_MLP // 2, True),
    (MLP_AT[0] + R_MLP // 2, R_MLP // 2 + ROWS - R_SMALL, True),
)

LK, HW, MK, OW = 8, 11, 13, 15

epsilon = 1e-06
keep_rate = 0.8
ROOT = HEAD**-0.5
LOG2E = 1.4426950408889634
f32, bf16 = jnp.float32, jnp.bfloat16


def hidden_row(tile):
    return tile // (CHUNK // C) * 2 * CHUNK + tile % (CHUNK // C) * C


def output_row(step):
    return step * 2 * CHUNK + CHUNK


def permutation():
    matrix = np.zeros((PERM, TOK), np.float32)
    base = 0
    for stride, side, cells in zip(STRIDES, SIDES, CELLS):
        for row_off in range(stride):
            for col_off in range(stride):
                for a in range(side):
                    for b in range(side):
                        token = (a * stride + row_off) * GRID + b * stride + col_off
                        matrix[base + a * side + b, token] = 1.0
                base += cells
    return matrix


def cell_places():
    places = np.full((2, sum(CELLS), 128), 99.0, np.float32)
    base = 0
    for side, cells in zip(SIDES, CELLS):
        for a in range(side):
            for b in range(side):
                places[0, base + a * side + b] = a
                places[1, base + a * side + b] = b
        base += cells
    return places


def nn(left, right):
    return jnp.dot(left, right, preferred_element_type=f32)


def nt(left, right):
    return lax.dot_general(left, right, (((1,), (1,)), ((), ())), preferred_element_type=f32)


def tn(left, right):
    return lax.dot_general(left, right, (((0,), (0,)), ((), ())), preferred_element_type=f32)


def gelu_parts(m):
    size = jnp.abs(m)
    t = pl.reciprocal(1.0 + (0.3275911 * 0.5**0.5) * size, approx=True)
    e = jnp.exp2(m * (m * (-0.5 * LOG2E)))
    poly = 0.5 * 1.061405429
    for coef in (-1.453152027, 1.421413741, -0.284496736, 0.254829592):
        poly = poly * t + 0.5 * coef
    poly = poly * t
    tail = poly * e
    slope = (poly - size * 0.3989422804014327) * e
    return jnp.maximum(m, 0.0) - size * tail, jnp.where(m >= 0, 1.0 - slope, slope)


def norm_parts(x):
    centred = x - jnp.mean(x, axis=-1, keepdims=True)
    scale = lax.rsqrt(jnp.mean(centred * centred, axis=-1, keepdims=True) + epsilon)
    return centred * scale, scale


def norm_back(du, xhat, scale, gain):
    dxhat = du * gain
    first = jnp.mean(dxhat, axis=-1, keepdims=True)
    second = jnp.mean(dxhat * xhat, axis=-1, keepdims=True)
    return scale * (dxhat - first - xhat * second)


def col_sum(x):
    return jnp.sum(x, axis=0, keepdims=True)


def folded(x):
    return jnp.sum(x.reshape(-1, 8, x.shape[-1]), axis=0)


class Summed:
    def __init__(self, place, piece, base, count, short, refs):
        self.seg, self.dp, self.segments, self.inner, self.outer = place
        self.piece, self.base, self.count = piece, base, count
        self.short = short
        (
            self.src,
            self.half_in,
            self.quarter_in,
            self.part_in,
            self.cross_in,
            self.whole_in,
            self.own,
            self.total,
            self.send,
            self.recv,
        ) = refs
        self.core, rest = self.dp % 2, self.dp // 2
        self.part, self.group = rest % self.inner, rest // self.inner
        self.half = count // 2
        self.quarter = self.half // self.segments
        self.share = self.quarter // self.inner

    def span(self, start, size):
        return pl.ds(pl.multiple_of(start, 16), size)

    def device(self, seg=None, core=None, part=None, group=None):
        seg = self.seg if seg is None else seg
        core = self.core if core is None else core
        part = self.part if part is None else part
        group = self.group if group is None else group
        return (seg, (group * self.inner + part) * 2 + core)

    def copy(self, slot, src, dst, device):
        made = pltpu.make_async_remote_copy(
            src_ref=src,
            dst_ref=dst,
            send_sem=self.send.at[self.piece, slot],
            recv_sem=self.recv.at[self.piece, slot],
            device_id=device,
            device_id_type=pl.DeviceIdType.MESH,
        )
        made.start()
        self.started.append(made)
        return made

    def half_at(self, core):
        return self.span(self.base + core * self.half, self.half)

    def own_at(self, seg, part=None):
        start = self.base // 2 + seg * self.quarter
        if part is None:
            return self.span(start, self.quarter)
        return self.span(start + part * self.share, self.share)

    def total_at(self, seg=None, part=None):
        start = self.base + self.core * self.half
        if seg is None:
            return self.span(start, self.half)
        start = start + seg * self.quarter
        if part is None:
            return self.span(start, self.quarter)
        return self.span(start + part * self.share, self.share)

    def steps(self):
        return 5 if self.short else 7

    def step(self, k):
        if k > 0:
            for made in self.copies(k - 1):
                made.wait_recv()
            self.gather(k)
        if k + 1 < self.steps():
            for made in self.copies(k):
                made.start()

    def drain(self):
        for k in range(self.steps() - 1):
            for made in self.copies(k):
                made.wait_send()

    def copy(self, slot, src, dst, device):
        return pltpu.make_async_remote_copy(
            src_ref=src,
            dst_ref=dst,
            send_sem=self.send.at[self.piece, slot],
            recv_sem=self.recv.at[self.piece, slot],
            device_id=device,
            device_id_type=pl.DeviceIdType.MESH,
        )

    def half_at(self, core):
        return self.span(self.base + core * self.half, self.half)

    def own_at(self, seg, part=None):
        start = self.base // 2 + seg * self.quarter
        if part is None:
            return self.span(start, self.quarter)
        return self.span(start + part * self.share, self.share)

    def total_at(self, seg=None, part=None):
        start = self.base + self.core * self.half
        if seg is None:
            return self.span(start, self.half)
        start = start + seg * self.quarter
        if part is None:
            return self.span(start, self.quarter)
        return self.span(start + part * self.share, self.share)

    def crossed(self):
        for d in range(1, self.segments * self.inner):
            yield d - 1, self.seg ^ (d // self.inner), self.part ^ (d % self.inner)

    def copies(self, k):
        return (self.short_copies if self.short else self.long_copies)(k)

    def pair_copies(self, back, slot):
        if back:
            at = self.total_at()
            src, dst = self.total.at[at, :], self.total.at[at, :]
        else:
            src = self.src.at[self.half_at(1 - self.core), :]
            dst = self.half_in.at[self.span(self.base // 2, self.half), :]
        return [self.copy(slot, src, dst, self.device(core=1 - self.core))]

    def long_copies(self, k):
        first, peers = 1, self.segments - 1
        if k in (0, 5):
            return self.pair_copies(k == 5, 0 if k == 0 else 1 + 2 * (peers + self.inner - 1))
        made = []
        if k == 1:
            at = self.span(self.base // 2 // self.segments, self.quarter)
            for d in range(1, self.segments):
                src = self.own.at[self.own_at(self.seg ^ d), :]
                dst = self.quarter_in.at[d - 1, at, :]
                made.append(self.copy(first + d - 1, src, dst, self.device(seg=self.seg ^ d)))
        first += peers
        if k == 2:
            at = self.span(self.share_in(), self.share)
            for d in range(1, self.inner):
                src = self.own.at[self.own_at(self.seg, self.part ^ d), :]
                dst = self.part_in.at[d - 1, at, :]
                made.append(self.copy(first + d - 1, src, dst, self.device(part=self.part ^ d)))
        first += self.inner - 1
        if k == 3:
            ref = self.total.at[self.total_at(self.seg, self.part), :]
            for d in range(1, self.inner):
                made.append(self.copy(first + d - 1, ref, ref, self.device(part=self.part ^ d)))
        first += self.inner - 1
        if k == 4:
            ref = self.total.at[self.total_at(self.seg), :]
            for d in range(1, self.segments):
                made.append(self.copy(first + d - 1, ref, ref, self.device(seg=self.seg ^ d)))
        return made

    def short_copies(self, k):
        peers = self.segments * self.inner - 1
        if k in (0, 3):
            return self.pair_copies(k == 3, 0 if k == 0 else 1 + 2 * peers)
        made = []
        at = self.span(self.share_in(), self.share)
        back = self.total.at[self.total_at(self.seg, self.part), :]
        for slot, seg, part in self.crossed():
            if k == 1:
                src, dst = self.own.at[self.own_at(seg, part), :], self.cross_in.at[slot, at, :]
            else:
                src = dst = back
            first = 1 + (k - 1) * peers
            made.append(self.copy(first + slot, src, dst, self.device(seg=seg, part=part)))
        return made

    def outer_copies(self):
        first = slots_of(self.segments, self.inner, 1)
        at = self.span(self.share_in(), self.share)
        src = self.own.at[self.own_at(self.seg, self.part), :]
        return [
            self.copy(
                first + d - 1, src, self.whole_in.at[d - 1, at, :], self.device(group=self.group ^ d)
            )
            for d in range(1, self.outer)
        ]

    def share_in(self):
        return self.base // 2 // self.segments // self.inner

    def gather(self, k):
        half = self.base // 2
        if k == 1:
            first = (self.src, self.base + self.core * self.half)
            self.add((self.own, half), first, [(self.half_in, half)], self.half)
        elif k == 2 and not self.short:
            mine = (self.own, half + self.seg * self.quarter)
            received = [(self.quarter_in.at[d], half // self.segments) for d in range(self.segments - 1)]
            self.add(mine, mine, received, self.quarter)
        elif k == (2 if self.short else 3):
            ref = self.cross_in if self.short else self.part_in
            received = [(ref.at[d], self.share_in()) for d in range(ref.shape[0])]
            start = self.seg * self.quarter + self.part * self.share
            mine = (self.own, half + start)
            into = (self.total, self.base + self.core * self.half + start)
            if self.outer > 1:
                self.add(mine, mine, received, self.share)
                for made in self.outer_copies():
                    made.start()
                for made in self.outer_copies():
                    made.wait_recv()
                for made in self.outer_copies():
                    made.wait_send()
                received = [(self.whole_in.at[d], self.share_in()) for d in range(self.outer - 1)]
            self.add(into, mine, received, self.share)

    def add(self, dst, first, others, count):
        step = next(size for size in (128, 96, 80, 64, 48, 32, 16) if count % size == 0)

        def body(t, carry):
            at = t * step
            total = first[0][self.span(first[1] + at, step), :].astype(f32)
            for ref, start in others:
                total = total + ref[self.span(start + at, step), :].astype(f32)
            dst[0][self.span(dst[1] + at, step), :] = total.astype(bf16)
            return carry

        lax.fori_loop(0, count // step, body, 0)


def slots_of(segments, inner, outer):
    return 2 + 2 * (segments * inner - 1) + (outer - 1)


def greet(seg, dp, segments, inner, outer):
    barrier = pltpu.get_barrier_semaphore()
    core, part, group = dp % 2, dp // 2 % inner, dp // 2 // inner
    peers = [(seg, dp + 1 - 2 * core)]
    peers += [
        (seg ^ (d // inner), (group * inner + (part ^ (d % inner))) * 2 + core)
        for d in range(1, segments * inner)
    ]
    peers += [(seg, ((group ^ d) * inner + part) * 2 + core) for d in range(1, outer)]
    for peer in peers:
        pl.semaphore_signal(
            barrier, inc=1, device_id=peer, device_id_type=pl.DeviceIdType.MESH
        )
    return lambda: pl.semaphore_wait(barrier, len(peers))


def sum_scratch(sizes):
    segments, inner, outer = sizes
    quarter = ROWS // 2 // segments
    share = quarter // inner
    slots = slots_of(*sizes)
    return [
        pltpu.VMEM((ROWS // 2, C), bf16),
        pltpu.VMEM((segments - 1, quarter, C), bf16),
        pltpu.VMEM((inner - 1, share, C), bf16),
        pltpu.VMEM((segments * inner - 1, share, C), bf16),
        pltpu.VMEM((max(outer - 1, 1), share, C), bf16),
        pltpu.VMEM((ROWS // 2, C), bf16),
        pltpu.VMEM((ROWS, C), bf16),
        pltpu.SemaphoreType.DMA((len(PIECES), slots)),
        pltpu.SemaphoreType.DMA((len(PIECES), slots)),
    ]


def compute_kernel(
    own,
    images,
    sizes,
    grid_ref,
    keep_ref,
    x_ref,
    cot_in,
    ng,
    ns,
    qw,
    qb,
    p4w,
    p2w,
    kvw,
    vb,
    lk,
    pw,
    pb,
    hw_in,
    hb,
    mk,
    mb,
    ow_in,
    ob,
    perm,
    perm_t_in,
    places,
    out_ref,
    dx_ref,
    summed_ref,
    xs,
    valid,
    um,
    u_all,
    ut,
    wc,
    ex,
    xh_a,
    xh_m,
    sc,
    u_a,
    q_a,
    p4,
    p2,
    xh_p,
    sc_p,
    ge_p,
    kin,
    wv,
    kb,
    vbd,
    pt,
    o_t,
    o_n,
    a_all,
    g_all,
    db,
    db_t,
    acc,
    kmask,
    near,
    small,
    pc,
    scale_ref,
    cot_ref,
    hw,
    ow,
    perm_t,
    out_st,
    dx_st,
    sems,
    gp,
    half_in,
    quarter_in,
    part_in,
    cross_in,
    whole_in,
    own_part,
    total_ref,
    send,
    recv,
):
    n = images
    rows = n * TOK
    seg, dp = lax.axis_index("segment"), lax.axis_index("dp")
    all_here = greet(seg, dp, *sizes)
    late = [
        pltpu.make_async_copy(src, dst, sems.at[k])
        for k, (src, dst) in enumerate(
            ((hw_in, hw), (ow_in, ow), (cot_in, cot_ref), (perm_t_in, perm_t))
        )
    ]
    for made in late:
        made.start()
    leaving = []

    def leave(src, dst):
        made = pltpu.make_async_copy(src, dst, sems.at[len(late) + len(leaving)])
        made.start()
        leaving.append(made)

    refs = (
        gp,
        half_in,
        quarter_in,
        part_in,
        cross_in,
        whole_in,
        own_part,
        total_ref,
        send,
        recv,
    )
    pieces = [
        Summed((seg, dp) + sizes, p, base, count, short, refs)
        for p, (base, count, short) in enumerate(PIECES)
    ]

    def move(*steps):
        for p, k in steps:
            pieces[p].step(k)
            if k + 1 == pieces[p].steps():
                rows_of = pl.ds(PIECES[p][0], PIECES[p][1])
                leave(total_ref.at[rows_of, :], summed_ref.at[rows_of, :])

    lane = lax.broadcasted_iota(jnp.int32, (8, 128), 1)[0:1]

    def head_lanes(h):
        return (lane >= h * HEAD) & (lane < (h + 1) * HEAD)

    def tiles(fn, step=TILE):
        sums = None
        for start in range(0, rows, step):
            got = fn(slice(start, start + step))
            if got is not None:
                sums = got if sums is None else [x + y for x, y in zip(sums, got)]
        return None if sums is None else [col_sum(x) for x in sums]

    def row(ref, j, k=None):
        return ref[j, pl.ds(k, 1), :] if k is not None else ref[pl.ds(j, 1), :]

    def shifted_rows(v, by):
        if by == 0:
            return v
        pad = jnp.zeros((abs(by), v.shape[1]), v.dtype)
        if by > 0:
            return jnp.concatenate([v[by:], pad], axis=0)
        return jnp.concatenate([pad, v[:by]], axis=0)

    col = lax.broadcasted_iota(jnp.int32, (GRID, GRID, 128), 1).reshape(TOK, 128)

    def taps_of(v):
        left = jnp.where(col > 0, pltpu.roll(v, 1, 0), 0.0)
        right = jnp.where(col < GRID - 1, pltpu.roll(v, TOK - 1, 0), 0.0)
        for row_off in range(3):
            for col_off, piece in enumerate((left, v, right)):
                yield row_off * 3 + col_off, shifted_rows(piece, (row_off - 1) * GRID)

    small[...] = jnp.zeros_like(small)
    sizes = []
    lane_row = lax.broadcasted_iota(jnp.int32, (TOK, 128), 1)
    for i in range(n):
        m_id, d_id = seg * own + i // (n // own), i % (n // own)
        high, wide = grid_ref[d_id, 0, m_id], grid_ref[d_id, 1, m_id]
        sizes.append((high, wide))
        line = lax.broadcasted_iota(jnp.int32, (GRID, GRID, 128), 0).reshape(TOK, 128)
        good = jnp.where((line < high) & (col < wide), 1.0, 0.0)
        valid[i * TOK : (i + 1) * TOK, :] = good
        for k in range(2 * BLOCKS):
            kept = keep_ref[d_id, k, m_id].astype(f32) / keep_rate
            scale_ref[i, k] = kept
        flags = jnp.where((lane_row == 16) | (lane_row == 48), 1.0, 0.0)
        for off, piece in taps_of(good):
            flags = jnp.where((lane_row == off) | (lane_row == 32 + off), piece, flags)
        for j in range(BLOCKS):
            u_all[j, i * TOK : (i + 1) * TOK, TAPS * C :] = flags.astype(bf16)
        base = 0
        for t in range(2):
            span = slice(base, base + CELLS[t])
            tall = (high + STRIDES[t] - 1) // STRIDES[t]
            across = (wide + STRIDES[t] - 1) // STRIDES[t]
            inside = (places[0, span, :] < tall.astype(f32)) & (
                places[1, span, :] < across.astype(f32)
            )
            kmask[i, span, :] = jnp.where(inside, 1.0, 0.0)
            base += CELLS[t]
    base = 0
    for t in range(2):
        span = slice(base, base + CELLS[t])
        a, b = places[0, span, :], places[1, span, :]
        for off in range(9):
            dr, dc = float(off // 3 - 1), float(off % 3 - 1)
            top = float(SIDES[t])
            ok = (a + dr >= 0) & (a + dr < top) & (b + dc >= 0) & (b + dc < top)
            near[off, span, :] = jnp.where(ok, 1.0, 0.0)
        base += CELLS[t]

    xs[...] = x_ref[...].astype(f32)

    def scaled(span, k):
        return valid[span, :] * scale_ref[span.start // TOK, k]

    def cell_spans(t):
        start = 0 if t == 0 else n * CELLS[0]
        return [slice(start + i * CELLS[t], start + (i + 1) * CELLS[t]) for i in range(n)]

    def cells_all(t):
        return slice(0, n * CELLS[0]) if t == 0 else slice(n * CELLS[0], n * sum(CELLS))

    place_span = (slice(0, CELLS[0]), slice(CELLS[0], sum(CELLS)))
    half = lane < 64
    own_half = (half, jnp.logical_not(half))

    def near_shift(t, off):
        return ((off // 3 - 1) * SIDES[t] + off % 3 - 1) % CELLS[t]

    def attention_forward(j):
        def first(ts):
            xhat, scale = norm_parts(xs[ts, :])
            xh_a[j, ts, :] = xhat
            sc[j, ts, 0:1] = scale
            u_a[j, ts, :] = (xhat * row(ng, j, 0) + row(ns, j, 0)).astype(bf16)

        tiles(first)
        for i in range(n):
            span = slice(i * TOK, (i + 1) * TOK)
            u = u_a[j, span, :]
            q_a[j, span, :] = (nn(u, qw[j]) + row(qb, j)).astype(bf16)
            um[:, i * C : (i + 1) * C] = (u.astype(f32) * valid[span, :]).astype(bf16)
        pc[...] = nn(perm[...], um[...]).astype(bf16)
        base = 0
        for t, ref in enumerate((p4, p2)):
            for k in range(STRIDES[t] ** 2):
                for i in range(n):
                    ref[j, i * CELLS[t] : (i + 1) * CELLS[t], k * C : (k + 1) * C] = pc[
                        base : base + CELLS[t], i * C : (i + 1) * C
                    ]
                base += CELLS[t]
        for t, (ref, weight) in enumerate(((p4, p4w), (p2, p2w))):
            xhat, scale = norm_parts(nn(ref[j], weight[j]))
            act, slope = gelu_parts(xhat * row(ng, j, 1 + t) + row(ns, j, 1 + t))
            act = act.astype(bf16)
            span = cells_all(t)
            xh_p[j, span, :] = xhat
            sc_p[j, span, :] = jnp.broadcast_to(scale, xhat.shape)
            ge_p[j, span, :] = slope
            kin[j, span, :] = act
            keyval = nn(act, kvw[j, t])
            turned = pltpu.roll(keyval, 64, 1)
            keys, vals = (keyval, turned) if t == 0 else (turned, keyval)
            bias = jnp.concatenate([row(vb, j, 0), row(vb, j, 1)], axis=1)
            kernel = jnp.concatenate([lk[j, :, 0, :], lk[j, :, 1, :]], axis=1)
            for i in range(n):
                part = slice(i * CELLS[t], (i + 1) * CELLS[t])
                w = (vals[part] + bias) * kmask[i, place_span[t], :]
                wv[j, cell_spans(t)[i], :] = w
                v = w
                for off in range(9):
                    by = near_shift(t, off)
                    moved = pltpu.roll(w, (CELLS[t] - by) % CELLS[t], 0) if by else w
                    v = v + moved * (near[off, place_span[t], :] * kernel[off : off + 1])
                for h in (2 * t, 2 * t + 1):
                    seg_rows = slice(*SEGS[h])
                    kb[j, i, seg_rows, :] = jnp.where(head_lanes(h), keys[part], 0.0).astype(bf16)
                    vbd[j, i, seg_rows, :] = jnp.where(head_lanes(h), v, 0.0).astype(bf16)
        for i in range(n):
            span = slice(i * TOK, (i + 1) * TOK)
            scores = nt(kb[j, i], q_a[j, span, :])
            for h, (low, top) in enumerate(SEGS):
                mask = kmask[i, place_span[h // 2], 0:1] > 0
                for c0 in range(0, TOK, 128):
                    c1 = min(c0 + 128, TOK)
                    s = jnp.where(mask, scores[low:top, c0:c1], -1e30)
                    e = jnp.exp2((s - jnp.max(s, axis=0, keepdims=True)) * (ROOT * LOG2E))
                    weight = e * pl.reciprocal(jnp.sum(e, axis=0, keepdims=True), approx=True)
                    pt[j, i, low:top, c0:c1] = weight.astype(bf16)
            mixed = tn(vbd[j, i], pt[j, i])
            o_t[j, i] = mixed.astype(bf16)
            o_n[span, :] = mixed.T.astype(bf16)
        for i in range(n):
            span = slice(i * TOK, (i + 1) * TOK)
            branch = nn(o_n[span, :], pw[j]) + row(pb, j)
            xs[span, :] = (xs[span, :] + scaled(span, 2 * j) * branch).astype(bf16).astype(f32)

    def build_wc(j):
        bias = row(hb, j)

        def tap(off, carry):
            factor = mk[off, j : j + 1, :] + jnp.where(off == 4, 1.0, 0.0)
            for r0 in range(0, C, 32):
                wc[j, pl.ds(pl.multiple_of(off * C + r0, 32), 32), :] = (
                    hw[j, r0 : r0 + 32, :].astype(f32) * factor
                ).astype(bf16)
            return carry

        lax.fori_loop(0, TAPS, tap, 0)
        ex[...] = jnp.zeros_like(ex)
        each = mk[:, j, :] * bias
        both = bias + row(mb, j)
        each_high = each.astype(bf16).astype(f32)
        both_high = both.astype(bf16).astype(f32)
        ex[0:9, :] = each_high
        ex[16:17, :] = both_high
        ex[32:41, :] = each - each_high
        ex[48:49, :] = both - both_high
        wc[j, TAPS * C :, :] = ex[...].astype(bf16)

    def mlp_forward(j):
        build_wc(j)

        def first(ts):
            xhat, scale = norm_parts(xs[ts, :])
            xh_m[j, ts, :] = xhat
            sc[j, ts, 1:2] = scale
            u = (xhat * row(ng, j, 3) + row(ns, j, 3)).astype(bf16).astype(f32)
            acc[0, ts, :] = u * valid[ts, :]

        tiles(first)
        for i in range(n):
            span = slice(i * TOK, (i + 1) * TOK)
            for off, piece in taps_of(acc[0, span, :]):
                u_all[j, span, off * C : (off + 1) * C] = piece.astype(bf16)

        for start in range(0, FF, CHUNK):
            cols = slice(start, start + CHUNK)
            for i in range(n):
                field = nn(u_all[j, i * TOK : (i + 1) * TOK, :], wc[j, :, cols])
                for r0 in range(0, TOK, 16):
                    act, slope = gelu_parts(field[r0 : r0 + 16])
                    part = slice(i * TOK + r0, i * TOK + r0 + 16)
                    a_all[j, part, cols] = act.astype(bf16)
                    g_all[j, part, cols] = slope.astype(bf16)
        for i in range(n):
            span = slice(i * TOK, (i + 1) * TOK)
            branch = nn(a_all[j, span, :], ow[j]) + row(ob, j)
            xs[span, :] = (xs[span, :] + scaled(span, 2 * j + 1) * branch).astype(bf16).astype(f32)

    def mlp_backward(j):
        sb = j * S_BLOCK

        def first(ts):
            grad = (xs[ts, :] * scaled(ts, 2 * j + 1)).astype(bf16)
            db[ts, :] = grad
            return [folded(grad.astype(f32))]

        (small[sb + S_OB : sb + S_OB + 1, :],) = tiles(first)
        db_t[j] = db[...].T
        for start in range(0, FF, CHUNK):
            cols = slice(start, start + CHUNK)
            for i in range(n):
                span = slice(i * TOK, (i + 1) * TOK)
                da = nt(db[span, :], ow[j, cols, :])
                g_all[j, span, cols] = (da * g_all[j, span, cols].astype(f32)).astype(bf16)
        if j == 0:
            move((0, 2))
        acc[...] = jnp.zeros_like(acc)
        for first_off in range(0, TAPS, 2):
            width = min(2, TAPS - first_off)
            for i in range(n):
                at = i * TOK
                moved = nt(
                    g_all[j, at : at + TOK, :], wc[j, first_off * C : (first_off + width) * C, :]
                )
                for s in range(width):
                    off = first_off + s
                    by = (off // 3 - 1) * GRID
                    piece = moved[:, s * C : (s + 1) * C]
                    if by >= 0:
                        acc[off % 3, at + by : at + TOK, :] += piece[: TOK - by]
                    else:
                        acc[off % 3, at : at + TOK + by, :] += piece[-by:]
        if j == 0:
            move((1, 1))
        for i in range(n):
            span = slice(i * TOK, (i + 1) * TOK)
            left = pltpu.roll(jnp.where(col > 0, acc[0, span, :], 0.0), TOK - 1, 0)
            right = pltpu.roll(jnp.where(col < GRID - 1, acc[2, span, :], 0.0), 1, 0)
            acc[1, span, :] = (acc[1, span, :] + left + right) * valid[span, :]

        def last(ts):
            du = acc[1, ts, :]
            xhat = xh_m[j, ts, :]
            back = norm_back(du, xhat, sc[j, ts, 1:2], row(ng, j, 3))
            xs[ts, :] = (xs[ts, :] + back).astype(bf16).astype(f32)
            return [folded(du * xhat), folded(du)]

        gain, shift = tiles(last)
        small[sb + S_GAIN + 3 : sb + S_GAIN + 4, :] = gain
        small[sb + S_SHIFT + 3 : sb + S_SHIFT + 4, :] = shift
        if j == 0:
            move((0, 3))

    def mlp_turn(j):
        for off in range(TAPS + 1):
            ut[off * C : (off + 1) * C, :] = u_all[j, :, off * C : (off + 1) * C].T

    def mlp_weights(j, step):
        base, sb = MLP_AT[j], j * S_BLOCK
        cols = slice(step * CHUNK, (step + 1) * CHUNK)
        dow = nn(db_t[j], a_all[j, :, cols])
        at = base + output_row(step)
        gp[at : at + CHUNK, :] = dow.T.astype(bf16)
        cross = nn(ut[...], g_all[j, :, cols])
        flag_rows = cross[TAPS * C : TAPS * C + 24]
        total = flag_rows[16:17]
        dhb = total
        weight = hw[j, :, cols].astype(f32)
        dweight = jnp.zeros((C, CHUNK), f32)
        b = hb[j : j + 1, cols]
        for off in range(TAPS):
            piece = cross[off * C : (off + 1) * C]
            factor = mk[off, j : j + 1, cols]
            flag = flag_rows[off : off + 1]
            dweight = dweight + piece * (factor + (1.0 if off == 4 else 0.0))
            dk = col_sum(piece * weight) + b * flag
            dhb = dhb + factor * flag
            for s in range(CHUNK // C):
                at = sb + S_MK + 16 * (step * (CHUNK // C) + s) + off
                small[at : at + 1, :] = dk[:, s * C : (s + 1) * C]
        for s in range(CHUNK // C):
            tile = step * (CHUNK // C) + s
            part = slice(s * C, (s + 1) * C)
            small[sb + S_HB + tile : sb + S_HB + tile + 1, :] = dhb[:, part]
            small[sb + S_MB + tile : sb + S_MB + tile + 1, :] = total[:, part]
            at = base + hidden_row(tile)
            gp[at : at + C, :] = dweight[:, part].astype(bf16)

    def attention_backward(j):
        base, sb = ATT_AT[j], j * S_BLOCK

        def first(ts):
            grad = (xs[ts, :] * scaled(ts, 2 * j)).astype(bf16)
            db[ts, :] = grad
            return [folded(grad.astype(f32))]

        (small[sb + S_PB : sb + S_PB + 1, :],) = tiles(first)
        dproj = jnp.zeros((C, C), f32)
        kernel = jnp.concatenate([lk[j, :, 0, :], lk[j, :, 1, :]], axis=1)
        dkernel = [jnp.zeros((1, C), f32) for _ in range(9)]
        dbias = jnp.zeros((1, C), f32)
        for i in range(n):
            span = slice(i * TOK, (i + 1) * TOK)
            dproj = dproj + nn(o_t[j, i], db[span, :])
            do = nt(db[span, :], pw[j]).astype(bf16)
            dprobs = nt(vbd[j, i], do)
            dvals = nn(pt[j, i], do)
            for low, top in SEGS:
                for c0 in range(0, TOK, 128):
                    c1 = min(c0 + 128, TOK)
                    weight = pt[j, i, low:top, c0:c1].astype(f32)
                    dweight = dprobs[low:top, c0:c1]
                    dot = jnp.sum(weight * dweight, axis=0, keepdims=True)
                    pt[j, i, low:top, c0:c1] = (weight * (dweight - dot)).astype(bf16)
            dkeys = nn(pt[j, i], q_a[j, span, :]) * ROOT
            dq = tn(kb[j, i], pt[j, i]) * ROOT
            o_n[span, :] = dq.T.astype(bf16)
            for t in range(2):
                dk = jnp.zeros((CELLS[t], C), f32)
                dv = jnp.zeros((CELLS[t], C), f32)
                for h in (2 * t, 2 * t + 1):
                    dk = dk + jnp.where(head_lanes(h), dkeys[slice(*SEGS[h])], 0.0)
                    dv = dv + jnp.where(head_lanes(h), dvals[slice(*SEGS[h])], 0.0)
                w = wv[j, cell_spans(t)[i], :]
                dw = dv
                for off in range(9):
                    by = near_shift(t, off)
                    part = dv * near[off, place_span[t], :]
                    moved = pltpu.roll(w, (CELLS[t] - by) % CELLS[t], 0) if by else w
                    dkernel[off] = dkernel[off] + col_sum(part * moved)
                    part = part * kernel[off : off + 1]
                    dw = dw + (pltpu.roll(part, by, 0) if by else part)
                dw = dw * kmask[i, place_span[t], :]
                dbias = dbias + col_sum(dw)
                if t == 0:
                    dkeyval = dk + pltpu.roll(dw, 64, 1)
                else:
                    dkeyval = pltpu.roll(dk, 64, 1) + dw
                wv[j, cell_spans(t)[i], :] = dkeyval
        gp[base + R_PROJ : base + R_PROJ + C, :] = dproj.astype(bf16)
        small[sb + S_VB : sb + S_VB + 1, :] = dbias
        for off in range(9):
            small[sb + S_LK + off : sb + S_LK + off + 1, :] = dkernel[off]
        base_perm = 0
        for t, (ref, weight) in enumerate(((p4, p4w), (p2, p2w))):
            span = cells_all(t)
            dkeyval = wv[j, span, :].astype(bf16)
            at = base + R_KV + t * C
            gp[at : at + C, :] = tn(kin[j, span, :], dkeyval).astype(bf16)
            dy = nt(dkeyval, kvw[j, t]) * ge_p[j, span, :]
            xhat = xh_p[j, span, :]
            small[sb + S_GAIN + 1 + t : sb + S_GAIN + 2 + t, :] = col_sum(dy * xhat)
            small[sb + S_SHIFT + 1 + t : sb + S_SHIFT + 2 + t, :] = col_sum(dy)
            dpool = norm_back(dy, xhat, sc_p[j, span, :], row(ng, j, 1 + t)).astype(bf16)
            at = base + (R_P4, R_P2)[t]
            for k in range(STRIDES[t] ** 2):
                gp[at + k * C : at + (k + 1) * C, :] = tn(
                    ref[j, :, k * C : (k + 1) * C], dpool
                ).astype(bf16)
                back = nt(dpool, weight[j, k * C : (k + 1) * C, :]).astype(bf16)
                for i in range(n):
                    pc[base_perm : base_perm + CELLS[t], i * C : (i + 1) * C] = back[
                        i * CELLS[t] : (i + 1) * CELLS[t]
                    ]
                base_perm += CELLS[t]
        at = base + R_Q
        gp[at : at + C, :] = tn(u_a[j], o_n[...]).astype(bf16)
        if j == 1:
            all_here()
            move((0, 0))
        else:
            move((2, 0), (0, 4), (1, 2))
        spread = nn(perm_t[...], pc[...])
        for i in range(n):
            span = slice(i * TOK, (i + 1) * TOK)
            back = nt(o_n[span, :], qw[j])
            acc[0, span, :] = back + spread[:, i * C : (i + 1) * C] * valid[span, :]

        def last(ts):
            du = acc[0, ts, :]
            xhat = xh_a[j, ts, :]
            back = norm_back(du, xhat, sc[j, ts, 0:1], row(ng, j, 0))
            xs[ts, :] = (xs[ts, :] + back).astype(bf16).astype(f32)
            return [folded(o_n[ts, :].astype(f32)), folded(du * xhat), folded(du)]

        bias, gain, shift = tiles(last)
        small[sb + S_QB : sb + S_QB + 1, :] = bias
        small[sb + S_GAIN : sb + S_GAIN + 1, :] = gain
        small[sb + S_SHIFT : sb + S_SHIFT + 1, :] = shift

    for j in range(BLOCKS):
        attention_forward(j)
        if j == 0:
            late[0].wait()
            late[1].wait()
        mlp_forward(j)
    out_st[...] = xs[...].astype(bf16)
    leave(out_st, out_ref)
    late[2].wait()
    late[3].wait()
    xs[...] = cot_ref[...].astype(f32)
    mlp_backward(1)
    attention_backward(1)
    mlp_turn(1)
    move((0, 1))
    mlp_weights(1, 0)
    mlp_weights(1, 1)
    move((1, 0))
    mlp_backward(0)
    attention_backward(0)
    dx_st[...] = xs[...].astype(bf16)
    leave(dx_st, dx_ref)
    mlp_turn(0)
    move((2, 1))
    mlp_weights(0, 0)
    move((3, 0), (1, 3), (0, 5))
    mlp_weights(0, 1)
    gp[R_SMALL:, :] = small[...].astype(bf16)
    move((4, 0), (3, 1), (2, 2), (1, 4), (0, 6))
    move((4, 1), (2, 3), (1, 5), (3, 2), (2, 4), (4, 2), (1, 6), (3, 3))
    move((2, 5), (4, 3), (3, 4), (2, 6), (4, 4))
    for piece in pieces:
        piece.drain()
    for made in leaving:
        made.wait()


def compute(own, images, grid_size, keep_mask, x, cot, weights):
    segments, pairs = lax.axis_size("segment"), lax.axis_size("dp") // 2
    inner = min(pairs, 4)
    sizes = (segments, inner, pairs // inner)
    n = images
    rows = n * TOK
    cells = n * sum(CELLS)
    vmem = pl.BlockSpec(memory_space=pltpu.VMEM)
    smem = pl.BlockSpec(memory_space=pltpu.SMEM)
    matrix = permutation()
    consts = (
        jnp.asarray(matrix, bf16),
        jnp.asarray(matrix.T, bf16),
        jnp.asarray(cell_places()),
    )
    B = BLOCKS
    scratch = [
        pltpu.VMEM((rows, C), f32),
        pltpu.VMEM((rows, C), f32),
        pltpu.VMEM((TOK, n * C), bf16),
        pltpu.VMEM((B, rows, UW), bf16),
        pltpu.VMEM((UW, rows), bf16),
        pltpu.VMEM((B, UW, FF), bf16),
        pltpu.VMEM((C, FF), f32),
        pltpu.VMEM((B, rows, C), f32),
        pltpu.VMEM((B, rows, C), f32),
        pltpu.VMEM((B, rows, C), f32),
        pltpu.VMEM((B, rows, C), bf16),
        pltpu.VMEM((B, rows, C), bf16),
        pltpu.VMEM((B, n * CELLS[0], 16 * C), bf16),
        pltpu.VMEM((B, n * CELLS[1], 4 * C), bf16),
        pltpu.VMEM((B, cells, C), f32),
        pltpu.VMEM((B, cells, C), f32),
        pltpu.VMEM((B, cells, C), f32),
        pltpu.VMEM((B, cells, C), bf16),
        pltpu.VMEM((B, cells, C), f32),
        pltpu.VMEM((B, n, KEYS, C), bf16),
        pltpu.VMEM((B, n, KEYS, C), bf16),
        pltpu.VMEM((B, n, KEYS, TOK), bf16),
        pltpu.VMEM((B, n, C, TOK), bf16),
        pltpu.VMEM((rows, C), bf16),
        pltpu.VMEM((B, rows, FF), bf16),
        pltpu.VMEM((B, rows, FF), bf16),
        pltpu.VMEM((rows, C), bf16),
        pltpu.VMEM((B, C, rows), bf16),
        pltpu.VMEM((3, rows, C), f32),
        pltpu.VMEM((n, sum(CELLS), C), f32),
        pltpu.VMEM((9, sum(CELLS), C), f32),
        pltpu.VMEM((ROWS - R_SMALL, C), f32),
        pltpu.VMEM((PERM, n * C), bf16),
        pltpu.SMEM((n, 2 * BLOCKS), f32),
        pltpu.VMEM(cot.shape, bf16),
        pltpu.VMEM(weights[HW].shape, bf16),
        pltpu.VMEM(weights[OW].shape, bf16),
        pltpu.VMEM((TOK, PERM), bf16),
        pltpu.VMEM((rows, C), bf16),
        pltpu.VMEM((rows, C), bf16),
        pltpu.SemaphoreType.DMA((6 + len(PIECES),)),
        pltpu.VMEM((ROWS, C), bf16),
    ] + sum_scratch(sizes)
    anywhere = pl.BlockSpec(memory_space=pl.ANY)
    operands = [vmem] * (2 + len(weights) + len(consts))
    for place in (1, 2 + HW, 2 + OW, 2 + len(weights) + 1):
        operands[place] = anywhere
    return pl.pallas_call(
        functools.partial(compute_kernel, own, images, sizes),
        out_shape=(
            jax.ShapeDtypeStruct((rows, C), bf16),
            jax.ShapeDtypeStruct((rows, C), bf16),
            jax.ShapeDtypeStruct((ROWS, C), bf16),
        ),
        in_specs=[smem, smem] + operands,
        out_specs=(anywhere,) * 3,
        scratch_shapes=scratch,
        compiler_params=pltpu.CompilerParams(
            collective_id=0, has_side_effects=True, vmem_limit_bytes=63 * 2**20
        ),
        name="compute",
    )(grid_size, keep_mask, x, cot, *weights, *consts)


def unpack_kernel(gp, out_in, dx_in, *refs):
    out_ref, dx_ref = refs[:2]
    gain, shift, qw, qb, p4, p2, kvw, vb, lk, pw, pb, hw, hb, mk, mb, ow, ob = refs[2:]
    out_ref[...] = out_in[...]
    dx_ref[...] = dx_in[...]
    for j in range(BLOCKS):
        att, mlp, sb = ATT_AT[j], MLP_AT[j], R_SMALL + j * S_BLOCK
        p4[j] = gp[att + R_P4 : att + R_P2, :].astype(f32)
        p2[j] = gp[att + R_P2 : att + R_KV, :].astype(f32)
        for t in range(2):
            kvw[j, t] = gp[att + R_KV + t * C : att + R_KV + (t + 1) * C, :].astype(f32)
        qw[j] = gp[att + R_Q : att + R_PROJ, :].astype(f32)
        pw[j] = gp[att + R_PROJ : att + R_ATT, :].astype(f32)
        for s in range(FF // C):
            at = mlp + hidden_row(s)
            hw[j, :, s * C : (s + 1) * C] = gp[at : at + C, :].astype(f32)
        for step in range(FF // CHUNK):
            at = mlp + output_row(step)
            ow[j, step * CHUNK : (step + 1) * CHUNK, :] = gp[at : at + CHUNK, :].astype(f32)
        head = gp[sb : sb + 48, :].astype(f32)
        gain[j] = head[S_GAIN : S_GAIN + 4]
        shift[j] = head[S_SHIFT : S_SHIFT + 4]
        qb[j : j + 1, :] = head[S_QB : S_QB + 1]
        vb[j, 0:1, :] = head[S_VB : S_VB + 1, 0:64]
        vb[j, 1:2, :] = head[S_VB : S_VB + 1, 64:128]
        pb[j : j + 1, :] = head[S_PB : S_PB + 1]
        ob[j : j + 1, :] = head[S_OB : S_OB + 1]
        lk[j, :, 0, :] = head[S_LK : S_LK + 9, 0:64]
        lk[j, :, 1, :] = head[S_LK : S_LK + 9, 64:128]
        for s in range(FF // C):
            part = slice(s * C, (s + 1) * C)
            hb[j : j + 1, part] = head[S_HB + s : S_HB + s + 1]
            mb[j : j + 1, part] = head[S_MB + s : S_MB + s + 1]
            at = sb + S_MK + 16 * s
            mk[:, j, part] = gp[at : at + 16, :].astype(f32)[0:9]


def unpack(packed, outputs, input_grad, weights):
    vmem = pl.BlockSpec(memory_space=pltpu.VMEM)
    streams = (jax.ShapeDtypeStruct(outputs.shape, bf16),) * 2
    return pl.pallas_call(
        unpack_kernel,
        out_shape=streams + tuple(jax.ShapeDtypeStruct(w.shape, f32) for w in weights),
        in_specs=[vmem] * 3,
        out_specs=(vmem,) * (2 + len(weights)),
        compiler_params=pltpu.CompilerParams(vmem_limit_bytes=63 * 2**20),
        name="unpack",
    )(packed, outputs, input_grad)


def on_device(inputs, grid_size, keep_mask, cotangent, *weights):
    own, per = inputs.shape[:2]
    images = own * per
    flat = (images * TOK, C)
    turned = list(weights)
    turned[LK] = jnp.transpose(turned[LK], (0, 2, 1, 3))
    turned[MK] = jnp.transpose(turned[MK], (1, 0, 2))
    outputs, input_grad, packed = compute(
        own,
        images,
        jnp.transpose(grid_size, (1, 2, 0)),
        jnp.transpose(keep_mask, (1, 2, 0)),
        inputs.reshape(flat),
        cotangent.reshape(flat),
        turned,
    )
    outputs, input_grad, *grads = unpack(packed, outputs, input_grad, turned)
    grads[LK] = jnp.transpose(grads[LK], (0, 2, 1, 3))
    grads[MK] = jnp.transpose(grads[MK], (1, 0, 2))
    return (outputs.reshape(inputs.shape), input_grad.reshape(inputs.shape)) + tuple(grads)


def solution(mesh):
    stream = P("segment", "dp", None, None)
    picked = P(None, "dp", None)
    return jax.shard_map(
        on_device,
        mesh=mesh,
        in_specs=(stream, picked, picked, stream) + (P(),) * 17,
        out_specs=(stream, stream) + (P(),) * 17,
        check_vma=False,
    )
```

```python
import functools

import jax
import jax.numpy as jnp
import numpy as np
from jax import lax
from jax.experimental import pallas as pl
from jax.experimental.pallas import tpu as pltpu
from jax.sharding import PartitionSpec as P

GRID = 24
TOK = GRID * GRID
C = 128
FF = 1024
HEAD = 32
BLOCKS = 2
SIDES = (6, 12)
STRIDES = (4, 2)
CELLS = (48, 144)
SEGS = ((0, 48), (48, 96), (96, 240), (240, 384))
KEYS = 384
PERM = 16 * 48 + 4 * 144
TAPS = 9
UW = TAPS * C + C
CHUNK = 512
TILE = 96

R_P4, R_P2, R_KV, R_Q, R_PROJ, R_ATT = 0, 2048, 2560, 2816, 2944, 3072
R_MLP = 2048
ATT_AT = (R_ATT, 0)
MLP_AT = (2 * R_ATT + R_MLP, 2 * R_ATT)
S_GAIN, S_SHIFT, S_QB, S_VB, S_PB, S_OB, S_LK, S_HB, S_MB, S_MK, S_BLOCK = (
    0,
    4,
    8,
    9,
    10,
    11,
    16,
    32,
    40,
    48,
    192,
)
R_SMALL = BLOCKS * (R_ATT + R_MLP)
ROWS = R_SMALL + 512
PIECES = (
    (ATT_AT[1], R_ATT),
    (ATT_AT[0], R_ATT),
    (MLP_AT[1], R_MLP),
    (MLP_AT[0], R_MLP // 2),
    (MLP_AT[0] + R_MLP // 2, R_MLP // 2 + ROWS - R_SMALL),
)

LK, HW, MK, OW = 8, 11, 13, 15

epsilon = 1e-06
keep_rate = 0.8
ROOT = HEAD**-0.5
LOG2E = 1.4426950408889634
f32, bf16 = jnp.float32, jnp.bfloat16


def hidden_row(tile):
    return tile // (CHUNK // C) * 2 * CHUNK + tile % (CHUNK // C) * C


def output_row(step):
    return step * 2 * CHUNK + CHUNK


def patch_tokens():
    tokens = np.full((8, PERM), -1.0, np.float32)
    base = 0
    for stride, side, cells in zip(STRIDES, SIDES, CELLS):
        for row_off in range(stride):
            for col_off in range(stride):
                for a in range(side):
                    for b in range(side):
                        token = (a * stride + row_off) * GRID + b * stride + col_off
                        tokens[:, base + a * side + b] = token
                base += cells
    return tokens


def cell_places():
    places = np.full((2, sum(CELLS), 128), 99.0, np.float32)
    base = 0
    for side, cells in zip(SIDES, CELLS):
        for a in range(side):
            for b in range(side):
                places[0, base + a * side + b] = a
                places[1, base + a * side + b] = b
        base += cells
    return places


def nn(left, right):
    return jnp.dot(left, right, preferred_element_type=f32)


def nt(left, right):
    return lax.dot_general(left, right, (((1,), (1,)), ((), ())), preferred_element_type=f32)


def tn(left, right):
    return lax.dot_general(left, right, (((0,), (0,)), ((), ())), preferred_element_type=f32)


def gelu_parts(m):
    size = jnp.abs(m)
    t = pl.reciprocal(1.0 + (0.3275911 * 0.5**0.5) * size, approx=True)
    e = jnp.exp2(m * (m * (-0.5 * LOG2E)))
    poly = 0.5 * 1.061405429
    for coef in (-1.453152027, 1.421413741, -0.284496736, 0.254829592):
        poly = poly * t + 0.5 * coef
    poly = poly * t
    tail = poly * e
    slope = (poly - size * 0.3989422804014327) * e
    return jnp.maximum(m, 0.0) - size * tail, jnp.where(m >= 0, 1.0 - slope, slope)


def norm_parts(x):
    centred = x - jnp.mean(x, axis=-1, keepdims=True)
    scale = lax.rsqrt(jnp.mean(centred * centred, axis=-1, keepdims=True) + epsilon)
    return centred * scale, scale


def norm_back(du, xhat, scale, gain):
    dxhat = du * gain
    first = jnp.mean(dxhat, axis=-1, keepdims=True)
    second = jnp.mean(dxhat * xhat, axis=-1, keepdims=True)
    return scale * (dxhat - first - xhat * second)


def col_sum(x):
    return jnp.sum(x, axis=0, keepdims=True)


def folded(x):
    return jnp.sum(x.reshape(-1, 8, x.shape[-1]), axis=0)


class Summed:
    STEPS = 7

    def __init__(self, place, piece, base, count, refs):
        self.seg, self.dp, self.segments, self.inner, self.outer = place
        self.piece, self.base = piece, base
        (
            self.src,
            self.half_in,
            self.quarter_in,
            self.part_in,
            self.whole_in,
            self.own,
            self.total,
            self.send,
            self.recv,
        ) = refs
        self.core, rest = self.dp % 2, self.dp // 2
        self.part, self.group = rest % self.inner, rest // self.inner
        self.half = count // 2
        self.quarter = self.half // self.segments
        self.share = self.quarter // self.inner
        quarters, shares = (self.segments - 1) * self.quarter, (self.inner - 1) * self.share
        self.moved = (self.half, quarters, shares, shares, quarters, self.half)
        self.at_quarter = self.seg * self.quarter
        self.at_share = self.at_quarter + self.part * self.share

    def span(self, start, size):
        return pl.ds(pl.multiple_of(start, 16), size)

    def device(self, seg=None, core=None, part=None, group=None):
        seg = self.seg if seg is None else seg
        core = self.core if core is None else core
        part = self.part if part is None else part
        group = self.group if group is None else group
        return (seg, (group * self.inner + part) * 2 + core)

    def copy(self, k, src, dst, device):
        return pltpu.make_async_remote_copy(
            src_ref=src,
            dst_ref=dst,
            send_sem=self.send.at[self.piece],
            recv_sem=self.recv.at[self.piece, k],
            device_id=device,
            device_id_type=pl.DeviceIdType.MESH,
        )

    def counted(self, k, count):
        ref = self.total.at[pl.ds(0, count), :]
        return self.copy(k, ref, ref, self.device(core=1 - self.core))

    def step(self, k):
        if k > 0:
            self.counted(k - 1, self.moved[k - 1]).wait_recv()
            self.gather(k)
        if k + 1 < self.STEPS:
            self.depart(k)

    def drain(self):
        count = sum(self.moved) + (self.outer - 1) * self.share
        self.counted(0, count).wait_send()

    def depart(self, k):
        half = self.base // 2
        mine = self.base + self.core * self.half
        if k == 0:
            src = self.src.at[self.span(self.base + (1 - self.core) * self.half, self.half), :]
            dst = self.half_in.at[self.span(half, self.half), :]
            self.copy(k, src, dst, self.device(core=1 - self.core)).start()
        elif k == 1:
            at = self.span(half // self.segments, self.quarter)
            for d in range(1, self.segments):
                to = self.seg ^ d
                src = self.own.at[self.span(half + to * self.quarter, self.quarter), :]
                dst = self.quarter_in.at[d - 1, at, :]
                self.copy(k, src, dst, self.device(seg=to)).start()
        elif k == 2:
            at = self.span(self.share_in(), self.share)
            for d in range(1, self.inner):
                to = self.part ^ d
                start = half + self.at_quarter + to * self.share
                src = self.own.at[self.span(start, self.share), :]
                self.copy(k, src, self.part_in.at[d - 1, at, :], self.device(part=to)).start()
        elif k == 3:
            ref = self.total.at[self.span(mine + self.at_share, self.share), :]
            for d in range(1, self.inner):
                self.copy(k, ref, ref, self.device(part=self.part ^ d)).start()
        elif k == 4:
            ref = self.total.at[self.span(mine + self.at_quarter, self.quarter), :]
            for d in range(1, self.segments):
                self.copy(k, ref, ref, self.device(seg=self.seg ^ d)).start()
        else:
            ref = self.total.at[self.span(mine, self.half), :]
            self.copy(k, ref, ref, self.device(core=1 - self.core)).start()

    def share_in(self):
        return self.base // 2 // self.segments // self.inner

    def gather(self, k):
        half = self.base // 2
        if k == 1:
            first = (self.src, self.base + self.core * self.half)
            self.add((self.own, half), first, [(self.half_in, half)], self.half)
        elif k == 2:
            mine = (self.own, half + self.at_quarter)
            at = half // self.segments
            received = [(self.quarter_in.at[d], at) for d in range(self.segments - 1)]
            self.add(mine, mine, received, self.quarter)
        elif k == 3:
            received = [(self.part_in.at[d], self.share_in()) for d in range(self.inner - 1)]
            mine = (self.own, half + self.at_share)
            into = (self.total, self.base + self.core * self.half + self.at_share)
            if self.outer > 1:
                self.add(mine, mine, received, self.share)
                slot = self.STEPS - 1
                src = self.own.at[self.span(mine[1], self.share), :]
                at = self.span(self.share_in(), self.share)
                for d in range(1, self.outer):
                    to = self.device(group=self.group ^ d)
                    self.copy(slot, src, self.whole_in.at[d - 1, at, :], to).start()
                self.counted(slot, (self.outer - 1) * self.share).wait_recv()
                received = [(self.whole_in.at[d], self.share_in()) for d in range(self.outer - 1)]
            self.add(into, mine, received, self.share)

    def add(self, dst, first, others, count):
        step = next(size for size in (128, 96, 80, 64, 48, 32, 16) if count % size == 0)

        def body(t, carry):
            at = t * step
            total = first[0][self.span(first[1] + at, step), :].astype(f32)
            for ref, start in others:
                total = total + ref[self.span(start + at, step), :].astype(f32)
            dst[0][self.span(dst[1] + at, step), :] = total.astype(bf16)
            return carry

        lax.fori_loop(0, count // step, body, 0)


def greet(seg, dp, segments, inner, outer):
    barrier = pltpu.get_barrier_semaphore()
    core, part, group = dp % 2, dp // 2 % inner, dp // 2 // inner
    peers = [(seg, dp + 1 - 2 * core)]
    peers += [(seg ^ d, dp) for d in range(1, segments)]
    peers += [(seg, (group * inner + (part ^ d)) * 2 + core) for d in range(1, inner)]
    peers += [(seg, ((group ^ d) * inner + part) * 2 + core) for d in range(1, outer)]
    for peer in peers:
        pl.semaphore_signal(
            barrier, inc=1, device_id=peer, device_id_type=pl.DeviceIdType.MESH
        )
    return lambda: pl.semaphore_wait(barrier, len(peers))


def sum_scratch(sizes):
    segments, inner, outer = sizes
    quarter = ROWS // 2 // segments
    share = quarter // inner
    return [
        pltpu.VMEM((ROWS // 2, C), bf16),
        pltpu.VMEM((segments - 1, quarter, C), bf16),
        pltpu.VMEM((inner - 1, share, C), bf16),
        pltpu.VMEM((max(outer - 1, 1), share, C), bf16),
        pltpu.VMEM((ROWS // 2, C), bf16),
        pltpu.VMEM((ROWS, C), bf16),
        pltpu.SemaphoreType.DMA((len(PIECES),)),
        pltpu.SemaphoreType.DMA((len(PIECES), Summed.STEPS)),
    ]


def compute_kernel(
    own,
    images,
    sizes,
    grid_ref,
    keep_ref,
    x_ref,
    cot_in,
    ng,
    ns,
    qw,
    qb,
    p4w,
    p2w,
    kvw,
    vb,
    lk,
    pw,
    pb,
    hw_in,
    hb,
    mk,
    mb,
    ow_in,
    ob,
    tokens,
    places,
    out_ref,
    dx_ref,
    summed_ref,
    xs,
    valid,
    um,
    u_all,
    ut,
    wc,
    ex,
    xh_a,
    xh_m,
    sc,
    u_a,
    q_a,
    p4,
    p2,
    xh_p,
    sc_p,
    ge_p,
    kin,
    wv,
    kb,
    vbd,
    pt,
    o_t,
    o_n,
    a_all,
    g_all,
    db,
    db_t,
    acc,
    kmask,
    near,
    small,
    pc,
    scale_ref,
    cot_ref,
    hw,
    ow,
    perm,
    perm_t,
    out_st,
    dx_st,
    sems,
    gp,
    half_in,
    quarter_in,
    part_in,
    whole_in,
    own_part,
    total_ref,
    send,
    recv,
):
    n = images
    rows = n * TOK
    seg, dp = lax.axis_index("segment"), lax.axis_index("dp")
    all_here = greet(seg, dp, *sizes)
    late = [
        pltpu.make_async_copy(src, dst, sems.at[k])
        for k, (src, dst) in enumerate(
            ((hw_in, hw), (ow_in, ow), (cot_in, cot_ref))
        )
    ]
    for made in late:
        made.start()
    leaving = []

    def leave(src, dst):
        made = pltpu.make_async_copy(src, dst, sems.at[len(late) + len(leaving)])
        made.start()
        leaving.append(made)

    refs = (
        gp,
        half_in,
        quarter_in,
        part_in,
        whole_in,
        own_part,
        total_ref,
        send,
        recv,
    )
    pieces = [
        Summed((seg, dp) + sizes, p, base, count, refs) for p, (base, count) in enumerate(PIECES)
    ]

    def move(*steps):
        for p, k in steps:
            pieces[p].step(k)
            if k + 1 == Summed.STEPS:
                rows_of = pl.ds(PIECES[p][0], PIECES[p][1])
                leave(total_ref.at[rows_of, :], summed_ref.at[rows_of, :])

    lane = lax.broadcasted_iota(jnp.int32, (8, 128), 1)[0:1]

    def head_lanes(h):
        return (lane >= h * HEAD) & (lane < (h + 1) * HEAD)

    def tiles(fn, step=TILE):
        sums = None
        for start in range(0, rows, step):
            got = fn(slice(start, start + step))
            if got is not None:
                sums = got if sums is None else [x + y for x, y in zip(sums, got)]
        return None if sums is None else [col_sum(x) for x in sums]

    def row(ref, j, k=None):
        return ref[j, pl.ds(k, 1), :] if k is not None else ref[pl.ds(j, 1), :]

    def shifted_rows(v, by):
        if by == 0:
            return v
        pad = jnp.zeros((abs(by), v.shape[1]), v.dtype)
        if by > 0:
            return jnp.concatenate([v[by:], pad], axis=0)
        return jnp.concatenate([pad, v[:by]], axis=0)

    col = lax.broadcasted_iota(jnp.int32, (GRID, GRID, 128), 1).reshape(TOK, 128)

    def taps_of(v):
        left = jnp.where(col > 0, pltpu.roll(v, 1, 0), 0.0)
        right = jnp.where(col < GRID - 1, pltpu.roll(v, TOK - 1, 0), 0.0)
        for row_off in range(3):
            for col_off, piece in enumerate((left, v, right)):
                yield row_off * 3 + col_off, shifted_rows(piece, (row_off - 1) * GRID)

    small[...] = jnp.zeros_like(small)
    sizes = []
    lane_row = lax.broadcasted_iota(jnp.int32, (TOK, 128), 1)
    for i in range(n):
        m_id, d_id = seg * own + i // (n // own), i % (n // own)
        high, wide = grid_ref[d_id, 0, m_id], grid_ref[d_id, 1, m_id]
        sizes.append((high, wide))
        line = lax.broadcasted_iota(jnp.int32, (GRID, GRID, 128), 0).reshape(TOK, 128)
        good = jnp.where((line < high) & (col < wide), 1.0, 0.0)
        valid[i * TOK : (i + 1) * TOK, :] = good
        for k in range(2 * BLOCKS):
            kept = keep_ref[d_id, k, m_id].astype(f32) / keep_rate
            scale_ref[i, k] = kept
        flags = jnp.where((lane_row == 16) | (lane_row == 48), 1.0, 0.0)
        for off, piece in taps_of(good):
            flags = jnp.where((lane_row == off) | (lane_row == 32 + off), piece, flags)
        for j in range(BLOCKS):
            u_all[j, i * TOK : (i + 1) * TOK, TAPS * C :] = flags.astype(bf16)
        base = 0
        for t in range(2):
            span = slice(base, base + CELLS[t])
            tall = (high + STRIDES[t] - 1) // STRIDES[t]
            across = (wide + STRIDES[t] - 1) // STRIDES[t]
            inside = (places[0, span, :] < tall.astype(f32)) & (
                places[1, span, :] < across.astype(f32)
            )
            kmask[i, span, :] = jnp.where(inside, 1.0, 0.0)
            base += CELLS[t]
    base = 0
    for t in range(2):
        span = slice(base, base + CELLS[t])
        a, b = places[0, span, :], places[1, span, :]
        for off in range(9):
            dr, dc = float(off // 3 - 1), float(off % 3 - 1)
            top = float(SIDES[t])
            ok = (a + dr >= 0) & (a + dr < top) & (b + dc >= 0) & (b + dc < top)
            near[off, span, :] = jnp.where(ok, 1.0, 0.0)
        base += CELLS[t]

    base = start = 0
    for t in range(2):
        span, stride = slice(start, start + CELLS[t]), STRIDES[t]
        corner = places[0, span, :] * float(stride * GRID) + places[1, span, :] * float(stride)
        for k in range(stride * stride):
            token = corner + float(k // stride * GRID + k % stride)
            for c0 in range(0, TOK, 128):
                width = min(128, TOK - c0)
                here = lax.broadcasted_iota(jnp.int32, (CELLS[t], width), 1).astype(f32) + float(c0)
                block = jnp.where(token[:, :width] == here, 1.0, 0.0)
                perm[base : base + CELLS[t], c0 : c0 + width] = block.astype(bf16)
            base += CELLS[t]
        start += CELLS[t]
    for r0 in range(0, TOK, TILE):
        here = lax.broadcasted_iota(jnp.int32, (TILE, PERM), 0).astype(f32) + float(r0)
        block = jnp.where(tokens[0:1, :] == here, 1.0, 0.0)
        perm_t[r0 : r0 + TILE, :] = block.astype(bf16)

    xs[...] = x_ref[...].astype(f32)

    def scaled(span, k):
        return valid[span, :] * scale_ref[span.start // TOK, k]

    def cell_spans(t):
        start = 0 if t == 0 else n * CELLS[0]
        return [slice(start + i * CELLS[t], start + (i + 1) * CELLS[t]) for i in range(n)]

    def cells_all(t):
        return slice(0, n * CELLS[0]) if t == 0 else slice(n * CELLS[0], n * sum(CELLS))

    place_span = (slice(0, CELLS[0]), slice(CELLS[0], sum(CELLS)))
    half = lane < 64
    own_half = (half, jnp.logical_not(half))

    def near_shift(t, off):
        return ((off // 3 - 1) * SIDES[t] + off % 3 - 1) % CELLS[t]

    def attention_forward(j):
        def first(ts):
            xhat, scale = norm_parts(xs[ts, :])
            xh_a[j, ts, :] = xhat
            sc[j, ts, 0:1] = scale
            u_a[j, ts, :] = (xhat * row(ng, j, 0) + row(ns, j, 0)).astype(bf16)

        tiles(first)
        for i in range(n):
            span = slice(i * TOK, (i + 1) * TOK)
            u = u_a[j, span, :]
            q_a[j, span, :] = (nn(u, qw[j]) + row(qb, j)).astype(bf16)
            um[:, i * C : (i + 1) * C] = (u.astype(f32) * valid[span, :]).astype(bf16)
        pc[...] = nn(perm[...], um[...]).astype(bf16)
        base = 0
        for t, ref in enumerate((p4, p2)):
            for k in range(STRIDES[t] ** 2):
                for i in range(n):
                    ref[j, i * CELLS[t] : (i + 1) * CELLS[t], k * C : (k + 1) * C] = pc[
                        base : base + CELLS[t], i * C : (i + 1) * C
                    ]
                base += CELLS[t]
        for t, (ref, weight) in enumerate(((p4, p4w), (p2, p2w))):
            xhat, scale = norm_parts(nn(ref[j], weight[j]))
            act, slope = gelu_parts(xhat * row(ng, j, 1 + t) + row(ns, j, 1 + t))
            act = act.astype(bf16)
            span = cells_all(t)
            xh_p[j, span, :] = xhat
            sc_p[j, span, :] = jnp.broadcast_to(scale, xhat.shape)
            ge_p[j, span, :] = slope
            kin[j, span, :] = act
            keyval = nn(act, kvw[j, t])
            turned = pltpu.roll(keyval, 64, 1)
            keys, vals = (keyval, turned) if t == 0 else (turned, keyval)
            bias = jnp.concatenate([row(vb, j, 0), row(vb, j, 1)], axis=1)
            kernel = jnp.concatenate([lk[j, :, 0, :], lk[j, :, 1, :]], axis=1)
            for i in range(n):
                part = slice(i * CELLS[t], (i + 1) * CELLS[t])
                w = (vals[part] + bias) * kmask[i, place_span[t], :]
                wv[j, cell_spans(t)[i], :] = w
                v = w
                for off in range(9):
                    by = near_shift(t, off)
                    moved = pltpu.roll(w, (CELLS[t] - by) % CELLS[t], 0) if by else w
                    v = v + moved * (near[off, place_span[t], :] * kernel[off : off + 1])
                for h in (2 * t, 2 * t + 1):
                    seg_rows = slice(*SEGS[h])
                    kb[j, i, seg_rows, :] = jnp.where(head_lanes(h), keys[part], 0.0).astype(bf16)
                    vbd[j, i, seg_rows, :] = jnp.where(head_lanes(h), v, 0.0).astype(bf16)
        for i in range(n):
            span = slice(i * TOK, (i + 1) * TOK)
            scores = nt(kb[j, i], q_a[j, span, :])
            for h, (low, top) in enumerate(SEGS):
                mask = kmask[i, place_span[h // 2], 0:1] > 0
                for c0 in range(0, TOK, 128):
                    c1 = min(c0 + 128, TOK)
                    s = jnp.where(mask, scores[low:top, c0:c1], -1e30)
                    e = jnp.exp2((s - jnp.max(s, axis=0, keepdims=True)) * (ROOT * LOG2E))
                    weight = e * pl.reciprocal(jnp.sum(e, axis=0, keepdims=True), approx=True)
                    pt[j, i, low:top, c0:c1] = weight.astype(bf16)
            mixed = tn(vbd[j, i], pt[j, i])
            o_t[j, i] = mixed.astype(bf16)
            o_n[span, :] = mixed.T.astype(bf16)
        for i in range(n):
            span = slice(i * TOK, (i + 1) * TOK)
            branch = nn(o_n[span, :], pw[j]) + row(pb, j)
            xs[span, :] = (xs[span, :] + scaled(span, 2 * j) * branch).astype(bf16).astype(f32)

    def build_wc(j):
        bias = row(hb, j)

        def tap(off, carry):
            factor = mk[off, j : j + 1, :] + jnp.where(off == 4, 1.0, 0.0)
            for r0 in range(0, C, 32):
                wc[j, pl.ds(pl.multiple_of(off * C + r0, 32), 32), :] = (
                    hw[j, r0 : r0 + 32, :].astype(f32) * factor
                ).astype(bf16)
            return carry

        lax.fori_loop(0, TAPS, tap, 0)
        ex[...] = jnp.zeros_like(ex)
        each = mk[:, j, :] * bias
        both = bias + row(mb, j)
        each_high = each.astype(bf16).astype(f32)
        both_high = both.astype(bf16).astype(f32)
        ex[0:9, :] = each_high
        ex[16:17, :] = both_high
        ex[32:41, :] = each - each_high
        ex[48:49, :] = both - both_high
        wc[j, TAPS * C :, :] = ex[...].astype(bf16)

    def mlp_forward(j):
        build_wc(j)

        def first(ts):
            xhat, scale = norm_parts(xs[ts, :])
            xh_m[j, ts, :] = xhat
            sc[j, ts, 1:2] = scale
            u = (xhat * row(ng, j, 3) + row(ns, j, 3)).astype(bf16).astype(f32)
            acc[0, ts, :] = u * valid[ts, :]

        tiles(first)
        for i in range(n):
            span = slice(i * TOK, (i + 1) * TOK)
            for off, piece in taps_of(acc[0, span, :]):
                u_all[j, span, off * C : (off + 1) * C] = piece.astype(bf16)

        for start in range(0, FF, CHUNK):
            cols = slice(start, start + CHUNK)
            for i in range(n):
                field = nn(u_all[j, i * TOK : (i + 1) * TOK, :], wc[j, :, cols])
                for r0 in range(0, TOK, 16):
                    act, slope = gelu_parts(field[r0 : r0 + 16])
                    part = slice(i * TOK + r0, i * TOK + r0 + 16)
                    a_all[j, part, cols] = act.astype(bf16)
                    g_all[j, part, cols] = slope.astype(bf16)
        for i in range(n):
            span = slice(i * TOK, (i + 1) * TOK)
            branch = nn(a_all[j, span, :], ow[j]) + row(ob, j)
            xs[span, :] = (xs[span, :] + scaled(span, 2 * j + 1) * branch).astype(bf16).astype(f32)

    def mlp_backward(j):
        sb = j * S_BLOCK

        def first(ts):
            grad = (xs[ts, :] * scaled(ts, 2 * j + 1)).astype(bf16)
            db[ts, :] = grad
            return [folded(grad.astype(f32))]

        (small[sb + S_OB : sb + S_OB + 1, :],) = tiles(first)
        db_t[j] = db[...].T
        for start in range(0, FF, CHUNK):
            cols = slice(start, start + CHUNK)
            for i in range(n):
                span = slice(i * TOK, (i + 1) * TOK)
                da = nt(db[span, :], ow[j, cols, :])
                g_all[j, span, cols] = (da * g_all[j, span, cols].astype(f32)).astype(bf16)
        if j == 0:
            move((0, 1))
        acc[...] = jnp.zeros_like(acc)
        for first_off in range(0, TAPS, 2):
            width = min(2, TAPS - first_off)
            for i in range(n):
                at = i * TOK
                moved = nt(
                    g_all[j, at : at + TOK, :], wc[j, first_off * C : (first_off + width) * C, :]
                )
                for s in range(width):
                    off = first_off + s
                    by = (off // 3 - 1) * GRID
                    piece = moved[:, s * C : (s + 1) * C]
                    if by >= 0:
                        acc[off % 3, at + by : at + TOK, :] += piece[: TOK - by]
                    else:
                        acc[off % 3, at : at + TOK + by, :] += piece[-by:]
        for i in range(n):
            span = slice(i * TOK, (i + 1) * TOK)
            left = pltpu.roll(jnp.where(col > 0, acc[0, span, :], 0.0), TOK - 1, 0)
            right = pltpu.roll(jnp.where(col < GRID - 1, acc[2, span, :], 0.0), 1, 0)
            acc[1, span, :] = (acc[1, span, :] + left + right) * valid[span, :]

        def last(ts):
            du = acc[1, ts, :]
            xhat = xh_m[j, ts, :]
            back = norm_back(du, xhat, sc[j, ts, 1:2], row(ng, j, 3))
            xs[ts, :] = (xs[ts, :] + back).astype(bf16).astype(f32)
            return [folded(du * xhat), folded(du)]

        gain, shift = tiles(last)
        small[sb + S_GAIN + 3 : sb + S_GAIN + 4, :] = gain
        small[sb + S_SHIFT + 3 : sb + S_SHIFT + 4, :] = shift

    def mlp_turn(j):
        for off in range(TAPS + 1):
            ut[off * C : (off + 1) * C, :] = u_all[j, :, off * C : (off + 1) * C].T

    def mlp_weights(j, step):
        base, sb = MLP_AT[j], j * S_BLOCK
        cols = slice(step * CHUNK, (step + 1) * CHUNK)
        dow = nn(db_t[j], a_all[j, :, cols])
        at = base + output_row(step)
        gp[at : at + CHUNK, :] = dow.T.astype(bf16)
        cross = nn(ut[...], g_all[j, :, cols])
        flag_rows = cross[TAPS * C : TAPS * C + 24]
        total = flag_rows[16:17]
        dhb = total
        weight = hw[j, :, cols].astype(f32)
        dweight = jnp.zeros((C, CHUNK), f32)
        b = hb[j : j + 1, cols]
        for off in range(TAPS):
            piece = cross[off * C : (off + 1) * C]
            factor = mk[off, j : j + 1, cols]
            flag = flag_rows[off : off + 1]
            dweight = dweight + piece * (factor + (1.0 if off == 4 else 0.0))
            dk = col_sum(piece * weight) + b * flag
            dhb = dhb + factor * flag
            for s in range(CHUNK // C):
                at = sb + S_MK + 16 * (step * (CHUNK // C) + s) + off
                small[at : at + 1, :] = dk[:, s * C : (s + 1) * C]
        for s in range(CHUNK // C):
            tile = step * (CHUNK // C) + s
            part = slice(s * C, (s + 1) * C)
            small[sb + S_HB + tile : sb + S_HB + tile + 1, :] = dhb[:, part]
            small[sb + S_MB + tile : sb + S_MB + tile + 1, :] = total[:, part]
            at = base + hidden_row(tile)
            gp[at : at + C, :] = dweight[:, part].astype(bf16)

    def attention_backward(j):
        base, sb = ATT_AT[j], j * S_BLOCK

        def first(ts):
            grad = (xs[ts, :] * scaled(ts, 2 * j)).astype(bf16)
            db[ts, :] = grad
            return [folded(grad.astype(f32))]

        (small[sb + S_PB : sb + S_PB + 1, :],) = tiles(first)
        dproj = jnp.zeros((C, C), f32)
        kernel = jnp.concatenate([lk[j, :, 0, :], lk[j, :, 1, :]], axis=1)
        dkernel = [jnp.zeros((1, C), f32) for _ in range(9)]
        dbias = jnp.zeros((1, C), f32)
        for i in range(n):
            span = slice(i * TOK, (i + 1) * TOK)
            dproj = dproj + nn(o_t[j, i], db[span, :])
            do = nt(db[span, :], pw[j]).astype(bf16)
            dprobs = nt(vbd[j, i], do)
            dvals = nn(pt[j, i], do)
            for low, top in SEGS:
                for c0 in range(0, TOK, 128):
                    c1 = min(c0 + 128, TOK)
                    weight = pt[j, i, low:top, c0:c1].astype(f32)
                    dweight = dprobs[low:top, c0:c1]
                    dot = jnp.sum(weight * dweight, axis=0, keepdims=True)
                    pt[j, i, low:top, c0:c1] = (weight * (dweight - dot)).astype(bf16)
            dkeys = nn(pt[j, i], q_a[j, span, :]) * ROOT
            dq = tn(kb[j, i], pt[j, i]) * ROOT
            o_n[span, :] = dq.T.astype(bf16)
            for t in range(2):
                dk = jnp.zeros((CELLS[t], C), f32)
                dv = jnp.zeros((CELLS[t], C), f32)
                for h in (2 * t, 2 * t + 1):
                    dk = dk + jnp.where(head_lanes(h), dkeys[slice(*SEGS[h])], 0.0)
                    dv = dv + jnp.where(head_lanes(h), dvals[slice(*SEGS[h])], 0.0)
                w = wv[j, cell_spans(t)[i], :]
                dw = dv
                for off in range(9):
                    by = near_shift(t, off)
                    part = dv * near[off, place_span[t], :]
                    moved = pltpu.roll(w, (CELLS[t] - by) % CELLS[t], 0) if by else w
                    dkernel[off] = dkernel[off] + col_sum(part * moved)
                    part = part * kernel[off : off + 1]
                    dw = dw + (pltpu.roll(part, by, 0) if by else part)
                dw = dw * kmask[i, place_span[t], :]
                dbias = dbias + col_sum(dw)
                if t == 0:
                    dkeyval = dk + pltpu.roll(dw, 64, 1)
                else:
                    dkeyval = pltpu.roll(dk, 64, 1) + dw
                wv[j, cell_spans(t)[i], :] = dkeyval
        gp[base + R_PROJ : base + R_PROJ + C, :] = dproj.astype(bf16)
        small[sb + S_VB : sb + S_VB + 1, :] = dbias
        for off in range(9):
            small[sb + S_LK + off : sb + S_LK + off + 1, :] = dkernel[off]
        base_perm = 0
        for t, (ref, weight) in enumerate(((p4, p4w), (p2, p2w))):
            span = cells_all(t)
            dkeyval = wv[j, span, :].astype(bf16)
            at = base + R_KV + t * C
            gp[at : at + C, :] = tn(kin[j, span, :], dkeyval).astype(bf16)
            dy = nt(dkeyval, kvw[j, t]) * ge_p[j, span, :]
            xhat = xh_p[j, span, :]
            small[sb + S_GAIN + 1 + t : sb + S_GAIN + 2 + t, :] = col_sum(dy * xhat)
            small[sb + S_SHIFT + 1 + t : sb + S_SHIFT + 2 + t, :] = col_sum(dy)
            dpool = norm_back(dy, xhat, sc_p[j, span, :], row(ng, j, 1 + t)).astype(bf16)
            at = base + (R_P4, R_P2)[t]
            for k in range(STRIDES[t] ** 2):
                gp[at + k * C : at + (k + 1) * C, :] = tn(
                    ref[j, :, k * C : (k + 1) * C], dpool
                ).astype(bf16)
                back = nt(dpool, weight[j, k * C : (k + 1) * C, :]).astype(bf16)
                for i in range(n):
                    pc[base_perm : base_perm + CELLS[t], i * C : (i + 1) * C] = back[
                        i * CELLS[t] : (i + 1) * CELLS[t]
                    ]
                base_perm += CELLS[t]
        at = base + R_Q
        gp[at : at + C, :] = tn(u_a[j], o_n[...]).astype(bf16)
        if j == 1:
            all_here()
            move((0, 0))
        else:
            move((0, 2), (1, 0))
        spread = nn(perm_t[...], pc[...])
        for i in range(n):
            span = slice(i * TOK, (i + 1) * TOK)
            back = nt(o_n[span, :], qw[j])
            acc[0, span, :] = back + spread[:, i * C : (i + 1) * C] * valid[span, :]

        def last(ts):
            du = acc[0, ts, :]
            xhat = xh_a[j, ts, :]
            back = norm_back(du, xhat, sc[j, ts, 0:1], row(ng, j, 0))
            xs[ts, :] = (xs[ts, :] + back).astype(bf16).astype(f32)
            return [folded(o_n[ts, :].astype(f32)), folded(du * xhat), folded(du)]

        bias, gain, shift = tiles(last)
        small[sb + S_QB : sb + S_QB + 1, :] = bias
        small[sb + S_GAIN : sb + S_GAIN + 1, :] = gain
        small[sb + S_SHIFT : sb + S_SHIFT + 1, :] = shift

    for j in range(BLOCKS):
        attention_forward(j)
        if j == 0:
            late[0].wait()
            late[1].wait()
        mlp_forward(j)
    out_st[...] = xs[...].astype(bf16)
    leave(out_st, out_ref)
    late[2].wait()
    xs[...] = cot_ref[...].astype(f32)
    mlp_backward(1)
    attention_backward(1)
    mlp_backward(0)
    attention_backward(0)
    dx_st[...] = xs[...].astype(bf16)
    leave(dx_st, dx_ref)
    mlp_turn(1)
    move((1, 1))
    mlp_weights(1, 0)
    move((0, 3))
    mlp_weights(1, 1)
    move((2, 0))
    mlp_turn(0)
    move((1, 2), (2, 1), (0, 4))
    mlp_weights(0, 0)
    move((3, 0))
    mlp_weights(0, 1)
    gp[R_SMALL:, :] = small[...].astype(bf16)
    move((4, 0), (1, 3), (3, 1), (2, 2), (4, 1))
    move((0, 5), (3, 2), (1, 4), (0, 6), (2, 3), (4, 2), (3, 3), (2, 4), (4, 3), (1, 5), (3, 4))
    move((1, 6), (4, 4), (2, 5), (3, 5), (2, 6), (3, 6), (4, 5), (4, 6))
    for piece in pieces:
        piece.drain()
    for made in leaving:
        made.wait()


def compute(own, images, grid_size, keep_mask, x, cot, weights):
    segments, pairs = lax.axis_size("segment"), lax.axis_size("dp") // 2
    inner = min(pairs, 4)
    sizes = (segments, inner, pairs // inner)
    n = images
    rows = n * TOK
    cells = n * sum(CELLS)
    vmem = pl.BlockSpec(memory_space=pltpu.VMEM)
    smem = pl.BlockSpec(memory_space=pltpu.SMEM)
    consts = (jnp.asarray(patch_tokens()), jnp.asarray(cell_places()))
    B = BLOCKS
    scratch = [
        pltpu.VMEM((rows, C), f32),
        pltpu.VMEM((rows, C), f32),
        pltpu.VMEM((TOK, n * C), bf16),
        pltpu.VMEM((B, rows, UW), bf16),
        pltpu.VMEM((UW, rows), bf16),
        pltpu.VMEM((B, UW, FF), bf16),
        pltpu.VMEM((C, FF), f32),
        pltpu.VMEM((B, rows, C), f32),
        pltpu.VMEM((B, rows, C), f32),
        pltpu.VMEM((B, rows, C), f32),
        pltpu.VMEM((B, rows, C), bf16),
        pltpu.VMEM((B, rows, C), bf16),
        pltpu.VMEM((B, n * CELLS[0], 16 * C), bf16),
        pltpu.VMEM((B, n * CELLS[1], 4 * C), bf16),
        pltpu.VMEM((B, cells, C), f32),
        pltpu.VMEM((B, cells, C), f32),
        pltpu.VMEM((B, cells, C), f32),
        pltpu.VMEM((B, cells, C), bf16),
        pltpu.VMEM((B, cells, C), f32),
        pltpu.VMEM((B, n, KEYS, C), bf16),
        pltpu.VMEM((B, n, KEYS, C), bf16),
        pltpu.VMEM((B, n, KEYS, TOK), bf16),
        pltpu.VMEM((B, n, C, TOK), bf16),
        pltpu.VMEM((rows, C), bf16),
        pltpu.VMEM((B, rows, FF), bf16),
        pltpu.VMEM((B, rows, FF), bf16),
        pltpu.VMEM((rows, C), bf16),
        pltpu.VMEM((B, C, rows), bf16),
        pltpu.VMEM((3, rows, C), f32),
        pltpu.VMEM((n, sum(CELLS), C), f32),
        pltpu.VMEM((9, sum(CELLS), C), f32),
        pltpu.VMEM((ROWS - R_SMALL, C), f32),
        pltpu.VMEM((PERM, n * C), bf16),
        pltpu.SMEM((n, 2 * BLOCKS), f32),
        pltpu.VMEM(cot.shape, bf16),
        pltpu.VMEM(weights[HW].shape, bf16),
        pltpu.VMEM(weights[OW].shape, bf16),
        pltpu.VMEM((PERM, TOK), bf16),
        pltpu.VMEM((TOK, PERM), bf16),
        pltpu.VMEM((rows, C), bf16),
        pltpu.VMEM((rows, C), bf16),
        pltpu.SemaphoreType.DMA((5 + len(PIECES),)),
        pltpu.VMEM((ROWS, C), bf16),
    ] + sum_scratch(sizes)
    anywhere = pl.BlockSpec(memory_space=pl.ANY)
    operands = [vmem] * (2 + len(weights) + len(consts))
    for place in (1, 2 + HW, 2 + OW):
        operands[place] = anywhere
    return pl.pallas_call(
        functools.partial(compute_kernel, own, images, sizes),
        out_shape=(
            jax.ShapeDtypeStruct((rows, C), bf16),
            jax.ShapeDtypeStruct((rows, C), bf16),
            jax.ShapeDtypeStruct((ROWS, C), bf16),
        ),
        in_specs=[smem, smem] + operands,
        out_specs=(anywhere,) * 3,
        scratch_shapes=scratch,
        compiler_params=pltpu.CompilerParams(
            collective_id=0, has_side_effects=True, vmem_limit_bytes=63 * 2**20
        ),
        name="compute",
    )(grid_size, keep_mask, x, cot, *weights, *consts)


def unpack_kernel(gp, out_in, dx_in, *refs):
    out_ref, dx_ref = refs[:2]
    gain, shift, qw, qb, p4, p2, kvw, vb, lk, pw, pb, hw, hb, mk, mb, ow, ob = refs[2:]
    out_ref[...] = out_in[...]
    dx_ref[...] = dx_in[...]
    for j in range(BLOCKS):
        att, mlp, sb = ATT_AT[j], MLP_AT[j], R_SMALL + j * S_BLOCK
        p4[j] = gp[att + R_P4 : att + R_P2, :].astype(f32)
        p2[j] = gp[att + R_P2 : att + R_KV, :].astype(f32)
        for t in range(2):
            kvw[j, t] = gp[att + R_KV + t * C : att + R_KV + (t + 1) * C, :].astype(f32)
        qw[j] = gp[att + R_Q : att + R_PROJ, :].astype(f32)
        pw[j] = gp[att + R_PROJ : att + R_ATT, :].astype(f32)
        for s in range(FF // C):
            at = mlp + hidden_row(s)
            hw[j, :, s * C : (s + 1) * C] = gp[at : at + C, :].astype(f32)
        for step in range(FF // CHUNK):
            at = mlp + output_row(step)
            ow[j, step * CHUNK : (step + 1) * CHUNK, :] = gp[at : at + CHUNK, :].astype(f32)
        head = gp[sb : sb + 48, :].astype(f32)
        gain[j] = head[S_GAIN : S_GAIN + 4]
        shift[j] = head[S_SHIFT : S_SHIFT + 4]
        qb[j : j + 1, :] = head[S_QB : S_QB + 1]
        vb[j, 0:1, :] = head[S_VB : S_VB + 1, 0:64]
        vb[j, 1:2, :] = head[S_VB : S_VB + 1, 64:128]
        pb[j : j + 1, :] = head[S_PB : S_PB + 1]
        ob[j : j + 1, :] = head[S_OB : S_OB + 1]
        lk[j, :, 0, :] = head[S_LK : S_LK + 9, 0:64]
        lk[j, :, 1, :] = head[S_LK : S_LK + 9, 64:128]
        for s in range(FF // C):
            part = slice(s * C, (s + 1) * C)
            hb[j : j + 1, part] = head[S_HB + s : S_HB + s + 1]
            mb[j : j + 1, part] = head[S_MB + s : S_MB + s + 1]
            at = sb + S_MK + 16 * s
            mk[:, j, part] = gp[at : at + 16, :].astype(f32)[0:9]


def unpack(packed, outputs, input_grad, weights):
    vmem = pl.BlockSpec(memory_space=pltpu.VMEM)
    streams = (jax.ShapeDtypeStruct(outputs.shape, bf16),) * 2
    return pl.pallas_call(
        unpack_kernel,
        out_shape=streams + tuple(jax.ShapeDtypeStruct(w.shape, f32) for w in weights),
        in_specs=[vmem] * 3,
        out_specs=(vmem,) * (2 + len(weights)),
        compiler_params=pltpu.CompilerParams(vmem_limit_bytes=63 * 2**20),
        name="unpack",
    )(packed, outputs, input_grad)


def on_device(inputs, grid_size, keep_mask, cotangent, *weights):
    own, per = inputs.shape[:2]
    images = own * per
    flat = (images * TOK, C)
    turned = list(weights)
    turned[LK] = jnp.transpose(turned[LK], (0, 2, 1, 3))
    turned[MK] = jnp.transpose(turned[MK], (1, 0, 2))
    outputs, input_grad, packed = compute(
        own,
        images,
        jnp.transpose(grid_size, (1, 2, 0)),
        jnp.transpose(keep_mask, (1, 2, 0)),
        inputs.reshape(flat),
        cotangent.reshape(flat),
        turned,
    )
    outputs, input_grad, *grads = unpack(packed, outputs, input_grad, turned)
    grads[LK] = jnp.transpose(grads[LK], (0, 2, 1, 3))
    grads[MK] = jnp.transpose(grads[MK], (1, 0, 2))
    return (outputs.reshape(inputs.shape), input_grad.reshape(inputs.shape)) + tuple(grads)


def solution(mesh):
    stream = P("segment", "dp", None, None)
    picked = P(None, "dp", None)
    return jax.shard_map(
        on_device,
        mesh=mesh,
        in_specs=(stream, picked, picked, stream) + (P(),) * 17,
        out_specs=(stream, stream) + (P(),) * 17,
        check_vma=False,
    )
```

```python
import functools

import jax
import jax.numpy as jnp
import numpy as np
from jax import lax
from jax.experimental import pallas as pl
from jax.experimental.pallas import tpu as pltpu
from jax.sharding import PartitionSpec as P

GRID = 24
TOK = GRID * GRID
C = 128
FF = 1024
HEAD = 32
BLOCKS = 2
SIDES = (6, 12)
STRIDES = (4, 2)
CELLS = (48, 144)
SEGS = ((0, 48), (48, 96), (96, 240), (240, 384))
KEYS = 384
PERM = 16 * 48 + 4 * 144
TAPS = 9
UW = TAPS * C + C
CHUNK = 512
TILE = 96

R_P4, R_P2, R_KV, R_Q, R_PROJ, R_ATT = 0, 2048, 2560, 2816, 2944, 3072
R_MLP = 2048
ATT_AT = (R_ATT, 0)
MLP_AT = (2 * R_ATT + R_MLP, 2 * R_ATT)
S_GAIN, S_SHIFT, S_QB, S_VB, S_PB, S_OB, S_LK, S_HB, S_MB, S_MK, S_BLOCK = (
    0,
    4,
    8,
    9,
    10,
    11,
    16,
    32,
    40,
    48,
    192,
)
R_SMALL = BLOCKS * (R_ATT + R_MLP)
ROWS = R_SMALL + 512
PIECES = (
    (ATT_AT[1], R_ATT),
    (ATT_AT[0], R_ATT),
    (MLP_AT[1], R_MLP),
    (MLP_AT[0], R_MLP // 2),
    (MLP_AT[0] + R_MLP // 2, R_MLP // 2 + ROWS - R_SMALL),
)

QW, P4, P2, KVW, LK, PW, HW, MK, OW = 2, 4, 5, 6, 8, 9, 11, 13, 15

epsilon = 1e-06
keep_rate = 0.8
ROOT = HEAD**-0.5
LOG2E = 1.4426950408889634
f32, bf16 = jnp.float32, jnp.bfloat16


def hidden_row(tile):
    return tile // (CHUNK // C) * 2 * CHUNK + tile % (CHUNK // C) * C


def output_row(step):
    return step * 2 * CHUNK + CHUNK


def patch_tokens():
    tokens = np.full((8, PERM), -1.0, np.float32)
    base = 0
    for stride, side, cells in zip(STRIDES, SIDES, CELLS):
        for row_off in range(stride):
            for col_off in range(stride):
                for a in range(side):
                    for b in range(side):
                        token = (a * stride + row_off) * GRID + b * stride + col_off
                        tokens[:, base + a * side + b] = token
                base += cells
    return tokens


def cell_places():
    places = np.full((2, sum(CELLS), 128), 99.0, np.float32)
    base = 0
    for side, cells in zip(SIDES, CELLS):
        for a in range(side):
            for b in range(side):
                places[0, base + a * side + b] = a
                places[1, base + a * side + b] = b
        base += cells
    return places


def nn(left, right):
    return jnp.dot(left, right, preferred_element_type=f32)


def nt(left, right):
    return lax.dot_general(left, right, (((1,), (1,)), ((), ())), preferred_element_type=f32)


def tn(left, right):
    return lax.dot_general(left, right, (((0,), (0,)), ((), ())), preferred_element_type=f32)


def gelu_parts(m):
    size = jnp.abs(m)
    t = pl.reciprocal(1.0 + (0.3275911 * 0.5**0.5) * size, approx=True)
    e = jnp.exp2(m * (m * (-0.5 * LOG2E)))
    poly = 0.5 * 1.061405429
    for coef in (-1.453152027, 1.421413741, -0.284496736, 0.254829592):
        poly = poly * t + 0.5 * coef
    poly = poly * t
    tail = poly * e
    slope = (poly - size * 0.3989422804014327) * e
    return jnp.maximum(m, 0.0) - size * tail, jnp.where(m >= 0, 1.0 - slope, slope)


def norm_parts(x):
    centred = x - jnp.mean(x, axis=-1, keepdims=True)
    scale = lax.rsqrt(jnp.mean(centred * centred, axis=-1, keepdims=True) + epsilon)
    return centred * scale, scale


def norm_back(du, xhat, scale, gain):
    dxhat = du * gain
    first = jnp.mean(dxhat, axis=-1, keepdims=True)
    second = jnp.mean(dxhat * xhat, axis=-1, keepdims=True)
    return scale * (dxhat - first - xhat * second)


def col_sum(x):
    return jnp.sum(x, axis=0, keepdims=True)


def folded(x):
    return jnp.sum(x.reshape(-1, 8, x.shape[-1]), axis=0)


class Summed:
    STEPS = 7

    def __init__(self, place, piece, base, count, refs):
        self.seg, self.dp, self.segments, self.inner, self.outer = place
        self.piece, self.base = piece, base
        (
            self.src,
            self.half_in,
            self.quarter_in,
            self.part_in,
            self.whole_in,
            self.own,
            self.total,
            self.send,
            self.recv,
        ) = refs
        self.core, rest = self.dp % 2, self.dp // 2
        self.part, self.group = rest % self.inner, rest // self.inner
        self.half = count // 2
        self.quarter = self.half // self.segments
        self.share = self.quarter // self.inner
        quarters, shares = (self.segments - 1) * self.quarter, (self.inner - 1) * self.share
        self.moved = (self.half, quarters, shares, shares, quarters, self.half)
        self.at_quarter = self.seg * self.quarter
        self.at_share = self.at_quarter + self.part * self.share

    def span(self, start, size):
        return pl.ds(pl.multiple_of(start, 16), size)

    def device(self, seg=None, core=None, part=None, group=None):
        seg = self.seg if seg is None else seg
        core = self.core if core is None else core
        part = self.part if part is None else part
        group = self.group if group is None else group
        return (seg, (group * self.inner + part) * 2 + core)

    def copy(self, k, src, dst, device):
        return pltpu.make_async_remote_copy(
            src_ref=src,
            dst_ref=dst,
            send_sem=self.send.at[self.piece],
            recv_sem=self.recv.at[self.piece, k],
            device_id=device,
            device_id_type=pl.DeviceIdType.MESH,
        )

    def counted(self, k, count):
        ref = self.total.at[pl.ds(0, count), :]
        return self.copy(k, ref, ref, self.device(core=1 - self.core))

    def step(self, k):
        if k > 0:
            self.counted(k - 1, self.moved[k - 1]).wait_recv()
            self.gather(k)
        if k + 1 < self.STEPS:
            self.depart(k)

    def drain(self):
        count = sum(self.moved) + (self.outer - 1) * self.share
        self.counted(0, count).wait_send()

    def depart(self, k):
        half = self.base // 2
        mine = self.base + self.core * self.half
        if k == 0:
            src = self.src.at[self.span(self.base + (1 - self.core) * self.half, self.half), :]
            dst = self.half_in.at[self.span(half, self.half), :]
            self.copy(k, src, dst, self.device(core=1 - self.core)).start()
        elif k == 1:
            at = self.span(half // self.segments, self.quarter)
            for d in range(1, self.segments):
                to = self.seg ^ d
                src = self.own.at[self.span(half + to * self.quarter, self.quarter), :]
                dst = self.quarter_in.at[d - 1, at, :]
                self.copy(k, src, dst, self.device(seg=to)).start()
        elif k == 2:
            at = self.span(self.share_in(), self.share)
            for d in range(1, self.inner):
                to = self.part ^ d
                start = half + self.at_quarter + to * self.share
                src = self.own.at[self.span(start, self.share), :]
                self.copy(k, src, self.part_in.at[d - 1, at, :], self.device(part=to)).start()
        elif k == 3:
            ref = self.total.at[self.span(mine + self.at_share, self.share), :]
            for d in range(1, self.inner):
                self.copy(k, ref, ref, self.device(part=self.part ^ d)).start()
        elif k == 4:
            ref = self.total.at[self.span(mine + self.at_quarter, self.quarter), :]
            for d in range(1, self.segments):
                self.copy(k, ref, ref, self.device(seg=self.seg ^ d)).start()
        else:
            ref = self.total.at[self.span(mine, self.half), :]
            self.copy(k, ref, ref, self.device(core=1 - self.core)).start()

    def share_in(self):
        return self.base // 2 // self.segments // self.inner

    def gather(self, k):
        half = self.base // 2
        if k == 1:
            first = (self.src, self.base + self.core * self.half)
            self.add((self.own, half), first, [(self.half_in, half)], self.half)
        elif k == 2:
            mine = (self.own, half + self.at_quarter)
            at = half // self.segments
            received = [(self.quarter_in.at[d], at) for d in range(self.segments - 1)]
            self.add(mine, mine, received, self.quarter)
        elif k == 3:
            received = [(self.part_in.at[d], self.share_in()) for d in range(self.inner - 1)]
            mine = (self.own, half + self.at_share)
            into = (self.total, self.base + self.core * self.half + self.at_share)
            if self.outer > 1:
                self.add(mine, mine, received, self.share)
                slot = self.STEPS - 1
                src = self.own.at[self.span(mine[1], self.share), :]
                at = self.span(self.share_in(), self.share)
                for d in range(1, self.outer):
                    to = self.device(group=self.group ^ d)
                    self.copy(slot, src, self.whole_in.at[d - 1, at, :], to).start()
                self.counted(slot, (self.outer - 1) * self.share).wait_recv()
                received = [(self.whole_in.at[d], self.share_in()) for d in range(self.outer - 1)]
            self.add(into, mine, received, self.share)

    def add(self, dst, first, others, count):
        step = next(size for size in (128, 96, 80, 64, 48, 32, 16) if count % size == 0)

        def body(t, carry):
            at = t * step
            total = first[0][self.span(first[1] + at, step), :].astype(f32)
            for ref, start in others:
                total = total + ref[self.span(start + at, step), :].astype(f32)
            dst[0][self.span(dst[1] + at, step), :] = total.astype(bf16)
            return carry

        lax.fori_loop(0, count // step, body, 0)


def greet(seg, dp, segments, inner, outer):
    barrier = pltpu.get_barrier_semaphore()
    core, part, group = dp % 2, dp // 2 % inner, dp // 2 // inner
    peers = [(seg, dp + 1 - 2 * core)]
    peers += [(seg ^ d, dp) for d in range(1, segments)]
    peers += [(seg, (group * inner + (part ^ d)) * 2 + core) for d in range(1, inner)]
    peers += [(seg, ((group ^ d) * inner + part) * 2 + core) for d in range(1, outer)]
    for peer in peers:
        pl.semaphore_signal(
            barrier, inc=1, device_id=peer, device_id_type=pl.DeviceIdType.MESH
        )
    return lambda: pl.semaphore_wait(barrier, len(peers))


def sum_scratch(sizes):
    segments, inner, outer = sizes
    quarter = ROWS // 2 // segments
    share = quarter // inner
    return [
        pltpu.VMEM((ROWS // 2, C), bf16),
        pltpu.VMEM((segments - 1, quarter, C), bf16),
        pltpu.VMEM((inner - 1, share, C), bf16),
        pltpu.VMEM((max(outer - 1, 1), share, C), bf16),
        pltpu.VMEM((ROWS // 2, C), bf16),
        pltpu.VMEM((ROWS, C), bf16),
        pltpu.SemaphoreType.DMA((len(PIECES),)),
        pltpu.SemaphoreType.DMA((len(PIECES), Summed.STEPS)),
    ]


def compute_kernel(
    own,
    images,
    sizes,
    grid_ref,
    keep_ref,
    x_ref,
    cot_in,
    ng,
    ns,
    qw,
    qb,
    p4w,
    p2w,
    kvw,
    vb,
    lk,
    pw,
    pb,
    hw,
    hb,
    mk,
    mb,
    ow,
    ob,
    tokens,
    places,
    out_ref,
    dx_ref,
    summed_ref,
    xs,
    valid,
    um,
    u_all,
    ut,
    wc,
    ex,
    xh_a,
    xh_m,
    sc,
    u_a,
    q_a,
    p4,
    p2,
    xh_p,
    sc_p,
    ge_p,
    kin,
    wv,
    kb,
    vbd,
    pt,
    o_t,
    o_n,
    a_all,
    g_all,
    db,
    db_t,
    acc,
    kmask,
    near,
    small,
    pc,
    scale_ref,
    cot_ref,
    perm,
    perm_t,
    out_st,
    dx_st,
    sems,
    gp,
    half_in,
    quarter_in,
    part_in,
    whole_in,
    own_part,
    total_ref,
    send,
    recv,
):
    n = images
    rows = n * TOK
    seg, dp = lax.axis_index("segment"), lax.axis_index("dp")
    all_here = greet(seg, dp, *sizes)
    late = pltpu.make_async_copy(cot_in, cot_ref, sems.at[0])
    late.start()
    leaving = []

    def leave(src, dst):
        made = pltpu.make_async_copy(src, dst, sems.at[1 + len(leaving)])
        made.start()
        leaving.append(made)

    refs = (
        gp,
        half_in,
        quarter_in,
        part_in,
        whole_in,
        own_part,
        total_ref,
        send,
        recv,
    )
    pieces = [
        Summed((seg, dp) + sizes, p, base, count, refs) for p, (base, count) in enumerate(PIECES)
    ]

    def move(*steps):
        for p, k in steps:
            pieces[p].step(k)
            if k + 1 == Summed.STEPS:
                rows_of = pl.ds(PIECES[p][0], PIECES[p][1])
                leave(total_ref.at[rows_of, :], summed_ref.at[rows_of, :])

    def move_if(now, *steps):
        pl.when(now)(lambda: move(*steps))

    lane = lax.broadcasted_iota(jnp.int32, (8, 128), 1)[0:1]

    def head_lanes(h):
        return (lane >= h * HEAD) & (lane < (h + 1) * HEAD)

    def tiles(fn, step=TILE):
        sums = None
        for start in range(0, rows, step):
            got = fn(slice(start, start + step))
            if got is not None:
                sums = got if sums is None else [x + y for x, y in zip(sums, got)]
        return None if sums is None else [col_sum(x) for x in sums]

    def row(ref, j, k=None):
        return ref[j, pl.ds(k, 1), :] if k is not None else ref[pl.ds(j, 1), :]

    def put(at, value):
        small[pl.ds(at, 1), :] = value

    def packed(start, count):
        return pl.ds(pl.multiple_of(start, 128), count)

    def shifted_rows(v, by):
        if by == 0:
            return v
        pad = jnp.zeros((abs(by), v.shape[1]), v.dtype)
        if by > 0:
            return jnp.concatenate([v[by:], pad], axis=0)
        return jnp.concatenate([pad, v[:by]], axis=0)

    col = lax.broadcasted_iota(jnp.int32, (GRID, GRID, 128), 1).reshape(TOK, 128)

    def taps_of(v):
        left = jnp.where(col > 0, pltpu.roll(v, 1, 0), 0.0)
        right = jnp.where(col < GRID - 1, pltpu.roll(v, TOK - 1, 0), 0.0)
        for row_off in range(3):
            for col_off, piece in enumerate((left, v, right)):
                yield row_off * 3 + col_off, shifted_rows(piece, (row_off - 1) * GRID)

    small[...] = jnp.zeros_like(small)
    sizes = []
    lane_row = lax.broadcasted_iota(jnp.int32, (TOK, 128), 1)
    tap = lane % 32
    down, across_by = tap // 3 - 1, tap % 3 - 1
    tap_lane = (tap < TAPS) & (lane < 64)
    for i in range(n):
        m_id, d_id = seg * own + i // (n // own), i % (n // own)
        high, wide = grid_ref[d_id, 0, m_id], grid_ref[d_id, 1, m_id]
        sizes.append((high, wide))
        line = lax.broadcasted_iota(jnp.int32, (GRID, GRID, 128), 0).reshape(TOK, 128)
        good = jnp.where((line < high) & (col < wide), 1.0, 0.0)
        valid[i * TOK : (i + 1) * TOK, :] = good
        for k in range(2 * BLOCKS):
            kept = keep_ref[d_id, k, m_id].astype(f32) / keep_rate
            scale_ref[i, k] = kept
        near_row, near_col = line + down, col + across_by
        there = (near_row >= 0) & (near_row < high) & (near_col >= 0) & (near_col < wide)
        ones = (lane_row == 16) | (lane_row == 48)
        flags = jnp.where(ones | (there & tap_lane), 1.0, 0.0)
        for j in range(BLOCKS):
            u_all[j, i * TOK : (i + 1) * TOK, TAPS * C :] = flags.astype(bf16)
        base = 0
        for t in range(2):
            span = slice(base, base + CELLS[t])
            tall = (high + STRIDES[t] - 1) // STRIDES[t]
            across = (wide + STRIDES[t] - 1) // STRIDES[t]
            inside = (places[0, span, :] < tall.astype(f32)) & (
                places[1, span, :] < across.astype(f32)
            )
            kmask[i, span, :] = jnp.where(inside, 1.0, 0.0)
            base += CELLS[t]
    base = 0
    for t in range(2):
        span = slice(base, base + CELLS[t])
        a, b = places[0, span, :], places[1, span, :]
        for off in range(9):
            dr, dc = float(off // 3 - 1), float(off % 3 - 1)
            top = float(SIDES[t])
            ok = (a + dr >= 0) & (a + dr < top) & (b + dc >= 0) & (b + dc < top)
            near[off, span, :] = jnp.where(ok, 1.0, 0.0)
        base += CELLS[t]

    base = start = 0
    for t in range(2):
        span, stride = slice(start, start + CELLS[t]), STRIDES[t]
        corner = places[0, span, :] * float(stride * GRID) + places[1, span, :] * float(stride)
        for k in range(stride * stride):
            token = corner + float(k // stride * GRID + k % stride)
            for c0 in range(0, TOK, 128):
                width = min(128, TOK - c0)
                here = lax.broadcasted_iota(jnp.int32, (CELLS[t], width), 1).astype(f32) + float(c0)
                block = jnp.where(token[:, :width] == here, 1.0, 0.0)
                perm[base : base + CELLS[t], c0 : c0 + width] = block.astype(bf16)
            base += CELLS[t]
        start += CELLS[t]
    for r0 in range(0, TOK, TILE):
        here = lax.broadcasted_iota(jnp.int32, (TILE, PERM), 0).astype(f32) + float(r0)
        block = jnp.where(tokens[0:1, :] == here, 1.0, 0.0)
        perm_t[r0 : r0 + TILE, :] = block.astype(bf16)

    xs[...] = x_ref[...].astype(f32)

    def scaled(span, k):
        return valid[span, :] * scale_ref[span.start // TOK, k]

    def cell_spans(t):
        start = 0 if t == 0 else n * CELLS[0]
        return [slice(start + i * CELLS[t], start + (i + 1) * CELLS[t]) for i in range(n)]

    def cells_all(t):
        return slice(0, n * CELLS[0]) if t == 0 else slice(n * CELLS[0], n * sum(CELLS))

    place_span = (slice(0, CELLS[0]), slice(CELLS[0], sum(CELLS)))
    half = lane < 64
    own_half = (half, jnp.logical_not(half))

    def near_shift(t, off):
        return ((off // 3 - 1) * SIDES[t] + off % 3 - 1) % CELLS[t]

    def attention_forward(j):
        build_wc(j)

        def first(ts):
            xhat, scale = norm_parts(xs[ts, :])
            xh_a[j, ts, :] = xhat
            sc[j, ts, 0:1] = scale
            u_a[j, ts, :] = (xhat * row(ng, j, 0) + row(ns, j, 0)).astype(bf16)

        tiles(first)
        for i in range(n):
            span = slice(i * TOK, (i + 1) * TOK)
            u = u_a[j, span, :]
            q_a[j, span, :] = (nn(u, qw[j]) + row(qb, j)).astype(bf16)
            um[:, i * C : (i + 1) * C] = (u.astype(f32) * valid[span, :]).astype(bf16)
        pc[...] = nn(perm[...], um[...]).astype(bf16)
        base = 0
        for t, ref in enumerate((p4, p2)):
            for k in range(STRIDES[t] ** 2):
                for i in range(n):
                    ref[j, i * CELLS[t] : (i + 1) * CELLS[t], k * C : (k + 1) * C] = pc[
                        base : base + CELLS[t], i * C : (i + 1) * C
                    ]
                base += CELLS[t]
        for t, (ref, weight) in enumerate(((p4, p4w), (p2, p2w))):
            xhat, scale = norm_parts(nn(ref[j], weight[j]))
            act, slope = gelu_parts(xhat * row(ng, j, 1 + t) + row(ns, j, 1 + t))
            act = act.astype(bf16)
            span = cells_all(t)
            xh_p[j, span, :] = xhat
            sc_p[j, span, :] = jnp.broadcast_to(scale, xhat.shape)
            ge_p[j, span, :] = slope
            kin[j, span, :] = act
            keyval = nn(act, kvw[j, t])
            turned = pltpu.roll(keyval, 64, 1)
            keys, vals = (keyval, turned) if t == 0 else (turned, keyval)
            bias = jnp.concatenate([row(vb, j, 0), row(vb, j, 1)], axis=1)
            kernel = jnp.concatenate([lk[j, :, 0, :], lk[j, :, 1, :]], axis=1)
            for i in range(n):
                part = slice(i * CELLS[t], (i + 1) * CELLS[t])
                w = (vals[part] + bias) * kmask[i, place_span[t], :]
                wv[j, cell_spans(t)[i], :] = w
                v = w
                for off in range(9):
                    by = near_shift(t, off)
                    moved = pltpu.roll(w, (CELLS[t] - by) % CELLS[t], 0) if by else w
                    v = v + moved * (near[off, place_span[t], :] * kernel[off : off + 1])
                for h in (2 * t, 2 * t + 1):
                    seg_rows = slice(*SEGS[h])
                    kb[j, i, seg_rows, :] = jnp.where(head_lanes(h), keys[part], 0.0).astype(bf16)
                    vbd[j, i, seg_rows, :] = jnp.where(head_lanes(h), v, 0.0).astype(bf16)
        for i in range(n):
            span = slice(i * TOK, (i + 1) * TOK)
            scores = nt(kb[j, i], q_a[j, span, :])
            for h, (low, top) in enumerate(SEGS):
                mask = kmask[i, place_span[h // 2], 0:1] > 0
                for c0 in range(0, TOK, 128):
                    c1 = min(c0 + 128, TOK)
                    s = jnp.where(mask, scores[low:top, c0:c1], -1e30)
                    e = jnp.exp2((s - jnp.max(s, axis=0, keepdims=True)) * (ROOT * LOG2E))
                    weight = e * pl.reciprocal(jnp.sum(e, axis=0, keepdims=True), approx=True)
                    pt[j, i, low:top, c0:c1] = weight.astype(bf16)
            mixed = tn(vbd[j, i], pt[j, i])
            o_t[j, i] = mixed.astype(bf16)
            o_n[span, :] = mixed.T.astype(bf16)
        for i in range(n):
            span = slice(i * TOK, (i + 1) * TOK)
            branch = nn(o_n[span, :], pw[j]) + row(pb, j)
            xs[span, :] = (xs[span, :] + scaled(span, 2 * j) * branch).astype(bf16).astype(f32)

    def build_wc(j):
        bias = row(hb, j)
        for r0 in range(0, C, 16):
            weight = hw[j, r0 : r0 + 16, :].astype(f32)
            for off in range(TAPS):
                factor = mk[off, pl.ds(j, 1), :] + (1.0 if off == 4 else 0.0)
                wc[j, off * C + r0 : off * C + r0 + 16, :] = (weight * factor).astype(bf16)
        ex[...] = jnp.zeros_like(ex)
        for off in range(TAPS + 1):
            at = off if off < TAPS else 16
            value = bias * mk[off, pl.ds(j, 1), :] if off < TAPS else bias + row(mb, j)
            high = value.astype(bf16).astype(f32)
            ex[at : at + 1, :] = high
            ex[at + 32 : at + 33, :] = value - high
        wc[j, TAPS * C :, :] = ex[...].astype(bf16)

    def mlp_forward(j):
        def first(ts):
            xhat, scale = norm_parts(xs[ts, :])
            xh_m[j, ts, :] = xhat
            sc[j, ts, 1:2] = scale
            u = (xhat * row(ng, j, 3) + row(ns, j, 3)).astype(bf16).astype(f32)
            acc[0, ts, :] = u * valid[ts, :]

        tiles(first)
        for i in range(n):
            span = slice(i * TOK, (i + 1) * TOK)
            for off, piece in taps_of(acc[0, span, :]):
                u_all[j, span, off * C : (off + 1) * C] = piece.astype(bf16)

        for start in range(0, FF, CHUNK):
            cols = slice(start, start + CHUNK)
            for i in range(n):
                field = nn(u_all[j, i * TOK : (i + 1) * TOK, :], wc[j, :, cols])
                for r0 in range(0, TOK, 16):
                    act, slope = gelu_parts(field[r0 : r0 + 16])
                    part = slice(i * TOK + r0, i * TOK + r0 + 16)
                    a_all[j, part, cols] = act.astype(bf16)
                    g_all[j, part, cols] = slope.astype(bf16)
        for i in range(n):
            span = slice(i * TOK, (i + 1) * TOK)
            branch = nn(a_all[j, span, :], ow[j]) + row(ob, j)
            xs[span, :] = (xs[span, :] + scaled(span, 2 * j + 1) * branch).astype(bf16).astype(f32)

    def mlp_backward(j):
        sb = j * S_BLOCK

        def first(ts):
            grad = (xs[ts, :] * scaled(ts, 2 * j + 1)).astype(bf16)
            db[ts, :] = grad
            return [folded(grad.astype(f32))]

        (small[sb + S_OB : sb + S_OB + 1, :],) = tiles(first)
        db_t[j] = db[...].T
        for start in range(0, FF, CHUNK):
            cols = slice(start, start + CHUNK)
            for i in range(n):
                span = slice(i * TOK, (i + 1) * TOK)
                da = nt(db[span, :], ow[j, cols, :])
                g_all[j, span, cols] = (da * g_all[j, span, cols].astype(f32)).astype(bf16)
        if j == 0:
            move((0, 1))
        acc[...] = jnp.zeros_like(acc)
        for first_off in range(0, TAPS, 2):
            width = min(2, TAPS - first_off)
            for i in range(n):
                at = i * TOK
                moved = nt(
                    g_all[j, at : at + TOK, :], wc[j, first_off * C : (first_off + width) * C, :]
                )
                for s in range(width):
                    off = first_off + s
                    by = (off // 3 - 1) * GRID
                    piece = moved[:, s * C : (s + 1) * C]
                    if by >= 0:
                        acc[off % 3, at + by : at + TOK, :] += piece[: TOK - by]
                    else:
                        acc[off % 3, at : at + TOK + by, :] += piece[-by:]
        for i in range(n):
            span = slice(i * TOK, (i + 1) * TOK)
            left = pltpu.roll(jnp.where(col > 0, acc[0, span, :], 0.0), TOK - 1, 0)
            right = pltpu.roll(jnp.where(col < GRID - 1, acc[2, span, :], 0.0), 1, 0)
            acc[1, span, :] = (acc[1, span, :] + left + right) * valid[span, :]

        def last(ts):
            du = acc[1, ts, :]
            xhat = xh_m[j, ts, :]
            back = norm_back(du, xhat, sc[j, ts, 1:2], row(ng, j, 3))
            xs[ts, :] = (xs[ts, :] + back).astype(bf16).astype(f32)
            return [folded(du * xhat), folded(du)]

        gain, shift = tiles(last)
        small[sb + S_GAIN + 3 : sb + S_GAIN + 4, :] = gain
        small[sb + S_SHIFT + 3 : sb + S_SHIFT + 4, :] = shift

    def mlp_turn(j):
        for off in range(TAPS + 1):
            ut[off * C : (off + 1) * C, :] = u_all[j, :, off * C : (off + 1) * C].T

    def mlp_weights(j, step):
        base, sb = MLP_AT[0] + j * (MLP_AT[1] - MLP_AT[0]), j * S_BLOCK
        cols = slice(step * CHUNK, (step + 1) * CHUNK)
        dow = nn(db_t[j], a_all[j, :, cols])
        gp[packed(base + output_row(step), CHUNK), :] = dow.T.astype(bf16)
        cross = nn(ut[...], g_all[j, :, cols])
        flag_rows = cross[TAPS * C : TAPS * C + 24]
        total = flag_rows[16:17]
        dhb = total
        weight = hw[j, :, cols].astype(f32)
        dweight = jnp.zeros((C, CHUNK), f32)
        b = hb[pl.ds(j, 1), cols]
        for off in range(TAPS):
            piece = cross[off * C : (off + 1) * C]
            factor = mk[off, pl.ds(j, 1), cols]
            flag = flag_rows[off : off + 1]
            dweight = dweight + piece * (factor + (1.0 if off == 4 else 0.0))
            dk = col_sum(piece * weight) + b * flag
            dhb = dhb + factor * flag
            for s in range(CHUNK // C):
                tile = step * (CHUNK // C) + s
                put(sb + S_MK + 16 * tile + off, dk[:, s * C : (s + 1) * C])
        for s in range(CHUNK // C):
            tile = step * (CHUNK // C) + s
            part = slice(s * C, (s + 1) * C)
            put(sb + S_HB + tile, dhb[:, part])
            put(sb + S_MB + tile, total[:, part])
            gp[packed(base + hidden_row(tile), C), :] = dweight[:, part].astype(bf16)

    def attention_backward(j):
        base, sb = ATT_AT[j], j * S_BLOCK

        def first(ts):
            grad = (xs[ts, :] * scaled(ts, 2 * j)).astype(bf16)
            db[ts, :] = grad
            return [folded(grad.astype(f32))]

        (small[sb + S_PB : sb + S_PB + 1, :],) = tiles(first)
        dproj = jnp.zeros((C, C), f32)
        kernel = jnp.concatenate([lk[j, :, 0, :], lk[j, :, 1, :]], axis=1)
        dkernel = [jnp.zeros((1, C), f32) for _ in range(9)]
        dbias = jnp.zeros((1, C), f32)
        for i in range(n):
            span = slice(i * TOK, (i + 1) * TOK)
            dproj = dproj + nn(o_t[j, i], db[span, :])
            do = nt(db[span, :], pw[j]).astype(bf16)
            dprobs = nt(vbd[j, i], do)
            dvals = nn(pt[j, i], do)
            for low, top in SEGS:
                for c0 in range(0, TOK, 128):
                    c1 = min(c0 + 128, TOK)
                    weight = pt[j, i, low:top, c0:c1].astype(f32)
                    dweight = dprobs[low:top, c0:c1]
                    dot = jnp.sum(weight * dweight, axis=0, keepdims=True)
                    pt[j, i, low:top, c0:c1] = (weight * (dweight - dot)).astype(bf16)
            dkeys = nn(pt[j, i], q_a[j, span, :]) * ROOT
            dq = tn(kb[j, i], pt[j, i]) * ROOT
            o_n[span, :] = dq.T.astype(bf16)
            for t in range(2):
                dk = jnp.zeros((CELLS[t], C), f32)
                dv = jnp.zeros((CELLS[t], C), f32)
                for h in (2 * t, 2 * t + 1):
                    dk = dk + jnp.where(head_lanes(h), dkeys[slice(*SEGS[h])], 0.0)
                    dv = dv + jnp.where(head_lanes(h), dvals[slice(*SEGS[h])], 0.0)
                w = wv[j, cell_spans(t)[i], :]
                dw = dv
                for off in range(9):
                    by = near_shift(t, off)
                    part = dv * near[off, place_span[t], :]
                    moved = pltpu.roll(w, (CELLS[t] - by) % CELLS[t], 0) if by else w
                    dkernel[off] = dkernel[off] + col_sum(part * moved)
                    part = part * kernel[off : off + 1]
                    dw = dw + (pltpu.roll(part, by, 0) if by else part)
                dw = dw * kmask[i, place_span[t], :]
                dbias = dbias + col_sum(dw)
                if t == 0:
                    dkeyval = dk + pltpu.roll(dw, 64, 1)
                else:
                    dkeyval = pltpu.roll(dk, 64, 1) + dw
                wv[j, cell_spans(t)[i], :] = dkeyval
        gp[base + R_PROJ : base + R_PROJ + C, :] = dproj.astype(bf16)
        small[sb + S_VB : sb + S_VB + 1, :] = dbias
        for off in range(9):
            small[sb + S_LK + off : sb + S_LK + off + 1, :] = dkernel[off]
        base_perm = 0
        for t, (ref, weight) in enumerate(((p4, p4w), (p2, p2w))):
            span = cells_all(t)
            dkeyval = wv[j, span, :].astype(bf16)
            at = base + R_KV + t * C
            gp[at : at + C, :] = tn(kin[j, span, :], dkeyval).astype(bf16)
            dy = nt(dkeyval, kvw[j, t]) * ge_p[j, span, :]
            xhat = xh_p[j, span, :]
            small[sb + S_GAIN + 1 + t : sb + S_GAIN + 2 + t, :] = col_sum(dy * xhat)
            small[sb + S_SHIFT + 1 + t : sb + S_SHIFT + 2 + t, :] = col_sum(dy)
            dpool = norm_back(dy, xhat, sc_p[j, span, :], row(ng, j, 1 + t)).astype(bf16)
            at = base + (R_P4, R_P2)[t]
            for k in range(STRIDES[t] ** 2):
                gp[at + k * C : at + (k + 1) * C, :] = tn(
                    ref[j, :, k * C : (k + 1) * C], dpool
                ).astype(bf16)
                back = nt(dpool, weight[j, k * C : (k + 1) * C, :]).astype(bf16)
                for i in range(n):
                    pc[base_perm : base_perm + CELLS[t], i * C : (i + 1) * C] = back[
                        i * CELLS[t] : (i + 1) * CELLS[t]
                    ]
                base_perm += CELLS[t]
        at = base + R_Q
        gp[at : at + C, :] = tn(u_a[j], o_n[...]).astype(bf16)
        if j == 1:
            all_here()
            move((0, 0))
        else:
            move((0, 2), (1, 0))
        spread = nn(perm_t[...], pc[...])
        for i in range(n):
            span = slice(i * TOK, (i + 1) * TOK)
            back = nt(o_n[span, :], qw[j])
            acc[0, span, :] = back + spread[:, i * C : (i + 1) * C] * valid[span, :]

        def last(ts):
            du = acc[0, ts, :]
            xhat = xh_a[j, ts, :]
            back = norm_back(du, xhat, sc[j, ts, 0:1], row(ng, j, 0))
            xs[ts, :] = (xs[ts, :] + back).astype(bf16).astype(f32)
            return [folded(o_n[ts, :].astype(f32)), folded(du * xhat), folded(du)]

        bias, gain, shift = tiles(last)
        small[sb + S_QB : sb + S_QB + 1, :] = bias
        small[sb + S_GAIN : sb + S_GAIN + 1, :] = gain
        small[sb + S_SHIFT : sb + S_SHIFT + 1, :] = shift

    def forward(j, carry):
        attention_forward(j)
        mlp_forward(j)
        return carry

    lax.fori_loop(0, BLOCKS, forward, 0)
    out_st[...] = xs[...].astype(bf16)
    leave(out_st, out_ref)
    late.wait()
    xs[...] = cot_ref[...].astype(f32)
    mlp_backward(1)
    attention_backward(1)
    mlp_backward(0)
    attention_backward(0)
    dx_st[...] = xs[...].astype(bf16)
    leave(dx_st, dx_ref)

    def weights(k, carry):
        j = BLOCKS - 1 - k
        mlp_turn(j)
        move_if(k == 0, (1, 1))
        move_if(k == 1, (1, 2), (2, 1), (0, 4))
        mlp_weights(j, 0)
        move_if(k == 0, (0, 3))
        move_if(k == 1, (3, 0))
        mlp_weights(j, 1)
        move_if(k == 0, (2, 0))
        return carry

    lax.fori_loop(0, BLOCKS, weights, 0)
    gp[R_SMALL:, :] = small[...].astype(bf16)
    move((4, 0), (1, 3), (3, 1), (2, 2), (4, 1))
    move((0, 5), (3, 2), (1, 4), (0, 6), (2, 3), (4, 2), (3, 3), (2, 4), (4, 3), (1, 5), (3, 4))
    move((1, 6), (4, 4), (2, 5), (3, 5), (2, 6), (3, 6), (4, 5), (4, 6))
    for piece in pieces:
        piece.drain()
    for made in leaving:
        made.wait()


def compute(own, images, grid_size, keep_mask, x, cot, weights):
    segments, pairs = lax.axis_size("segment"), lax.axis_size("dp") // 2
    inner = min(pairs, 4)
    sizes = (segments, inner, pairs // inner)
    n = images
    rows = n * TOK
    cells = n * sum(CELLS)
    vmem = pl.BlockSpec(memory_space=pltpu.VMEM)
    smem = pl.BlockSpec(memory_space=pltpu.SMEM)
    consts = (jnp.asarray(patch_tokens()), jnp.asarray(cell_places()))
    B = BLOCKS
    scratch = [
        pltpu.VMEM((rows, C), f32),
        pltpu.VMEM((rows, C), f32),
        pltpu.VMEM((TOK, n * C), bf16),
        pltpu.VMEM((B, rows, UW), bf16),
        pltpu.VMEM((UW, rows), bf16),
        pltpu.VMEM((B, UW, FF), bf16),
        pltpu.VMEM((C, FF), f32),
        pltpu.VMEM((B, rows, C), f32),
        pltpu.VMEM((B, rows, C), f32),
        pltpu.VMEM((B, rows, C), f32),
        pltpu.VMEM((B, rows, C), bf16),
        pltpu.VMEM((B, rows, C), bf16),
        pltpu.VMEM((B, n * CELLS[0], 16 * C), bf16),
        pltpu.VMEM((B, n * CELLS[1], 4 * C), bf16),
        pltpu.VMEM((B, cells, C), f32),
        pltpu.VMEM((B, cells, C), f32),
        pltpu.VMEM((B, cells, C), f32),
        pltpu.VMEM((B, cells, C), bf16),
        pltpu.VMEM((B, cells, C), f32),
        pltpu.VMEM((B, n, KEYS, C), bf16),
        pltpu.VMEM((B, n, KEYS, C), bf16),
        pltpu.VMEM((B, n, KEYS, TOK), bf16),
        pltpu.VMEM((B, n, C, TOK), bf16),
        pltpu.VMEM((rows, C), bf16),
        pltpu.VMEM((B, rows, FF), bf16),
        pltpu.VMEM((B, rows, FF), bf16),
        pltpu.VMEM((rows, C), bf16),
        pltpu.VMEM((B, C, rows), bf16),
        pltpu.VMEM((3, rows, C), f32),
        pltpu.VMEM((n, sum(CELLS), C), f32),
        pltpu.VMEM((9, sum(CELLS), C), f32),
        pltpu.VMEM((ROWS - R_SMALL, C), f32),
        pltpu.VMEM((PERM, n * C), bf16),
        pltpu.SMEM((n, 2 * BLOCKS), f32),
        pltpu.VMEM(cot.shape, bf16),
        pltpu.VMEM((PERM, TOK), bf16),
        pltpu.VMEM((TOK, PERM), bf16),
        pltpu.VMEM((rows, C), bf16),
        pltpu.VMEM((rows, C), bf16),
        pltpu.SemaphoreType.DMA((3 + len(PIECES),)),
        pltpu.VMEM((ROWS, C), bf16),
    ] + sum_scratch(sizes)
    anywhere = pl.BlockSpec(memory_space=pl.ANY)
    operands = [vmem] * (2 + len(weights) + len(consts))
    operands[1] = anywhere
    return pl.pallas_call(
        functools.partial(compute_kernel, own, images, sizes),
        out_shape=(
            jax.ShapeDtypeStruct((rows, C), bf16),
            jax.ShapeDtypeStruct((rows, C), bf16),
            jax.ShapeDtypeStruct((ROWS, C), bf16),
        ),
        in_specs=[smem, smem] + operands,
        out_specs=(anywhere,) * 3,
        scratch_shapes=scratch,
        compiler_params=pltpu.CompilerParams(
            collective_id=0, has_side_effects=True, vmem_limit_bytes=63 * 2**20
        ),
        name="compute",
    )(grid_size, keep_mask, x, cot, *weights, *consts)


def unpack_kernel(att, mlp, rest, out_in, dx_in, *refs):
    out_ref, dx_ref = refs[:2]
    gain, shift, qw, qb, p4, p2, kvw, vb, lk, pw, pb, hw, hb, mk, mb, ow, ob = refs[2:]
    out_ref[...] = out_in[...]
    dx_ref[...] = dx_in[...]
    p4[0] = att[R_P4:R_P2, :].astype(f32)
    p2[0] = att[R_P2:R_KV, :].astype(f32)
    for t in range(2):
        kvw[0, t] = att[R_KV + t * C : R_KV + (t + 1) * C, :].astype(f32)
    qw[0] = att[R_Q:R_PROJ, :].astype(f32)
    pw[0] = att[R_PROJ:R_ATT, :].astype(f32)
    for s in range(FF // C):
        hw[0, :, s * C : (s + 1) * C] = mlp[hidden_row(s) : hidden_row(s) + C, :].astype(f32)
    for step in range(FF // CHUNK):
        at = output_row(step)
        ow[0, step * CHUNK : (step + 1) * CHUNK, :] = mlp[at : at + CHUNK, :].astype(f32)

    @pl.when(pl.program_id(0) == BLOCKS - 1)
    def _():
        for j in range(BLOCKS):
            sb = j * S_BLOCK
            head = rest[sb : sb + 48, :].astype(f32)
            gain[j] = head[S_GAIN : S_GAIN + 4]
            shift[j] = head[S_SHIFT : S_SHIFT + 4]
            qb[j : j + 1, :] = head[S_QB : S_QB + 1]
            vb[j, 0:1, :] = head[S_VB : S_VB + 1, 0:64]
            vb[j, 1:2, :] = head[S_VB : S_VB + 1, 64:128]
            pb[j : j + 1, :] = head[S_PB : S_PB + 1]
            ob[j : j + 1, :] = head[S_OB : S_OB + 1]
            lk[j, :, 0, :] = head[S_LK : S_LK + 9, 0:64]
            lk[j, :, 1, :] = head[S_LK : S_LK + 9, 64:128]
            for s in range(FF // C):
                part = slice(s * C, (s + 1) * C)
                hb[j : j + 1, part] = head[S_HB + s : S_HB + s + 1]
                mb[j : j + 1, part] = head[S_MB + s : S_MB + s + 1]
                at = sb + S_MK + 16 * s
                mk[:, j, part] = rest[at : at + 16, :].astype(f32)[0:9]


def unpack(packed, outputs, input_grad, weights):
    streams = (jax.ShapeDtypeStruct(outputs.shape, bf16),) * 2
    by_block = {QW, P4, P2, KVW, PW, HW, OW}
    rest = ROWS - R_SMALL
    stream = pl.BlockSpec((outputs.shape[0] // BLOCKS, C), lambda k: (k, 0))
    specs = []
    for place, w in enumerate(weights):
        if place in by_block:
            zeros = (0,) * (w.ndim - 1)
            specs.append(pl.BlockSpec((1,) + w.shape[1:], lambda k, z=zeros: (BLOCKS - 1 - k,) + z))
        else:
            zeros = (0,) * w.ndim
            specs.append(pl.BlockSpec(w.shape, lambda k, z=zeros: z))
    return pl.pallas_call(
        unpack_kernel,
        out_shape=streams + tuple(jax.ShapeDtypeStruct(w.shape, f32) for w in weights),
        grid=(BLOCKS,),
        in_specs=[
            pl.BlockSpec((R_ATT, C), lambda k: (k, 0)),
            pl.BlockSpec((R_MLP, C), lambda k: (MLP_AT[BLOCKS - 1] // R_MLP + k, 0)),
            pl.BlockSpec((rest, C), lambda k: (R_SMALL // rest, 0)),
            stream,
            stream,
        ],
        out_specs=(stream, stream) + tuple(specs),
        compiler_params=pltpu.CompilerParams(vmem_limit_bytes=63 * 2**20),
        name="unpack",
    )(packed, packed, packed, outputs, input_grad)


def on_device(inputs, grid_size, keep_mask, cotangent, *weights):
    own, per = inputs.shape[:2]
    images = own * per
    flat = (images * TOK, C)
    turned = list(weights)
    turned[LK] = jnp.transpose(turned[LK], (0, 2, 1, 3))
    turned[MK] = jnp.transpose(turned[MK], (1, 0, 2))
    outputs, input_grad, packed = compute(
        own,
        images,
        jnp.transpose(grid_size, (1, 2, 0)),
        jnp.transpose(keep_mask, (1, 2, 0)),
        inputs.reshape(flat),
        cotangent.reshape(flat),
        turned,
    )
    outputs, input_grad, *grads = unpack(packed, outputs, input_grad, turned)
    grads[LK] = jnp.transpose(grads[LK], (0, 2, 1, 3))
    grads[MK] = jnp.transpose(grads[MK], (1, 0, 2))
    return (outputs.reshape(inputs.shape), input_grad.reshape(inputs.shape)) + tuple(grads)


def solution(mesh):
    stream = P("segment", "dp", None, None)
    picked = P(None, "dp", None)
    return jax.shard_map(
        on_device,
        mesh=mesh,
        in_specs=(stream, picked, picked, stream) + (P(),) * 17,
        out_specs=(stream, stream) + (P(),) * 17,
        check_vma=False,
    )
```

```python
import functools

import jax
import jax.numpy as jnp
import numpy as np
from jax import lax
from jax.experimental import pallas as pl
from jax.experimental.pallas import tpu as pltpu
from jax.sharding import PartitionSpec as P

GRID = 24
TOK = GRID * GRID
C = 128
FF = 1024
HEAD = 32
BLOCKS = 2
SIDES = (6, 12)
STRIDES = (4, 2)
CELLS = (48, 144)
SEGS = ((0, 48), (48, 96), (96, 240), (240, 384))
KEYS = 384
PERM = 16 * 48 + 4 * 144
TAPS = 9
UW = TAPS * C + C
CHUNK = 256
TILE = 96

R_P4, R_P2, R_KV, R_Q, R_PROJ, R_ATT = 0, 2048, 2560, 2816, 2944, 3072
R_MLP = 2048
ATT_AT = (R_ATT, 0)
MLP_AT = (2 * R_ATT + R_MLP, 2 * R_ATT)
S_GAIN, S_SHIFT, S_QB, S_VB, S_PB, S_OB, S_LK, S_HB, S_MB, S_MK, S_BLOCK = (
    0,
    4,
    8,
    9,
    10,
    11,
    16,
    32,
    40,
    48,
    192,
)
R_SMALL = BLOCKS * (R_ATT + R_MLP)
ROWS = R_SMALL + 512
PIECES = (
    (ATT_AT[1], R_ATT),
    (ATT_AT[0], R_ATT),
    (MLP_AT[1], R_MLP),
    (MLP_AT[0], R_MLP - 2 * CHUNK),
    (R_SMALL - 2 * CHUNK, 2 * CHUNK + ROWS - R_SMALL),
)

QW, P4, P2, KVW, LK, PW, HW, MK, OW = 2, 4, 5, 6, 8, 9, 11, 13, 15

epsilon = 1e-06
keep_rate = 0.8
ROOT = HEAD**-0.5
LOG2E = 1.4426950408889634
f32, bf16 = jnp.float32, jnp.bfloat16


def hidden_row(tile):
    return tile // (CHUNK // C) * 2 * CHUNK + tile % (CHUNK // C) * C


def output_row(step):
    return step * 2 * CHUNK + CHUNK


def patch_tokens():
    tokens = np.full((8, PERM), -1.0, np.float32)
    base = 0
    for stride, side, cells in zip(STRIDES, SIDES, CELLS):
        for row_off in range(stride):
            for col_off in range(stride):
                for a in range(side):
                    for b in range(side):
                        token = (a * stride + row_off) * GRID + b * stride + col_off
                        tokens[:, base + a * side + b] = token
                base += cells
    return tokens


def cell_places():
    places = np.full((2, sum(CELLS), 128), 99.0, np.float32)
    base = 0
    for side, cells in zip(SIDES, CELLS):
        for a in range(side):
            for b in range(side):
                places[0, base + a * side + b] = a
                places[1, base + a * side + b] = b
        base += cells
    return places


def nn(left, right):
    return jnp.dot(left, right, preferred_element_type=f32)


def nt(left, right):
    return lax.dot_general(left, right, (((1,), (1,)), ((), ())), preferred_element_type=f32)


def tn(left, right):
    return lax.dot_general(left, right, (((0,), (0,)), ((), ())), preferred_element_type=f32)


def gelu_parts(m):
    size = jnp.abs(m)
    t = pl.reciprocal(1.0 + (0.3275911 * 0.5**0.5) * size, approx=True)
    e = jnp.exp2(m * (m * (-0.5 * LOG2E)))
    poly = 0.5 * 1.061405429
    for coef in (-1.453152027, 1.421413741, -0.284496736, 0.254829592):
        poly = poly * t + 0.5 * coef
    poly = poly * t
    tail = poly * e
    slope = (poly - size * 0.3989422804014327) * e
    return jnp.maximum(m, 0.0) - size * tail, jnp.where(m >= 0, 1.0 - slope, slope)


def norm_parts(x):
    centred = x - jnp.mean(x, axis=-1, keepdims=True)
    scale = lax.rsqrt(jnp.mean(centred * centred, axis=-1, keepdims=True) + epsilon)
    return centred * scale, scale


def norm_back(du, xhat, scale, gain):
    dxhat = du * gain
    first = jnp.mean(dxhat, axis=-1, keepdims=True)
    second = jnp.mean(dxhat * xhat, axis=-1, keepdims=True)
    return scale * (dxhat - first - xhat * second)


def col_sum(x):
    return jnp.sum(x, axis=0, keepdims=True)


def folded(x):
    return jnp.sum(x.reshape(-1, 8, x.shape[-1]), axis=0)


class Summed:
    STEPS = 7

    def __init__(self, place, piece, base, count, refs):
        self.seg, self.dp, self.segments, self.inner, self.outer = place
        self.piece, self.base = piece, base
        (
            self.src,
            self.half_in,
            self.quarter_in,
            self.part_in,
            self.whole_in,
            self.own,
            self.total,
            self.send,
            self.recv,
        ) = refs
        self.core, rest = self.dp % 2, self.dp // 2
        self.part, self.group = rest % self.inner, rest // self.inner
        self.half = count // 2
        self.quarter = self.half // self.segments
        self.share = self.quarter // self.inner
        quarters, shares = (self.segments - 1) * self.quarter, (self.inner - 1) * self.share
        self.moved = (self.half, quarters, shares, shares, quarters, self.half)
        self.at_quarter = self.seg * self.quarter
        self.at_share = self.at_quarter + self.part * self.share

    def span(self, start, size):
        return pl.ds(pl.multiple_of(start, 16), size)

    def device(self, seg=None, core=None, part=None, group=None):
        seg = self.seg if seg is None else seg
        core = self.core if core is None else core
        part = self.part if part is None else part
        group = self.group if group is None else group
        return (seg, (group * self.inner + part) * 2 + core)

    def copy(self, k, src, dst, device):
        return pltpu.make_async_remote_copy(
            src_ref=src,
            dst_ref=dst,
            send_sem=self.send.at[self.piece],
            recv_sem=self.recv.at[self.piece, k],
            device_id=device,
            device_id_type=pl.DeviceIdType.MESH,
        )

    def counted(self, k, count):
        ref = self.total.at[pl.ds(0, count), :]
        return self.copy(k, ref, ref, self.device(core=1 - self.core))

    def step(self, k):
        if k > 0:
            self.counted(k - 1, self.moved[k - 1]).wait_recv()
            self.gather(k)
        if k + 1 < self.STEPS:
            self.depart(k)

    def drain(self):
        count = sum(self.moved) + (self.outer - 1) * self.share
        self.counted(0, count).wait_send()

    def depart(self, k):
        half = self.base // 2
        mine = self.base + self.core * self.half
        if k == 0:
            src = self.src.at[self.span(self.base + (1 - self.core) * self.half, self.half), :]
            dst = self.half_in.at[self.span(half, self.half), :]
            self.copy(k, src, dst, self.device(core=1 - self.core)).start()
        elif k == 1:
            at = self.span(half // self.segments, self.quarter)
            for d in range(1, self.segments):
                to = self.seg ^ d
                src = self.own.at[self.span(half + to * self.quarter, self.quarter), :]
                dst = self.quarter_in.at[d - 1, at, :]
                self.copy(k, src, dst, self.device(seg=to)).start()
        elif k == 2:
            at = self.span(self.share_in(), self.share)
            for d in range(1, self.inner):
                to = self.part ^ d
                start = half + self.at_quarter + to * self.share
                src = self.own.at[self.span(start, self.share), :]
                self.copy(k, src, self.part_in.at[d - 1, at, :], self.device(part=to)).start()
        elif k == 3:
            ref = self.total.at[self.span(mine + self.at_share, self.share), :]
            for d in range(1, self.inner):
                self.copy(k, ref, ref, self.device(part=self.part ^ d)).start()
        elif k == 4:
            ref = self.total.at[self.span(mine + self.at_quarter, self.quarter), :]
            for d in range(1, self.segments):
                self.copy(k, ref, ref, self.device(seg=self.seg ^ d)).start()
        else:
            ref = self.total.at[self.span(mine, self.half), :]
            self.copy(k, ref, ref, self.device(core=1 - self.core)).start()

    def share_in(self):
        return self.base // 2 // self.segments // self.inner

    def gather(self, k):
        half = self.base // 2
        if k == 1:
            first = (self.src, self.base + self.core * self.half)
            self.add((self.own, half), first, [(self.half_in, half)], self.half)
        elif k == 2:
            mine = (self.own, half + self.at_quarter)
            at = half // self.segments
            received = [(self.quarter_in.at[d], at) for d in range(self.segments - 1)]
            self.add(mine, mine, received, self.quarter)
        elif k == 3:
            received = [(self.part_in.at[d], self.share_in()) for d in range(self.inner - 1)]
            mine = (self.own, half + self.at_share)
            into = (self.total, self.base + self.core * self.half + self.at_share)
            if self.outer > 1:
                self.add(mine, mine, received, self.share)
                slot = self.STEPS - 1
                src = self.own.at[self.span(mine[1], self.share), :]
                at = self.span(self.share_in(), self.share)
                for d in range(1, self.outer):
                    to = self.device(group=self.group ^ d)
                    self.copy(slot, src, self.whole_in.at[d - 1, at, :], to).start()
                self.counted(slot, (self.outer - 1) * self.share).wait_recv()
                received = [(self.whole_in.at[d], self.share_in()) for d in range(self.outer - 1)]
            self.add(into, mine, received, self.share)

    def add(self, dst, first, others, count):
        step = next(size for size in (128, 96, 80, 64, 48, 32, 16) if count % size == 0)

        def body(t, carry):
            at = t * step
            total = first[0][self.span(first[1] + at, step), :].astype(f32)
            for ref, start in others:
                total = total + ref[self.span(start + at, step), :].astype(f32)
            dst[0][self.span(dst[1] + at, step), :] = total.astype(bf16)
            return carry

        lax.fori_loop(0, count // step, body, 0)


def greet(seg, dp, segments, inner, outer):
    barrier = pltpu.get_barrier_semaphore()
    core, part, group = dp % 2, dp // 2 % inner, dp // 2 // inner
    peers = [(seg, dp + 1 - 2 * core)]
    peers += [(seg ^ d, dp) for d in range(1, segments)]
    peers += [(seg, (group * inner + (part ^ d)) * 2 + core) for d in range(1, inner)]
    peers += [(seg, ((group ^ d) * inner + part) * 2 + core) for d in range(1, outer)]
    for peer in peers:
        pl.semaphore_signal(
            barrier, inc=1, device_id=peer, device_id_type=pl.DeviceIdType.MESH
        )
    return lambda: pl.semaphore_wait(barrier, len(peers))


def sum_scratch(sizes):
    segments, inner, outer = sizes
    quarter = ROWS // 2 // segments
    share = quarter // inner
    return [
        pltpu.VMEM((ROWS // 2, C), bf16),
        pltpu.VMEM((segments - 1, quarter, C), bf16),
        pltpu.VMEM((inner - 1, share, C), bf16),
        pltpu.VMEM((max(outer - 1, 1), share, C), bf16),
        pltpu.VMEM((ROWS // 2, C), bf16),
        pltpu.VMEM((ROWS, C), bf16),
        pltpu.SemaphoreType.DMA((len(PIECES),)),
        pltpu.SemaphoreType.DMA((len(PIECES), Summed.STEPS)),
    ]


def compute_kernel(
    own,
    images,
    sizes,
    grid_ref,
    keep_ref,
    x_ref,
    cot_in,
    ng,
    ns,
    qw,
    qb,
    p4w_in,
    p2w_in,
    kvw,
    vb,
    lk,
    pw,
    pb,
    hw_in,
    hb,
    mk,
    mb,
    ow_in,
    ob,
    tokens,
    places,
    out_ref,
    dx_ref,
    summed_ref,
    xs,
    valid,
    um,
    u_all,
    ut,
    wc,
    ex,
    xh_a,
    xh_m,
    sc,
    u_a,
    q_a,
    p4,
    p2,
    xh_p,
    sc_p,
    ge_p,
    kin,
    wv,
    kb,
    vbd,
    pt,
    o_t,
    o_n,
    a_all,
    g_all,
    db,
    db_t,
    acc,
    kmask,
    near,
    small,
    pc,
    scale_ref,
    cot_ref,
    hw,
    p4w,
    p2w,
    ow,
    perm,
    perm_t,
    out_st,
    dx_st,
    sems,
    gp,
    half_in,
    quarter_in,
    part_in,
    whole_in,
    own_part,
    total_ref,
    send,
    recv,
):
    n = images
    rows = n * TOK
    seg, dp = lax.axis_index("segment"), lax.axis_index("dp")
    all_here = greet(seg, dp, *sizes)
    late = [
        pltpu.make_async_copy(src, dst, sems.at[k])
        for k, (src, dst) in enumerate(
            ((hw_in, hw), (p4w_in, p4w), (p2w_in, p2w), (ow_in, ow), (cot_in, cot_ref))
        )
    ]
    for made in late:
        made.start()
    leaving = []

    def leave(src, dst):
        made = pltpu.make_async_copy(src, dst, sems.at[len(late) + len(leaving)])
        made.start()
        leaving.append(made)

    refs = (
        gp,
        half_in,
        quarter_in,
        part_in,
        whole_in,
        own_part,
        total_ref,
        send,
        recv,
    )
    pieces = [
        Summed((seg, dp) + sizes, p, base, count, refs) for p, (base, count) in enumerate(PIECES)
    ]

    def move(*steps):
        for p, k in steps:
            pieces[p].step(k)
            if k + 1 == Summed.STEPS:
                rows_of = pl.ds(PIECES[p][0], PIECES[p][1])
                leave(total_ref.at[rows_of, :], summed_ref.at[rows_of, :])

    def move_if(now, *steps):
        pl.when(now)(lambda: move(*steps))

    lane = lax.broadcasted_iota(jnp.int32, (8, 128), 1)[0:1]

    def head_lanes(h):
        return (lane >= h * HEAD) & (lane < (h + 1) * HEAD)

    def tiles(fn, step=TILE):
        sums = None
        for start in range(0, rows, step):
            got = fn(slice(start, start + step))
            if got is not None:
                sums = got if sums is None else [x + y for x, y in zip(sums, got)]
        return None if sums is None else [col_sum(x) for x in sums]

    def row(ref, j, k=None):
        return ref[j, pl.ds(k, 1), :] if k is not None else ref[pl.ds(j, 1), :]

    def put(at, value):
        small[pl.ds(at, 1), :] = value

    def packed(start, count):
        return pl.ds(pl.multiple_of(start, 128), count)

    def shifted_rows(v, by):
        if by == 0:
            return v
        pad = jnp.zeros((abs(by), v.shape[1]), v.dtype)
        if by > 0:
            return jnp.concatenate([v[by:], pad], axis=0)
        return jnp.concatenate([pad, v[:by]], axis=0)

    col = lax.broadcasted_iota(jnp.int32, (GRID, GRID, 128), 1).reshape(TOK, 128)

    def taps_of(v):
        left = jnp.where(col > 0, pltpu.roll(v, 1, 0), 0.0)
        right = jnp.where(col < GRID - 1, pltpu.roll(v, TOK - 1, 0), 0.0)
        for row_off in range(3):
            for col_off, piece in enumerate((left, v, right)):
                yield row_off * 3 + col_off, shifted_rows(piece, (row_off - 1) * GRID)

    small[...] = jnp.zeros_like(small)
    sizes = []
    lane_row = lax.broadcasted_iota(jnp.int32, (TOK, 128), 1)
    tap = lane % 32
    down, across_by = tap // 3 - 1, tap % 3 - 1
    tap_lane = (tap < TAPS) & (lane < 64)
    for i in range(n):
        m_id, d_id = seg * own + i // (n // own), i % (n // own)
        high, wide = grid_ref[d_id, 0, m_id], grid_ref[d_id, 1, m_id]
        sizes.append((high, wide))
        line = lax.broadcasted_iota(jnp.int32, (GRID, GRID, 128), 0).reshape(TOK, 128)
        good = jnp.where((line < high) & (col < wide), 1.0, 0.0)
        valid[i * TOK : (i + 1) * TOK, :] = good
        for k in range(2 * BLOCKS):
            kept = keep_ref[d_id, k, m_id].astype(f32) / keep_rate
            scale_ref[i, k] = kept
        near_row, near_col = line + down, col + across_by
        there = (near_row >= 0) & (near_row < high) & (near_col >= 0) & (near_col < wide)
        ones = (lane_row == 16) | (lane_row == 48)
        flags = jnp.where(ones | (there & tap_lane), 1.0, 0.0)
        for j in range(BLOCKS):
            u_all[j, i * TOK : (i + 1) * TOK, TAPS * C :] = flags.astype(bf16)
        base = 0
        for t in range(2):
            span = slice(base, base + CELLS[t])
            tall = (high + STRIDES[t] - 1) // STRIDES[t]
            across = (wide + STRIDES[t] - 1) // STRIDES[t]
            inside = (places[0, span, :] < tall.astype(f32)) & (
                places[1, span, :] < across.astype(f32)
            )
            kmask[i, span, :] = jnp.where(inside, 1.0, 0.0)
            base += CELLS[t]
    base = 0
    for t in range(2):
        span = slice(base, base + CELLS[t])
        a, b = places[0, span, :], places[1, span, :]
        for off in range(9):
            dr, dc = float(off // 3 - 1), float(off % 3 - 1)
            top = float(SIDES[t])
            ok = (a + dr >= 0) & (a + dr < top) & (b + dc >= 0) & (b + dc < top)
            near[off, span, :] = jnp.where(ok, 1.0, 0.0)
        base += CELLS[t]

    base = start = 0
    for t in range(2):
        span, stride = slice(start, start + CELLS[t]), STRIDES[t]
        corner = places[0, span, :] * float(stride * GRID) + places[1, span, :] * float(stride)
        for k in range(stride * stride):
            token = corner + float(k // stride * GRID + k % stride)
            for c0 in range(0, TOK, 128):
                width = min(128, TOK - c0)
                here = lax.broadcasted_iota(jnp.int32, (CELLS[t], width), 1).astype(f32) + float(c0)
                block = jnp.where(token[:, :width] == here, 1.0, 0.0)
                perm[base : base + CELLS[t], c0 : c0 + width] = block.astype(bf16)
            base += CELLS[t]
        start += CELLS[t]
    for r0 in range(0, TOK, TILE):
        here = lax.broadcasted_iota(jnp.int32, (TILE, PERM), 0).astype(f32) + float(r0)
        block = jnp.where(tokens[0:1, :] == here, 1.0, 0.0)
        perm_t[r0 : r0 + TILE, :] = block.astype(bf16)

    xs[...] = x_ref[...].astype(f32)

    def scaled(span, k):
        return valid[span, :] * scale_ref[span.start // TOK, k]

    def cell_spans(t):
        start = 0 if t == 0 else n * CELLS[0]
        return [slice(start + i * CELLS[t], start + (i + 1) * CELLS[t]) for i in range(n)]

    def cells_all(t):
        return slice(0, n * CELLS[0]) if t == 0 else slice(n * CELLS[0], n * sum(CELLS))

    place_span = (slice(0, CELLS[0]), slice(CELLS[0], sum(CELLS)))
    half = lane < 64
    own_half = (half, jnp.logical_not(half))

    def near_shift(t, off):
        return ((off // 3 - 1) * SIDES[t] + off % 3 - 1) % CELLS[t]

    def attention_forward(j):
        build_wc(j)

        def first(ts):
            xhat, scale = norm_parts(xs[ts, :])
            xh_a[j, ts, :] = xhat
            sc[j, ts, 0:1] = scale
            u_a[j, ts, :] = (xhat * row(ng, j, 0) + row(ns, j, 0)).astype(bf16)

        tiles(first)
        for i in range(n):
            span = slice(i * TOK, (i + 1) * TOK)
            u = u_a[j, span, :]
            q_a[j, span, :] = (nn(u, qw[j]) + row(qb, j)).astype(bf16)
            um[:, i * C : (i + 1) * C] = (u.astype(f32) * valid[span, :]).astype(bf16)
        pc[...] = nn(perm[...], um[...]).astype(bf16)
        base = 0
        for t, ref in enumerate((p4, p2)):
            for k in range(STRIDES[t] ** 2):
                for i in range(n):
                    ref[j, i * CELLS[t] : (i + 1) * CELLS[t], k * C : (k + 1) * C] = pc[
                        base : base + CELLS[t], i * C : (i + 1) * C
                    ]
                base += CELLS[t]
        for t, (ref, weight) in enumerate(((p4, p4w), (p2, p2w))):
            xhat, scale = norm_parts(nn(ref[j], weight[j]))
            act, slope = gelu_parts(xhat * row(ng, j, 1 + t) + row(ns, j, 1 + t))
            act = act.astype(bf16)
            span = cells_all(t)
            xh_p[j, span, :] = xhat
            sc_p[j, span, :] = jnp.broadcast_to(scale, xhat.shape)
            ge_p[j, span, :] = slope
            kin[j, span, :] = act
            keyval = nn(act, kvw[j, t])
            turned = pltpu.roll(keyval, 64, 1)
            keys, vals = (keyval, turned) if t == 0 else (turned, keyval)
            bias = jnp.concatenate([row(vb, j, 0), row(vb, j, 1)], axis=1)
            kernel = jnp.concatenate([lk[j, :, 0, :], lk[j, :, 1, :]], axis=1)
            for i in range(n):
                part = slice(i * CELLS[t], (i + 1) * CELLS[t])
                w = (vals[part] + bias) * kmask[i, place_span[t], :]
                wv[j, cell_spans(t)[i], :] = w
                v = w
                for off in range(9):
                    by = near_shift(t, off)
                    moved = pltpu.roll(w, (CELLS[t] - by) % CELLS[t], 0) if by else w
                    v = v + moved * (near[off, place_span[t], :] * kernel[off : off + 1])
                for h in (2 * t, 2 * t + 1):
                    seg_rows = slice(*SEGS[h])
                    kb[j, i, seg_rows, :] = jnp.where(head_lanes(h), keys[part], 0.0).astype(bf16)
                    vbd[j, i, seg_rows, :] = jnp.where(head_lanes(h), v, 0.0).astype(bf16)
        for i in range(n):
            span = slice(i * TOK, (i + 1) * TOK)
            scores = nt(kb[j, i], q_a[j, span, :])
            for h, (low, top) in enumerate(SEGS):
                mask = kmask[i, place_span[h // 2], 0:1] > 0
                for c0 in range(0, TOK, 128):
                    c1 = min(c0 + 128, TOK)
                    s = jnp.where(mask, scores[low:top, c0:c1], -1e30)
                    e = jnp.exp2((s - jnp.max(s, axis=0, keepdims=True)) * (ROOT * LOG2E))
                    weight = e * pl.reciprocal(jnp.sum(e, axis=0, keepdims=True), approx=True)
                    pt[j, i, low:top, c0:c1] = weight.astype(bf16)
            mixed = tn(vbd[j, i], pt[j, i])
            o_t[j, i] = mixed.astype(bf16)
            o_n[span, :] = mixed.T.astype(bf16)
        for i in range(n):
            span = slice(i * TOK, (i + 1) * TOK)
            branch = nn(o_n[span, :], pw[j]) + row(pb, j)
            xs[span, :] = (xs[span, :] + scaled(span, 2 * j) * branch).astype(bf16).astype(f32)

    def build_wc(j):
        bias = row(hb, j)
        for r0 in range(0, C, 16):
            weight = hw[j, r0 : r0 + 16, :].astype(f32)
            for off in range(TAPS):
                factor = mk[off, pl.ds(j, 1), :] + (1.0 if off == 4 else 0.0)
                wc[j, off * C + r0 : off * C + r0 + 16, :] = (weight * factor).astype(bf16)
        ex[...] = jnp.zeros_like(ex)
        for off in range(TAPS + 1):
            at = off if off < TAPS else 16
            value = bias * mk[off, pl.ds(j, 1), :] if off < TAPS else bias + row(mb, j)
            high = value.astype(bf16).astype(f32)
            ex[at : at + 1, :] = high
            ex[at + 32 : at + 33, :] = value - high
        wc[j, TAPS * C :, :] = ex[...].astype(bf16)

    def mlp_forward(j):
        def first(ts):
            xhat, scale = norm_parts(xs[ts, :])
            xh_m[j, ts, :] = xhat
            sc[j, ts, 1:2] = scale
            u = (xhat * row(ng, j, 3) + row(ns, j, 3)).astype(bf16).astype(f32)
            acc[0, ts, :] = u * valid[ts, :]

        tiles(first)
        for i in range(n):
            span = slice(i * TOK, (i + 1) * TOK)
            for off, piece in taps_of(acc[0, span, :]):
                u_all[j, span, off * C : (off + 1) * C] = piece.astype(bf16)

        for start in range(0, FF, CHUNK):
            cols = slice(start, start + CHUNK)
            field = nn(u_all[j], wc[j, :, cols])
            for r0 in range(0, rows, 32):
                part = slice(r0, r0 + 32)
                act, slope = gelu_parts(field[part])
                a_all[j, part, cols] = act.astype(bf16)
                g_all[j, part, cols] = slope.astype(bf16)
        for i in range(n):
            span = slice(i * TOK, (i + 1) * TOK)
            branch = nn(a_all[j, span, :], ow[j]) + row(ob, j)
            xs[span, :] = (xs[span, :] + scaled(span, 2 * j + 1) * branch).astype(bf16).astype(f32)

    def mlp_backward(j):
        sb = j * S_BLOCK

        def first(ts):
            grad = (xs[ts, :] * scaled(ts, 2 * j + 1)).astype(bf16)
            db[ts, :] = grad
            return [folded(grad.astype(f32))]

        (small[sb + S_OB : sb + S_OB + 1, :],) = tiles(first)
        db_t[j] = db[...].T
        for start in range(0, FF, CHUNK):
            cols = slice(start, start + CHUNK)
            da = nt(db[...], ow[j, cols, :])
            g_all[j, :, cols] = (da * g_all[j, :, cols].astype(f32)).astype(bf16)
        if j == 0:
            move((0, 1))
        acc[...] = jnp.zeros_like(acc)
        for first_off in range(0, TAPS, 2):
            width = min(2, TAPS - first_off)
            moved = nt(g_all[j], wc[j, first_off * C : (first_off + width) * C, :])
            for s in range(width):
                off = first_off + s
                by = (off // 3 - 1) * GRID
                for i in range(n):
                    at = i * TOK
                    piece = moved[at : at + TOK, s * C : (s + 1) * C]
                    if by >= 0:
                        acc[off % 3, at + by : at + TOK, :] += piece[: TOK - by]
                    else:
                        acc[off % 3, at : at + TOK + by, :] += piece[-by:]
        for i in range(n):
            span = slice(i * TOK, (i + 1) * TOK)
            left = pltpu.roll(jnp.where(col > 0, acc[0, span, :], 0.0), TOK - 1, 0)
            right = pltpu.roll(jnp.where(col < GRID - 1, acc[2, span, :], 0.0), 1, 0)
            acc[1, span, :] = (acc[1, span, :] + left + right) * valid[span, :]

        def last(ts):
            du = acc[1, ts, :]
            xhat = xh_m[j, ts, :]
            back = norm_back(du, xhat, sc[j, ts, 1:2], row(ng, j, 3))
            xs[ts, :] = (xs[ts, :] + back).astype(bf16).astype(f32)
            return [folded(du * xhat), folded(du)]

        gain, shift = tiles(last)
        small[sb + S_GAIN + 3 : sb + S_GAIN + 4, :] = gain
        small[sb + S_SHIFT + 3 : sb + S_SHIFT + 4, :] = shift

    def mlp_turn(j):
        for off in range(TAPS + 1):
            ut[off * C : (off + 1) * C, :] = u_all[j, :, off * C : (off + 1) * C].T

    def mlp_weights(j, step):
        base, sb = MLP_AT[0] + j * (MLP_AT[1] - MLP_AT[0]), j * S_BLOCK
        cols = slice(step * CHUNK, (step + 1) * CHUNK)
        dow = nn(db_t[j], a_all[j, :, cols])
        gp[packed(base + output_row(step), CHUNK), :] = dow.T.astype(bf16)
        cross = nn(ut[...], g_all[j, :, cols])
        flag_rows = cross[TAPS * C : TAPS * C + 24]
        total = flag_rows[16:17]
        dhb = total
        weight = hw[j, :, cols].astype(f32)
        dweight = jnp.zeros((C, CHUNK), f32)
        b = hb[pl.ds(j, 1), cols]
        for off in range(TAPS):
            piece = cross[off * C : (off + 1) * C]
            factor = mk[off, pl.ds(j, 1), cols]
            flag = flag_rows[off : off + 1]
            dweight = dweight + piece * (factor + (1.0 if off == 4 else 0.0))
            dk = col_sum(piece * weight) + b * flag
            dhb = dhb + factor * flag
            for s in range(CHUNK // C):
                tile = step * (CHUNK // C) + s
                put(sb + S_MK + 16 * tile + off, dk[:, s * C : (s + 1) * C])
        for s in range(CHUNK // C):
            tile = step * (CHUNK // C) + s
            part = slice(s * C, (s + 1) * C)
            put(sb + S_HB + tile, dhb[:, part])
            put(sb + S_MB + tile, total[:, part])
            gp[packed(base + hidden_row(tile), C), :] = dweight[:, part].astype(bf16)

    def attention_backward(j):
        base, sb = ATT_AT[j], j * S_BLOCK

        def first(ts):
            grad = (xs[ts, :] * scaled(ts, 2 * j)).astype(bf16)
            db[ts, :] = grad
            return [folded(grad.astype(f32))]

        (small[sb + S_PB : sb + S_PB + 1, :],) = tiles(first)
        dproj = jnp.zeros((C, C), f32)
        kernel = jnp.concatenate([lk[j, :, 0, :], lk[j, :, 1, :]], axis=1)
        dkernel = [jnp.zeros((1, C), f32) for _ in range(9)]
        dbias = jnp.zeros((1, C), f32)
        for i in range(n):
            span = slice(i * TOK, (i + 1) * TOK)
            dproj = dproj + nn(o_t[j, i], db[span, :])
            do = nt(db[span, :], pw[j]).astype(bf16)
            dprobs = nt(vbd[j, i], do)
            dvals = nn(pt[j, i], do)
            for low, top in SEGS:
                for c0 in range(0, TOK, 128):
                    c1 = min(c0 + 128, TOK)
                    weight = pt[j, i, low:top, c0:c1].astype(f32)
                    dweight = dprobs[low:top, c0:c1]
                    dot = jnp.sum(weight * dweight, axis=0, keepdims=True)
                    pt[j, i, low:top, c0:c1] = (weight * (dweight - dot)).astype(bf16)
            dkeys = nn(pt[j, i], q_a[j, span, :]) * ROOT
            dq = tn(kb[j, i], pt[j, i]) * ROOT
            o_n[span, :] = dq.T.astype(bf16)
            for t in range(2):
                dk = jnp.zeros((CELLS[t], C), f32)
                dv = jnp.zeros((CELLS[t], C), f32)
                for h in (2 * t, 2 * t + 1):
                    dk = dk + jnp.where(head_lanes(h), dkeys[slice(*SEGS[h])], 0.0)
                    dv = dv + jnp.where(head_lanes(h), dvals[slice(*SEGS[h])], 0.0)
                w = wv[j, cell_spans(t)[i], :]
                dw = dv
                for off in range(9):
                    by = near_shift(t, off)
                    part = dv * near[off, place_span[t], :]
                    moved = pltpu.roll(w, (CELLS[t] - by) % CELLS[t], 0) if by else w
                    dkernel[off] = dkernel[off] + col_sum(part * moved)
                    part = part * kernel[off : off + 1]
                    dw = dw + (pltpu.roll(part, by, 0) if by else part)
                dw = dw * kmask[i, place_span[t], :]
                dbias = dbias + col_sum(dw)
                if t == 0:
                    dkeyval = dk + pltpu.roll(dw, 64, 1)
                else:
                    dkeyval = pltpu.roll(dk, 64, 1) + dw
                wv[j, cell_spans(t)[i], :] = dkeyval
        if j == 0:
            move((0, 2))
        gp[base + R_PROJ : base + R_PROJ + C, :] = dproj.astype(bf16)
        small[sb + S_VB : sb + S_VB + 1, :] = dbias
        for off in range(9):
            small[sb + S_LK + off : sb + S_LK + off + 1, :] = dkernel[off]
        base_perm = 0
        for t, (ref, weight) in enumerate(((p4, p4w), (p2, p2w))):
            span = cells_all(t)
            dkeyval = wv[j, span, :].astype(bf16)
            at = base + R_KV + t * C
            gp[at : at + C, :] = tn(kin[j, span, :], dkeyval).astype(bf16)
            dy = nt(dkeyval, kvw[j, t]) * ge_p[j, span, :]
            xhat = xh_p[j, span, :]
            small[sb + S_GAIN + 1 + t : sb + S_GAIN + 2 + t, :] = col_sum(dy * xhat)
            small[sb + S_SHIFT + 1 + t : sb + S_SHIFT + 2 + t, :] = col_sum(dy)
            dpool = norm_back(dy, xhat, sc_p[j, span, :], row(ng, j, 1 + t)).astype(bf16)
            at = base + (R_P4, R_P2)[t]
            taps = STRIDES[t] ** 2
            gp[at : at + taps * C, :] = tn(ref[j], dpool).astype(bf16)
            back = nt(dpool, weight[j]).astype(bf16)
            for k in range(taps):
                for i in range(n):
                    pc[base_perm : base_perm + CELLS[t], i * C : (i + 1) * C] = back[
                        i * CELLS[t] : (i + 1) * CELLS[t], k * C : (k + 1) * C
                    ]
                base_perm += CELLS[t]
        at = base + R_Q
        gp[at : at + C, :] = tn(u_a[j], o_n[...]).astype(bf16)
        if j == 1:
            all_here()
            move((0, 0))
        else:
            move((1, 0))
        spread = nn(perm_t[...], pc[...])
        for i in range(n):
            span = slice(i * TOK, (i + 1) * TOK)
            back = nt(o_n[span, :], qw[j])
            acc[0, span, :] = back + spread[:, i * C : (i + 1) * C] * valid[span, :]

        def last(ts):
            du = acc[0, ts, :]
            xhat = xh_a[j, ts, :]
            back = norm_back(du, xhat, sc[j, ts, 0:1], row(ng, j, 0))
            xs[ts, :] = (xs[ts, :] + back).astype(bf16).astype(f32)
            return [folded(o_n[ts, :].astype(f32)), folded(du * xhat), folded(du)]

        bias, gain, shift = tiles(last)
        small[sb + S_QB : sb + S_QB + 1, :] = bias
        small[sb + S_GAIN : sb + S_GAIN + 1, :] = gain
        small[sb + S_SHIFT : sb + S_SHIFT + 1, :] = shift

    def forward(j, carry):
        attention_forward(j)
        mlp_forward(j)
        return carry

    for made in late:
        made.wait()
    lax.fori_loop(0, BLOCKS, forward, 0)
    out_st[...] = xs[...].astype(bf16)
    leave(out_st, out_ref)
    xs[...] = cot_ref[...].astype(f32)
    mlp_backward(1)
    attention_backward(1)
    mlp_backward(0)
    attention_backward(0)
    dx_st[...] = xs[...].astype(bf16)
    leave(dx_st, dx_ref)

    def weights(k, carry):
        j = BLOCKS - 1 - k
        mlp_turn(j)
        move_if(k == 0, (1, 1), (0, 3))
        move_if(k == 1, (2, 1))
        mlp_weights(j, 0)
        mlp_weights(j, 1)
        move_if(k == 1, (1, 3))
        mlp_weights(j, 2)
        move_if(k == 1, (3, 0), (0, 5))
        mlp_weights(j, 3)
        move_if(k == 0, (2, 0), (0, 4), (1, 2))
        return carry

    lax.fori_loop(0, BLOCKS, weights, 0)
    gp[R_SMALL:, :] = small[...].astype(bf16)
    move((4, 0), (3, 1), (2, 2), (0, 6), (4, 1), (1, 4), (3, 2), (2, 3), (4, 2), (3, 3), (2, 4))
    move((1, 5), (4, 3), (3, 4), (1, 6), (4, 4), (2, 5), (2, 6), (3, 5), (4, 5), (3, 6), (4, 6))
    for piece in pieces:
        piece.drain()
    for made in leaving:
        made.wait()


def compute(own, images, grid_size, keep_mask, x, cot, weights):
    segments, pairs = lax.axis_size("segment"), lax.axis_size("dp") // 2
    inner = min(pairs, 4)
    sizes = (segments, inner, pairs // inner)
    n = images
    rows = n * TOK
    cells = n * sum(CELLS)
    vmem = pl.BlockSpec(memory_space=pltpu.VMEM)
    smem = pl.BlockSpec(memory_space=pltpu.SMEM)
    consts = (jnp.asarray(patch_tokens()), jnp.asarray(cell_places()))
    B = BLOCKS
    scratch = [
        pltpu.VMEM((rows, C), f32),
        pltpu.VMEM((rows, C), f32),
        pltpu.VMEM((TOK, n * C), bf16),
        pltpu.VMEM((B, rows, UW), bf16),
        pltpu.VMEM((UW, rows), bf16),
        pltpu.VMEM((B, UW, FF), bf16),
        pltpu.VMEM((C, FF), f32),
        pltpu.VMEM((B, rows, C), f32),
        pltpu.VMEM((B, rows, C), f32),
        pltpu.VMEM((B, rows, C), f32),
        pltpu.VMEM((B, rows, C), bf16),
        pltpu.VMEM((B, rows, C), bf16),
        pltpu.VMEM((B, n * CELLS[0], 16 * C), bf16),
        pltpu.VMEM((B, n * CELLS[1], 4 * C), bf16),
        pltpu.VMEM((B, cells, C), f32),
        pltpu.VMEM((B, cells, C), f32),
        pltpu.VMEM((B, cells, C), f32),
        pltpu.VMEM((B, cells, C), bf16),
        pltpu.VMEM((B, cells, C), f32),
        pltpu.VMEM((B, n, KEYS, C), bf16),
        pltpu.VMEM((B, n, KEYS, C), bf16),
        pltpu.VMEM((B, n, KEYS, TOK), bf16),
        pltpu.VMEM((B, n, C, TOK), bf16),
        pltpu.VMEM((rows, C), bf16),
        pltpu.VMEM((B, rows, FF), bf16),
        pltpu.VMEM((B, rows, FF), bf16),
        pltpu.VMEM((rows, C), bf16),
        pltpu.VMEM((B, C, rows), bf16),
        pltpu.VMEM((3, rows, C), f32),
        pltpu.VMEM((n, sum(CELLS), C), f32),
        pltpu.VMEM((9, sum(CELLS), C), f32),
        pltpu.VMEM((ROWS - R_SMALL, C), f32),
        pltpu.VMEM((PERM, n * C), bf16),
        pltpu.SMEM((n, 2 * BLOCKS), f32),
        pltpu.VMEM(cot.shape, bf16),
        pltpu.VMEM(weights[HW].shape, bf16),
        pltpu.VMEM(weights[P4].shape, bf16),
        pltpu.VMEM(weights[P2].shape, bf16),
        pltpu.VMEM(weights[OW].shape, bf16),
        pltpu.VMEM((PERM, TOK), bf16),
        pltpu.VMEM((TOK, PERM), bf16),
        pltpu.VMEM((rows, C), bf16),
        pltpu.VMEM((rows, C), bf16),
        pltpu.SemaphoreType.DMA((7 + len(PIECES),)),
        pltpu.VMEM((ROWS, C), bf16),
    ] + sum_scratch(sizes)
    anywhere = pl.BlockSpec(memory_space=pl.ANY)
    operands = [vmem] * (2 + len(weights) + len(consts))
    for place in (1, 2 + HW, 2 + P4, 2 + P2, 2 + OW):
        operands[place] = anywhere
    return pl.pallas_call(
        functools.partial(compute_kernel, own, images, sizes),
        out_shape=(
            jax.ShapeDtypeStruct((rows, C), bf16),
            jax.ShapeDtypeStruct((rows, C), bf16),
            jax.ShapeDtypeStruct((ROWS, C), bf16),
        ),
        in_specs=[smem, smem] + operands,
        out_specs=(anywhere,) * 3,
        scratch_shapes=scratch,
        compiler_params=pltpu.CompilerParams(
            collective_id=0, has_side_effects=True, vmem_limit_bytes=63 * 2**20
        ),
        name="compute",
    )(grid_size, keep_mask, x, cot, *weights, *consts)


def unpack_kernel(att, mlp, rest, out_in, dx_in, *refs):
    out_ref, dx_ref = refs[:2]
    gain, shift, qw, qb, p4, p2, kvw, vb, lk, pw, pb, hw, hb, mk, mb, ow, ob = refs[2:]
    out_ref[...] = out_in[...]
    dx_ref[...] = dx_in[...]
    p4[0] = att[R_P4:R_P2, :].astype(f32)
    p2[0] = att[R_P2:R_KV, :].astype(f32)
    for t in range(2):
        kvw[0, t] = att[R_KV + t * C : R_KV + (t + 1) * C, :].astype(f32)
    qw[0] = att[R_Q:R_PROJ, :].astype(f32)
    pw[0] = att[R_PROJ:R_ATT, :].astype(f32)
    for s in range(FF // C):
        hw[0, :, s * C : (s + 1) * C] = mlp[hidden_row(s) : hidden_row(s) + C, :].astype(f32)
    for step in range(FF // CHUNK):
        at = output_row(step)
        ow[0, step * CHUNK : (step + 1) * CHUNK, :] = mlp[at : at + CHUNK, :].astype(f32)

    @pl.when(pl.program_id(0) == BLOCKS - 1)
    def _():
        for j in range(BLOCKS):
            sb = j * S_BLOCK
            head = rest[sb : sb + 48, :].astype(f32)
            gain[j] = head[S_GAIN : S_GAIN + 4]
            shift[j] = head[S_SHIFT : S_SHIFT + 4]
            qb[j : j + 1, :] = head[S_QB : S_QB + 1]
            vb[j, 0:1, :] = head[S_VB : S_VB + 1, 0:64]
            vb[j, 1:2, :] = head[S_VB : S_VB + 1, 64:128]
            pb[j : j + 1, :] = head[S_PB : S_PB + 1]
            ob[j : j + 1, :] = head[S_OB : S_OB + 1]
            lk[j, :, 0, :] = head[S_LK : S_LK + 9, 0:64]
            lk[j, :, 1, :] = head[S_LK : S_LK + 9, 64:128]
            for s in range(FF // C):
                part = slice(s * C, (s + 1) * C)
                hb[j : j + 1, part] = head[S_HB + s : S_HB + s + 1]
                mb[j : j + 1, part] = head[S_MB + s : S_MB + s + 1]
                at = sb + S_MK + 16 * s
                mk[:, j, part] = rest[at : at + 16, :].astype(f32)[0:9]


def unpack(packed, outputs, input_grad, weights):
    streams = (jax.ShapeDtypeStruct(outputs.shape, bf16),) * 2
    by_block = {QW, P4, P2, KVW, PW, HW, OW}
    rest = ROWS - R_SMALL
    stream = pl.BlockSpec((outputs.shape[0] // BLOCKS, C), lambda k: (k, 0))
    specs = []
    for place, w in enumerate(weights):
        if place in by_block:
            zeros = (0,) * (w.ndim - 1)
            specs.append(pl.BlockSpec((1,) + w.shape[1:], lambda k, z=zeros: (BLOCKS - 1 - k,) + z))
        else:
            zeros = (0,) * w.ndim
            specs.append(pl.BlockSpec(w.shape, lambda k, z=zeros: z))
    return pl.pallas_call(
        unpack_kernel,
        out_shape=streams + tuple(jax.ShapeDtypeStruct(w.shape, f32) for w in weights),
        grid=(BLOCKS,),
        in_specs=[
            pl.BlockSpec((R_ATT, C), lambda k: (k, 0)),
            pl.BlockSpec((R_MLP, C), lambda k: (MLP_AT[BLOCKS - 1] // R_MLP + k, 0)),
            pl.BlockSpec((rest, C), lambda k: (R_SMALL // rest, 0)),
            stream,
            stream,
        ],
        out_specs=(stream, stream) + tuple(specs),
        compiler_params=pltpu.CompilerParams(vmem_limit_bytes=63 * 2**20),
        name="unpack",
    )(packed, packed, packed, outputs, input_grad)


def on_device(inputs, grid_size, keep_mask, cotangent, *weights):
    own, per = inputs.shape[:2]
    images = own * per
    flat = (images * TOK, C)
    turned = list(weights)
    turned[LK] = jnp.transpose(turned[LK], (0, 2, 1, 3))
    turned[MK] = jnp.transpose(turned[MK], (1, 0, 2))
    outputs, input_grad, packed = compute(
        own,
        images,
        jnp.transpose(grid_size, (1, 2, 0)),
        jnp.transpose(keep_mask, (1, 2, 0)),
        inputs.reshape(flat),
        cotangent.reshape(flat),
        turned,
    )
    outputs, input_grad, *grads = unpack(packed, outputs, input_grad, turned)
    grads[LK] = jnp.transpose(grads[LK], (0, 2, 1, 3))
    grads[MK] = jnp.transpose(grads[MK], (1, 0, 2))
    return (outputs.reshape(inputs.shape), input_grad.reshape(inputs.shape)) + tuple(grads)


def solution(mesh):
    stream = P("segment", "dp", None, None)
    picked = P(None, "dp", None)
    return jax.shard_map(
        on_device,
        mesh=mesh,
        in_specs=(stream, picked, picked, stream) + (P(),) * 17,
        out_specs=(stream, stream) + (P(),) * 17,
        check_vma=False,
    )
```

```python
import functools

import jax
import jax.numpy as jnp
import numpy as np
from jax import lax
from jax.experimental import pallas as pl
from jax.experimental.pallas import tpu as pltpu
from jax.sharding import PartitionSpec as P

GRID = 24
TOK = GRID * GRID
C = 128
FF = 1024
HEAD = 32
BLOCKS = 2
SIDES = (6, 12)
STRIDES = (4, 2)
CELLS = (48, 144)
SEGS = ((0, 48), (48, 96), (96, 240), (240, 384))
KEYS = 384
PERM = 16 * 48 + 4 * 144
TAPS = 9
UW = TAPS * C + C
CHUNK = 512
TILE = 96

R_P4, R_P2, R_KV, R_Q, R_PROJ, R_ATT = 0, 2048, 2560, 2816, 2944, 3072
R_MLP = 2048
ATT_AT = (R_ATT, 0)
MLP_AT = (2 * R_ATT + R_MLP, 2 * R_ATT)
S_GAIN, S_SHIFT, S_QB, S_VB, S_PB, S_OB, S_LK, S_HB, S_MB, S_MK, S_BLOCK = (
    0,
    4,
    8,
    9,
    10,
    11,
    16,
    32,
    40,
    48,
    192,
)
R_SMALL = BLOCKS * (R_ATT + R_MLP)
ROWS = R_SMALL + 512
PIECES = (
    (ATT_AT[1], R_ATT),
    (ATT_AT[0], R_ATT),
    (MLP_AT[1], R_MLP),
    (MLP_AT[0], R_MLP // 2),
    (MLP_AT[0] + R_MLP // 2, R_MLP // 2 + ROWS - R_SMALL),
)

QW, P4, P2, KVW, LK, PW, HW, MK, OW = 2, 4, 5, 6, 8, 9, 11, 13, 15

epsilon = 1e-06
keep_rate = 0.8
ROOT = HEAD**-0.5
LOG2E = 1.4426950408889634
f32, bf16 = jnp.float32, jnp.bfloat16


def hidden_row(tile):
    return tile // (CHUNK // C) * 2 * CHUNK + tile % (CHUNK // C) * C


def output_row(step):
    return step * 2 * CHUNK + CHUNK


def patch_tokens():
    tokens = np.full((8, PERM), -1.0, np.float32)
    base = 0
    for stride, side, cells in zip(STRIDES, SIDES, CELLS):
        for row_off in range(stride):
            for col_off in range(stride):
                for a in range(side):
                    for b in range(side):
                        token = (a * stride + row_off) * GRID + b * stride + col_off
                        tokens[:, base + a * side + b] = token
                base += cells
    return tokens


def cell_places():
    places = np.full((2, sum(CELLS), 128), 99.0, np.float32)
    base = 0
    for side, cells in zip(SIDES, CELLS):
        for a in range(side):
            for b in range(side):
                places[0, base + a * side + b] = a
                places[1, base + a * side + b] = b
        base += cells
    return places


def nn(left, right):
    return jnp.dot(left, right, preferred_element_type=f32)


def nt(left, right):
    return lax.dot_general(left, right, (((1,), (1,)), ((), ())), preferred_element_type=f32)


def tn(left, right):
    return lax.dot_general(left, right, (((0,), (0,)), ((), ())), preferred_element_type=f32)


def gelu_parts(m):
    size = jnp.abs(m)
    t = pl.reciprocal(1.0 + (0.3275911 * 0.5**0.5) * size, approx=True)
    e = jnp.exp2(m * (m * (-0.5 * LOG2E)))
    poly = 0.5 * 1.061405429
    for coef in (-1.453152027, 1.421413741, -0.284496736, 0.254829592):
        poly = poly * t + 0.5 * coef
    poly = poly * t
    tail = poly * e
    slope = (poly - size * 0.3989422804014327) * e
    return jnp.maximum(m, 0.0) - size * tail, jnp.where(m >= 0, 1.0 - slope, slope)


def norm_parts(x):
    centred = x - jnp.mean(x, axis=-1, keepdims=True)
    scale = lax.rsqrt(jnp.mean(centred * centred, axis=-1, keepdims=True) + epsilon)
    return centred * scale, scale


def norm_back(du, xhat, scale, gain):
    dxhat = du * gain
    first = jnp.mean(dxhat, axis=-1, keepdims=True)
    second = jnp.mean(dxhat * xhat, axis=-1, keepdims=True)
    return scale * (dxhat - first - xhat * second)


def col_sum(x):
    return jnp.sum(x, axis=0, keepdims=True)


def folded(x):
    return jnp.sum(x.reshape(-1, 8, x.shape[-1]), axis=0)


class Summed:
    STEPS = 7

    def __init__(self, place, piece, base, count, refs):
        self.seg, self.dp, self.segments, self.inner, self.outer = place
        self.piece, self.base = piece, base
        (
            self.src,
            self.half_in,
            self.quarter_in,
            self.part_in,
            self.whole_in,
            self.own,
            self.total,
            self.send,
            self.recv,
        ) = refs
        self.core, rest = self.dp % 2, self.dp // 2
        self.part, self.group = rest % self.inner, rest // self.inner
        self.half = count // 2
        self.quarter = self.half // self.segments
        self.share = self.quarter // self.inner
        quarters, shares = (self.segments - 1) * self.quarter, (self.inner - 1) * self.share
        self.moved = (self.half, quarters, shares, shares, quarters, self.half)
        self.at_quarter = self.seg * self.quarter
        self.at_share = self.at_quarter + self.part * self.share

    def span(self, start, size):
        return pl.ds(pl.multiple_of(start, 16), size)

    def device(self, seg=None, core=None, part=None, group=None):
        seg = self.seg if seg is None else seg
        core = self.core if core is None else core
        part = self.part if part is None else part
        group = self.group if group is None else group
        return (seg, (group * self.inner + part) * 2 + core)

    def copy(self, k, src, dst, device):
        return pltpu.make_async_remote_copy(
            src_ref=src,
            dst_ref=dst,
            send_sem=self.send.at[self.piece],
            recv_sem=self.recv.at[self.piece, k],
            device_id=device,
            device_id_type=pl.DeviceIdType.MESH,
        )

    def counted(self, k, count):
        ref = self.total.at[pl.ds(0, count), :]
        return self.copy(k, ref, ref, self.device(core=1 - self.core))

    def step(self, k):
        if k > 0:
            self.counted(k - 1, self.moved[k - 1]).wait_recv()
            self.gather(k)
        if k + 1 < self.STEPS:
            self.depart(k)

    def drain(self):
        count = sum(self.moved) + (self.outer - 1) * self.share
        self.counted(0, count).wait_send()

    def depart(self, k):
        half = self.base // 2
        mine = self.base + self.core * self.half
        if k == 0:
            src = self.src.at[self.span(self.base + (1 - self.core) * self.half, self.half), :]
            dst = self.half_in.at[self.span(half, self.half), :]
            self.copy(k, src, dst, self.device(core=1 - self.core)).start()
        elif k == 1:
            at = self.span(half // self.segments, self.quarter)
            for d in range(1, self.segments):
                to = self.seg ^ d
                src = self.own.at[self.span(half + to * self.quarter, self.quarter), :]
                dst = self.quarter_in.at[d - 1, at, :]
                self.copy(k, src, dst, self.device(seg=to)).start()
        elif k == 2:
            at = self.span(self.share_in(), self.share)
            for d in range(1, self.inner):
                to = self.part ^ d
                start = half + self.at_quarter + to * self.share
                src = self.own.at[self.span(start, self.share), :]
                self.copy(k, src, self.part_in.at[d - 1, at, :], self.device(part=to)).start()
        elif k == 3:
            ref = self.total.at[self.span(mine + self.at_share, self.share), :]
            for d in range(1, self.inner):
                self.copy(k, ref, ref, self.device(part=self.part ^ d)).start()
        elif k == 4:
            ref = self.total.at[self.span(mine + self.at_quarter, self.quarter), :]
            for d in range(1, self.segments):
                self.copy(k, ref, ref, self.device(seg=self.seg ^ d)).start()
        else:
            ref = self.total.at[self.span(mine, self.half), :]
            self.copy(k, ref, ref, self.device(core=1 - self.core)).start()

    def share_in(self):
        return self.base // 2 // self.segments // self.inner

    def gather(self, k):
        half = self.base // 2
        if k == 1:
            first = (self.src, self.base + self.core * self.half)
            self.add((self.own, half), first, [(self.half_in, half)], self.half)
        elif k == 2:
            mine = (self.own, half + self.at_quarter)
            at = half // self.segments
            received = [(self.quarter_in.at[d], at) for d in range(self.segments - 1)]
            self.add(mine, mine, received, self.quarter)
        elif k == 3:
            received = [(self.part_in.at[d], self.share_in()) for d in range(self.inner - 1)]
            mine = (self.own, half + self.at_share)
            into = (self.total, self.base + self.core * self.half + self.at_share)
            if self.outer > 1:
                self.add(mine, mine, received, self.share)
                slot = self.STEPS - 1
                src = self.own.at[self.span(mine[1], self.share), :]
                at = self.span(self.share_in(), self.share)
                for d in range(1, self.outer):
                    to = self.device(group=self.group ^ d)
                    self.copy(slot, src, self.whole_in.at[d - 1, at, :], to).start()
                self.counted(slot, (self.outer - 1) * self.share).wait_recv()
                received = [(self.whole_in.at[d], self.share_in()) for d in range(self.outer - 1)]
            self.add(into, mine, received, self.share)

    def add(self, dst, first, others, count):
        step = next(size for size in (128, 96, 80, 64, 48, 32, 16) if count % size == 0)

        def body(t, carry):
            at = t * step
            total = first[0][self.span(first[1] + at, step), :].astype(f32)
            for ref, start in others:
                total = total + ref[self.span(start + at, step), :].astype(f32)
            dst[0][self.span(dst[1] + at, step), :] = total.astype(bf16)
            return carry

        lax.fori_loop(0, count // step, body, 0)


def greet(seg, dp, segments, inner, outer):
    barrier = pltpu.get_barrier_semaphore()
    core, part, group = dp % 2, dp // 2 % inner, dp // 2 // inner
    peers = [(seg, dp + 1 - 2 * core)]
    peers += [(seg ^ d, dp) for d in range(1, segments)]
    peers += [(seg, (group * inner + (part ^ d)) * 2 + core) for d in range(1, inner)]
    peers += [(seg, ((group ^ d) * inner + part) * 2 + core) for d in range(1, outer)]
    for peer in peers:
        pl.semaphore_signal(
            barrier, inc=1, device_id=peer, device_id_type=pl.DeviceIdType.MESH
        )
    return lambda: pl.semaphore_wait(barrier, len(peers))


def sum_scratch(sizes):
    segments, inner, outer = sizes
    quarter = ROWS // 2 // segments
    share = quarter // inner
    return [
        pltpu.VMEM((ROWS // 2, C), bf16),
        pltpu.VMEM((segments - 1, quarter, C), bf16),
        pltpu.VMEM((inner - 1, share, C), bf16),
        pltpu.VMEM((max(outer - 1, 1), share, C), bf16),
        pltpu.VMEM((ROWS // 2, C), bf16),
        pltpu.VMEM((ROWS, C), bf16),
        pltpu.SemaphoreType.DMA((len(PIECES),)),
        pltpu.SemaphoreType.DMA((len(PIECES), Summed.STEPS)),
    ]


def compute_kernel(
    own,
    images,
    sizes,
    grid_ref,
    keep_ref,
    x_ref,
    cot_in,
    ng,
    ns,
    qw,
    qb,
    p4w_in,
    p2w_in,
    kvw,
    vb,
    lk,
    pw,
    pb,
    hw_in,
    hb,
    mk,
    mb,
    ow_in,
    ob,
    tokens,
    places,
    out_ref,
    dx_ref,
    summed_ref,
    xs,
    valid,
    um,
    u_all,
    ut,
    wc,
    ex,
    xh_a,
    xh_m,
    sc,
    u_a,
    q_a,
    p4,
    p2,
    xh_p,
    sc_p,
    ge_p,
    kin,
    wv,
    kb,
    vbd,
    pt,
    o_t,
    o_n,
    a_all,
    g_all,
    db,
    db_t,
    acc,
    kmask,
    near,
    small,
    pc,
    scale_ref,
    cot_ref,
    hw,
    p4w,
    p2w,
    ow,
    perm,
    perm_t,
    out_st,
    dx_st,
    sems,
    gp,
    half_in,
    quarter_in,
    part_in,
    whole_in,
    own_part,
    total_ref,
    send,
    recv,
):
    n = images
    rows = n * TOK
    seg, dp = lax.axis_index("segment"), lax.axis_index("dp")
    all_here = greet(seg, dp, *sizes)
    late = [
        pltpu.make_async_copy(src, dst, sems.at[k])
        for k, (src, dst) in enumerate(
            ((hw_in, hw), (p4w_in, p4w), (p2w_in, p2w), (ow_in, ow), (cot_in, cot_ref))
        )
    ]
    for made in late:
        made.start()
    leaving = []

    def leave(src, dst):
        made = pltpu.make_async_copy(src, dst, sems.at[len(late) + len(leaving)])
        made.start()
        leaving.append(made)

    refs = (
        gp,
        half_in,
        quarter_in,
        part_in,
        whole_in,
        own_part,
        total_ref,
        send,
        recv,
    )
    pieces = [
        Summed((seg, dp) + sizes, p, base, count, refs) for p, (base, count) in enumerate(PIECES)
    ]

    def move(*steps):
        for p, k in steps:
            pieces[p].step(k)
            if k + 1 == Summed.STEPS:
                rows_of = pl.ds(PIECES[p][0], PIECES[p][1])
                leave(total_ref.at[rows_of, :], summed_ref.at[rows_of, :])

    def move_if(now, *steps):
        pl.when(now)(lambda: move(*steps))

    lane = lax.broadcasted_iota(jnp.int32, (8, 128), 1)[0:1]

    def head_lanes(h):
        return (lane >= h * HEAD) & (lane < (h + 1) * HEAD)

    def tiles(fn, step=TILE):
        sums = None
        for start in range(0, rows, step):
            got = fn(slice(start, start + step))
            if got is not None:
                sums = got if sums is None else [x + y for x, y in zip(sums, got)]
        return None if sums is None else [col_sum(x) for x in sums]

    def row(ref, j, k=None):
        return ref[j, pl.ds(k, 1), :] if k is not None else ref[pl.ds(j, 1), :]

    def put(at, value):
        small[pl.ds(at, 1), :] = value

    def packed(start, count):
        return pl.ds(pl.multiple_of(start, 128), count)

    def shifted_rows(v, by):
        if by == 0:
            return v
        pad = jnp.zeros((abs(by), v.shape[1]), v.dtype)
        if by > 0:
            return jnp.concatenate([v[by:], pad], axis=0)
        return jnp.concatenate([pad, v[:by]], axis=0)

    col = lax.broadcasted_iota(jnp.int32, (GRID, GRID, 128), 1).reshape(TOK, 128)

    def taps_of(v):
        left = jnp.where(col > 0, pltpu.roll(v, 1, 0), 0.0)
        right = jnp.where(col < GRID - 1, pltpu.roll(v, TOK - 1, 0), 0.0)
        for row_off in range(3):
            for col_off, piece in enumerate((left, v, right)):
                yield row_off * 3 + col_off, shifted_rows(piece, (row_off - 1) * GRID)

    small[...] = jnp.zeros_like(small)
    sizes = []
    lane_row = lax.broadcasted_iota(jnp.int32, (TOK, 128), 1)
    tap = lane % 32
    down, across_by = tap // 3 - 1, tap % 3 - 1
    tap_lane = (tap < TAPS) & (lane < 64)
    for i in range(n):
        m_id, d_id = seg * own + i // (n // own), i % (n // own)
        high, wide = grid_ref[d_id, 0, m_id], grid_ref[d_id, 1, m_id]
        sizes.append((high, wide))
        line = lax.broadcasted_iota(jnp.int32, (GRID, GRID, 128), 0).reshape(TOK, 128)
        good = jnp.where((line < high) & (col < wide), 1.0, 0.0)
        valid[i * TOK : (i + 1) * TOK, :] = good
        for k in range(2 * BLOCKS):
            kept = keep_ref[d_id, k, m_id].astype(f32) / keep_rate
            scale_ref[i, k] = kept
        near_row, near_col = line + down, col + across_by
        there = (near_row >= 0) & (near_row < high) & (near_col >= 0) & (near_col < wide)
        ones = (lane_row == 16) | (lane_row == 48)
        flags = jnp.where(ones | (there & tap_lane), 1.0, 0.0)
        for j in range(BLOCKS):
            u_all[j, i * TOK : (i + 1) * TOK, TAPS * C :] = flags.astype(bf16)
        base = 0
        for t in range(2):
            span = slice(base, base + CELLS[t])
            tall = (high + STRIDES[t] - 1) // STRIDES[t]
            across = (wide + STRIDES[t] - 1) // STRIDES[t]
            inside = (places[0, span, :] < tall.astype(f32)) & (
                places[1, span, :] < across.astype(f32)
            )
            kmask[i, span, :] = jnp.where(inside, 1.0, 0.0)
            base += CELLS[t]
    base = 0
    for t in range(2):
        span = slice(base, base + CELLS[t])
        a, b = places[0, span, :], places[1, span, :]
        for off in range(9):
            dr, dc = float(off // 3 - 1), float(off % 3 - 1)
            top = float(SIDES[t])
            ok = (a + dr >= 0) & (a + dr < top) & (b + dc >= 0) & (b + dc < top)
            near[off, span, :] = jnp.where(ok, 1.0, 0.0)
        base += CELLS[t]

    base = start = 0
    for t in range(2):
        span, stride = slice(start, start + CELLS[t]), STRIDES[t]
        corner = places[0, span, :] * float(stride * GRID) + places[1, span, :] * float(stride)
        for k in range(stride * stride):
            token = corner + float(k // stride * GRID + k % stride)
            for c0 in range(0, TOK, 128):
                width = min(128, TOK - c0)
                here = lax.broadcasted_iota(jnp.int32, (CELLS[t], width), 1).astype(f32) + float(c0)
                block = jnp.where(token[:, :width] == here, 1.0, 0.0)
                perm[base : base + CELLS[t], c0 : c0 + width] = block.astype(bf16)
            base += CELLS[t]
        start += CELLS[t]
    for r0 in range(0, TOK, TILE):
        here = lax.broadcasted_iota(jnp.int32, (TILE, PERM), 0).astype(f32) + float(r0)
        block = jnp.where(tokens[0:1, :] == here, 1.0, 0.0)
        perm_t[r0 : r0 + TILE, :] = block.astype(bf16)

    xs[...] = x_ref[...].astype(f32)

    def scaled(span, k):
        return valid[span, :] * scale_ref[span.start // TOK, k]

    def cell_spans(t):
        start = 0 if t == 0 else n * CELLS[0]
        return [slice(start + i * CELLS[t], start + (i + 1) * CELLS[t]) for i in range(n)]

    def cells_all(t):
        return slice(0, n * CELLS[0]) if t == 0 else slice(n * CELLS[0], n * sum(CELLS))

    place_span = (slice(0, CELLS[0]), slice(CELLS[0], sum(CELLS)))
    half = lane < 64
    own_half = (half, jnp.logical_not(half))

    def near_shift(t, off):
        return ((off // 3 - 1) * SIDES[t] + off % 3 - 1) % CELLS[t]

    def attention_forward(j):
        build_wc(j)

        def first(ts):
            xhat, scale = norm_parts(xs[ts, :])
            xh_a[j, ts, :] = xhat
            sc[j, ts, 0:1] = scale
            u_a[j, ts, :] = (xhat * row(ng, j, 0) + row(ns, j, 0)).astype(bf16)

        tiles(first)
        for i in range(n):
            span = slice(i * TOK, (i + 1) * TOK)
            u = u_a[j, span, :]
            q_a[j, span, :] = (nn(u, qw[j]) + row(qb, j)).astype(bf16)
            um[:, i * C : (i + 1) * C] = (u.astype(f32) * valid[span, :]).astype(bf16)
        pc[...] = nn(perm[...], um[...]).astype(bf16)
        base = 0
        for t, ref in enumerate((p4, p2)):
            for k in range(STRIDES[t] ** 2):
                for i in range(n):
                    ref[j, i * CELLS[t] : (i + 1) * CELLS[t], k * C : (k + 1) * C] = pc[
                        base : base + CELLS[t], i * C : (i + 1) * C
                    ]
                base += CELLS[t]
        for t, (ref, weight) in enumerate(((p4, p4w), (p2, p2w))):
            xhat, scale = norm_parts(nn(ref[j], weight[j]))
            act, slope = gelu_parts(xhat * row(ng, j, 1 + t) + row(ns, j, 1 + t))
            act = act.astype(bf16)
            span = cells_all(t)
            xh_p[j, span, :] = xhat
            sc_p[j, span, :] = jnp.broadcast_to(scale, xhat.shape)
            ge_p[j, span, :] = slope
            kin[j, span, :] = act
            keyval = nn(act, kvw[j, t])
            turned = pltpu.roll(keyval, 64, 1)
            keys, vals = (keyval, turned) if t == 0 else (turned, keyval)
            bias = jnp.concatenate([row(vb, j, 0), row(vb, j, 1)], axis=1)
            kernel = jnp.concatenate([lk[j, :, 0, :], lk[j, :, 1, :]], axis=1)
            for i in range(n):
                part = slice(i * CELLS[t], (i + 1) * CELLS[t])
                w = (vals[part] + bias) * kmask[i, place_span[t], :]
                wv[j, cell_spans(t)[i], :] = w
                v = w
                for off in range(9):
                    by = near_shift(t, off)
                    moved = pltpu.roll(w, (CELLS[t] - by) % CELLS[t], 0) if by else w
                    v = v + moved * (near[off, place_span[t], :] * kernel[off : off + 1])
                for h in (2 * t, 2 * t + 1):
                    seg_rows = slice(*SEGS[h])
                    kb[j, i, seg_rows, :] = jnp.where(head_lanes(h), keys[part], 0.0).astype(bf16)
                    vbd[j, i, seg_rows, :] = jnp.where(head_lanes(h), v, 0.0).astype(bf16)
        for i in range(n):
            span = slice(i * TOK, (i + 1) * TOK)
            scores = nt(kb[j, i], q_a[j, span, :])
            for h, (low, top) in enumerate(SEGS):
                mask = kmask[i, place_span[h // 2], 0:1] > 0
                for c0 in range(0, TOK, 128):
                    c1 = min(c0 + 128, TOK)
                    s = jnp.where(mask, scores[low:top, c0:c1], -1e30)
                    e = jnp.exp2((s - jnp.max(s, axis=0, keepdims=True)) * (ROOT * LOG2E))
                    weight = e * pl.reciprocal(jnp.sum(e, axis=0, keepdims=True), approx=True)
                    pt[j, i, low:top, c0:c1] = weight.astype(bf16)
            mixed = tn(vbd[j, i], pt[j, i])
            o_t[j, i] = mixed.astype(bf16)
            o_n[span, :] = mixed.T.astype(bf16)
        for i in range(n):
            span = slice(i * TOK, (i + 1) * TOK)
            branch = nn(o_n[span, :], pw[j]) + row(pb, j)
            xs[span, :] = (xs[span, :] + scaled(span, 2 * j) * branch).astype(bf16).astype(f32)

    def build_wc(j):
        bias = row(hb, j)
        for r0 in range(0, C, 16):
            weight = hw[j, r0 : r0 + 16, :].astype(f32)
            for off in range(TAPS):
                factor = mk[off, pl.ds(j, 1), :] + (1.0 if off == 4 else 0.0)
                wc[j, off * C + r0 : off * C + r0 + 16, :] = (weight * factor).astype(bf16)
        ex[...] = jnp.zeros_like(ex)
        for off in range(TAPS + 1):
            at = off if off < TAPS else 16
            value = bias * mk[off, pl.ds(j, 1), :] if off < TAPS else bias + row(mb, j)
            high = value.astype(bf16).astype(f32)
            ex[at : at + 1, :] = high
            ex[at + 32 : at + 33, :] = value - high
        wc[j, TAPS * C :, :] = ex[...].astype(bf16)

    def mlp_forward(j):
        def first(ts):
            xhat, scale = norm_parts(xs[ts, :])
            xh_m[j, ts, :] = xhat
            sc[j, ts, 1:2] = scale
            u = (xhat * row(ng, j, 3) + row(ns, j, 3)).astype(bf16).astype(f32)
            acc[ts, :] = u * valid[ts, :]

        tiles(first)
        for i in range(n):
            span = slice(i * TOK, (i + 1) * TOK)
            for off, piece in taps_of(acc[span, :]):
                u_all[j, span, off * C : (off + 1) * C] = piece.astype(bf16)

        for i in range(n):
            field = nn(u_all[j, i * TOK : (i + 1) * TOK, :], wc[j])
            for r0 in range(0, TOK, 16):
                part = slice(i * TOK + r0, i * TOK + r0 + 16)
                for start in range(0, FF, CHUNK):
                    cols = slice(start, start + CHUNK)
                    act, slope = gelu_parts(field[r0 : r0 + 16, cols])
                    a_all[j, part, cols] = act.astype(bf16)
                    g_all[j, part, cols] = slope.astype(bf16)
        for i in range(n):
            span = slice(i * TOK, (i + 1) * TOK)
            branch = nn(a_all[j, span, :], ow[j]) + row(ob, j)
            xs[span, :] = (xs[span, :] + scaled(span, 2 * j + 1) * branch).astype(bf16).astype(f32)

    def mlp_backward(j):
        sb = j * S_BLOCK

        def first(ts):
            grad = (xs[ts, :] * scaled(ts, 2 * j + 1)).astype(bf16)
            db[ts, :] = grad
            return [folded(grad.astype(f32))]

        (small[sb + S_OB : sb + S_OB + 1, :],) = tiles(first)
        db_t[j] = db[...].T
        for i in range(n):
            span = slice(i * TOK, (i + 1) * TOK)
            da = nt(db[span, :], ow[j])
            g_all[j, span, :] = (da * g_all[j, span, :].astype(f32)).astype(bf16)
        if j == 0:
            move((0, 1))
        for i in range(n):
            span = slice(i * TOK, (i + 1) * TOK)
            moved = nt(g_all[j, span, :], wc[j, : TAPS * C, :])
            sides = []
            for col_off in range(3):
                total = None
                for row_off in range(3):
                    off = row_off * 3 + col_off
                    piece = shifted_rows(moved[:, off * C : (off + 1) * C], (1 - row_off) * GRID)
                    total = piece if total is None else total + piece
                sides.append(total)
            left = pltpu.roll(jnp.where(col > 0, sides[0], 0.0), TOK - 1, 0)
            right = pltpu.roll(jnp.where(col < GRID - 1, sides[2], 0.0), 1, 0)
            acc[span, :] = (sides[1] + left + right) * valid[span, :]

        def last(ts):
            du = acc[ts, :]
            xhat = xh_m[j, ts, :]
            back = norm_back(du, xhat, sc[j, ts, 1:2], row(ng, j, 3))
            xs[ts, :] = (xs[ts, :] + back).astype(bf16).astype(f32)
            return [folded(du * xhat), folded(du)]

        gain, shift = tiles(last)
        small[sb + S_GAIN + 3 : sb + S_GAIN + 4, :] = gain
        small[sb + S_SHIFT + 3 : sb + S_SHIFT + 4, :] = shift

    def mlp_turn(j):
        for off in range(TAPS + 1):
            ut[off * C : (off + 1) * C, :] = u_all[j, :, off * C : (off + 1) * C].T

    def mlp_weights(j, step):
        base, sb = MLP_AT[0] + j * (MLP_AT[1] - MLP_AT[0]), j * S_BLOCK
        cols = slice(step * CHUNK, (step + 1) * CHUNK)
        dow = nn(db_t[j], a_all[j, :, cols])
        gp[packed(base + output_row(step), CHUNK), :] = dow.T.astype(bf16)
        cross = nn(ut[...], g_all[j, :, cols])
        flag_rows = cross[TAPS * C : TAPS * C + 24]
        total = flag_rows[16:17]
        dhb = total
        weight = hw[j, :, cols].astype(f32)
        dweight = jnp.zeros((C, CHUNK), f32)
        b = hb[pl.ds(j, 1), cols]
        for off in range(TAPS):
            piece = cross[off * C : (off + 1) * C]
            factor = mk[off, pl.ds(j, 1), cols]
            flag = flag_rows[off : off + 1]
            dweight = dweight + piece * (factor + (1.0 if off == 4 else 0.0))
            dk = col_sum(piece * weight) + b * flag
            dhb = dhb + factor * flag
            for s in range(CHUNK // C):
                tile = step * (CHUNK // C) + s
                put(sb + S_MK + 16 * tile + off, dk[:, s * C : (s + 1) * C])
        for s in range(CHUNK // C):
            tile = step * (CHUNK // C) + s
            part = slice(s * C, (s + 1) * C)
            put(sb + S_HB + tile, dhb[:, part])
            put(sb + S_MB + tile, total[:, part])
            gp[packed(base + hidden_row(tile), C), :] = dweight[:, part].astype(bf16)

    def attention_backward(j):
        base, sb = ATT_AT[j], j * S_BLOCK

        def first(ts):
            grad = (xs[ts, :] * scaled(ts, 2 * j)).astype(bf16)
            db[ts, :] = grad
            return [folded(grad.astype(f32))]

        (small[sb + S_PB : sb + S_PB + 1, :],) = tiles(first)
        dproj = jnp.zeros((C, C), f32)
        kernel = jnp.concatenate([lk[j, :, 0, :], lk[j, :, 1, :]], axis=1)
        dkernel = [jnp.zeros((1, C), f32) for _ in range(9)]
        dbias = jnp.zeros((1, C), f32)
        for i in range(n):
            span = slice(i * TOK, (i + 1) * TOK)
            dproj = dproj + nn(o_t[j, i], db[span, :])
            do = nt(db[span, :], pw[j]).astype(bf16)
            dprobs = nt(vbd[j, i], do)
            dvals = nn(pt[j, i], do)
            for low, top in SEGS:
                for c0 in range(0, TOK, 128):
                    c1 = min(c0 + 128, TOK)
                    weight = pt[j, i, low:top, c0:c1].astype(f32)
                    dweight = dprobs[low:top, c0:c1]
                    dot = jnp.sum(weight * dweight, axis=0, keepdims=True)
                    pt[j, i, low:top, c0:c1] = (weight * (dweight - dot)).astype(bf16)
            dkeys = nn(pt[j, i], q_a[j, span, :]) * ROOT
            dq = tn(kb[j, i], pt[j, i]) * ROOT
            o_n[span, :] = dq.T.astype(bf16)
            for t in range(2):
                dk = jnp.zeros((CELLS[t], C), f32)
                dv = jnp.zeros((CELLS[t], C), f32)
                for h in (2 * t, 2 * t + 1):
                    dk = dk + jnp.where(head_lanes(h), dkeys[slice(*SEGS[h])], 0.0)
                    dv = dv + jnp.where(head_lanes(h), dvals[slice(*SEGS[h])], 0.0)
                w = wv[j, cell_spans(t)[i], :]
                dw = dv
                for off in range(9):
                    by = near_shift(t, off)
                    part = dv * near[off, place_span[t], :]
                    moved = pltpu.roll(w, (CELLS[t] - by) % CELLS[t], 0) if by else w
                    dkernel[off] = dkernel[off] + col_sum(part * moved)
                    part = part * kernel[off : off + 1]
                    dw = dw + (pltpu.roll(part, by, 0) if by else part)
                dw = dw * kmask[i, place_span[t], :]
                dbias = dbias + col_sum(dw)
                if t == 0:
                    dkeyval = dk + pltpu.roll(dw, 64, 1)
                else:
                    dkeyval = pltpu.roll(dk, 64, 1) + dw
                wv[j, cell_spans(t)[i], :] = dkeyval
        gp[base + R_PROJ : base + R_PROJ + C, :] = dproj.astype(bf16)
        small[sb + S_VB : sb + S_VB + 1, :] = dbias
        for off in range(9):
            small[sb + S_LK + off : sb + S_LK + off + 1, :] = dkernel[off]
        base_perm = 0
        for t, (ref, weight) in enumerate(((p4, p4w), (p2, p2w))):
            span = cells_all(t)
            dkeyval = wv[j, span, :].astype(bf16)
            at = base + R_KV + t * C
            gp[at : at + C, :] = tn(kin[j, span, :], dkeyval).astype(bf16)
            dy = nt(dkeyval, kvw[j, t]) * ge_p[j, span, :]
            xhat = xh_p[j, span, :]
            small[sb + S_GAIN + 1 + t : sb + S_GAIN + 2 + t, :] = col_sum(dy * xhat)
            small[sb + S_SHIFT + 1 + t : sb + S_SHIFT + 2 + t, :] = col_sum(dy)
            dpool = norm_back(dy, xhat, sc_p[j, span, :], row(ng, j, 1 + t)).astype(bf16)
            at = base + (R_P4, R_P2)[t]
            for k in range(STRIDES[t] ** 2):
                gp[at + k * C : at + (k + 1) * C, :] = tn(
                    ref[j, :, k * C : (k + 1) * C], dpool
                ).astype(bf16)
                back = nt(dpool, weight[j, k * C : (k + 1) * C, :]).astype(bf16)
                for i in range(n):
                    pc[base_perm : base_perm + CELLS[t], i * C : (i + 1) * C] = back[
                        i * CELLS[t] : (i + 1) * CELLS[t]
                    ]
                base_perm += CELLS[t]
        at = base + R_Q
        gp[at : at + C, :] = tn(u_a[j], o_n[...]).astype(bf16)
        if j == 1:
            all_here()
            move((0, 0))
        else:
            move((0, 2), (1, 0))
        spread = nn(perm_t[...], pc[...])
        for i in range(n):
            span = slice(i * TOK, (i + 1) * TOK)
            back = nt(o_n[span, :], qw[j])
            acc[span, :] = back + spread[:, i * C : (i + 1) * C] * valid[span, :]

        def last(ts):
            du = acc[ts, :]
            xhat = xh_a[j, ts, :]
            back = norm_back(du, xhat, sc[j, ts, 0:1], row(ng, j, 0))
            xs[ts, :] = (xs[ts, :] + back).astype(bf16).astype(f32)
            return [folded(o_n[ts, :].astype(f32)), folded(du * xhat), folded(du)]

        bias, gain, shift = tiles(last)
        small[sb + S_QB : sb + S_QB + 1, :] = bias
        small[sb + S_GAIN : sb + S_GAIN + 1, :] = gain
        small[sb + S_SHIFT : sb + S_SHIFT + 1, :] = shift

    def forward(j, carry):
        attention_forward(j)
        mlp_forward(j)
        return carry

    for made in late:
        made.wait()
    lax.fori_loop(0, BLOCKS, forward, 0)
    out_st[...] = xs[...].astype(bf16)
    leave(out_st, out_ref)
    xs[...] = cot_ref[...].astype(f32)
    mlp_backward(1)
    attention_backward(1)
    mlp_backward(0)
    attention_backward(0)
    dx_st[...] = xs[...].astype(bf16)
    leave(dx_st, dx_ref)

    def weights(k, carry):
        j = BLOCKS - 1 - k
        mlp_turn(j)
        move_if(k == 0, (1, 1))
        move_if(k == 1, (1, 2), (2, 1), (0, 4))
        mlp_weights(j, 0)
        move_if(k == 0, (0, 3))
        move_if(k == 1, (3, 0))
        mlp_weights(j, 1)
        move_if(k == 0, (2, 0))
        return carry

    lax.fori_loop(0, BLOCKS, weights, 0)
    gp[R_SMALL:, :] = small[...].astype(bf16)
    move((4, 0), (1, 3), (3, 1), (2, 2), (4, 1))
    move((0, 5), (3, 2), (1, 4), (0, 6), (2, 3), (4, 2), (3, 3), (2, 4), (4, 3), (1, 5), (3, 4))
    move((1, 6), (4, 4), (2, 5), (3, 5), (2, 6), (3, 6), (4, 5), (4, 6))
    for piece in pieces:
        piece.drain()
    for made in leaving:
        made.wait()


def compute(own, images, grid_size, keep_mask, x, cot, weights):
    segments, pairs = lax.axis_size("segment"), lax.axis_size("dp") // 2
    inner = min(pairs, 4)
    sizes = (segments, inner, pairs // inner)
    n = images
    rows = n * TOK
    cells = n * sum(CELLS)
    vmem = pl.BlockSpec(memory_space=pltpu.VMEM)
    smem = pl.BlockSpec(memory_space=pltpu.SMEM)
    consts = (jnp.asarray(patch_tokens()), jnp.asarray(cell_places()))
    B = BLOCKS
    scratch = [
        pltpu.VMEM((rows, C), f32),
        pltpu.VMEM((rows, C), f32),
        pltpu.VMEM((TOK, n * C), bf16),
        pltpu.VMEM((B, rows, UW), bf16),
        pltpu.VMEM((UW, rows), bf16),
        pltpu.VMEM((B, UW, FF), bf16),
        pltpu.VMEM((C, FF), f32),
        pltpu.VMEM((B, rows, C), f32),
        pltpu.VMEM((B, rows, C), f32),
        pltpu.VMEM((B, rows, C), f32),
        pltpu.VMEM((B, rows, C), bf16),
        pltpu.VMEM((B, rows, C), bf16),
        pltpu.VMEM((B, n * CELLS[0], 16 * C), bf16),
        pltpu.VMEM((B, n * CELLS[1], 4 * C), bf16),
        pltpu.VMEM((B, cells, C), f32),
        pltpu.VMEM((B, cells, C), f32),
        pltpu.VMEM((B, cells, C), f32),
        pltpu.VMEM((B, cells, C), bf16),
        pltpu.VMEM((B, cells, C), f32),
        pltpu.VMEM((B, n, KEYS, C), bf16),
        pltpu.VMEM((B, n, KEYS, C), bf16),
        pltpu.VMEM((B, n, KEYS, TOK), bf16),
        pltpu.VMEM((B, n, C, TOK), bf16),
        pltpu.VMEM((rows, C), bf16),
        pltpu.VMEM((B, rows, FF), bf16),
        pltpu.VMEM((B, rows, FF), bf16),
        pltpu.VMEM((rows, C), bf16),
        pltpu.VMEM((B, C, rows), bf16),
        pltpu.VMEM((rows, C), f32),
        pltpu.VMEM((n, sum(CELLS), C), f32),
        pltpu.VMEM((9, sum(CELLS), C), f32),
        pltpu.VMEM((ROWS - R_SMALL, C), f32),
        pltpu.VMEM((PERM, n * C), bf16),
        pltpu.SMEM((n, 2 * BLOCKS), f32),
        pltpu.VMEM(cot.shape, bf16),
        pltpu.VMEM(weights[HW].shape, bf16),
        pltpu.VMEM(weights[P4].shape, bf16),
        pltpu.VMEM(weights[P2].shape, bf16),
        pltpu.VMEM(weights[OW].shape, bf16),
        pltpu.VMEM((PERM, TOK), bf16),
        pltpu.VMEM((TOK, PERM), bf16),
        pltpu.VMEM((rows, C), bf16),
        pltpu.VMEM((rows, C), bf16),
        pltpu.SemaphoreType.DMA((7 + len(PIECES),)),
        pltpu.VMEM((ROWS, C), bf16),
    ] + sum_scratch(sizes)
    anywhere = pl.BlockSpec(memory_space=pl.ANY)
    operands = [vmem] * (2 + len(weights) + len(consts))
    for place in (1, 2 + HW, 2 + P4, 2 + P2, 2 + OW):
        operands[place] = anywhere
    return pl.pallas_call(
        functools.partial(compute_kernel, own, images, sizes),
        out_shape=(
            jax.ShapeDtypeStruct((rows, C), bf16),
            jax.ShapeDtypeStruct((rows, C), bf16),
            jax.ShapeDtypeStruct((ROWS, C), bf16),
        ),
        in_specs=[smem, smem] + operands,
        out_specs=(anywhere,) * 3,
        scratch_shapes=scratch,
        compiler_params=pltpu.CompilerParams(
            collective_id=0, has_side_effects=True, vmem_limit_bytes=63 * 2**20
        ),
        name="compute",
    )(grid_size, keep_mask, x, cot, *weights, *consts)


def unpack_kernel(att, mlp, rest, out_in, dx_in, *refs):
    out_ref, dx_ref = refs[:2]
    gain, shift, qw, qb, p4, p2, kvw, vb, lk, pw, pb, hw, hb, mk, mb, ow, ob = refs[2:]
    out_ref[...] = out_in[...]
    dx_ref[...] = dx_in[...]
    p4[0] = att[R_P4:R_P2, :].astype(f32)
    p2[0] = att[R_P2:R_KV, :].astype(f32)
    for t in range(2):
        kvw[0, t] = att[R_KV + t * C : R_KV + (t + 1) * C, :].astype(f32)
    qw[0] = att[R_Q:R_PROJ, :].astype(f32)
    pw[0] = att[R_PROJ:R_ATT, :].astype(f32)
    for s in range(FF // C):
        hw[0, :, s * C : (s + 1) * C] = mlp[hidden_row(s) : hidden_row(s) + C, :].astype(f32)
    for step in range(FF // CHUNK):
        at = output_row(step)
        ow[0, step * CHUNK : (step + 1) * CHUNK, :] = mlp[at : at + CHUNK, :].astype(f32)

    @pl.when(pl.program_id(0) == BLOCKS - 1)
    def _():
        for j in range(BLOCKS):
            sb = j * S_BLOCK
            head = rest[sb : sb + 48, :].astype(f32)
            gain[j] = head[S_GAIN : S_GAIN + 4]
            shift[j] = head[S_SHIFT : S_SHIFT + 4]
            qb[j : j + 1, :] = head[S_QB : S_QB + 1]
            vb[j, 0:1, :] = head[S_VB : S_VB + 1, 0:64]
            vb[j, 1:2, :] = head[S_VB : S_VB + 1, 64:128]
            pb[j : j + 1, :] = head[S_PB : S_PB + 1]
            ob[j : j + 1, :] = head[S_OB : S_OB + 1]
            lk[j, :, 0, :] = head[S_LK : S_LK + 9, 0:64]
            lk[j, :, 1, :] = head[S_LK : S_LK + 9, 64:128]
            for s in range(FF // C):
                part = slice(s * C, (s + 1) * C)
                hb[j : j + 1, part] = head[S_HB + s : S_HB + s + 1]
                mb[j : j + 1, part] = head[S_MB + s : S_MB + s + 1]
                at = sb + S_MK + 16 * s
                mk[:, j, part] = rest[at : at + 16, :].astype(f32)[0:9]


def unpack(packed, outputs, input_grad, weights):
    streams = (jax.ShapeDtypeStruct(outputs.shape, bf16),) * 2
    by_block = {QW, P4, P2, KVW, PW, HW, OW}
    rest = ROWS - R_SMALL
    stream = pl.BlockSpec((outputs.shape[0] // BLOCKS, C), lambda k: (k, 0))
    specs = []
    for place, w in enumerate(weights):
        if place in by_block:
            zeros = (0,) * (w.ndim - 1)
            specs.append(pl.BlockSpec((1,) + w.shape[1:], lambda k, z=zeros: (BLOCKS - 1 - k,) + z))
        else:
            zeros = (0,) * w.ndim
            specs.append(pl.BlockSpec(w.shape, lambda k, z=zeros: z))
    return pl.pallas_call(
        unpack_kernel,
        out_shape=streams + tuple(jax.ShapeDtypeStruct(w.shape, f32) for w in weights),
        grid=(BLOCKS,),
        in_specs=[
            pl.BlockSpec((R_ATT, C), lambda k: (k, 0)),
            pl.BlockSpec((R_MLP, C), lambda k: (MLP_AT[BLOCKS - 1] // R_MLP + k, 0)),
            pl.BlockSpec((rest, C), lambda k: (R_SMALL // rest, 0)),
            stream,
            stream,
        ],
        out_specs=(stream, stream) + tuple(specs),
        compiler_params=pltpu.CompilerParams(vmem_limit_bytes=63 * 2**20),
        name="unpack",
    )(packed, packed, packed, outputs, input_grad)


def on_device(inputs, grid_size, keep_mask, cotangent, *weights):
    own, per = inputs.shape[:2]
    images = own * per
    flat = (images * TOK, C)
    turned = list(weights)
    turned[LK] = jnp.transpose(turned[LK], (0, 2, 1, 3))
    turned[MK] = jnp.transpose(turned[MK], (1, 0, 2))
    outputs, input_grad, packed = compute(
        own,
        images,
        jnp.transpose(grid_size, (1, 2, 0)),
        jnp.transpose(keep_mask, (1, 2, 0)),
        inputs.reshape(flat),
        cotangent.reshape(flat),
        turned,
    )
    outputs, input_grad, *grads = unpack(packed, outputs, input_grad, turned)
    grads[LK] = jnp.transpose(grads[LK], (0, 2, 1, 3))
    grads[MK] = jnp.transpose(grads[MK], (1, 0, 2))
    return (outputs.reshape(inputs.shape), input_grad.reshape(inputs.shape)) + tuple(grads)


def solution(mesh):
    stream = P("segment", "dp", None, None)
    picked = P(None, "dp", None)
    return jax.shard_map(
        on_device,
        mesh=mesh,
        in_specs=(stream, picked, picked, stream) + (P(),) * 17,
        out_specs=(stream, stream) + (P(),) * 17,
        check_vma=False,
    )
```

```python
import functools

import jax
import jax.numpy as jnp
import numpy as np
from jax import lax
from jax.experimental import pallas as pl
from jax.experimental.pallas import tpu as pltpu
from jax.sharding import PartitionSpec as P

GRID = 24
TOK = GRID * GRID
C = 128
FF = 1024
HEAD = 32
BLOCKS = 2
SIDES = (6, 12)
STRIDES = (4, 2)
WIDTHS = (8, 12)
CELLS = (48, 144)
SEGS = ((0, 48), (48, 96), (96, 240), (240, 384))
KEYS = 384
GROUP = 4 * GRID
GROUPS = TOK // GROUP
PATCH = (8, 24)
PATCHES = 16 * PATCH[0] + 4 * PATCH[1]
TAPS = 9
UW = TAPS * C + C
CHUNK = 512
TILE = 96

R_P4, R_P2, R_KV, R_Q, R_PROJ, R_ATT = 0, 2048, 2560, 2816, 2944, 3072
R_MLP = 2048
ATT_AT = (R_ATT, 0)
MLP_AT = (2 * R_ATT + R_MLP, 2 * R_ATT)
S_GAIN, S_SHIFT, S_QB, S_VB, S_PB, S_OB, S_LK, S_HB, S_MB, S_MK, S_BLOCK = (
    0,
    4,
    8,
    9,
    10,
    11,
    16,
    32,
    40,
    48,
    192,
)
R_SMALL = BLOCKS * (R_ATT + R_MLP)
ROWS = R_SMALL + 512
PIECES = (
    (ATT_AT[1], R_ATT),
    (ATT_AT[0], R_ATT),
    (MLP_AT[1], R_MLP),
    (MLP_AT[0], R_MLP // 2),
    (MLP_AT[0] + R_MLP // 2, R_MLP // 2 + ROWS - R_SMALL),
)

QW, P4, P2, KVW, LK, PW, HW, MK, OW = 2, 4, 5, 6, 8, 9, 11, 13, 15

epsilon = 1e-06
keep_rate = 0.8
ROOT = HEAD**-0.5
LOG2E = 1.4426950408889634
f32, bf16 = jnp.float32, jnp.bfloat16


def hidden_row(tile):
    return tile // (CHUNK // C) * 2 * CHUNK + tile % (CHUNK // C) * C


def output_row(step):
    return step * 2 * CHUNK + CHUNK


def patch_matrix():
    matrix = np.zeros((PATCHES, GROUP), np.float32)
    base = 0
    for stride, side, width, count in zip(STRIDES, SIDES, WIDTHS, PATCH):
        for row_off in range(stride):
            for col_off in range(stride):
                for a in range(4 // stride):
                    for b in range(side):
                        token = (a * stride + row_off) * GRID + b * stride + col_off
                        matrix[base + a * width + b, token] = 1.0
                base += count
    return matrix


def cell_places():
    places = np.full((2, sum(CELLS), 128), 99.0, np.float32)
    base = 0
    for side, width, cells in zip(SIDES, WIDTHS, CELLS):
        for a in range(side):
            for b in range(side):
                places[0, base + a * width + b] = a
                places[1, base + a * width + b] = b
        base += cells
    return places


def nn(left, right):
    return jnp.dot(left, right, preferred_element_type=f32)


def nt(left, right):
    return lax.dot_general(left, right, (((1,), (1,)), ((), ())), preferred_element_type=f32)


def tn(left, right):
    return lax.dot_general(left, right, (((0,), (0,)), ((), ())), preferred_element_type=f32)


def gelu_parts(m):
    size = jnp.abs(m)
    t = pl.reciprocal(1.0 + (0.3275911 * 0.5**0.5) * size, approx=True)
    e = jnp.exp2(m * (m * (-0.5 * LOG2E)))
    poly = 0.5 * 1.061405429
    for coef in (-1.453152027, 1.421413741, -0.284496736, 0.254829592):
        poly = poly * t + 0.5 * coef
    poly = poly * t
    tail = poly * e
    slope = (poly - size * 0.3989422804014327) * e
    return jnp.maximum(m, 0.0) - size * tail, jnp.where(m >= 0, 1.0 - slope, slope)


def norm_parts(x):
    centred = x - jnp.mean(x, axis=-1, keepdims=True)
    scale = lax.rsqrt(jnp.mean(centred * centred, axis=-1, keepdims=True) + epsilon)
    return centred * scale, scale


def norm_back(du, xhat, scale, gain):
    dxhat = du * gain
    first = jnp.mean(dxhat, axis=-1, keepdims=True)
    second = jnp.mean(dxhat * xhat, axis=-1, keepdims=True)
    return scale * (dxhat - first - xhat * second)


def col_sum(x):
    return jnp.sum(x, axis=0, keepdims=True)


def folded(x):
    return jnp.sum(x.reshape(-1, 8, x.shape[-1]), axis=0)


class Summed:
    STEPS = 7

    def __init__(self, place, piece, base, count, refs):
        self.seg, self.dp, self.segments, self.inner, self.outer = place
        self.piece, self.base = piece, base
        (
            self.src,
            self.half_in,
            self.quarter_in,
            self.part_in,
            self.whole_in,
            self.own,
            self.total,
            self.send,
            self.recv,
        ) = refs
        self.core, rest = self.dp % 2, self.dp // 2
        self.part, self.group = rest % self.inner, rest // self.inner
        self.half = count // 2
        self.quarter = self.half // self.segments
        self.share = self.quarter // self.inner
        quarters, shares = (self.segments - 1) * self.quarter, (self.inner - 1) * self.share
        self.moved = (self.half, quarters, shares, shares, quarters, self.half)
        self.at_quarter = self.seg * self.quarter
        self.at_share = self.at_quarter + self.part * self.share

    def span(self, start, size):
        return pl.ds(pl.multiple_of(start, 16), size)

    def device(self, seg=None, core=None, part=None, group=None):
        seg = self.seg if seg is None else seg
        core = self.core if core is None else core
        part = self.part if part is None else part
        group = self.group if group is None else group
        return (seg, (group * self.inner + part) * 2 + core)

    def copy(self, k, src, dst, device):
        return pltpu.make_async_remote_copy(
            src_ref=src,
            dst_ref=dst,
            send_sem=self.send.at[self.piece],
            recv_sem=self.recv.at[self.piece, k],
            device_id=device,
            device_id_type=pl.DeviceIdType.MESH,
        )

    def counted(self, k, count):
        ref = self.total.at[pl.ds(0, count), :]
        return self.copy(k, ref, ref, self.device(core=1 - self.core))

    def step(self, k):
        if k > 0:
            self.counted(k - 1, self.moved[k - 1]).wait_recv()
            self.gather(k)
        if k + 1 < self.STEPS:
            self.depart(k)

    def drain(self):
        count = sum(self.moved) + (self.outer - 1) * self.share
        self.counted(0, count).wait_send()

    def depart(self, k):
        half = self.base // 2
        mine = self.base + self.core * self.half
        if k == 0:
            src = self.src.at[self.span(self.base + (1 - self.core) * self.half, self.half), :]
            dst = self.half_in.at[self.span(half, self.half), :]
            self.copy(k, src, dst, self.device(core=1 - self.core)).start()
        elif k == 1:
            at = self.span(half // self.segments, self.quarter)
            for d in range(1, self.segments):
                to = self.seg ^ d
                src = self.own.at[self.span(half + to * self.quarter, self.quarter), :]
                dst = self.quarter_in.at[d - 1, at, :]
                self.copy(k, src, dst, self.device(seg=to)).start()
        elif k == 2:
            at = self.span(self.share_in(), self.share)
            for d in range(1, self.inner):
                to = self.part ^ d
                start = half + self.at_quarter + to * self.share
                src = self.own.at[self.span(start, self.share), :]
                self.copy(k, src, self.part_in.at[d - 1, at, :], self.device(part=to)).start()
        elif k == 3:
            ref = self.total.at[self.span(mine + self.at_share, self.share), :]
            for d in range(1, self.inner):
                self.copy(k, ref, ref, self.device(part=self.part ^ d)).start()
        elif k == 4:
            ref = self.total.at[self.span(mine + self.at_quarter, self.quarter), :]
            for d in range(1, self.segments):
                self.copy(k, ref, ref, self.device(seg=self.seg ^ d)).start()
        else:
            ref = self.total.at[self.span(mine, self.half), :]
            self.copy(k, ref, ref, self.device(core=1 - self.core)).start()

    def share_in(self):
        return self.base // 2 // self.segments // self.inner

    def gather(self, k):
        half = self.base // 2
        if k == 1:
            first = (self.src, self.base + self.core * self.half)
            self.add((self.own, half), first, [(self.half_in, half)], self.half)
        elif k == 2:
            mine = (self.own, half + self.at_quarter)
            at = half // self.segments
            received = [(self.quarter_in.at[d], at) for d in range(self.segments - 1)]
            self.add(mine, mine, received, self.quarter)
        elif k == 3:
            received = [(self.part_in.at[d], self.share_in()) for d in range(self.inner - 1)]
            mine = (self.own, half + self.at_share)
            into = (self.total, self.base + self.core * self.half + self.at_share)
            if self.outer > 1:
                self.add(mine, mine, received, self.share)
                slot = self.STEPS - 1
                src = self.own.at[self.span(mine[1], self.share), :]
                at = self.span(self.share_in(), self.share)
                for d in range(1, self.outer):
                    to = self.device(group=self.group ^ d)
                    self.copy(slot, src, self.whole_in.at[d - 1, at, :], to).start()
                self.counted(slot, (self.outer - 1) * self.share).wait_recv()
                received = [(self.whole_in.at[d], self.share_in()) for d in range(self.outer - 1)]
            self.add(into, mine, received, self.share)

    def add(self, dst, first, others, count):
        step = next(size for size in (512, 384, 256, 192, 128, 96, 64, 48, 32, 16) if count % size == 0)

        def body(t, carry):
            at = t * step
            total = first[0][self.span(first[1] + at, step), :].astype(f32)
            for ref, start in others:
                total = total + ref[self.span(start + at, step), :].astype(f32)
            dst[0][self.span(dst[1] + at, step), :] = total.astype(bf16)
            return carry

        lax.fori_loop(0, count // step, body, 0)


def greet(seg, dp, segments, inner, outer):
    barrier = pltpu.get_barrier_semaphore()
    core, part, group = dp % 2, dp // 2 % inner, dp // 2 // inner
    peers = [(seg, dp + 1 - 2 * core)]
    peers += [(seg ^ d, dp) for d in range(1, segments)]
    peers += [(seg, (group * inner + (part ^ d)) * 2 + core) for d in range(1, inner)]
    peers += [(seg, ((group ^ d) * inner + part) * 2 + core) for d in range(1, outer)]
    for peer in peers:
        pl.semaphore_signal(
            barrier, inc=1, device_id=peer, device_id_type=pl.DeviceIdType.MESH
        )
    return lambda: pl.semaphore_wait(barrier, len(peers))


def sum_scratch(sizes):
    segments, inner, outer = sizes
    quarter = ROWS // 2 // segments
    share = quarter // inner
    return [
        pltpu.VMEM((ROWS // 2, C), bf16),
        pltpu.VMEM((segments - 1, quarter, C), bf16),
        pltpu.VMEM((inner - 1, share, C), bf16),
        pltpu.VMEM((max(outer - 1, 1), share, C), bf16),
        pltpu.VMEM((ROWS // 2, C), bf16),
        pltpu.VMEM((ROWS, C), bf16),
        pltpu.SemaphoreType.DMA((len(PIECES),)),
        pltpu.SemaphoreType.DMA((len(PIECES), Summed.STEPS)),
    ]


def compute_kernel(
    own,
    images,
    sizes,
    grid_ref,
    keep_ref,
    x_ref,
    cot_in,
    ng,
    ns,
    qw,
    qb,
    p4w_in,
    p2w_in,
    kvw,
    vb,
    lk,
    pw,
    pb,
    hw_in,
    hb,
    mk,
    mb,
    ow_in,
    ob,
    to_patches,
    from_patches,
    places,
    out_ref,
    dx_ref,
    summed_ref,
    xs,
    valid,
    um,
    u_all,
    ut,
    wc,
    ex,
    xh_a,
    xh_m,
    sc,
    u_a,
    q_a,
    p4,
    p2,
    xh_p,
    sc_p,
    ge_p,
    kin,
    wv,
    kb,
    vbd,
    pt,
    o_t,
    o_n,
    a_all,
    g_all,
    db,
    db_t,
    acc,
    kmask,
    near,
    small,
    scale_ref,
    cot_ref,
    hw,
    p4w,
    p2w,
    ow,
    out_st,
    dx_st,
    sems,
    gp,
    half_in,
    quarter_in,
    part_in,
    whole_in,
    own_part,
    total_ref,
    send,
    recv,
):
    n = images
    rows = n * TOK
    seg, dp = lax.axis_index("segment"), lax.axis_index("dp")
    all_here = greet(seg, dp, *sizes)
    late = [
        pltpu.make_async_copy(src, dst, sems.at[k])
        for k, (src, dst) in enumerate(
            ((hw_in, hw), (p4w_in, p4w), (p2w_in, p2w), (ow_in, ow), (cot_in, cot_ref))
        )
    ]
    for made in late:
        made.start()
    leaving = []

    def leave(src, dst):
        made = pltpu.make_async_copy(src, dst, sems.at[len(late) + len(leaving)])
        made.start()
        leaving.append(made)

    refs = (
        gp,
        half_in,
        quarter_in,
        part_in,
        whole_in,
        own_part,
        total_ref,
        send,
        recv,
    )
    pieces = [
        Summed((seg, dp) + sizes, p, base, count, refs) for p, (base, count) in enumerate(PIECES)
    ]

    def move(*steps):
        for p, k in steps:
            pieces[p].step(k)
            if k + 1 == Summed.STEPS:
                rows_of = pl.ds(PIECES[p][0], PIECES[p][1])
                leave(total_ref.at[rows_of, :], summed_ref.at[rows_of, :])

    def move_if(now, *steps):
        pl.when(now)(lambda: move(*steps))

    lane = lax.broadcasted_iota(jnp.int32, (8, 128), 1)[0:1]

    def head_lanes(h):
        return (lane >= h * HEAD) & (lane < (h + 1) * HEAD)

    def tiles(fn, step=TILE):
        sums = None
        for start in range(0, rows, step):
            got = fn(slice(start, start + step))
            if got is not None:
                sums = got if sums is None else [x + y for x, y in zip(sums, got)]
        return None if sums is None else [col_sum(x) for x in sums]

    def row(ref, j, k=None):
        return ref[j, pl.ds(k, 1), :] if k is not None else ref[pl.ds(j, 1), :]

    def put(at, value):
        small[pl.ds(at, 1), :] = value

    def packed(start, count):
        return pl.ds(pl.multiple_of(start, 128), count)

    def shifted_rows(v, by):
        if by == 0:
            return v
        pad = jnp.zeros((abs(by), v.shape[1]), v.dtype)
        if by > 0:
            return jnp.concatenate([v[by:], pad], axis=0)
        return jnp.concatenate([pad, v[:by]], axis=0)

    col = lax.broadcasted_iota(jnp.int32, (GRID, GRID, 128), 1).reshape(TOK, 128)

    def taps_of(v):
        left = jnp.where(col > 0, pltpu.roll(v, 1, 0), 0.0)
        right = jnp.where(col < GRID - 1, pltpu.roll(v, TOK - 1, 0), 0.0)
        for row_off in range(3):
            for col_off, piece in enumerate((left, v, right)):
                yield row_off * 3 + col_off, shifted_rows(piece, (row_off - 1) * GRID)

    small[...] = jnp.zeros_like(small)
    sizes = []
    lane_row = lax.broadcasted_iota(jnp.int32, (TOK, 128), 1)
    tap = lane % 32
    down, across_by = tap // 3 - 1, tap % 3 - 1
    tap_lane = (tap < TAPS) & (lane < 64)
    for i in range(n):
        m_id, d_id = seg * own + i // (n // own), i % (n // own)
        high, wide = grid_ref[d_id, 0, m_id], grid_ref[d_id, 1, m_id]
        sizes.append((high, wide))
        line = lax.broadcasted_iota(jnp.int32, (GRID, GRID, 128), 0).reshape(TOK, 128)
        good = jnp.where((line < high) & (col < wide), 1.0, 0.0)
        valid[i * TOK : (i + 1) * TOK, :] = good
        for k in range(2 * BLOCKS):
            kept = keep_ref[d_id, k, m_id].astype(f32) / keep_rate
            scale_ref[i, k] = kept
        near_row, near_col = line + down, col + across_by
        there = (near_row >= 0) & (near_row < high) & (near_col >= 0) & (near_col < wide)
        ones = (lane_row == 16) | (lane_row == 48)
        flags = jnp.where(ones | (there & tap_lane), 1.0, 0.0)
        for j in range(BLOCKS):
            u_all[j, i * TOK : (i + 1) * TOK, TAPS * C :] = flags.astype(bf16)
        base = 0
        for t in range(2):
            span = slice(base, base + CELLS[t])
            tall = (high + STRIDES[t] - 1) // STRIDES[t]
            across = (wide + STRIDES[t] - 1) // STRIDES[t]
            inside = (places[0, span, :] < tall.astype(f32)) & (
                places[1, span, :] < across.astype(f32)
            )
            kmask[i, span, :] = jnp.where(inside, 1.0, 0.0)
            base += CELLS[t]
    base = 0
    for t in range(2):
        span = slice(base, base + CELLS[t])
        a, b = places[0, span, :], places[1, span, :]
        for off in range(9):
            dr, dc = float(off // 3 - 1), float(off % 3 - 1)
            top = float(SIDES[t])
            ok = (a + dr >= 0) & (a + dr < top) & (b + dc >= 0) & (b + dc < top)
            near[off, span, :] = jnp.where(ok, 1.0, 0.0)
        base += CELLS[t]

    xs[...] = x_ref[...].astype(f32)

    def scaled(span, k):
        return valid[span, :] * scale_ref[span.start // TOK, k]

    def cell_spans(t):
        start = 0 if t == 0 else n * CELLS[0]
        return [slice(start + i * CELLS[t], start + (i + 1) * CELLS[t]) for i in range(n)]

    def cells_all(t):
        return slice(0, n * CELLS[0]) if t == 0 else slice(n * CELLS[0], n * sum(CELLS))

    place_span = (slice(0, CELLS[0]), slice(CELLS[0], sum(CELLS)))
    half = lane < 64
    own_half = (half, jnp.logical_not(half))

    def near_shift(t, off):
        return ((off // 3 - 1) * WIDTHS[t] + off % 3 - 1) % CELLS[t]

    def attention_forward(j):
        build_wc(j)

        def first(ts):
            xhat, scale = norm_parts(xs[ts, :])
            xh_a[j, ts, :] = xhat
            sc[j, ts, 0:1] = scale
            u_a[j, ts, :] = (xhat * row(ng, j, 0) + row(ns, j, 0)).astype(bf16)

        tiles(first)
        for i in range(n):
            span = slice(i * TOK, (i + 1) * TOK)
            u = u_a[j, span, :]
            q_a[j, span, :] = (nn(u, qw[j]) + row(qb, j)).astype(bf16)
            um[:, i * C : (i + 1) * C] = (u.astype(f32) * valid[span, :]).astype(bf16)
        groups = [
            nn(to_patches[...], um[g * GROUP : (g + 1) * GROUP, :]) for g in range(GROUPS)
        ]
        base = 0
        for t, ref in enumerate((p4, p2)):
            for k in range(STRIDES[t] ** 2):
                for i in range(n):
                    pieces = [x[base : base + PATCH[t], i * C : (i + 1) * C] for x in groups]
                    part = slice(i * CELLS[t], (i + 1) * CELLS[t])
                    ref[j, part, k * C : (k + 1) * C] = jnp.concatenate(pieces, axis=0).astype(bf16)
                base += PATCH[t]
        for t, (ref, weight) in enumerate(((p4, p4w), (p2, p2w))):
            xhat, scale = norm_parts(nn(ref[j], weight[j]))
            act, slope = gelu_parts(xhat * row(ng, j, 1 + t) + row(ns, j, 1 + t))
            act = act.astype(bf16)
            span = cells_all(t)
            xh_p[j, span, :] = xhat
            sc_p[j, span, :] = jnp.broadcast_to(scale, xhat.shape)
            ge_p[j, span, :] = slope
            kin[j, span, :] = act
            keyval = nn(act, kvw[j, t])
            turned = pltpu.roll(keyval, 64, 1)
            keys, vals = (keyval, turned) if t == 0 else (turned, keyval)
            bias = jnp.concatenate([row(vb, j, 0), row(vb, j, 1)], axis=1)
            kernel = jnp.concatenate([lk[j, :, 0, :], lk[j, :, 1, :]], axis=1)
            for i in range(n):
                part = slice(i * CELLS[t], (i + 1) * CELLS[t])
                w = (vals[part] + bias) * kmask[i, place_span[t], :]
                wv[j, cell_spans(t)[i], :] = w
                v = w
                for off in range(9):
                    by = near_shift(t, off)
                    moved = pltpu.roll(w, (CELLS[t] - by) % CELLS[t], 0) if by else w
                    v = v + moved * (near[off, place_span[t], :] * kernel[off : off + 1])
                for h in (2 * t, 2 * t + 1):
                    seg_rows = slice(*SEGS[h])
                    kb[j, i, seg_rows, :] = jnp.where(head_lanes(h), keys[part], 0.0).astype(bf16)
                    vbd[j, i, seg_rows, :] = jnp.where(head_lanes(h), v, 0.0).astype(bf16)
        for i in range(n):
            span = slice(i * TOK, (i + 1) * TOK)
            scores = nt(kb[j, i], q_a[j, span, :])
            for h, (low, top) in enumerate(SEGS):
                mask = kmask[i, place_span[h // 2], 0:1] > 0
                for c0 in range(0, TOK, 128):
                    c1 = min(c0 + 128, TOK)
                    s = jnp.where(mask, scores[low:top, c0:c1], -1e30)
                    e = jnp.exp2((s - jnp.max(s, axis=0, keepdims=True)) * (ROOT * LOG2E))
                    weight = e * pl.reciprocal(jnp.sum(e, axis=0, keepdims=True), approx=True)
                    pt[j, i, low:top, c0:c1] = weight.astype(bf16)
            mixed = tn(vbd[j, i], pt[j, i])
            o_t[j, i] = mixed.astype(bf16)
            o_n[span, :] = mixed.T.astype(bf16)
        for i in range(n):
            span = slice(i * TOK, (i + 1) * TOK)
            branch = nn(o_n[span, :], pw[j]) + row(pb, j)
            xs[span, :] = (xs[span, :] + scaled(span, 2 * j) * branch).astype(bf16).astype(f32)

    def build_wc(j):
        bias = row(hb, j)
        for r0 in range(0, C, 16):
            weight = hw[j, r0 : r0 + 16, :].astype(f32)
            for off in range(TAPS):
                factor = mk[off, pl.ds(j, 1), :] + (1.0 if off == 4 else 0.0)
                wc[j, off * C + r0 : off * C + r0 + 16, :] = (weight * factor).astype(bf16)
        ex[...] = jnp.zeros_like(ex)
        for off in range(TAPS + 1):
            at = off if off < TAPS else 16
            value = bias * mk[off, pl.ds(j, 1), :] if off < TAPS else bias + row(mb, j)
            high = value.astype(bf16).astype(f32)
            ex[at : at + 1, :] = high
            ex[at + 32 : at + 33, :] = value - high
        wc[j, TAPS * C :, :] = ex[...].astype(bf16)

    def mlp_forward(j):
        def first(ts):
            xhat, scale = norm_parts(xs[ts, :])
            xh_m[j, ts, :] = xhat
            sc[j, ts, 1:2] = scale
            u = (xhat * row(ng, j, 3) + row(ns, j, 3)).astype(bf16).astype(f32)
            acc[ts, :] = u * valid[ts, :]

        tiles(first)
        for i in range(n):
            span = slice(i * TOK, (i + 1) * TOK)
            for off, piece in taps_of(acc[span, :]):
                u_all[j, span, off * C : (off + 1) * C] = piece.astype(bf16)

        for i in range(n):
            field = nn(u_all[j, i * TOK : (i + 1) * TOK, :], wc[j])
            for r0 in range(0, TOK, 16):
                part = slice(i * TOK + r0, i * TOK + r0 + 16)
                for start in range(0, FF, CHUNK):
                    cols = slice(start, start + CHUNK)
                    act, slope = gelu_parts(field[r0 : r0 + 16, cols])
                    a_all[j, part, cols] = act.astype(bf16)
                    g_all[j, part, cols] = slope.astype(bf16)
        for i in range(n):
            span = slice(i * TOK, (i + 1) * TOK)
            branch = nn(a_all[j, span, :], ow[j]) + row(ob, j)
            xs[span, :] = (xs[span, :] + scaled(span, 2 * j + 1) * branch).astype(bf16).astype(f32)

    def mlp_backward(j):
        sb = j * S_BLOCK

        def first(ts):
            grad = (xs[ts, :] * scaled(ts, 2 * j + 1)).astype(bf16)
            db[ts, :] = grad
            return [folded(grad.astype(f32))]

        (small[sb + S_OB : sb + S_OB + 1, :],) = tiles(first)
        db_t[j] = db[...].T
        for i in range(n):
            span = slice(i * TOK, (i + 1) * TOK)
            da = nt(db[span, :], ow[j])
            g_all[j, span, :] = (da * g_all[j, span, :].astype(f32)).astype(bf16)
        if j == 0:
            move((0, 1))
        for i in range(n):
            span = slice(i * TOK, (i + 1) * TOK)
            moved = nt(g_all[j, span, :], wc[j, : TAPS * C, :])
            sides = []
            for col_off in range(3):
                total = None
                for row_off in range(3):
                    off = row_off * 3 + col_off
                    piece = shifted_rows(moved[:, off * C : (off + 1) * C], (1 - row_off) * GRID)
                    total = piece if total is None else total + piece
                sides.append(total)
            left = pltpu.roll(jnp.where(col > 0, sides[0], 0.0), TOK - 1, 0)
            right = pltpu.roll(jnp.where(col < GRID - 1, sides[2], 0.0), 1, 0)
            acc[span, :] = (sides[1] + left + right) * valid[span, :]

        def last(ts):
            du = acc[ts, :]
            xhat = xh_m[j, ts, :]
            back = norm_back(du, xhat, sc[j, ts, 1:2], row(ng, j, 3))
            xs[ts, :] = (xs[ts, :] + back).astype(bf16).astype(f32)
            return [folded(du * xhat), folded(du)]

        gain, shift = tiles(last)
        small[sb + S_GAIN + 3 : sb + S_GAIN + 4, :] = gain
        small[sb + S_SHIFT + 3 : sb + S_SHIFT + 4, :] = shift

    def mlp_turn(j):
        for off in range(TAPS + 1):
            ut[off * C : (off + 1) * C, :] = u_all[j, :, off * C : (off + 1) * C].T

    def mlp_weights(j, step):
        base, sb = MLP_AT[0] + j * (MLP_AT[1] - MLP_AT[0]), j * S_BLOCK
        cols = slice(step * CHUNK, (step + 1) * CHUNK)
        dow = nn(db_t[j], a_all[j, :, cols])
        gp[packed(base + output_row(step), CHUNK), :] = dow.T.astype(bf16)
        cross = nn(ut[...], g_all[j, :, cols])
        flag_rows = cross[TAPS * C : TAPS * C + 24]
        total = flag_rows[16:17]
        dhb = total
        weight = hw[j, :, cols].astype(f32)
        dweight = jnp.zeros((C, CHUNK), f32)
        b = hb[pl.ds(j, 1), cols]
        for off in range(TAPS):
            piece = cross[off * C : (off + 1) * C]
            factor = mk[off, pl.ds(j, 1), cols]
            flag = flag_rows[off : off + 1]
            dweight = dweight + piece * (factor + (1.0 if off == 4 else 0.0))
            dk = col_sum(piece * weight) + b * flag
            dhb = dhb + factor * flag
            for s in range(CHUNK // C):
                tile = step * (CHUNK // C) + s
                put(sb + S_MK + 16 * tile + off, dk[:, s * C : (s + 1) * C])
        for s in range(CHUNK // C):
            tile = step * (CHUNK // C) + s
            part = slice(s * C, (s + 1) * C)
            put(sb + S_HB + tile, dhb[:, part])
            put(sb + S_MB + tile, total[:, part])
            gp[packed(base + hidden_row(tile), C), :] = dweight[:, part].astype(bf16)

    def attention_backward(j):
        base, sb = ATT_AT[j], j * S_BLOCK

        def first(ts):
            grad = (xs[ts, :] * scaled(ts, 2 * j)).astype(bf16)
            db[ts, :] = grad
            return [folded(grad.astype(f32))]

        (small[sb + S_PB : sb + S_PB + 1, :],) = tiles(first)
        dproj = jnp.zeros((C, C), f32)
        kernel = jnp.concatenate([lk[j, :, 0, :], lk[j, :, 1, :]], axis=1)
        dkernel = [jnp.zeros((1, C), f32) for _ in range(9)]
        dbias = jnp.zeros((1, C), f32)
        for i in range(n):
            span = slice(i * TOK, (i + 1) * TOK)
            dproj = dproj + nn(o_t[j, i], db[span, :])
            do = nt(db[span, :], pw[j]).astype(bf16)
            dprobs = nt(vbd[j, i], do)
            dvals = nn(pt[j, i], do)
            for low, top in SEGS:
                for c0 in range(0, TOK, 128):
                    c1 = min(c0 + 128, TOK)
                    weight = pt[j, i, low:top, c0:c1].astype(f32)
                    dweight = dprobs[low:top, c0:c1]
                    dot = jnp.sum(weight * dweight, axis=0, keepdims=True)
                    pt[j, i, low:top, c0:c1] = (weight * (dweight - dot)).astype(bf16)
            dkeys = nn(pt[j, i], q_a[j, span, :]) * ROOT
            dq = tn(kb[j, i], pt[j, i]) * ROOT
            o_n[span, :] = dq.T.astype(bf16)
            for t in range(2):
                dk = jnp.zeros((CELLS[t], C), f32)
                dv = jnp.zeros((CELLS[t], C), f32)
                for h in (2 * t, 2 * t + 1):
                    dk = dk + jnp.where(head_lanes(h), dkeys[slice(*SEGS[h])], 0.0)
                    dv = dv + jnp.where(head_lanes(h), dvals[slice(*SEGS[h])], 0.0)
                w = wv[j, cell_spans(t)[i], :]
                dw = dv
                for off in range(9):
                    by = near_shift(t, off)
                    part = dv * near[off, place_span[t], :]
                    moved = pltpu.roll(w, (CELLS[t] - by) % CELLS[t], 0) if by else w
                    dkernel[off] = dkernel[off] + col_sum(part * moved)
                    part = part * kernel[off : off + 1]
                    dw = dw + (pltpu.roll(part, by, 0) if by else part)
                dw = dw * kmask[i, place_span[t], :]
                dbias = dbias + col_sum(dw)
                if t == 0:
                    dkeyval = dk + pltpu.roll(dw, 64, 1)
                else:
                    dkeyval = pltpu.roll(dk, 64, 1) + dw
                wv[j, cell_spans(t)[i], :] = dkeyval
        gp[base + R_PROJ : base + R_PROJ + C, :] = dproj.astype(bf16)
        small[sb + S_VB : sb + S_VB + 1, :] = dbias
        for off in range(9):
            small[sb + S_LK + off : sb + S_LK + off + 1, :] = dkernel[off]
        backs = []
        for t, (ref, weight) in enumerate(((p4, p4w), (p2, p2w))):
            span = cells_all(t)
            dkeyval = wv[j, span, :].astype(bf16)
            at = base + R_KV + t * C
            gp[at : at + C, :] = tn(kin[j, span, :], dkeyval).astype(bf16)
            dy = nt(dkeyval, kvw[j, t]) * ge_p[j, span, :]
            xhat = xh_p[j, span, :]
            small[sb + S_GAIN + 1 + t : sb + S_GAIN + 2 + t, :] = col_sum(dy * xhat)
            small[sb + S_SHIFT + 1 + t : sb + S_SHIFT + 2 + t, :] = col_sum(dy)
            dpool = norm_back(dy, xhat, sc_p[j, span, :], row(ng, j, 1 + t)).astype(bf16)
            at = base + (R_P4, R_P2)[t]
            for k in range(STRIDES[t] ** 2):
                gp[at + k * C : at + (k + 1) * C, :] = tn(
                    ref[j, :, k * C : (k + 1) * C], dpool
                ).astype(bf16)
                backs.append((t, nt(dpool, weight[j, k * C : (k + 1) * C, :])))
        at = base + R_Q
        gp[at : at + C, :] = tn(u_a[j], o_n[...]).astype(bf16)
        if j == 1:
            all_here()
            move((0, 0))
        else:
            move((0, 2), (1, 0))
        for i in range(n):
            span = slice(i * TOK, (i + 1) * TOK)
            acc[span, :] = nt(o_n[span, :], qw[j])
        for g in range(GROUPS):
            images_of = []
            for i in range(n):
                pieces = [
                    back[i * CELLS[t] + g * PATCH[t] : i * CELLS[t] + (g + 1) * PATCH[t]]
                    for t, back in backs
                ]
                images_of.append(jnp.concatenate(pieces, axis=0).astype(bf16))
            spread = nn(from_patches[...], jnp.concatenate(images_of, axis=1))
            for i in range(n):
                span = slice(i * TOK + g * GROUP, i * TOK + (g + 1) * GROUP)
                acc[span, :] += spread[:, i * C : (i + 1) * C] * valid[span, :]

        def last(ts):
            du = acc[ts, :]
            xhat = xh_a[j, ts, :]
            back = norm_back(du, xhat, sc[j, ts, 0:1], row(ng, j, 0))
            xs[ts, :] = (xs[ts, :] + back).astype(bf16).astype(f32)
            return [folded(o_n[ts, :].astype(f32)), folded(du * xhat), folded(du)]

        bias, gain, shift = tiles(last)
        small[sb + S_QB : sb + S_QB + 1, :] = bias
        small[sb + S_GAIN : sb + S_GAIN + 1, :] = gain
        small[sb + S_SHIFT : sb + S_SHIFT + 1, :] = shift

    def forward(j, carry):
        attention_forward(j)
        mlp_forward(j)
        return carry

    for made in late:
        made.wait()
    lax.fori_loop(0, BLOCKS, forward, 0)
    out_st[...] = xs[...].astype(bf16)
    leave(out_st, out_ref)
    xs[...] = cot_ref[...].astype(f32)
    mlp_backward(1)
    attention_backward(1)
    mlp_turn(1)
    mlp_backward(0)
    attention_backward(0)
    dx_st[...] = xs[...].astype(bf16)
    leave(dx_st, dx_ref)

    def weights(k, carry):
        j = BLOCKS - 1 - k
        pl.when(k == 1)(lambda: mlp_turn(0))
        move_if(k == 0, (1, 1))
        move_if(k == 1, (1, 2), (2, 1), (0, 4))
        mlp_weights(j, 0)
        move_if(k == 0, (0, 3))
        move_if(k == 1, (3, 0))
        mlp_weights(j, 1)
        move_if(k == 0, (2, 0))
        return carry

    lax.fori_loop(0, BLOCKS, weights, 0)
    gp[R_SMALL:, :] = small[...].astype(bf16)
    move((4, 0), (1, 3), (3, 1), (2, 2), (4, 1))
    move((0, 5), (3, 2), (1, 4), (0, 6), (2, 3), (4, 2), (3, 3), (2, 4), (4, 3), (1, 5), (3, 4))
    move((1, 6), (4, 4), (2, 5), (3, 5), (2, 6), (3, 6), (4, 5), (4, 6))
    for piece in pieces:
        piece.drain()
    for made in leaving:
        made.wait()


def compute(own, images, grid_size, keep_mask, x, cot, weights):
    segments, pairs = lax.axis_size("segment"), lax.axis_size("dp") // 2
    inner = min(pairs, 4)
    sizes = (segments, inner, pairs // inner)
    n = images
    rows = n * TOK
    cells = n * sum(CELLS)
    vmem = pl.BlockSpec(memory_space=pltpu.VMEM)
    smem = pl.BlockSpec(memory_space=pltpu.SMEM)
    matrix = patch_matrix()
    consts = (
        jnp.asarray(matrix, bf16),
        jnp.asarray(matrix.T, bf16),
        jnp.asarray(cell_places()),
    )
    B = BLOCKS
    scratch = [
        pltpu.VMEM((rows, C), f32),
        pltpu.VMEM((rows, C), f32),
        pltpu.VMEM((TOK, n * C), bf16),
        pltpu.VMEM((B, rows, UW), bf16),
        pltpu.VMEM((UW, rows), bf16),
        pltpu.VMEM((B, UW, FF), bf16),
        pltpu.VMEM((C, FF), f32),
        pltpu.VMEM((B, rows, C), f32),
        pltpu.VMEM((B, rows, C), f32),
        pltpu.VMEM((B, rows, C), f32),
        pltpu.VMEM((B, rows, C), bf16),
        pltpu.VMEM((B, rows, C), bf16),
        pltpu.VMEM((B, n * CELLS[0], 16 * C), bf16),
        pltpu.VMEM((B, n * CELLS[1], 4 * C), bf16),
        pltpu.VMEM((B, cells, C), f32),
        pltpu.VMEM((B, cells, C), f32),
        pltpu.VMEM((B, cells, C), f32),
        pltpu.VMEM((B, cells, C), bf16),
        pltpu.VMEM((B, cells, C), f32),
        pltpu.VMEM((B, n, KEYS, C), bf16),
        pltpu.VMEM((B, n, KEYS, C), bf16),
        pltpu.VMEM((B, n, KEYS, TOK), bf16),
        pltpu.VMEM((B, n, C, TOK), bf16),
        pltpu.VMEM((rows, C), bf16),
        pltpu.VMEM((B, rows, FF), bf16),
        pltpu.VMEM((B, rows, FF), bf16),
        pltpu.VMEM((rows, C), bf16),
        pltpu.VMEM((B, C, rows), bf16),
        pltpu.VMEM((rows, C), f32),
        pltpu.VMEM((n, sum(CELLS), C), f32),
        pltpu.VMEM((9, sum(CELLS), C), f32),
        pltpu.VMEM((ROWS - R_SMALL, C), f32),
        pltpu.SMEM((n, 2 * BLOCKS), f32),
        pltpu.VMEM(cot.shape, bf16),
        pltpu.VMEM(weights[HW].shape, bf16),
        pltpu.VMEM(weights[P4].shape, bf16),
        pltpu.VMEM(weights[P2].shape, bf16),
        pltpu.VMEM(weights[OW].shape, bf16),
        pltpu.VMEM((rows, C), bf16),
        pltpu.VMEM((rows, C), bf16),
        pltpu.SemaphoreType.DMA((7 + len(PIECES),)),
        pltpu.VMEM((ROWS, C), bf16),
    ] + sum_scratch(sizes)
    anywhere = pl.BlockSpec(memory_space=pl.ANY)
    operands = [vmem] * (2 + len(weights) + len(consts))
    for place in (1, 2 + HW, 2 + P4, 2 + P2, 2 + OW):
        operands[place] = anywhere
    return pl.pallas_call(
        functools.partial(compute_kernel, own, images, sizes),
        out_shape=(
            jax.ShapeDtypeStruct((rows, C), bf16),
            jax.ShapeDtypeStruct((rows, C), bf16),
            jax.ShapeDtypeStruct((ROWS, C), bf16),
        ),
        in_specs=[smem, smem] + operands,
        out_specs=(anywhere,) * 3,
        scratch_shapes=scratch,
        compiler_params=pltpu.CompilerParams(
            collective_id=0, has_side_effects=True, vmem_limit_bytes=63 * 2**20
        ),
        name="compute",
    )(grid_size, keep_mask, x, cot, *weights, *consts)


def unpack_kernel(att, mlp, rest, out_in, dx_in, *refs):
    out_ref, dx_ref = refs[:2]
    gain, shift, qw, qb, p4, p2, kvw, vb, lk, pw, pb, hw, hb, mk, mb, ow, ob = refs[2:]
    out_ref[...] = out_in[...]
    dx_ref[...] = dx_in[...]
    p4[0] = att[R_P4:R_P2, :].astype(f32)
    p2[0] = att[R_P2:R_KV, :].astype(f32)
    for t in range(2):
        kvw[0, t] = att[R_KV + t * C : R_KV + (t + 1) * C, :].astype(f32)
    qw[0] = att[R_Q:R_PROJ, :].astype(f32)
    pw[0] = att[R_PROJ:R_ATT, :].astype(f32)
    for s in range(FF // C):
        hw[0, :, s * C : (s + 1) * C] = mlp[hidden_row(s) : hidden_row(s) + C, :].astype(f32)
    for step in range(FF // CHUNK):
        at = output_row(step)
        ow[0, step * CHUNK : (step + 1) * CHUNK, :] = mlp[at : at + CHUNK, :].astype(f32)

    @pl.when(pl.program_id(0) == BLOCKS - 1)
    def _():
        for j in range(BLOCKS):
            sb = j * S_BLOCK
            head = rest[sb : sb + 48, :].astype(f32)
            gain[j] = head[S_GAIN : S_GAIN + 4]
            shift[j] = head[S_SHIFT : S_SHIFT + 4]
            qb[j : j + 1, :] = head[S_QB : S_QB + 1]
            vb[j, 0:1, :] = head[S_VB : S_VB + 1, 0:64]
            vb[j, 1:2, :] = head[S_VB : S_VB + 1, 64:128]
            pb[j : j + 1, :] = head[S_PB : S_PB + 1]
            ob[j : j + 1, :] = head[S_OB : S_OB + 1]
            lk[j, :, 0, :] = head[S_LK : S_LK + 9, 0:64]
            lk[j, :, 1, :] = head[S_LK : S_LK + 9, 64:128]
            for s in range(FF // C):
                part = slice(s * C, (s + 1) * C)
                hb[j : j + 1, part] = head[S_HB + s : S_HB + s + 1]
                mb[j : j + 1, part] = head[S_MB + s : S_MB + s + 1]
                at = sb + S_MK + 16 * s
                mk[:, j, part] = rest[at : at + 16, :].astype(f32)[0:9]


def unpack(packed, outputs, input_grad, weights):
    streams = (jax.ShapeDtypeStruct(outputs.shape, bf16),) * 2
    by_block = {QW, P4, P2, KVW, PW, HW, OW}
    rest = ROWS - R_SMALL
    stream = pl.BlockSpec((outputs.shape[0] // BLOCKS, C), lambda k: (k, 0))
    specs = []
    for place, w in enumerate(weights):
        if place in by_block:
            zeros = (0,) * (w.ndim - 1)
            specs.append(pl.BlockSpec((1,) + w.shape[1:], lambda k, z=zeros: (BLOCKS - 1 - k,) + z))
        else:
            zeros = (0,) * w.ndim
            specs.append(pl.BlockSpec(w.shape, lambda k, z=zeros: z))
    return pl.pallas_call(
        unpack_kernel,
        out_shape=streams + tuple(jax.ShapeDtypeStruct(w.shape, f32) for w in weights),
        grid=(BLOCKS,),
        in_specs=[
            pl.BlockSpec((R_ATT, C), lambda k: (k, 0)),
            pl.BlockSpec((R_MLP, C), lambda k: (MLP_AT[BLOCKS - 1] // R_MLP + k, 0)),
            pl.BlockSpec((rest, C), lambda k: (R_SMALL // rest, 0)),
            stream,
            stream,
        ],
        out_specs=(stream, stream) + tuple(specs),
        compiler_params=pltpu.CompilerParams(vmem_limit_bytes=63 * 2**20),
        name="unpack",
    )(packed, packed, packed, outputs, input_grad)


def on_device(inputs, grid_size, keep_mask, cotangent, *weights):
    own, per = inputs.shape[:2]
    images = own * per
    flat = (images * TOK, C)
    turned = list(weights)
    turned[LK] = jnp.transpose(turned[LK], (0, 2, 1, 3))
    turned[MK] = jnp.transpose(turned[MK], (1, 0, 2))
    outputs, input_grad, packed = compute(
        own,
        images,
        jnp.transpose(grid_size, (1, 2, 0)),
        jnp.transpose(keep_mask, (1, 2, 0)),
        inputs.reshape(flat),
        cotangent.reshape(flat),
        turned,
    )
    outputs, input_grad, *grads = unpack(packed, outputs, input_grad, turned)
    grads[LK] = jnp.transpose(grads[LK], (0, 2, 1, 3))
    grads[MK] = jnp.transpose(grads[MK], (1, 0, 2))
    return (outputs.reshape(inputs.shape), input_grad.reshape(inputs.shape)) + tuple(grads)


def solution(mesh):
    stream = P("segment", "dp", None, None)
    picked = P(None, "dp", None)
    return jax.shard_map(
        on_device,
        mesh=mesh,
        in_specs=(stream, picked, picked, stream) + (P(),) * 17,
        out_specs=(stream, stream) + (P(),) * 17,
        check_vma=False,
    )
```

```python
import functools

import jax
import jax.numpy as jnp
import numpy as np
from jax import lax
from jax.experimental import pallas as pl
from jax.experimental.pallas import tpu as pltpu
from jax.sharding import PartitionSpec as P

GRID = 24
TOK = GRID * GRID
C = 128
FF = 1024
HEAD = 32
BLOCKS = 2
SIDES = (6, 12)
STRIDES = (4, 2)
WIDTHS = (8, 12)
CELLS = (48, 144)
SEGS = ((0, 48), (48, 96), (96, 240), (240, 384))
KEYS = 384
GROUP = 4 * GRID
GROUPS = TOK // GROUP
PATCH = (8, 24)
PATCHES = 16 * PATCH[0] + 4 * PATCH[1]
TAPS = 9
UW = TAPS * C + C
CHUNK = 512
TILE = 96

R_P4, R_P2, R_KV, R_Q, R_PROJ, R_ATT = 0, 2048, 2560, 2816, 2944, 3072
R_MLP = 2048
ATT_AT = (R_ATT, 0)
MLP_AT = (2 * R_ATT + R_MLP, 2 * R_ATT)
S_GAIN, S_SHIFT, S_QB, S_VB, S_PB, S_OB, S_LK, S_HB, S_MB, S_MK, S_BLOCK = (
    0,
    4,
    8,
    9,
    10,
    11,
    16,
    32,
    40,
    48,
    192,
)
R_SMALL = BLOCKS * (R_ATT + R_MLP)
ROWS = R_SMALL + 512
PIECES = (
    (ATT_AT[1], R_ATT),
    (ATT_AT[0], R_ATT),
    (MLP_AT[1], R_MLP),
    (MLP_AT[0], R_MLP // 2),
    (MLP_AT[0] + R_MLP // 2, R_MLP // 2 + ROWS - R_SMALL),
)

QW, P4, P2, KVW, LK, PW, HW, MK, OW = 2, 4, 5, 6, 8, 9, 11, 13, 15

epsilon = 1e-06
keep_rate = 0.8
ROOT = HEAD**-0.5
LOG2E = 1.4426950408889634
f32, bf16 = jnp.float32, jnp.bfloat16


def hidden_row(tile):
    return tile // (CHUNK // C) * 2 * CHUNK + tile % (CHUNK // C) * C


def output_row(step):
    return step * 2 * CHUNK + CHUNK


def patch_matrix():
    matrix = np.zeros((PATCHES, GROUP), np.float32)
    base = 0
    for stride, side, width, count in zip(STRIDES, SIDES, WIDTHS, PATCH):
        for row_off in range(stride):
            for col_off in range(stride):
                for a in range(4 // stride):
                    for b in range(side):
                        token = (a * stride + row_off) * GRID + b * stride + col_off
                        matrix[base + a * width + b, token] = 1.0
                base += count
    return matrix


def cell_places():
    places = np.full((2, sum(CELLS), 128), 99.0, np.float32)
    base = 0
    for side, width, cells in zip(SIDES, WIDTHS, CELLS):
        for a in range(side):
            for b in range(side):
                places[0, base + a * width + b] = a
                places[1, base + a * width + b] = b
        base += cells
    return places


def nn(left, right):
    return jnp.dot(left, right, preferred_element_type=f32)


def nt(left, right):
    return lax.dot_general(left, right, (((1,), (1,)), ((), ())), preferred_element_type=f32)


def tn(left, right):
    return lax.dot_general(left, right, (((0,), (0,)), ((), ())), preferred_element_type=f32)


def gelu_parts(m):
    size = jnp.abs(m)
    t = pl.reciprocal(1.0 + (0.3275911 * 0.5**0.5) * size, approx=True)
    e = jnp.exp2(m * (m * (-0.5 * LOG2E)))
    poly = 0.5 * 1.061405429
    for coef in (-1.453152027, 1.421413741, -0.284496736, 0.254829592):
        poly = poly * t + 0.5 * coef
    poly = poly * t
    tail = poly * e
    slope = (poly - size * 0.3989422804014327) * e
    return jnp.maximum(m, 0.0) - size * tail, jnp.where(m >= 0, 1.0 - slope, slope)


def norm_parts(x):
    centred = x - jnp.mean(x, axis=-1, keepdims=True)
    scale = lax.rsqrt(jnp.mean(centred * centred, axis=-1, keepdims=True) + epsilon)
    return centred * scale, scale


def norm_back(du, xhat, scale, gain):
    dxhat = du * gain
    first = jnp.mean(dxhat, axis=-1, keepdims=True)
    second = jnp.mean(dxhat * xhat, axis=-1, keepdims=True)
    return scale * (dxhat - first - xhat * second)


def col_sum(x):
    return jnp.sum(x, axis=0, keepdims=True)


def folded(x):
    return jnp.sum(x.reshape(-1, 8, x.shape[-1]), axis=0)


class Summed:
    STEPS = 7

    def __init__(self, place, piece, base, count, refs):
        self.seg, self.dp, self.segments, self.inner, self.outer = place
        self.piece, self.base = piece, base
        (
            self.src,
            self.half_in,
            self.quarter_in,
            self.part_in,
            self.whole_in,
            self.own,
            self.total,
            self.send,
            self.recv,
        ) = refs
        self.core, rest = self.dp % 2, self.dp // 2
        self.part, self.group = rest % self.inner, rest // self.inner
        self.half = count // 2
        self.quarter = self.half // self.segments
        self.share = self.quarter // self.inner
        quarters, shares = (self.segments - 1) * self.quarter, (self.inner - 1) * self.share
        self.moved = (self.half, quarters, shares, shares, quarters, self.half)
        self.at_quarter = self.seg * self.quarter
        self.at_share = self.at_quarter + self.part * self.share

    def span(self, start, size):
        return pl.ds(pl.multiple_of(start, 16), size)

    def device(self, seg=None, core=None, part=None, group=None):
        seg = self.seg if seg is None else seg
        core = self.core if core is None else core
        part = self.part if part is None else part
        group = self.group if group is None else group
        return (seg, (group * self.inner + part) * 2 + core)

    def copy(self, k, src, dst, device):
        return pltpu.make_async_remote_copy(
            src_ref=src,
            dst_ref=dst,
            send_sem=self.send.at[self.piece],
            recv_sem=self.recv.at[self.piece, k],
            device_id=device,
            device_id_type=pl.DeviceIdType.MESH,
        )

    def counted(self, k, count):
        ref = self.total.at[pl.ds(0, count), :]
        return self.copy(k, ref, ref, self.device(core=1 - self.core))

    def step(self, k):
        if k > 0:
            self.counted(k - 1, self.moved[k - 1]).wait_recv()
            self.gather(k)
        if k + 1 < self.STEPS:
            self.depart(k)

    def drain(self):
        count = sum(self.moved) + (self.outer - 1) * self.share
        self.counted(0, count).wait_send()

    def depart(self, k):
        half = self.base // 2
        mine = self.base + self.core * self.half
        if k == 0:
            src = self.src.at[self.span(self.base + (1 - self.core) * self.half, self.half), :]
            dst = self.half_in.at[self.span(half, self.half), :]
            self.copy(k, src, dst, self.device(core=1 - self.core)).start()
        elif k == 1:
            at = self.span(half // self.segments, self.quarter)
            for d in range(1, self.segments):
                to = self.seg ^ d
                src = self.own.at[self.span(half + to * self.quarter, self.quarter), :]
                dst = self.quarter_in.at[d - 1, at, :]
                self.copy(k, src, dst, self.device(seg=to)).start()
        elif k == 2:
            at = self.span(self.share_in(), self.share)
            for d in range(1, self.inner):
                to = self.part ^ d
                start = half + self.at_quarter + to * self.share
                src = self.own.at[self.span(start, self.share), :]
                self.copy(k, src, self.part_in.at[d - 1, at, :], self.device(part=to)).start()
        elif k == 3:
            ref = self.total.at[self.span(mine + self.at_share, self.share), :]
            for d in range(1, self.inner):
                self.copy(k, ref, ref, self.device(part=self.part ^ d)).start()
        elif k == 4:
            ref = self.total.at[self.span(mine + self.at_quarter, self.quarter), :]
            for d in range(1, self.segments):
                self.copy(k, ref, ref, self.device(seg=self.seg ^ d)).start()
        else:
            ref = self.total.at[self.span(mine, self.half), :]
            self.copy(k, ref, ref, self.device(core=1 - self.core)).start()

    def share_in(self):
        return self.base // 2 // self.segments // self.inner

    def gather(self, k):
        half = self.base // 2
        if k == 1:
            first = (self.src, self.base + self.core * self.half)
            self.add((self.own, half), first, [(self.half_in, half)], self.half)
        elif k == 2:
            mine = (self.own, half + self.at_quarter)
            at = half // self.segments
            received = [(self.quarter_in.at[d], at) for d in range(self.segments - 1)]
            self.add(mine, mine, received, self.quarter)
        elif k == 3:
            received = [(self.part_in.at[d], self.share_in()) for d in range(self.inner - 1)]
            mine = (self.own, half + self.at_share)
            into = (self.total, self.base + self.core * self.half + self.at_share)
            if self.outer > 1:
                self.add(mine, mine, received, self.share)
                slot = self.STEPS - 1
                src = self.own.at[self.span(mine[1], self.share), :]
                at = self.span(self.share_in(), self.share)
                for d in range(1, self.outer):
                    to = self.device(group=self.group ^ d)
                    self.copy(slot, src, self.whole_in.at[d - 1, at, :], to).start()
                self.counted(slot, (self.outer - 1) * self.share).wait_recv()
                received = [(self.whole_in.at[d], self.share_in()) for d in range(self.outer - 1)]
            self.add(into, mine, received, self.share)

    def add(self, dst, first, others, count):
        step = next(size for size in (512, 384, 256, 192, 128, 96, 64, 48, 32, 16) if count % size == 0)

        def body(t, carry):
            at = t * step
            total = first[0][self.span(first[1] + at, step), :].astype(f32)
            for ref, start in others:
                total = total + ref[self.span(start + at, step), :].astype(f32)
            dst[0][self.span(dst[1] + at, step), :] = total.astype(bf16)
            return carry

        lax.fori_loop(0, count // step, body, 0)


def greet(seg, dp, segments, inner, outer):
    barrier = pltpu.get_barrier_semaphore()
    core, part, group = dp % 2, dp // 2 % inner, dp // 2 // inner
    peers = [(seg, dp + 1 - 2 * core)]
    peers += [(seg ^ d, dp) for d in range(1, segments)]
    peers += [(seg, (group * inner + (part ^ d)) * 2 + core) for d in range(1, inner)]
    peers += [(seg, ((group ^ d) * inner + part) * 2 + core) for d in range(1, outer)]
    for peer in peers:
        pl.semaphore_signal(
            barrier, inc=1, device_id=peer, device_id_type=pl.DeviceIdType.MESH
        )
    return lambda: pl.semaphore_wait(barrier, len(peers))


def sum_scratch(sizes):
    segments, inner, outer = sizes
    quarter = ROWS // 2 // segments
    share = quarter // inner
    return [
        pltpu.VMEM((ROWS // 2, C), bf16),
        pltpu.VMEM((segments - 1, quarter, C), bf16),
        pltpu.VMEM((inner - 1, share, C), bf16),
        pltpu.VMEM((max(outer - 1, 1), share, C), bf16),
        pltpu.VMEM((ROWS // 2, C), bf16),
        pltpu.VMEM((ROWS, C), bf16),
        pltpu.SemaphoreType.DMA((len(PIECES),)),
        pltpu.SemaphoreType.DMA((len(PIECES), Summed.STEPS)),
    ]


def compute_kernel(
    own,
    images,
    sizes,
    grid_ref,
    keep_ref,
    x_ref,
    cot_in,
    ng,
    ns,
    qw,
    qb,
    p4w_in,
    p2w_in,
    kvw,
    vb,
    lk,
    pw,
    pb,
    hw_in,
    hb,
    mk,
    mb,
    ow_in,
    ob,
    to_patches,
    from_patches,
    places,
    out_ref,
    dx_ref,
    summed_ref,
    xs,
    valid,
    um,
    u_all,
    ut,
    wc,
    ex,
    xh_a,
    xh_m,
    sc,
    u_a,
    q_a,
    p4,
    p2,
    xh_p,
    sc_p,
    ge_p,
    kin,
    wv,
    kb,
    vbd,
    pt,
    o_t,
    o_n,
    a_all,
    g_all,
    db,
    db_t,
    acc,
    kmask,
    near,
    small,
    scale_ref,
    cot_ref,
    hw,
    p4w,
    p2w,
    ow,
    out_st,
    dx_st,
    sems,
    gp,
    half_in,
    quarter_in,
    part_in,
    whole_in,
    own_part,
    total_ref,
    send,
    recv,
):
    n = images
    rows = n * TOK
    seg, dp = lax.axis_index("segment"), lax.axis_index("dp")
    all_here = greet(seg, dp, *sizes)
    late = [
        pltpu.make_async_copy(src, dst, sems.at[k])
        for k, (src, dst) in enumerate(
            ((hw_in, hw), (p4w_in, p4w), (p2w_in, p2w), (ow_in, ow), (cot_in, cot_ref))
        )
    ]
    for made in late:
        made.start()
    leaving = []

    def leave(src, dst):
        made = pltpu.make_async_copy(src, dst, sems.at[len(late) + len(leaving)])
        made.start()
        leaving.append(made)

    refs = (
        gp,
        half_in,
        quarter_in,
        part_in,
        whole_in,
        own_part,
        total_ref,
        send,
        recv,
    )
    pieces = [
        Summed((seg, dp) + sizes, p, base, count, refs) for p, (base, count) in enumerate(PIECES)
    ]

    def move(*steps):
        for p, k in steps:
            pieces[p].step(k)
            if k + 1 == Summed.STEPS:
                rows_of = pl.ds(PIECES[p][0], PIECES[p][1])
                leave(total_ref.at[rows_of, :], summed_ref.at[rows_of, :])

    lane = lax.broadcasted_iota(jnp.int32, (8, 128), 1)[0:1]

    def head_lanes(h):
        return (lane >= h * HEAD) & (lane < (h + 1) * HEAD)

    def tiles(fn, step=TILE):
        sums = None
        for start in range(0, rows, step):
            got = fn(slice(start, start + step))
            if got is not None:
                sums = got if sums is None else [x + y for x, y in zip(sums, got)]
        return None if sums is None else [col_sum(x) for x in sums]

    def row(ref, j, k=None):
        return ref[j, pl.ds(k, 1), :] if k is not None else ref[pl.ds(j, 1), :]

    def put(at, value):
        small[pl.ds(at, 1), :] = value

    def packed(start, count):
        return pl.ds(start, count)

    def shifted_rows(v, by):
        if by == 0:
            return v
        pad = jnp.zeros((abs(by), v.shape[1]), v.dtype)
        if by > 0:
            return jnp.concatenate([v[by:], pad], axis=0)
        return jnp.concatenate([pad, v[:by]], axis=0)

    col = lax.broadcasted_iota(jnp.int32, (GRID, GRID, 128), 1).reshape(TOK, 128)

    def taps_of(v):
        left = jnp.where(col > 0, pltpu.roll(v, 1, 0), 0.0)
        right = jnp.where(col < GRID - 1, pltpu.roll(v, TOK - 1, 0), 0.0)
        for row_off in range(3):
            for col_off, piece in enumerate((left, v, right)):
                yield row_off * 3 + col_off, shifted_rows(piece, (row_off - 1) * GRID)

    small[...] = jnp.zeros_like(small)
    sizes = []
    lane_row = lax.broadcasted_iota(jnp.int32, (TOK, 128), 1)
    tap = lane % 32
    down, across_by = tap // 3 - 1, tap % 3 - 1
    tap_lane = (tap < TAPS) & (lane < 64)
    for i in range(n):
        m_id, d_id = seg * own + i // (n // own), i % (n // own)
        high, wide = grid_ref[d_id, 0, m_id], grid_ref[d_id, 1, m_id]
        sizes.append((high, wide))
        line = lax.broadcasted_iota(jnp.int32, (GRID, GRID, 128), 0).reshape(TOK, 128)
        good = jnp.where((line < high) & (col < wide), 1.0, 0.0)
        valid[i * TOK : (i + 1) * TOK, :] = good
        for k in range(2 * BLOCKS):
            kept = keep_ref[d_id, k, m_id].astype(f32) / keep_rate
            scale_ref[i, k] = kept
        near_row, near_col = line + down, col + across_by
        there = (near_row >= 0) & (near_row < high) & (near_col >= 0) & (near_col < wide)
        ones = (lane_row == 16) | (lane_row == 48)
        flags = jnp.where(ones | (there & tap_lane), 1.0, 0.0)
        for j in range(BLOCKS):
            u_all[j, i * TOK : (i + 1) * TOK, TAPS * C :] = flags.astype(bf16)
        base = 0
        for t in range(2):
            span = slice(base, base + CELLS[t])
            tall = (high + STRIDES[t] - 1) // STRIDES[t]
            across = (wide + STRIDES[t] - 1) // STRIDES[t]
            inside = (places[0, span, :] < tall.astype(f32)) & (
                places[1, span, :] < across.astype(f32)
            )
            kmask[i, span, :] = jnp.where(inside, 1.0, 0.0)
            base += CELLS[t]
    base = 0
    for t in range(2):
        span = slice(base, base + CELLS[t])
        a, b = places[0, span, :], places[1, span, :]
        for off in range(9):
            dr, dc = float(off // 3 - 1), float(off % 3 - 1)
            top = float(SIDES[t])
            ok = (a + dr >= 0) & (a + dr < top) & (b + dc >= 0) & (b + dc < top)
            near[off, span, :] = jnp.where(ok, 1.0, 0.0)
        base += CELLS[t]

    xs[...] = x_ref[...].astype(f32)

    def scaled(span, k):
        return valid[span, :] * scale_ref[span.start // TOK, k]

    def cell_spans(t):
        start = 0 if t == 0 else n * CELLS[0]
        return [slice(start + i * CELLS[t], start + (i + 1) * CELLS[t]) for i in range(n)]

    def cells_all(t):
        return slice(0, n * CELLS[0]) if t == 0 else slice(n * CELLS[0], n * sum(CELLS))

    place_span = (slice(0, CELLS[0]), slice(CELLS[0], sum(CELLS)))
    half = lane < 64
    own_half = (half, jnp.logical_not(half))

    def near_shift(t, off):
        return ((off // 3 - 1) * WIDTHS[t] + off % 3 - 1) % CELLS[t]

    def attention_forward(j):
        build_wc(j)

        def first(ts):
            xhat, scale = norm_parts(xs[ts, :])
            xh_a[j, ts, :] = xhat
            sc[j, ts, 0:1] = scale
            u_a[j, ts, :] = (xhat * row(ng, j, 0) + row(ns, j, 0)).astype(bf16)

        tiles(first)
        for i in range(n):
            span = slice(i * TOK, (i + 1) * TOK)
            u = u_a[j, span, :]
            q_a[j, span, :] = (nn(u, qw[j]) + row(qb, j)).astype(bf16)
            um[:, i * C : (i + 1) * C] = (u.astype(f32) * valid[span, :]).astype(bf16)
        groups = [
            nn(to_patches[...], um[g * GROUP : (g + 1) * GROUP, :]) for g in range(GROUPS)
        ]
        base = 0
        for t, ref in enumerate((p4, p2)):
            for k in range(STRIDES[t] ** 2):
                for i in range(n):
                    pieces = [x[base : base + PATCH[t], i * C : (i + 1) * C] for x in groups]
                    part = slice(i * CELLS[t], (i + 1) * CELLS[t])
                    ref[j, part, k * C : (k + 1) * C] = jnp.concatenate(pieces, axis=0).astype(bf16)
                base += PATCH[t]
        for t, (ref, weight) in enumerate(((p4, p4w), (p2, p2w))):
            xhat, scale = norm_parts(nn(ref[j], weight[j]))
            act, slope = gelu_parts(xhat * row(ng, j, 1 + t) + row(ns, j, 1 + t))
            act = act.astype(bf16)
            span = cells_all(t)
            xh_p[j, span, :] = xhat
            sc_p[j, span, :] = jnp.broadcast_to(scale, xhat.shape)
            ge_p[j, span, :] = slope
            kin[j, span, :] = act
            keyval = nn(act, kvw[j, t])
            turned = pltpu.roll(keyval, 64, 1)
            keys, vals = (keyval, turned) if t == 0 else (turned, keyval)
            bias = jnp.concatenate([row(vb, j, 0), row(vb, j, 1)], axis=1)
            kernel = jnp.concatenate([lk[j, :, 0, :], lk[j, :, 1, :]], axis=1)
            for i in range(n):
                part = slice(i * CELLS[t], (i + 1) * CELLS[t])
                w = (vals[part] + bias) * kmask[i, place_span[t], :]
                wv[j, cell_spans(t)[i], :] = w
                v = w
                for off in range(9):
                    by = near_shift(t, off)
                    moved = pltpu.roll(w, (CELLS[t] - by) % CELLS[t], 0) if by else w
                    v = v + moved * (near[off, place_span[t], :] * kernel[off : off + 1])
                for h in (2 * t, 2 * t + 1):
                    seg_rows = slice(*SEGS[h])
                    kb[j, i, seg_rows, :] = jnp.where(head_lanes(h), keys[part], 0.0).astype(bf16)
                    vbd[j, i, seg_rows, :] = jnp.where(head_lanes(h), v, 0.0).astype(bf16)
        for i in range(n):
            span = slice(i * TOK, (i + 1) * TOK)
            scores = nt(kb[j, i], q_a[j, span, :])
            for h, (low, top) in enumerate(SEGS):
                mask = kmask[i, place_span[h // 2], 0:1] > 0
                for c0 in range(0, TOK, 128):
                    c1 = min(c0 + 128, TOK)
                    s = jnp.where(mask, scores[low:top, c0:c1], -1e30)
                    e = jnp.exp2((s - jnp.max(s, axis=0, keepdims=True)) * (ROOT * LOG2E))
                    weight = e * pl.reciprocal(jnp.sum(e, axis=0, keepdims=True), approx=True)
                    pt[j, i, low:top, c0:c1] = weight.astype(bf16)
            mixed = tn(vbd[j, i], pt[j, i])
            o_t[j, i] = mixed.astype(bf16)
            o_n[span, :] = mixed.T.astype(bf16)
        for i in range(n):
            span = slice(i * TOK, (i + 1) * TOK)
            branch = nn(o_n[span, :], pw[j]) + row(pb, j)
            xs[span, :] = (xs[span, :] + scaled(span, 2 * j) * branch).astype(bf16).astype(f32)

    def build_wc(j):
        bias = row(hb, j)
        for r0 in range(0, C, 16):
            weight = hw[j, r0 : r0 + 16, :].astype(f32)
            for off in range(TAPS):
                factor = mk[off, pl.ds(j, 1), :] + (1.0 if off == 4 else 0.0)
                wc[j, off * C + r0 : off * C + r0 + 16, :] = (weight * factor).astype(bf16)
        ex[...] = jnp.zeros_like(ex)
        for off in range(TAPS + 1):
            at = off if off < TAPS else 16
            value = bias * mk[off, pl.ds(j, 1), :] if off < TAPS else bias + row(mb, j)
            high = value.astype(bf16).astype(f32)
            ex[at : at + 1, :] = high
            ex[at + 32 : at + 33, :] = value - high
        wc[j, TAPS * C :, :] = ex[...].astype(bf16)

    def mlp_forward(j):
        def first(ts):
            xhat, scale = norm_parts(xs[ts, :])
            xh_m[j, ts, :] = xhat
            sc[j, ts, 1:2] = scale
            u = (xhat * row(ng, j, 3) + row(ns, j, 3)).astype(bf16).astype(f32)
            acc[ts, :] = u * valid[ts, :]

        tiles(first)
        for i in range(n):
            span = slice(i * TOK, (i + 1) * TOK)
            for off, piece in taps_of(acc[span, :]):
                u_all[j, span, off * C : (off + 1) * C] = piece.astype(bf16)

        for i in range(n):
            field = nn(u_all[j, i * TOK : (i + 1) * TOK, :], wc[j])
            for r0 in range(0, TOK, 16):
                part = slice(i * TOK + r0, i * TOK + r0 + 16)
                for start in range(0, FF, CHUNK):
                    cols = slice(start, start + CHUNK)
                    act, slope = gelu_parts(field[r0 : r0 + 16, cols])
                    a_all[j, part, cols] = act.astype(bf16)
                    g_all[j, part, cols] = slope.astype(bf16)
        for i in range(n):
            span = slice(i * TOK, (i + 1) * TOK)
            branch = nn(a_all[j, span, :], ow[j]) + row(ob, j)
            xs[span, :] = (xs[span, :] + scaled(span, 2 * j + 1) * branch).astype(bf16).astype(f32)

    def mlp_backward(j):
        sb = j * S_BLOCK

        def first(ts):
            grad = (xs[ts, :] * scaled(ts, 2 * j + 1)).astype(bf16)
            db[ts, :] = grad
            return [folded(grad.astype(f32))]

        (small[sb + S_OB : sb + S_OB + 1, :],) = tiles(first)
        db_t[j] = db[...].T
        for i in range(n):
            span = slice(i * TOK, (i + 1) * TOK)
            da = nt(db[span, :], ow[j])
            g_all[j, span, :] = (da * g_all[j, span, :].astype(f32)).astype(bf16)
        if j == 0:
            move((0, 1))
        for i in range(n):
            span = slice(i * TOK, (i + 1) * TOK)
            moved = nt(g_all[j, span, :], wc[j, : TAPS * C, :])
            sides = []
            for col_off in range(3):
                total = None
                for row_off in range(3):
                    off = row_off * 3 + col_off
                    piece = shifted_rows(moved[:, off * C : (off + 1) * C], (1 - row_off) * GRID)
                    total = piece if total is None else total + piece
                sides.append(total)
            left = pltpu.roll(jnp.where(col > 0, sides[0], 0.0), TOK - 1, 0)
            right = pltpu.roll(jnp.where(col < GRID - 1, sides[2], 0.0), 1, 0)
            acc[span, :] = (sides[1] + left + right) * valid[span, :]

        if j == 0:
            mlp_weights(1, 0)

        def last(ts):
            du = acc[ts, :]
            xhat = xh_m[j, ts, :]
            back = norm_back(du, xhat, sc[j, ts, 1:2], row(ng, j, 3))
            xs[ts, :] = (xs[ts, :] + back).astype(bf16).astype(f32)
            return [folded(du * xhat), folded(du)]

        gain, shift = tiles(last)
        small[sb + S_GAIN + 3 : sb + S_GAIN + 4, :] = gain
        small[sb + S_SHIFT + 3 : sb + S_SHIFT + 4, :] = shift

    def mlp_turn(j):
        for off in range(TAPS + 1):
            ut[j, off * C : (off + 1) * C, :] = u_all[j, :, off * C : (off + 1) * C].T

    def mlp_weights(j, step):
        base, sb = MLP_AT[0] + j * (MLP_AT[1] - MLP_AT[0]), j * S_BLOCK
        cols = slice(step * CHUNK, (step + 1) * CHUNK)
        dow = nn(db_t[j], a_all[j, :, cols])
        gp[packed(base + output_row(step), CHUNK), :] = dow.T.astype(bf16)
        cross = nn(ut[j], g_all[j, :, cols])
        flag_rows = cross[TAPS * C : TAPS * C + 24]
        total = flag_rows[16:17]
        dhb = total
        weight = hw[j, :, cols].astype(f32)
        dweight = jnp.zeros((C, CHUNK), f32)
        b = hb[pl.ds(j, 1), cols]
        for off in range(TAPS):
            piece = cross[off * C : (off + 1) * C]
            factor = mk[off, pl.ds(j, 1), cols]
            flag = flag_rows[off : off + 1]
            dweight = dweight + piece * (factor + (1.0 if off == 4 else 0.0))
            dk = col_sum(piece * weight) + b * flag
            dhb = dhb + factor * flag
            for s in range(CHUNK // C):
                tile = step * (CHUNK // C) + s
                put(sb + S_MK + 16 * tile + off, dk[:, s * C : (s + 1) * C])
        for s in range(CHUNK // C):
            tile = step * (CHUNK // C) + s
            part = slice(s * C, (s + 1) * C)
            put(sb + S_HB + tile, dhb[:, part])
            put(sb + S_MB + tile, total[:, part])
            gp[packed(base + hidden_row(tile), C), :] = dweight[:, part].astype(bf16)

    def attention_backward(j):
        base, sb = ATT_AT[j], j * S_BLOCK

        def first(ts):
            grad = (xs[ts, :] * scaled(ts, 2 * j)).astype(bf16)
            db[ts, :] = grad
            return [folded(grad.astype(f32))]

        (small[sb + S_PB : sb + S_PB + 1, :],) = tiles(first)
        dproj = jnp.zeros((C, C), f32)
        kernel = jnp.concatenate([lk[j, :, 0, :], lk[j, :, 1, :]], axis=1)
        dkernel = [jnp.zeros((1, C), f32) for _ in range(9)]
        dbias = jnp.zeros((1, C), f32)
        for i in range(n):
            span = slice(i * TOK, (i + 1) * TOK)
            dproj = dproj + nn(o_t[j, i], db[span, :])
            do = nt(db[span, :], pw[j]).astype(bf16)
            dprobs = nt(vbd[j, i], do)
            dvals = nn(pt[j, i], do)
            for low, top in SEGS:
                for c0 in range(0, TOK, 128):
                    c1 = min(c0 + 128, TOK)
                    weight = pt[j, i, low:top, c0:c1].astype(f32)
                    dweight = dprobs[low:top, c0:c1]
                    dot = jnp.sum(weight * dweight, axis=0, keepdims=True)
                    pt[j, i, low:top, c0:c1] = (weight * (dweight - dot)).astype(bf16)
            dkeys = nn(pt[j, i], q_a[j, span, :]) * ROOT
            dq = tn(kb[j, i], pt[j, i]) * ROOT
            o_n[span, :] = dq.T.astype(bf16)
            for t in range(2):
                dk = jnp.zeros((CELLS[t], C), f32)
                dv = jnp.zeros((CELLS[t], C), f32)
                for h in (2 * t, 2 * t + 1):
                    dk = dk + jnp.where(head_lanes(h), dkeys[slice(*SEGS[h])], 0.0)
                    dv = dv + jnp.where(head_lanes(h), dvals[slice(*SEGS[h])], 0.0)
                w = wv[j, cell_spans(t)[i], :]
                dw = dv
                for off in range(9):
                    by = near_shift(t, off)
                    part = dv * near[off, place_span[t], :]
                    moved = pltpu.roll(w, (CELLS[t] - by) % CELLS[t], 0) if by else w
                    dkernel[off] = dkernel[off] + col_sum(part * moved)
                    part = part * kernel[off : off + 1]
                    dw = dw + (pltpu.roll(part, by, 0) if by else part)
                dw = dw * kmask[i, place_span[t], :]
                dbias = dbias + col_sum(dw)
                if t == 0:
                    dkeyval = dk + pltpu.roll(dw, 64, 1)
                else:
                    dkeyval = pltpu.roll(dk, 64, 1) + dw
                wv[j, cell_spans(t)[i], :] = dkeyval
            if j == 0 and i == 0:
                mlp_weights(1, 1)
        gp[base + R_PROJ : base + R_PROJ + C, :] = dproj.astype(bf16)
        small[sb + S_VB : sb + S_VB + 1, :] = dbias
        for off in range(9):
            small[sb + S_LK + off : sb + S_LK + off + 1, :] = dkernel[off]
        backs = []
        for t, (ref, weight) in enumerate(((p4, p4w), (p2, p2w))):
            span = cells_all(t)
            dkeyval = wv[j, span, :].astype(bf16)
            at = base + R_KV + t * C
            gp[at : at + C, :] = tn(kin[j, span, :], dkeyval).astype(bf16)
            dy = nt(dkeyval, kvw[j, t]) * ge_p[j, span, :]
            xhat = xh_p[j, span, :]
            small[sb + S_GAIN + 1 + t : sb + S_GAIN + 2 + t, :] = col_sum(dy * xhat)
            small[sb + S_SHIFT + 1 + t : sb + S_SHIFT + 2 + t, :] = col_sum(dy)
            dpool = norm_back(dy, xhat, sc_p[j, span, :], row(ng, j, 1 + t)).astype(bf16)
            at = base + (R_P4, R_P2)[t]
            for k in range(STRIDES[t] ** 2):
                gp[at + k * C : at + (k + 1) * C, :] = tn(
                    ref[j, :, k * C : (k + 1) * C], dpool
                ).astype(bf16)
                backs.append((t, nt(dpool, weight[j, k * C : (k + 1) * C, :])))
        at = base + R_Q
        gp[at : at + C, :] = tn(u_a[j], o_n[...]).astype(bf16)
        if j == 1:
            all_here()
            move((0, 0))
        else:
            move((1, 0), (2, 0), (0, 2))
        for i in range(n):
            span = slice(i * TOK, (i + 1) * TOK)
            acc[span, :] = nt(o_n[span, :], qw[j])
        for g in range(GROUPS):
            images_of = []
            for i in range(n):
                pieces = [
                    back[i * CELLS[t] + g * PATCH[t] : i * CELLS[t] + (g + 1) * PATCH[t]]
                    for t, back in backs
                ]
                images_of.append(jnp.concatenate(pieces, axis=0).astype(bf16))
            spread = nn(from_patches[...], jnp.concatenate(images_of, axis=1))
            for i in range(n):
                span = slice(i * TOK + g * GROUP, i * TOK + (g + 1) * GROUP)
                acc[span, :] += spread[:, i * C : (i + 1) * C] * valid[span, :]

        def last(ts):
            du = acc[ts, :]
            xhat = xh_a[j, ts, :]
            back = norm_back(du, xhat, sc[j, ts, 0:1], row(ng, j, 0))
            xs[ts, :] = (xs[ts, :] + back).astype(bf16).astype(f32)
            return [folded(o_n[ts, :].astype(f32)), folded(du * xhat), folded(du)]

        bias, gain, shift = tiles(last)
        small[sb + S_QB : sb + S_QB + 1, :] = bias
        small[sb + S_GAIN : sb + S_GAIN + 1, :] = gain
        small[sb + S_SHIFT : sb + S_SHIFT + 1, :] = shift

    def forward(j, carry):
        attention_forward(j)
        mlp_forward(j)
        return carry

    for made in late:
        made.wait()
    lax.fori_loop(0, BLOCKS, forward, 0)
    out_st[...] = xs[...].astype(bf16)
    leave(out_st, out_ref)
    xs[...] = cot_ref[...].astype(f32)
    mlp_backward(1)
    attention_backward(1)
    mlp_turn(1)
    mlp_backward(0)
    mlp_turn(0)
    attention_backward(0)
    dx_st[...] = xs[...].astype(bf16)
    leave(dx_st, dx_ref)
    move((1, 1), (2, 1))
    mlp_weights(0, 0)
    move((3, 0), (0, 3))
    mlp_weights(0, 1)
    gp[R_SMALL:, :] = small[...].astype(bf16)
    move((4, 0), (3, 1), (1, 2), (4, 1), (0, 4), (2, 2), (3, 2), (1, 3), (4, 2), (2, 3), (3, 3))
    move((0, 5), (1, 4), (4, 3), (0, 6), (2, 4), (3, 4), (4, 4), (1, 5), (1, 6), (2, 5), (3, 5))
    move((2, 6), (3, 6), (4, 5), (4, 6))
    for piece in pieces:
        piece.drain()
    for made in leaving:
        made.wait()


def compute(own, images, grid_size, keep_mask, x, cot, weights):
    segments, pairs = lax.axis_size("segment"), lax.axis_size("dp") // 2
    inner = min(pairs, 4)
    sizes = (segments, inner, pairs // inner)
    n = images
    rows = n * TOK
    cells = n * sum(CELLS)
    vmem = pl.BlockSpec(memory_space=pltpu.VMEM)
    smem = pl.BlockSpec(memory_space=pltpu.SMEM)
    matrix = patch_matrix()
    consts = (
        jnp.asarray(matrix, bf16),
        jnp.asarray(matrix.T, bf16),
        jnp.asarray(cell_places()),
    )
    B = BLOCKS
    scratch = [
        pltpu.VMEM((rows, C), f32),
        pltpu.VMEM((rows, C), f32),
        pltpu.VMEM((TOK, n * C), bf16),
        pltpu.VMEM((B, rows, UW), bf16),
        pltpu.VMEM((B, UW, rows), bf16),
        pltpu.VMEM((B, UW, FF), bf16),
        pltpu.VMEM((C, FF), f32),
        pltpu.VMEM((B, rows, C), f32),
        pltpu.VMEM((B, rows, C), f32),
        pltpu.VMEM((B, rows, C), f32),
        pltpu.VMEM((B, rows, C), bf16),
        pltpu.VMEM((B, rows, C), bf16),
        pltpu.VMEM((B, n * CELLS[0], 16 * C), bf16),
        pltpu.VMEM((B, n * CELLS[1], 4 * C), bf16),
        pltpu.VMEM((B, cells, C), f32),
        pltpu.VMEM((B, cells, C), f32),
        pltpu.VMEM((B, cells, C), f32),
        pltpu.VMEM((B, cells, C), bf16),
        pltpu.VMEM((B, cells, C), f32),
        pltpu.VMEM((B, n, KEYS, C), bf16),
        pltpu.VMEM((B, n, KEYS, C), bf16),
        pltpu.VMEM((B, n, KEYS, TOK), bf16),
        pltpu.VMEM((B, n, C, TOK), bf16),
        pltpu.VMEM((rows, C), bf16),
        pltpu.VMEM((B, rows, FF), bf16),
        pltpu.VMEM((B, rows, FF), bf16),
        pltpu.VMEM((rows, C), bf16),
        pltpu.VMEM((B, C, rows), bf16),
        pltpu.VMEM((rows, C), f32),
        pltpu.VMEM((n, sum(CELLS), C), f32),
        pltpu.VMEM((9, sum(CELLS), C), f32),
        pltpu.VMEM((ROWS - R_SMALL, C), f32),
        pltpu.SMEM((n, 2 * BLOCKS), f32),
        pltpu.VMEM(cot.shape, bf16),
        pltpu.VMEM(weights[HW].shape, bf16),
        pltpu.VMEM(weights[P4].shape, bf16),
        pltpu.VMEM(weights[P2].shape, bf16),
        pltpu.VMEM(weights[OW].shape, bf16),
        pltpu.VMEM((rows, C), bf16),
        pltpu.VMEM((rows, C), bf16),
        pltpu.SemaphoreType.DMA((7 + len(PIECES),)),
        pltpu.VMEM((ROWS, C), bf16),
    ] + sum_scratch(sizes)
    anywhere = pl.BlockSpec(memory_space=pl.ANY)
    operands = [vmem] * (2 + len(weights) + len(consts))
    for place in (1, 2 + HW, 2 + P4, 2 + P2, 2 + OW):
        operands[place] = anywhere
    return pl.pallas_call(
        functools.partial(compute_kernel, own, images, sizes),
        out_shape=(
            jax.ShapeDtypeStruct((rows, C), bf16),
            jax.ShapeDtypeStruct((rows, C), bf16),
            jax.ShapeDtypeStruct((ROWS, C), bf16),
        ),
        in_specs=[smem, smem] + operands,
        out_specs=(anywhere,) * 3,
        scratch_shapes=scratch,
        compiler_params=pltpu.CompilerParams(
            collective_id=0, has_side_effects=True, vmem_limit_bytes=63 * 2**20
        ),
        name="compute",
    )(grid_size, keep_mask, x, cot, *weights, *consts)


def unpack_kernel(att, mlp, rest, out_in, dx_in, *refs):
    out_ref, dx_ref = refs[:2]
    gain, shift, qw, qb, p4, p2, kvw, vb, lk, pw, pb, hw, hb, mk, mb, ow, ob = refs[2:]
    out_ref[...] = out_in[...]
    dx_ref[...] = dx_in[...]
    p4[0] = att[R_P4:R_P2, :].astype(f32)
    p2[0] = att[R_P2:R_KV, :].astype(f32)
    for t in range(2):
        kvw[0, t] = att[R_KV + t * C : R_KV + (t + 1) * C, :].astype(f32)
    qw[0] = att[R_Q:R_PROJ, :].astype(f32)
    pw[0] = att[R_PROJ:R_ATT, :].astype(f32)
    for s in range(FF // C):
        hw[0, :, s * C : (s + 1) * C] = mlp[hidden_row(s) : hidden_row(s) + C, :].astype(f32)
    for step in range(FF // CHUNK):
        at = output_row(step)
        ow[0, step * CHUNK : (step + 1) * CHUNK, :] = mlp[at : at + CHUNK, :].astype(f32)

    @pl.when(pl.program_id(0) == BLOCKS - 1)
    def _():
        for j in range(BLOCKS):
            sb = j * S_BLOCK
            head = rest[sb : sb + 48, :].astype(f32)
            gain[j] = head[S_GAIN : S_GAIN + 4]
            shift[j] = head[S_SHIFT : S_SHIFT + 4]
            qb[j : j + 1, :] = head[S_QB : S_QB + 1]
            vb[j, 0:1, :] = head[S_VB : S_VB + 1, 0:64]
            vb[j, 1:2, :] = head[S_VB : S_VB + 1, 64:128]
            pb[j : j + 1, :] = head[S_PB : S_PB + 1]
            ob[j : j + 1, :] = head[S_OB : S_OB + 1]
            lk[j, :, 0, :] = head[S_LK : S_LK + 9, 0:64]
            lk[j, :, 1, :] = head[S_LK : S_LK + 9, 64:128]
            for s in range(FF // C):
                part = slice(s * C, (s + 1) * C)
                hb[j : j + 1, part] = head[S_HB + s : S_HB + s + 1]
                mb[j : j + 1, part] = head[S_MB + s : S_MB + s + 1]
                at = sb + S_MK + 16 * s
                mk[:, j, part] = rest[at : at + 16, :].astype(f32)[0:9]


def unpack(packed, outputs, input_grad, weights):
    streams = (jax.ShapeDtypeStruct(outputs.shape, bf16),) * 2
    by_block = {QW, P4, P2, KVW, PW, HW, OW}
    rest = ROWS - R_SMALL
    stream = pl.BlockSpec((outputs.shape[0] // BLOCKS, C), lambda k: (k, 0))
    specs = []
    for place, w in enumerate(weights):
        if place in by_block:
            zeros = (0,) * (w.ndim - 1)
            specs.append(pl.BlockSpec((1,) + w.shape[1:], lambda k, z=zeros: (BLOCKS - 1 - k,) + z))
        else:
            zeros = (0,) * w.ndim
            specs.append(pl.BlockSpec(w.shape, lambda k, z=zeros: z))
    return pl.pallas_call(
        unpack_kernel,
        out_shape=streams + tuple(jax.ShapeDtypeStruct(w.shape, f32) for w in weights),
        grid=(BLOCKS,),
        in_specs=[
            pl.BlockSpec((R_ATT, C), lambda k: (k, 0)),
            pl.BlockSpec((R_MLP, C), lambda k: (MLP_AT[BLOCKS - 1] // R_MLP + k, 0)),
            pl.BlockSpec((rest, C), lambda k: (R_SMALL // rest, 0)),
            stream,
            stream,
        ],
        out_specs=(stream, stream) + tuple(specs),
        compiler_params=pltpu.CompilerParams(vmem_limit_bytes=63 * 2**20),
        name="unpack",
    )(packed, packed, packed, outputs, input_grad)


def on_device(inputs, grid_size, keep_mask, cotangent, *weights):
    own, per = inputs.shape[:2]
    images = own * per
    flat = (images * TOK, C)
    turned = list(weights)
    turned[LK] = jnp.transpose(turned[LK], (0, 2, 1, 3))
    turned[MK] = jnp.transpose(turned[MK], (1, 0, 2))
    outputs, input_grad, packed = compute(
        own,
        images,
        jnp.transpose(grid_size, (1, 2, 0)),
        jnp.transpose(keep_mask, (1, 2, 0)),
        inputs.reshape(flat),
        cotangent.reshape(flat),
        turned,
    )
    outputs, input_grad, *grads = unpack(packed, outputs, input_grad, turned)
    grads[LK] = jnp.transpose(grads[LK], (0, 2, 1, 3))
    grads[MK] = jnp.transpose(grads[MK], (1, 0, 2))
    return (outputs.reshape(inputs.shape), input_grad.reshape(inputs.shape)) + tuple(grads)


def solution(mesh):
    stream = P("segment", "dp", None, None)
    picked = P(None, "dp", None)
    return jax.shard_map(
        on_device,
        mesh=mesh,
        in_specs=(stream, picked, picked, stream) + (P(),) * 17,
        out_specs=(stream, stream) + (P(),) * 17,
        check_vma=False,
    )
```
